32 devices in a mesh: dp: 8 (over y, x, core), tensor: 4 (over z).
Axes of the slice: x: 2, y: 2, z: 4, core: 2. Of those that a mesh axis runs over, the one named last changes fastest.
Arguments:
- inputs: bfloat16 [2, 8, 1024, 1024], P(None, 'dp', 'tensor'), may hold values from -6 to 6
- cotangent: bfloat16 [2, 8, 1024, 1024], P(None, 'dp', 'tensor'), may hold values from -6 to 6
- lengths: int32 [2, 8], P(None, 'dp'), may hold values from 256 to 1024, as said below
- qkv_weight: bfloat16 [1024, 3, 1024], P('dp', None, 'tensor'), may hold values from -0.1875 to 0.1875
- attn_out_weight: bfloat16 [1024, 1024], P('dp', 'tensor'), may hold values from -1.5 to 1.5
- ffn_in_weight: bfloat16 [1024, 2, 2624], P('dp', None, 'tensor'), may hold values from -0.1875 to 0.1875
- ffn_out_weight: bfloat16 [1024, 2624], P('dp', 'tensor'), may hold values from -0.125 to 0.125
- norm_gains: float32 [2, 1024], replicated, may hold values from 0.5 to 1.5
- qkv_moment: float32 [1024, 3, 1024], P('dp', None, 'tensor'), may hold values from -384 to 384
- attn_out_moment: float32 [1024, 1024], P('dp', 'tensor'), may hold values from -64 to 64
- ffn_in_moment: float32 [1024, 2, 2624], P('dp', None, 'tensor'), may hold values from -320 to 320
- ffn_out_moment: float32 [1024, 2624], P('dp', 'tensor'), may hold values from -512 to 512
- gain_first: float32 [2, 1024], replicated, may hold values from -80 to 80
- gain_second: float32 [2, 1024], replicated, may hold values from 655.36 to 2621.44
Outputs:
- outputs: bfloat16 [2, 8, 1024, 1024], P(None, 'dp', 'tensor')
- input_grad: float32 [2, 8, 1024, 1024], P(None, 'dp', 'tensor')
- qkv_moment_new: float32 [1024, 3, 1024], P('dp', None, 'tensor')
- qkv_weight_new: float32 [1024, 3, 1024], P('dp', None, 'tensor')
- attn_out_moment_new: float32 [1024, 1024], P('dp', 'tensor')
- attn_out_weight_new: float32 [1024, 1024], P('dp', 'tensor')
- ffn_in_moment_new: float32 [1024, 2, 2624], P('dp', None, 'tensor')
- ffn_in_weight_new: float32 [1024, 2, 2624], P('dp', None, 'tensor')
- ffn_out_moment_new: float32 [1024, 2624], P('dp', 'tensor')
- ffn_out_weight_new: float32 [1024, 2624], P('dp', 'tensor')
- gain_first_new: float32 [2, 1024], replicated
- gain_second_new: float32 [2, 1024], replicated
- norm_gains_new: float32 [2, 1024], replicated
The draws below stay inside these ranges and needn't reach their ends.
Inputs may be any that keep to these rules, and one draw needn't show every extreme that they name: lengths[m, s] counts the real tokens of sequence s of micro-batch m, which stand first in its slot; in every column s some micro-batch's sequence fills its whole slot of 1024.
All inputs are finite; a program needn't handle non-finite values.
Results may differ from the reference program's by a relative error of at most 0.013.
Values may be sent and summed in bfloat16 or wider, within the bound.
A program may use at most 192 MiB of HBM per device.

```python
import math
import jax
import jax.numpy as jnp
from jax import lax

D = 1024
HEADS = 16
FF = 2624
HEAD_DIM = 64
SEQ = 1024
MB = 2
NS_ITERS = 5
STEP = 10
NSEQ = 8


def draw_lengths(key, part):
    first_key, second_key = jax.random.split(key)
    base_lengths = jax.random.randint(first_key, (MB, NSEQ), SEQ // 4, SEQ + 1)
    chosen = jax.random.randint(second_key, (NSEQ,), 0, MB)
    longest = jnp.arange(MB)[:, None] == chosen[None, :]
    return jnp.where(longest, SEQ, base_lengths).astype(jnp.int32)


def level_of(rng, shape, pieces, low, high):
    level, own = 1.0, jax.random.fold_in(rng, 6)
    for axis_at, shards_of in pieces:
        draws = jnp.exp(jax.random.uniform(jax.random.fold_in(own, axis_at), (shards_of,), jnp.float32, low / len(pieces), high / len(pieces)))
        level = level * jnp.repeat(draws, shape[axis_at] // shards_of).reshape([-1 if axis == axis_at else 1 for axis in range(len(shape))])
    return level


def centred(own_key, shape, deviation, most, cuts=(), dtype=jnp.bfloat16):
    factor_of = level_of(own_key, shape, cuts, -0.22, 0.18) if cuts else 1.0
    entries = jax.random.normal(own_key, shape, jnp.float32) * deviation * factor_of
    return jnp.minimum(jnp.maximum(entries, -most), most).astype(dtype)


def setup_inputs(seed: int = 0) -> dict:
    arg_keys = jax.random.split(jax.random.key(seed), 15)
    return {
        "inputs": centred(arg_keys[0], (MB, NSEQ, SEQ, D), 1.0, 6.0, ((1, 8), (2, 4))),
        "cotangent": centred(arg_keys[1], (MB, NSEQ, SEQ, D), 1.0, 6.0, ((1, 8), (2, 4))),
        "lengths": draw_lengths(jax.random.fold_in(arg_keys[14], 71), 0),
        "qkv_weight": centred(arg_keys[3], (D, 3, D), D ** -0.5, 0.1875, ((0, 8), (2, 4))),
        "attn_out_weight": centred(arg_keys[4], (D, D), (D // 64) ** -0.5, 1.5, ((0, 8), (1, 4))),
        "ffn_in_weight": centred(arg_keys[5], (D, 2, FF), D ** -0.5, 0.1875, ((0, 8), (2, 4))),
        "ffn_out_weight": centred(arg_keys[6], (D, FF), FF ** -0.5, 0.125, ((0, 8), (1, 4))),
        "norm_gains": jnp.clip(1.0 + 0.1 * jax.random.normal(arg_keys[7], (2, D), jnp.float32), 0.5, 1.5),
        "qkv_moment": centred(arg_keys[8], (D, 3, D), (0.5 * (MB * NSEQ * SEQ) ** 0.5), 384.0, ((0, 8), (2, 4)), jnp.float32),
        "attn_out_moment": centred(arg_keys[9], (D, D), (0.08 * (MB * NSEQ * SEQ) ** 0.5), 64.0, ((0, 8), (1, 4)), jnp.float32),
        "ffn_in_moment": centred(arg_keys[10], (D, 2, FF), (0.4 * (MB * NSEQ * SEQ) ** 0.5), 320.0, ((0, 8), (2, 4)), jnp.float32),
        "ffn_out_moment": centred(arg_keys[11], (D, FF), (0.65 * (MB * NSEQ * SEQ) ** 0.5), 512.0, ((0, 8), (1, 4)), jnp.float32),
        "gain_first": centred(arg_keys[12], (2, D), (0.1 * (MB * NSEQ * SEQ) ** 0.5), 80.0, (), jnp.float32),
        "gain_second": jnp.clip(jnp.exp(jax.random.uniform(arg_keys[13], (2, D), jnp.float32, math.log(655.36), math.log(2621.44))), 655.36, 2621.44),
    }


@jax.custom_vjp
def low(v):
    return lax.optimization_barrier(v.astype(jnp.bfloat16)).astype(jnp.float32)

@jax.custom_vjp
def low_back(v):
    return v

def low_keep(v):
    return (low(v), None)

def low_pass(kept, grad):
    return (grad,)

def back_keep(v):
    return (v, None)

def back_low(kept, grad):
    return (low(grad),)
low.defvjp(low_keep, low_pass)
low_back.defvjp(back_keep, back_low)
ROPE_BASE = 160000.0
NORM_EPS = 1e-05
MASK_VALUE = -1e+30
MOMENTUM = 0.95
MUON_RATE = 0.1
DECAY_RATE = 0.01
QUINTIC_ONE = 3.4445
QUINTIC_THREE = -4.775
QUINTIC_FIVE = 2.0315
NORM_FLOOR = 1e-07
BETA_ONE = 0.9
BETA_TWO = 0.95
ADAM_RATE = 0.2
ADAM_EPS = 1e-08

def rotary(length):
    half_size = HEAD_DIM // 2
    exponents = jnp.arange(half_size).astype(jnp.float32) / half_size
    frequency = jnp.power(ROPE_BASE, -exponents)
    angles = jnp.arange(length).astype(jnp.float32)[:, None] * frequency[None, :]
    return (jnp.cos(angles), jnp.sin(angles))

def rotate(vectors, cosine_table, sine_table):
    half_size = vectors.shape[-1] // 2
    first_half = vectors[..., :half_size]
    second_half = vectors[..., half_size:]
    cos_part = cosine_table[:, None, :]
    sin_part = sine_table[:, None, :]
    return jnp.concatenate([first_half * cos_part - second_half * sin_part, second_half * cos_part + first_half * sin_part], axis=-1)

def layer_norm(vectors, gain):
    centre = vectors - lax.optimization_barrier(jnp.mean(vectors, axis=-1, keepdims=True))
    variance = lax.optimization_barrier(jnp.mean(centre * centre, axis=-1, keepdims=True))
    return centre * lax.rsqrt(variance + NORM_EPS) * gain

def matmul(left, right):
    return jnp.dot(left, right, precision=lax.Precision.HIGHEST)

def forward(rows_in, qkv_weight, attn_out_weight, ffn_in_weight, ffn_out_weight, norm_gains, length):
    seq_len = rows_in.shape[0]
    cosine_table, sine_table = rotary(seq_len)
    normed_one = low(layer_norm(rows_in, norm_gains[0]))
    projected = low_back(matmul(normed_one, qkv_weight.reshape(D, 3 * D))).reshape(seq_len, 3, HEADS, HEAD_DIM)
    queries = low(rotate(projected[:, 0], cosine_table, sine_table))
    key_rows = low(rotate(projected[:, 1], cosine_table, sine_table))
    values = low(projected[:, 2])
    scores = jnp.einsum('qhd,khd->hqk', queries, key_rows, precision=lax.Precision.HIGHEST) * (1.0 / math.sqrt(HEAD_DIM))
    scores = low_back(scores)
    key_valid = jnp.arange(seq_len) < length
    scores = jnp.where(key_valid[None, None, :], scores, MASK_VALUE)
    probabilities = low(jax.nn.softmax(scores, axis=-1))
    context = jnp.einsum('hqk,khd->qhd', probabilities, values, precision=lax.Precision.HIGHEST)
    context = low(low_back(context)).reshape(seq_len, D)
    branch = low_back(matmul(context, attn_out_weight.T))
    middle = rows_in + branch
    normed_two = low(layer_norm(middle, norm_gains[1]))
    gate_up = low_back(matmul(normed_two, ffn_in_weight.reshape(D, 2 * FF)))
    hidden = low(jax.nn.gelu(gate_up[:, :FF], approximate=False) * gate_up[:, FF:])
    return middle + low_back(matmul(hidden, ffn_out_weight.T))

def muon(weight, moment, gradient):
    moment_new = MOMENTUM * moment + gradient
    matrix = moment_new.reshape(D, -1)
    full_width = matrix.shape[1]
    matrix = matrix / (jnp.sqrt(jnp.sum(matrix * matrix)) + NORM_FLOOR)
    for sweep_index in range(NS_ITERS):
        gram_matrix = matmul(matrix, matrix.T)
        product = matmul(gram_matrix, matrix)
        matrix = QUINTIC_ONE * matrix + QUINTIC_THREE * product + QUINTIC_FIVE * matmul(gram_matrix, product)
    ortho_step = matrix.reshape(weight.shape)
    weight_new = weight * (1.0 - MUON_RATE * DECAY_RATE) - MUON_RATE * 0.2 * math.sqrt(full_width) * ortho_step
    return (moment_new, weight_new)

def reference(inputs, cotangent, lengths, qkv_weight, attn_out_weight, ffn_in_weight, ffn_out_weight, norm_gains, qkv_moment, attn_out_moment, ffn_in_moment, ffn_out_moment, gain_first, gain_second):
    params = (qkv_weight.astype(jnp.float32), attn_out_weight.astype(jnp.float32), ffn_in_weight.astype(jnp.float32), ffn_out_weight.astype(jnp.float32), norm_gains)
    seq_total = MB * NSEQ
    rows_all = inputs.astype(jnp.float32).reshape(seq_total, SEQ, D)
    grads_all = cotangent.astype(jnp.float32).reshape(seq_total, SEQ, D)
    spans = lengths.reshape(seq_total)

    def one_sequence(totals, entry):
        rows_in, grad_rows, span_value = entry

        def run_layer(rows_arg, qkv_arg, attn_arg, ffn_in_arg, ffn_out_arg, gains_arg):
            return forward(rows_arg, qkv_arg, attn_arg, ffn_in_arg, ffn_out_arg, gains_arg, span_value)
        result, pull_back = jax.vjp(run_layer, rows_in, *params)
        pulled = pull_back(grad_rows)
        totals = tuple((total_part + grad_part for total_part, grad_part in zip(totals, pulled[1:])))
        return (totals, (result.astype(jnp.bfloat16), pulled[0]))
    initial = tuple((jnp.zeros_like(param) for param in params))
    totals, (result_rows, input_rows) = lax.scan(one_sequence, initial, (rows_all, grads_all, spans))
    outputs = result_rows.reshape(MB, NSEQ, SEQ, D)
    input_grad = input_rows.reshape(MB, NSEQ, SEQ, D)
    qkv_moment_new, qkv_weight_new = muon(params[0], qkv_moment, totals[0])
    attn_out_moment_new, attn_out_weight_new = muon(params[1], attn_out_moment, totals[1])
    ffn_in_moment_new, ffn_in_weight_new = muon(params[2], ffn_in_moment, totals[2])
    ffn_out_moment_new, ffn_out_weight_new = muon(params[3], ffn_out_moment, totals[3])
    gain_grad = totals[4]
    gain_first_new = BETA_ONE * gain_first + (1.0 - BETA_ONE) * gain_grad
    gain_second_new = BETA_TWO * gain_second + (1.0 - BETA_TWO) * gain_grad * gain_grad
    first_hat = gain_first_new / (1.0 - BETA_ONE ** STEP)
    second_hat = gain_second_new / (1.0 - BETA_TWO ** STEP)
    norm_gains_new = norm_gains - ADAM_RATE * (first_hat / (jnp.sqrt(second_hat) + ADAM_EPS) + DECAY_RATE * norm_gains)
    return (outputs, input_grad, qkv_moment_new, qkv_weight_new, attn_out_moment_new, attn_out_weight_new, ffn_in_moment_new, ffn_in_weight_new, ffn_out_moment_new, ffn_out_weight_new, gain_first_new, gain_second_new, norm_gains_new)
```

```python
import functools
import math

import jax
import jax.numpy as jnp
from jax import lax
from jax.experimental import pallas as pl
from jax.experimental.pallas import tpu as pltpu
from jax.sharding import PartitionSpec as P

HEAD_DIM = 64
NS_ITERS = 5
STEP = 10


ROPE_BASE = 160000.0
NORM_EPS = 1e-05
MASK_VALUE = -1e30
MOMENTUM = 0.95
MUON_RATE = 0.1
DECAY_RATE = 0.01
QUINTIC_ONE = 3.4445
QUINTIC_THREE = -4.775
QUINTIC_FIVE = 2.0315
NORM_FLOOR = 1e-07
BETA_ONE = 0.9
BETA_TWO = 0.95
ADAM_RATE = 0.2
ADAM_EPS = 1e-08
BOTH = ("dp", "tensor")
MESH = pl.DeviceIdType.MESH


def rotary(first, length):
    half_size = HEAD_DIM // 2
    exponents = jnp.arange(half_size).astype(jnp.float32) / half_size
    frequency = jnp.power(ROPE_BASE, -exponents)
    positions = (first + jnp.arange(length)).astype(jnp.float32)
    angles = positions[:, None] * frequency[None, :]
    return (jnp.cos(angles), jnp.sin(angles))


def rotate(vectors, cosine_table, sine_table):
    half_size = vectors.shape[-1] // 2
    first_half = vectors[..., :half_size]
    second_half = vectors[..., half_size:]
    cos_part = cosine_table[:, None, :]
    sin_part = sine_table[:, None, :]
    return jnp.concatenate(
        [
            first_half * cos_part - second_half * sin_part,
            second_half * cos_part + first_half * sin_part,
        ],
        axis=-1,
    )


def layer_norm_parts(vectors, gain):
    centre = vectors - jnp.mean(vectors, axis=-1, keepdims=True)
    inverse = lax.rsqrt(jnp.mean(centre * centre, axis=-1, keepdims=True) + NORM_EPS)
    normed = centre * inverse
    return (normed, inverse, normed * gain)


def layer_norm_back(grad_out, normed, inverse, gain):
    grad_normed = grad_out * gain
    mean_grad = jnp.mean(grad_normed, axis=-1, keepdims=True)
    mean_cross = jnp.mean(grad_normed * normed, axis=-1, keepdims=True)
    return (
        inverse * (grad_normed - mean_grad - normed * mean_cross),
        jnp.sum(grad_out * normed, axis=0),
    )


def einsum(spec, *operands):
    return jnp.einsum(spec, *operands, preferred_element_type=jnp.float32)


def low(values):
    return values.astype(jnp.bfloat16)


def attention_forward(queries, key_rows, values, key_valid):
    score_scale = 1.0 / math.sqrt(queries.shape[-1])
    scores = einsum("qhd,khd->hqk", queries, key_rows) * score_scale
    scores = jnp.where(key_valid, scores, MASK_VALUE)
    highest = jnp.max(scores, axis=-1, keepdims=True)
    exponent = jnp.exp(scores - highest)
    row_total = jnp.sum(exponent, axis=-1, keepdims=True)
    context = einsum("hqk,khd->qhd", low(exponent / row_total), values)
    return (context, highest[..., 0] + jnp.log(row_total[..., 0]))


def attention_backward(queries, key_rows, values, log_total, grad_context, key_valid):
    score_scale = 1.0 / math.sqrt(queries.shape[-1])
    scores = einsum("qhd,khd->hqk", queries, key_rows) * score_scale
    scores = jnp.where(key_valid, scores, MASK_VALUE)
    soft_weights = jnp.exp(scores - log_total[..., None])
    grad_probs = einsum("qhd,khd->hqk", grad_context, values)
    inner_sum = jnp.sum(soft_weights * grad_probs, axis=-1, keepdims=True)
    grad_scores = low(soft_weights * (grad_probs - inner_sum))
    grad_query = einsum("hqk,khd->qhd", grad_scores, key_rows) * score_scale
    grad_keys = einsum("hqk,qhd->khd", grad_scores, queries) * score_scale
    grad_values = einsum("hqk,qhd->khd", low(soft_weights), grad_context)
    return (grad_query, grad_keys, grad_values)


def exchange_lists(chip_count, tensor_count):
    first_list, second_list = [], []
    for chip in range(chip_count):
        for core in range(2):
            for slot in range(tensor_count):
                for micro in range(2):
                    source = (2 * chip + core) * tensor_count + slot
                    target = (2 * chip + slot // 2) * tensor_count + 2 * micro + core
                    pair = (source, target)
                    (first_list if slot % 2 == micro else second_list).append(pair)
    return (first_list, second_list)


def to_sequences(blocks, lists, odd, upper):
    first = lax.ppermute(jnp.where(odd, blocks[1], blocks[0]), BOTH, lists[0])
    second = lax.ppermute(jnp.where(odd, blocks[0], blocks[1]), BOTH, lists[1])
    return jnp.where(
        upper, jnp.concatenate([second, first]), jnp.concatenate([first, second])
    )


def from_sequences(rows, lists, odd, upper):
    half = rows.shape[0] // 2
    top, bottom = rows[:half], rows[half:]
    back = [[(target, source) for source, target in pairs] for pairs in lists]
    first = lax.ppermute(jnp.where(upper, bottom, top), BOTH, back[0])
    second = lax.ppermute(jnp.where(upper, top, bottom), BOTH, back[1])
    return jnp.where(odd, jnp.stack([second, first]), jnp.stack([first, second]))


def swap_partner(values):
    count = lax.axis_size("dp")
    return lax.ppermute(values, "dp", [(index, index ^ 1) for index in range(count)])


def mean_split(matrix):
    mean = jnp.trace(matrix) / matrix.shape[0]
    return (mean, matrix - mean * jnp.eye(matrix.shape[0], dtype=jnp.float32))


def split_product(left, right):
    left_mean, left_rest = left
    right_mean, right_rest = right
    product = einsum("ij,jk->ik", low(left_rest), low(right_rest))
    product = product + left_mean * right_rest + right_mean * left_rest
    mean, rest = mean_split(product)
    return (mean + left_mean * right_mean, rest)


def newton_schulz(gram):
    factor = 1.0 / (jnp.sqrt(jnp.trace(gram)) + NORM_FLOOR)
    iterate = mean_split(gram * (factor * factor))
    whole = None
    for sweep_index in range(NS_ITERS):
        square = split_product(iterate, iterate)
        poly = (
            QUINTIC_ONE + QUINTIC_THREE * iterate[0] + QUINTIC_FIVE * square[0],
            QUINTIC_THREE * iterate[1] + QUINTIC_FIVE * square[1],
        )
        whole = poly if whole is None else split_product(poly, whole)
        if sweep_index < NS_ITERS - 1:
            iterate = split_product(poly, split_product(poly, iterate))
    return (whole[0] * factor, whole[1] * factor)


def step_of(rows):
    return next(step for step in (128, 64, 32, 16) if rows % step == 0)


def lanes(block):
    return pl.ds(pl.multiple_of(block * 128, 128), 128)

def neighbours():
    me = lax.axis_index("dp")
    core, across, down = lax.rem(me, 2), lax.rem(lax.div(me, 2), 2), lax.div(me, 4)
    return (me, me + 1 - 2 * core, me + 2 - 4 * across, me + 4 - 8 * down)

def greet(plane, others, planes):
    barrier = pltpu.get_barrier_semaphore()
    me = lax.axis_index("dp")
    for other in others:
        pl.semaphore_signal(barrier, inc=1, device_id=(other, plane), device_id_type=MESH)
    for other in planes:
        pl.semaphore_signal(barrier, inc=1, device_id=(me, other), device_id_type=MESH)
    pl.semaphore_wait(barrier, len(others) + len(planes))

def gather_kernel(count, *refs):
    shards, wholes = refs[:count], refs[count : 2 * count]
    (own_sem, send_z, recv_z, send_x, recv_x, send_y, recv_y, send_d, recv_d, send_c, recv_c) = refs[2 * count :]
    me, partner, across, down = neighbours()
    plane = lax.axis_index("tensor")
    diagonal = across + down - me
    planes = [lax.rem(plane + offset, 4) for offset in (1, 2, 3)]
    greet(plane, (partner, across, down), planes)
    started = []

    def remote(source, target, send, recv, device):
        copy = pltpu.make_async_remote_copy(source, target, send, recv, device_id=device, device_id_type=MESH)
        copy.start()
        started.append(copy)

    def spread(part, source, slot, block):
        view = wholes[part].at[slot, :, lanes(block)]
        remote(source, view, send_x.at[part, slot], recv_x.at[part, slot], (across, plane))
        remote(source, view, send_y.at[part, slot], recv_y.at[part, slot], (down, plane))
        remote(source, view, send_c.at[part, slot, 0], recv_c.at[part, slot, 0], (partner, plane))

    def landed(part, slot, block, sem):
        view = wholes[part].at[slot, :, lanes(block)]
        pltpu.make_async_copy(view, view, sem).wait()
        return view

    locals_ = []
    def stage_first(part):
        view = wholes[part].at[plane, :, lanes(me)]
        copy = pltpu.make_async_copy(shards[part], view, own_sem.at[part])
        copy.start()
        locals_.append(copy)
        for index, other in enumerate(planes):
            remote(shards[part], view, send_z.at[part, index], recv_z.at[part, index], (me, other))
        spread(part, shards[part], plane, me)

    def stage_z(part):
        for index, offset in enumerate((1, 2, 3)):
            slot = lax.rem(plane + 4 - offset, 4)
            view = landed(part, slot, me, recv_z.at[part, index])
            spread(part, view, slot, me)

    def stage_xy(part):
        for slot in range(4):
            view = landed(part, slot, across, recv_x.at[part, slot])
            remote(view, view, send_c.at[part, slot, 1], recv_c.at[part, slot, 1], (partner, plane))
            if slot < 2:
                remote(view, view, send_d.at[part, slot], recv_d.at[part, slot], (down, plane))
            view = landed(part, slot, down, recv_y.at[part, slot])
            remote(view, view, send_c.at[part, slot, 2], recv_c.at[part, slot, 2], (partner, plane))
            if slot >= 2:
                remote(view, view, send_d.at[part, slot], recv_d.at[part, slot], (across, plane))

    def stage_diagonal(part):
        for slot in range(4):
            view = landed(part, slot, diagonal, recv_d.at[part, slot])
            remote(view, view, send_c.at[part, slot, 3], recv_c.at[part, slot, 3], (partner, plane))

    stages = (stage_first, stage_z, stage_xy, stage_diagonal)
    for part in range(count):
        stage_first(part)
    for step in range(count + 2):
        for stage in (3, 2, 1):
            part = step - (stage - 1)
            if 0 <= part < count:
                stages[stage](part)
    flip = lambda block: block + 1 - 2 * lax.rem(block, 2)
    for part in range(count):
        for slot in range(4):
            for index, block in enumerate((me, across, down, diagonal)):
                landed(part, slot, flip(block), recv_c.at[part, slot, index])
    for copy in locals_:
        copy.wait()
    for copy in started:
        copy.wait_send()

def gather_blocks(shards, collective_id):
    count = len(shards)
    sem = pltpu.SemaphoreType.DMA
    return pl.pallas_call(
        functools.partial(gather_kernel, count),
        out_shape=[jax.ShapeDtypeStruct((4, s.shape[0], 1024), s.dtype) for s in shards],
        in_specs=[pl.BlockSpec(memory_space=pl.ANY)] * count,
        out_specs=[pl.BlockSpec(memory_space=pl.ANY)] * count,
        scratch_shapes=[sem((count,)), sem((count, 3)), sem((count, 3))] + [sem((count, 4))] * 6 + [sem((count, 4, 4))] * 2,
        compiler_params=pltpu.CompilerParams(collective_id=collective_id, has_side_effects=True),
        name="gather_blocks",
    )(*shards)


def add_into(target, source, rows, step):
    @pl.loop(0, rows // step)
    def _(index):
        window = pl.ds(pl.multiple_of(index * step, step), step)
        total = target[:, window].astype(jnp.float32) + source[:, window].astype(jnp.float32)
        target[:, window] = total.astype(jnp.bfloat16)


def scatter_kernel(count, *refs):
    grads, sums = refs[:count], refs[count : 2 * count]
    own, from_core, from_x, from_y, from_yx, from_xy, from_z = (
        refs[(2 + index) * count : (3 + index) * count] for index in range(7)
    )
    (load_sem, send_c, recv_c, send_x, recv_x, send_y, recv_y, send_yx, recv_yx, send_xy, recv_xy, send_z, recv_z) = refs[9 * count :]
    me, partner, across, down = neighbours()
    plane = lax.axis_index("tensor")
    planes = [lax.rem(plane + offset, 4) for offset in (1, 2, 3)]
    greet(plane, (partner, across, down), planes)
    flip = lambda block: block + 1 - 2 * lax.rem(block, 2)
    blocks = (me, across, down, across + down - me)
    started = []

    def remote(source, target, send, recv, device):
        copy = pltpu.make_async_remote_copy(source, target, send, recv, device_id=device, device_id_type=MESH)
        copy.start()
        started.append(copy)

    def wait(view, sem):
        pltpu.make_async_copy(view, view, sem).wait()

    order = (3, 1, 2, 0)
    def stage_core(part):
        for index in order:
            remote(grads[part].at[:, :, lanes(flip(blocks[index]))], from_core[part].at[index],
                   send_c.at[part, index], recv_c.at[part, index], (partner, plane))
            pltpu.make_async_copy(grads[part].at[:, :, lanes(blocks[index])], own[part].at[index], load_sem.at[part, index]).start()

    def stage_first(part):
        rows = sums[part].shape[0]
        for index in order:
            wait(own[part].at[index], load_sem.at[part, index])
            wait(from_core[part].at[index], recv_c.at[part, index])
            add_into(own[part].at[index], from_core[part].at[index], rows, step_of(rows))
            if index % 2 == 1:
                remote(own[part].at[index, 0:2], from_x[part].at[index // 2], send_x.at[part, index // 2], recv_x.at[part, index // 2], (across, plane))
            if index // 2 == 1:
                remote(own[part].at[index, 2:4], from_y[part].at[index % 2], send_y.at[part, index % 2], recv_y.at[part, index % 2], (down, plane))

    def stage_second(part):
        rows = sums[part].shape[0]
        for side in (1, 0):
            wait(from_x[part].at[side], recv_x.at[part, side])
            add_into(own[part].at[2 * side, 0:2], from_x[part].at[side], rows, step_of(rows))
            wait(from_y[part].at[side], recv_y.at[part, side])
            add_into(own[part].at[side, 2:4], from_y[part].at[side], rows, step_of(rows))
            if side == 1:
                remote(own[part].at[2, 0:2], from_yx[part], send_yx.at[part], recv_yx.at[part], (down, plane))
                remote(own[part].at[1, 2:4], from_xy[part], send_xy.at[part], recv_xy.at[part], (across, plane))

    def stage_third(part):
        rows = sums[part].shape[0]
        wait(from_yx[part], recv_yx.at[part])
        add_into(own[part].at[0, 0:2], from_yx[part], rows, step_of(rows))
        wait(from_xy[part], recv_xy.at[part])
        add_into(own[part].at[0, 2:4], from_xy[part], rows, step_of(rows))
        for index, other in enumerate(planes):
            remote(own[part].at[0, other], from_z[part].at[index], send_z.at[part, index], recv_z.at[part, index], (me, other))

    def stage_last(part):
        rows = sums[part].shape[0]
        step = step_of(rows)
        for index in range(3):
            wait(from_z[part].at[index], recv_z.at[part, index])
        @pl.loop(0, rows // step)
        def _(index):
            window = pl.ds(pl.multiple_of(index * step, step), step)
            total = own[part][0, plane, window].astype(jnp.float32)
            for other in range(3):
                total = total + from_z[part][other, window].astype(jnp.float32)
            sums[part][window] = total

    stages = (stage_core, stage_first, stage_second, stage_third, stage_last)
    for part in range(count):
        stage_core(part)
    for step in range(count + 3):
        for stage in (4, 3, 2, 1):
            part = step - (stage - 1)
            if 0 <= part < count:
                stages[stage](part)
    for copy in started:
        copy.wait_send()

def scatter_grads(grads, collective_id):
    count = len(grads)
    rows = [g.shape[1] for g in grads]
    sem = pltpu.SemaphoreType.DMA
    vm = lambda *lead: [pltpu.VMEM(lead + (r, 128), jnp.bfloat16) for r in rows]
    scratch = vm(4, 4) + vm(4, 4) + vm(2, 2) + vm(2, 2) + vm(2) + vm(2) + vm(3)
    sems = [sem((count, 4))] * 3 + [sem((count, 2))] * 4 + [sem((count,))] * 4 + [sem((count, 3))] * 2
    return pl.pallas_call(
        functools.partial(scatter_kernel, count),
        out_shape=[jax.ShapeDtypeStruct((r, 128), jnp.float32) for r in rows],
        in_specs=[pl.BlockSpec(memory_space=pl.ANY)] * count,
        out_specs=[pl.BlockSpec(memory_space=pltpu.VMEM)] * count,
        scratch_shapes=scratch + sems,
        compiler_params=pltpu.CompilerParams(collective_id=collective_id, has_side_effects=True, vmem_limit_bytes=58 * 1024 * 1024),
        name="scatter_grads",
    )(*grads)


def gather_weights(weights):
    tensor_count, dp_count = lax.axis_size("tensor"), lax.axis_size("dp")
    shards = [
        weight.transpose(1, 2, 0) if weight.ndim == 3 else weight.T for weight in weights
    ]
    shards = [shard.reshape(-1, shard.shape[-1]) for shard in shards]
    if (tensor_count, dp_count, shards[0].shape[1]) == (4, 8, 128):
        return gather_blocks(shards, 1)
    wholes = [lax.all_gather(shard, ("tensor", "dp")) for shard in shards]
    wholes = [
        whole.reshape(tensor_count, dp_count, *whole.shape[1:]).transpose(0, 2, 1, 3)
        for whole in wholes
    ]
    return [whole.reshape(*whole.shape[:2], -1) for whole in wholes]


def reduce_grads(grads):
    tensor_count, dp_count = lax.axis_size("tensor"), lax.axis_size("dp")
    if (tensor_count, dp_count, grads[0].shape[2]) == (4, 8, 1024):
        return scatter_grads(grads, 2)
    sums = []
    for grad in grads:
        blocks = grad.reshape(*grad.shape[:2], dp_count, -1).transpose(0, 2, 1, 3)
        blocks = blocks.reshape(-1, *blocks.shape[2:])
        part = lax.psum_scatter(blocks, ("tensor", "dp"), scatter_dimension=0, tiled=True)
        sums.append(part[0].astype(jnp.float32))
    return sums


def on_device(
    inputs,
    cotangent,
    lengths,
    qkv_weight,
    attn_out_weight,
    ffn_in_weight,
    ffn_out_weight,
    norm_gains,
    qkv_moment,
    attn_out_moment,
    ffn_in_moment,
    ffn_out_moment,
    gain_first,
    gain_second,
):
    tensor_count = lax.axis_size("tensor")
    dp_count = lax.axis_size("dp")
    dp_index = lax.axis_index("dp")
    tensor_index = lax.axis_index("tensor")
    core = dp_index % 2
    odd = tensor_index % 2 == 1
    upper = tensor_index >= tensor_count // 2
    lists = exchange_lists(dp_count // 2, tensor_count)
    weights = (qkv_weight, attn_out_weight, ffn_in_weight, ffn_out_weight)
    row_count = qkv_weight.shape[0]

    rows_low = to_sequences(inputs[:, 0], lists, odd, upper)
    qkv_all, attn_all, ffn_in_all, ffn_out_all = gather_weights(weights)
    cotangent_low = to_sequences(cotangent[:, 0], lists, odd, upper)
    rows_in = rows_low.astype(jnp.float32)
    grad_rows = cotangent_low.astype(jnp.float32)
    local_rows = rows_in.shape[0]
    own_lengths = swap_partner(lengths)
    both_lengths = jnp.where(
        core == 0,
        jnp.concatenate([lengths, own_lengths], 1),
        jnp.concatenate([own_lengths, lengths], 1),
    )
    length = lax.dynamic_index_in_dim(both_lengths.reshape(-1), tensor_index, 0, keepdims=False)
    first_row = core * local_rows
    cosine_table, sine_table = rotary(first_row, local_rows)
    own_positions = first_row + jnp.arange(local_rows)
    other_positions = (1 - core) * local_rows + jnp.arange(local_rows)
    key_valid = (jnp.concatenate([own_positions, other_positions]) < length)[None, None, :]

    normed_one, inverse_one, scaled_one = layer_norm_parts(rows_in, norm_gains[0])
    low_one = low(scaled_one)
    width = rows_in.shape[1]
    heads = width // HEAD_DIM
    qkv_rows = qkv_all.reshape(-1, width)
    attn_rows = attn_all.reshape(-1, width)
    ffn_in_rows = ffn_in_all.reshape(-1, width)
    ffn_out_rows = ffn_out_all.reshape(-1, width)
    projected = einsum("sk,nk->sn", low_one, qkv_rows)
    projected = projected.reshape(local_rows, tensor_count, 3, -1, HEAD_DIM)
    projected = projected.transpose(2, 0, 1, 3, 4).reshape(3, local_rows, heads, HEAD_DIM)
    queries = low(rotate(projected[0], cosine_table, sine_table))
    own_keys = low(rotate(projected[1], cosine_table, sine_table))
    own_values = low(projected[2])
    own_pair = jnp.stack([own_keys, own_values])
    pair = jnp.concatenate([own_pair, swap_partner(own_pair)], axis=1)
    context, log_total = attention_forward(queries, pair[0], pair[1], key_valid)
    context_low = low(context).reshape(local_rows, width)
    middle = rows_in + einsum("sk,kn->sn", context_low, attn_rows)
    normed_two, inverse_two, scaled_two = layer_norm_parts(middle, norm_gains[1])
    low_two = low(scaled_two)
    gate_up = einsum("kn,sn->ks", ffn_in_rows, low_two)
    gate_up = gate_up.reshape(tensor_count, 2, -1, local_rows)

    def activate(gate_part, up_part):
        return jax.nn.gelu(gate_part, approximate=False) * up_part

    hidden, activate_back = jax.vjp(activate, gate_up[:, 0], gate_up[:, 1])
    hidden_low = low(hidden).reshape(-1, local_rows)
    result = low(middle + einsum("ks,kn->sn", hidden_low, ffn_out_rows))
    outputs = from_sequences(result, lists, odd, upper)[:, None]

    grad_hidden = einsum("kn,sn->ks", ffn_out_rows, cotangent_low)
    grad_ffn_out = low(einsum("ks,sn->kn", hidden_low, cotangent_low))
    grad_gate, grad_up = activate_back(grad_hidden.reshape(hidden.shape))
    grad_gate_up = low(jnp.stack([grad_gate, grad_up], axis=1)).reshape(-1, local_rows)
    grad_ffn_in = low(einsum("ks,sn->kn", grad_gate_up, low_two))
    grad_scaled_two = einsum("ks,kn->sn", grad_gate_up, ffn_in_rows)
    grad_from_two, gain_two = layer_norm_back(
        grad_scaled_two, normed_two, inverse_two, norm_gains[1]
    )
    grad_middle = grad_rows + grad_from_two
    grad_branch = low(grad_middle)
    grad_context = low(einsum("sn,kn->sk", grad_branch, attn_rows))
    grad_attn_out = low(einsum("sk,sn->kn", context_low, grad_branch))
    grad_query, grad_keys, grad_values = attention_backward(
        queries,
        pair[0],
        pair[1],
        log_total,
        grad_context.reshape(local_rows, heads, HEAD_DIM),
        key_valid,
    )
    grad_pair = jnp.stack([grad_keys, grad_values])
    grad_pair = grad_pair[:, :local_rows] + swap_partner(low(grad_pair[:, local_rows:])).astype(
        jnp.float32
    )
    grad_projected = jnp.stack(
        [
            rotate(grad_query, cosine_table, -sine_table),
            rotate(grad_pair[0], cosine_table, -sine_table),
            grad_pair[1],
        ]
    )
    grad_projected = low(grad_projected).reshape(3, local_rows, tensor_count, -1)
    grad_projected = grad_projected.transpose(1, 2, 0, 3).reshape(local_rows, -1)
    grad_qkv = low(einsum("sk,sn->kn", grad_projected, low_one))
    grads = (grad_qkv, grad_attn_out, grad_ffn_in, grad_ffn_out)
    grads = [grad.reshape(tensor_count, -1, width) for grad in grads]
    sums = reduce_grads(grads[::-1])[::-1]
    grad_scaled_one = einsum("sk,kn->sn", grad_projected, qkv_rows)
    grad_from_one, gain_one = layer_norm_back(
        grad_scaled_one, normed_one, inverse_one, norm_gains[0]
    )
    grad_input = grad_middle + grad_from_one
    input_grad = from_sequences(low(grad_input), lists, odd, upper)[:, None].astype(jnp.float32)

    moments = (qkv_moment, attn_out_moment, ffn_in_moment, ffn_out_moment)
    sums = [
        part.reshape(*moment.shape[1:], row_count).transpose(
            (2, 0, 1) if moment.ndim == 3 else (1, 0)
        )
        for part, moment in zip(sums, moments)
    ]
    new_moments = [MOMENTUM * moment + part for moment, part in zip(moments, sums)]
    gain_grad = lax.psum(jnp.stack([gain_one, gain_two]), BOTH)
    flattened = [low(moment).reshape(row_count, -1) for moment in new_moments]
    local_widths = [matrix.shape[1] for matrix in flattened]
    widest = max(local_widths)
    stacked = jnp.stack(
        [jnp.pad(matrix, ((0, 0), (0, widest - matrix.shape[1]))) for matrix in flattened]
    )
    owned = lax.all_to_all(stacked, "tensor", split_axis=0, concat_axis=0, tiled=True)
    whole = lax.all_gather(owned, "dp", axis=1, tiled=True)
    gram = einsum("tik,tjk->ij", whole, whole)
    mean, rest = newton_schulz(gram)
    own_rows = lax.dynamic_slice_in_dim(rest, dp_index * row_count, row_count, 0)
    own_whole = lax.dynamic_slice_in_dim(whole, dp_index * row_count, row_count, 1)
    step_rows = low(einsum("ij,tjk->tik", low(own_rows), whole) + mean * own_whole)
    returned = lax.all_to_all(step_rows, "tensor", split_axis=0, concat_axis=0, tiled=True)
    new_weights = []
    for index, (weight, width) in enumerate(zip(weights, local_widths)):
        ortho_step = returned[index, :, :width].reshape(weight.shape).astype(jnp.float32)
        new_weights.append(
            weight.astype(jnp.float32) * (1.0 - MUON_RATE * DECAY_RATE)
            - MUON_RATE * 0.2 * math.sqrt(width * tensor_count) * ortho_step
        )
    gain_first_new = BETA_ONE * gain_first + (1.0 - BETA_ONE) * gain_grad
    gain_second_new = BETA_TWO * gain_second + (1.0 - BETA_TWO) * gain_grad * gain_grad
    first_hat = gain_first_new / (1.0 - BETA_ONE**STEP)
    second_hat = gain_second_new / (1.0 - BETA_TWO**STEP)
    norm_gains_new = norm_gains - ADAM_RATE * (
        first_hat / (jnp.sqrt(second_hat) + ADAM_EPS) + DECAY_RATE * norm_gains
    )
    return (
        outputs,
        input_grad,
        new_moments[0],
        new_weights[0],
        new_moments[1],
        new_weights[1],
        new_moments[2],
        new_weights[2],
        new_moments[3],
        new_weights[3],
        gain_first_new,
        gain_second_new,
        norm_gains_new,
    )


def solution(mesh):
    in_specs = (
        P(None, "dp", "tensor", None),
        P(None, "dp", "tensor", None),
        P(None, "dp"),
        P("dp", None, "tensor"),
        P("dp", "tensor"),
        P("dp", None, "tensor"),
        P("dp", "tensor"),
        P(),
        P("dp", None, "tensor"),
        P("dp", "tensor"),
        P("dp", None, "tensor"),
        P("dp", "tensor"),
        P(),
        P(),
    )
    out_specs = (
        P(None, "dp", "tensor", None),
        P(None, "dp", "tensor", None),
        P("dp", None, "tensor"),
        P("dp", None, "tensor"),
        P("dp", "tensor"),
        P("dp", "tensor"),
        P("dp", None, "tensor"),
        P("dp", None, "tensor"),
        P("dp", "tensor"),
        P("dp", "tensor"),
        P(),
        P(),
        P(),
    )
    return jax.shard_map(
        on_device, mesh=mesh, in_specs=in_specs, out_specs=out_specs, check_vma=False
    )
```

```python
import functools
import math

import jax
import jax.numpy as jnp
from jax import lax
from jax.experimental import pallas as pl
from jax.experimental.pallas import tpu as pltpu
from jax.sharding import PartitionSpec as P

HEAD_DIM = 64
NS_ITERS = 5
STEP = 10


ROPE_BASE = 160000.0
NORM_EPS = 1e-05
MASK_VALUE = -1e30
MOMENTUM = 0.95
MUON_RATE = 0.1
DECAY_RATE = 0.01
QUINTIC_ONE = 3.4445
QUINTIC_THREE = -4.775
QUINTIC_FIVE = 2.0315
NORM_FLOOR = 1e-07
BETA_ONE = 0.9
BETA_TWO = 0.95
ADAM_RATE = 0.2
ADAM_EPS = 1e-08
BOTH = ("dp", "tensor")
MESH = pl.DeviceIdType.MESH


def rotary(first, length):
    half_size = HEAD_DIM // 2
    exponents = jnp.arange(half_size).astype(jnp.float32) / half_size
    frequency = jnp.power(ROPE_BASE, -exponents)
    positions = (first + jnp.arange(length)).astype(jnp.float32)
    angles = positions[:, None] * frequency[None, :]
    return (jnp.cos(angles), jnp.sin(angles))


def rotate(vectors, cosine_table, sine_table):
    half_size = vectors.shape[-1] // 2
    first_half = vectors[..., :half_size]
    second_half = vectors[..., half_size:]
    cos_part = cosine_table[:, None, :]
    sin_part = sine_table[:, None, :]
    return jnp.concatenate(
        [
            first_half * cos_part - second_half * sin_part,
            second_half * cos_part + first_half * sin_part,
        ],
        axis=-1,
    )


def layer_norm_parts(vectors, gain):
    centre = vectors - jnp.mean(vectors, axis=-1, keepdims=True)
    inverse = lax.rsqrt(jnp.mean(centre * centre, axis=-1, keepdims=True) + NORM_EPS)
    normed = centre * inverse
    return (normed, inverse, normed * gain)


def layer_norm_back(grad_out, normed, inverse, gain):
    grad_normed = grad_out * gain
    mean_grad = jnp.mean(grad_normed, axis=-1, keepdims=True)
    mean_cross = jnp.mean(grad_normed * normed, axis=-1, keepdims=True)
    return (
        inverse * (grad_normed - mean_grad - normed * mean_cross),
        jnp.sum(grad_out * normed, axis=0),
    )


def einsum(spec, *operands):
    return jnp.einsum(spec, *operands, preferred_element_type=jnp.float32)


def low(values):
    return values.astype(jnp.bfloat16)


def attention_forward(queries, key_rows, values, key_valid):
    score_scale = 1.0 / math.sqrt(queries.shape[-1])
    scores = einsum("qhd,khd->hqk", queries, key_rows) * score_scale
    scores = jnp.where(key_valid, scores, MASK_VALUE)
    highest = jnp.max(scores, axis=-1, keepdims=True)
    exponent = jnp.exp(scores - highest)
    row_total = jnp.sum(exponent, axis=-1, keepdims=True)
    context = einsum("hqk,khd->qhd", low(exponent / row_total), values)
    return (context, highest[..., 0] + jnp.log(row_total[..., 0]))


def attention_backward(queries, key_rows, values, log_total, grad_context, key_valid):
    score_scale = 1.0 / math.sqrt(queries.shape[-1])
    scores = einsum("qhd,khd->hqk", queries, key_rows) * score_scale
    scores = jnp.where(key_valid, scores, MASK_VALUE)
    soft_weights = jnp.exp(scores - log_total[..., None])
    grad_probs = einsum("qhd,khd->hqk", grad_context, values)
    inner_sum = jnp.sum(soft_weights * grad_probs, axis=-1, keepdims=True)
    grad_scores = low(soft_weights * (grad_probs - inner_sum))
    grad_query = einsum("hqk,khd->qhd", grad_scores, key_rows) * score_scale
    grad_keys = einsum("hqk,qhd->khd", grad_scores, queries) * score_scale
    grad_values = einsum("hqk,qhd->khd", low(soft_weights), grad_context)
    return (grad_query, grad_keys, grad_values)


def exchange_lists(chip_count, tensor_count):
    first_list, second_list = [], []
    for chip in range(chip_count):
        for core in range(2):
            for slot in range(tensor_count):
                for micro in range(2):
                    source = (2 * chip + core) * tensor_count + slot
                    target = (2 * chip + slot // 2) * tensor_count + 2 * micro + core
                    pair = (source, target)
                    (first_list if slot % 2 == micro else second_list).append(pair)
    return (first_list, second_list)


def to_sequences(blocks, lists, odd, upper):
    first = lax.ppermute(jnp.where(odd, blocks[1], blocks[0]), BOTH, lists[0])
    second = lax.ppermute(jnp.where(odd, blocks[0], blocks[1]), BOTH, lists[1])
    return jnp.where(
        upper, jnp.concatenate([second, first]), jnp.concatenate([first, second])
    )


def from_sequences(rows, lists, odd, upper):
    half = rows.shape[0] // 2
    top, bottom = rows[:half], rows[half:]
    back = [[(target, source) for source, target in pairs] for pairs in lists]
    first = lax.ppermute(jnp.where(upper, bottom, top), BOTH, back[0])
    second = lax.ppermute(jnp.where(upper, top, bottom), BOTH, back[1])
    return jnp.where(odd, jnp.stack([second, first]), jnp.stack([first, second]))


def swap_partner(values):
    count = lax.axis_size("dp")
    return lax.ppermute(values, "dp", [(index, index ^ 1) for index in range(count)])


def mean_split(matrix):
    mean = jnp.trace(matrix) / matrix.shape[0]
    return (mean, matrix - mean * jnp.eye(matrix.shape[0], dtype=jnp.float32))


def split_product(left, right):
    left_mean, left_rest = left
    right_mean, right_rest = right
    product = einsum("ij,jk->ik", low(left_rest), low(right_rest))
    product = product + left_mean * right_rest + right_mean * left_rest
    mean, rest = mean_split(product)
    return (mean + left_mean * right_mean, rest)


def newton_schulz(gram):
    factor = 1.0 / (jnp.sqrt(jnp.trace(gram)) + NORM_FLOOR)
    iterate = mean_split(gram * (factor * factor))
    whole = None
    for sweep_index in range(NS_ITERS):
        square = split_product(iterate, iterate)
        poly = (
            QUINTIC_ONE + QUINTIC_THREE * iterate[0] + QUINTIC_FIVE * square[0],
            QUINTIC_THREE * iterate[1] + QUINTIC_FIVE * square[1],
        )
        whole = poly if whole is None else split_product(poly, whole)
        if sweep_index < NS_ITERS - 1:
            iterate = split_product(poly, split_product(poly, iterate))
    return (whole[0] * factor, whole[1] * factor)


def step_of(rows):
    return next(step for step in (128, 64, 32, 16) if rows % step == 0)


def lanes(block):
    return pl.ds(pl.multiple_of(block * 128, 128), 128)

def neighbours():
    me = lax.axis_index("dp")
    core, across, down = lax.rem(me, 2), lax.rem(lax.div(me, 2), 2), lax.div(me, 4)
    return (me, me + 1 - 2 * core, me + 2 - 4 * across, me + 4 - 8 * down)

def greet(plane, others, planes):
    barrier = pltpu.get_barrier_semaphore()
    me = lax.axis_index("dp")
    for other in others:
        pl.semaphore_signal(barrier, inc=1, device_id=(other, plane), device_id_type=MESH)
    for other in planes:
        pl.semaphore_signal(barrier, inc=1, device_id=(me, other), device_id_type=MESH)
    pl.semaphore_wait(barrier, len(others) + len(planes))

def gather_kernel(count, *refs):
    shards, wholes = refs[:count], refs[count : 2 * count]
    (own_sem, send_z, recv_z, send_x, recv_x, send_y, recv_y, send_d, recv_d, send_c, recv_c) = refs[2 * count :]
    me, partner, across, down = neighbours()
    plane = lax.axis_index("tensor")
    diagonal = across + down - me
    planes = [lax.rem(plane + offset, 4) for offset in (1, 2, 3)]
    greet(plane, (partner, across, down), planes)
    started = []

    def remote(source, target, send, recv, device):
        copy = pltpu.make_async_remote_copy(source, target, send, recv, device_id=device, device_id_type=MESH)
        copy.start()
        started.append(copy)

    def spread(part, source, slot, block):
        view = wholes[part].at[slot, :, lanes(block)]
        remote(source, view, send_x.at[part, slot], recv_x.at[part, slot], (across, plane))
        remote(source, view, send_y.at[part, slot], recv_y.at[part, slot], (down, plane))
        remote(source, view, send_c.at[part, slot, 0], recv_c.at[part, slot, 0], (partner, plane))

    def landed(part, slot, block, sem):
        view = wholes[part].at[slot, :, lanes(block)]
        pltpu.make_async_copy(view, view, sem).wait()
        return view

    locals_ = []
    def stage_first(part):
        view = wholes[part].at[plane, :, lanes(me)]
        copy = pltpu.make_async_copy(shards[part], view, own_sem.at[part])
        copy.start()
        locals_.append(copy)
        for index, other in enumerate(planes):
            remote(shards[part], view, send_z.at[part, index], recv_z.at[part, index], (me, other))
        spread(part, shards[part], plane, me)

    def stage_z(part):
        for index, offset in enumerate((1, 2, 3)):
            slot = lax.rem(plane + 4 - offset, 4)
            view = landed(part, slot, me, recv_z.at[part, index])
            spread(part, view, slot, me)

    def stage_xy(part):
        for slot in range(4):
            view = landed(part, slot, across, recv_x.at[part, slot])
            remote(view, view, send_c.at[part, slot, 1], recv_c.at[part, slot, 1], (partner, plane))
            if slot < 2:
                remote(view, view, send_d.at[part, slot], recv_d.at[part, slot], (down, plane))
            view = landed(part, slot, down, recv_y.at[part, slot])
            remote(view, view, send_c.at[part, slot, 2], recv_c.at[part, slot, 2], (partner, plane))
            if slot >= 2:
                remote(view, view, send_d.at[part, slot], recv_d.at[part, slot], (across, plane))

    def stage_diagonal(part):
        for slot in range(4):
            view = landed(part, slot, diagonal, recv_d.at[part, slot])
            remote(view, view, send_c.at[part, slot, 3], recv_c.at[part, slot, 3], (partner, plane))

    stages = (stage_first, stage_z, stage_xy, stage_diagonal)
    for part in range(count):
        stage_first(part)
    for step in range(count + 2):
        for stage in (3, 2, 1):
            part = step - (stage - 1)
            if 0 <= part < count:
                stages[stage](part)
    flip = lambda block: block + 1 - 2 * lax.rem(block, 2)
    for part in range(count):
        for slot in range(4):
            for index, block in enumerate((me, across, down, diagonal)):
                landed(part, slot, flip(block), recv_c.at[part, slot, index])
    for copy in locals_:
        copy.wait()
    for copy in started:
        copy.wait_send()

def gather_blocks(shards, collective_id):
    count = len(shards)
    sem = pltpu.SemaphoreType.DMA
    return pl.pallas_call(
        functools.partial(gather_kernel, count),
        out_shape=[jax.ShapeDtypeStruct((4, s.shape[0], 1024), s.dtype) for s in shards],
        in_specs=[pl.BlockSpec(memory_space=pl.ANY)] * count,
        out_specs=[pl.BlockSpec(memory_space=pl.ANY)] * count,
        scratch_shapes=[sem((count,)), sem((count, 3)), sem((count, 3))] + [sem((count, 4))] * 6 + [sem((count, 4, 4))] * 2,
        compiler_params=pltpu.CompilerParams(collective_id=collective_id, has_side_effects=True),
        name="gather_blocks",
    )(*shards)


def add_into(target, source, rows, step):
    @pl.loop(0, rows // step)
    def _(index):
        window = pl.ds(pl.multiple_of(index * step, step), step)
        total = target[:, window].astype(jnp.float32) + source[:, window].astype(jnp.float32)
        target[:, window] = total.astype(jnp.bfloat16)


def scatter_kernel(count, *refs):
    grads, sums = refs[:count], refs[count : 2 * count]
    own, from_core, from_x, from_y, from_yx, from_xy, from_z = (
        refs[(2 + index) * count : (3 + index) * count] for index in range(7)
    )
    (load_sem, send_c, recv_c, send_x, recv_x, send_y, recv_y, send_yx, recv_yx, send_xy, recv_xy, send_z, recv_z) = refs[9 * count :]
    me, partner, across, down = neighbours()
    plane = lax.axis_index("tensor")
    planes = [lax.rem(plane + offset, 4) for offset in (1, 2, 3)]
    greet(plane, (partner, across, down), planes)
    flip = lambda block: block + 1 - 2 * lax.rem(block, 2)
    blocks = (me, across, down, across + down - me)
    started = []

    def remote(source, target, send, recv, device):
        copy = pltpu.make_async_remote_copy(source, target, send, recv, device_id=device, device_id_type=MESH)
        copy.start()
        started.append(copy)

    def wait(view, sem):
        pltpu.make_async_copy(view, view, sem).wait()

    order = (3, 1, 2, 0)
    def stage_core(part):
        for index in order:
            remote(grads[part].at[:, :, lanes(flip(blocks[index]))], from_core[part].at[index],
                   send_c.at[part, index], recv_c.at[part, index], (partner, plane))
            pltpu.make_async_copy(grads[part].at[:, :, lanes(blocks[index])], own[part].at[index], load_sem.at[part, index]).start()

    def stage_first(part):
        rows = sums[part].shape[0]
        for index in order:
            wait(own[part].at[index], load_sem.at[part, index])
            wait(from_core[part].at[index], recv_c.at[part, index])
            add_into(own[part].at[index], from_core[part].at[index], rows, step_of(rows))
            if index % 2 == 1:
                remote(own[part].at[index, 0:2], from_x[part].at[index // 2], send_x.at[part, index // 2], recv_x.at[part, index // 2], (across, plane))
            if index // 2 == 1:
                remote(own[part].at[index, 2:4], from_y[part].at[index % 2], send_y.at[part, index % 2], recv_y.at[part, index % 2], (down, plane))

    def stage_second(part):
        rows = sums[part].shape[0]
        for side in (1, 0):
            wait(from_x[part].at[side], recv_x.at[part, side])
            add_into(own[part].at[2 * side, 0:2], from_x[part].at[side], rows, step_of(rows))
            wait(from_y[part].at[side], recv_y.at[part, side])
            add_into(own[part].at[side, 2:4], from_y[part].at[side], rows, step_of(rows))
            if side == 1:
                remote(own[part].at[2, 0:2], from_yx[part], send_yx.at[part], recv_yx.at[part], (down, plane))
                remote(own[part].at[1, 2:4], from_xy[part], send_xy.at[part], recv_xy.at[part], (across, plane))

    def stage_third(part):
        rows = sums[part].shape[0]
        wait(from_yx[part], recv_yx.at[part])
        add_into(own[part].at[0, 0:2], from_yx[part], rows, step_of(rows))
        wait(from_xy[part], recv_xy.at[part])
        add_into(own[part].at[0, 2:4], from_xy[part], rows, step_of(rows))
        for index, other in enumerate(planes):
            remote(own[part].at[0, other], from_z[part].at[index], send_z.at[part, index], recv_z.at[part, index], (me, other))

    def stage_last(part):
        rows = sums[part].shape[0]
        step = step_of(rows)
        for index in range(3):
            wait(from_z[part].at[index], recv_z.at[part, index])
        @pl.loop(0, rows // step)
        def _(index):
            window = pl.ds(pl.multiple_of(index * step, step), step)
            total = own[part][0, plane, window].astype(jnp.float32)
            for other in range(3):
                total = total + from_z[part][other, window].astype(jnp.float32)
            sums[part][window] = total

    stages = (stage_core, stage_first, stage_second, stage_third, stage_last)
    for part in range(count):
        stage_core(part)
    for step in range(count + 3):
        for stage in (4, 3, 2, 1):
            part = step - (stage - 1)
            if 0 <= part < count:
                stages[stage](part)
    for copy in started:
        copy.wait_send()

def scatter_grads(grads, collective_id):
    count = len(grads)
    rows = [g.shape[1] for g in grads]
    sem = pltpu.SemaphoreType.DMA
    vm = lambda *lead: [pltpu.VMEM(lead + (r, 128), jnp.bfloat16) for r in rows]
    scratch = vm(4, 4) + vm(4, 4) + vm(2, 2) + vm(2, 2) + vm(2) + vm(2) + vm(3)
    sems = [sem((count, 4))] * 3 + [sem((count, 2))] * 4 + [sem((count,))] * 4 + [sem((count, 3))] * 2
    return pl.pallas_call(
        functools.partial(scatter_kernel, count),
        out_shape=[jax.ShapeDtypeStruct((r, 128), jnp.float32) for r in rows],
        in_specs=[pl.BlockSpec(memory_space=pl.ANY)] * count,
        out_specs=[pl.BlockSpec(memory_space=pltpu.VMEM)] * count,
        scratch_shapes=scratch + sems,
        compiler_params=pltpu.CompilerParams(collective_id=collective_id, has_side_effects=True, vmem_limit_bytes=58 * 1024 * 1024),
        name="scatter_grads",
    )(*grads)


def owner_kernel(rows, *refs):
    count = len(rows)
    shards, gain, whole, gain_out = refs[:count], refs[count], refs[count + 1], refs[count + 2]
    (gain_parts, own_sem, send_z, recv_z, send_x, recv_x, send_y, recv_y, send_d, recv_d, send_c, recv_c, send_g, recv_g) = refs[count + 3 :]
    me, partner, across, down = neighbours()
    plane = lax.axis_index("tensor")
    diagonal = across + down - me
    planes = [lax.rem(plane + offset, 4) for offset in (1, 2, 3)]
    greet(plane, (partner, across, down), planes)
    flip = lambda block: block + 1 - 2 * lax.rem(block, 2)

    def remote(source, target, send, recv, device):
        copy = pltpu.make_async_remote_copy(source, target, send, recv, device_id=device, device_id_type=MESH)
        copy.start()
        return copy

    def wait(view, sem):
        pltpu.make_async_copy(view, view, sem).wait()

    def place(part, slot, block):
        height = rows[part]
        first = pl.multiple_of(slot * height, 16)
        return whole.at[pl.ds(first, height), lanes(block)]

    for part in range(count):
        @pl.when(plane != part)
        def _():
            offset = lax.rem(plane + 3 - part, 4)
            remote(shards[part], place(part, plane, me), send_z.at[part], recv_z.at[offset], (me, part))
    gain_copies = [
        remote(gain, gain_parts.at[index], send_g.at[index], recv_g.at[index], (me, other))
        for index, other in enumerate(planes)
    ]

    def spread(part, source, slot):
        view = place(part, slot, me)
        remote(source, view, send_x.at[slot], recv_x.at[slot], (across, plane))
        remote(source, view, send_y.at[slot], recv_y.at[slot], (down, plane))
        remote(source, view, send_c.at[slot, 0], recv_c.at[slot, 0], (partner, plane))

    for part in range(count):
        @pl.when(plane == part)
        def _():
            pltpu.make_async_copy(shards[part], place(part, part, me), own_sem).start()
            spread(part, shards[part], part)
            for distance in (1, 3, 2):
                slot = (part + distance) % 4
                view = place(part, slot, me)
                wait(view, recv_z.at[(slot + 3 - part) % 4])
                spread(part, view, slot)
            for slot in range(4):
                view = place(part, slot, across)
                wait(view, recv_x.at[slot])
                remote(view, view, send_c.at[slot, 1], recv_c.at[slot, 1], (partner, plane))
                if slot < 2:
                    remote(view, view, send_d.at[slot], recv_d.at[slot], (down, plane))
                view = place(part, slot, down)
                wait(view, recv_y.at[slot])
                remote(view, view, send_c.at[slot, 2], recv_c.at[slot, 2], (partner, plane))
                if slot >= 2:
                    remote(view, view, send_d.at[slot], recv_d.at[slot], (across, plane))

    total = gain[...]
    for index in range(3):
        gain_copies[index].wait()
        total = total + gain_parts[index]
    gain_out[...] = total
    for index, other in ((3, across), (4, down), (5, partner)):
        copy = remote(gain_out, gain_parts.at[index], send_g.at[index], recv_g.at[index], (other, plane))
        copy.wait()
        gain_out[...] = gain_out[...] + gain_parts[index]

    for part in range(count):
        @pl.when(plane == part)
        def _():
            for slot in range(4):
                view = place(part, slot, diagonal)
                wait(view, recv_d.at[slot])
                remote(view, view, send_c.at[slot, 3], recv_c.at[slot, 3], (partner, plane))
            for slot in range(4):
                for index, block in enumerate((me, across, down, diagonal)):
                    wait(place(part, slot, flip(block)), recv_c.at[slot, index])
            wait(place(part, part, me), own_sem)
            for slot in range(4):
                view = place(part, slot, me)
                for sem in (send_x.at[slot], send_y.at[slot], send_d.at[slot]):
                    wait(view, sem)
                for index in range(4):
                    wait(view, send_c.at[slot, index])
        @pl.when(plane != part)
        def _():
            wait(shards[part], send_z.at[part])

def own_matrix(shards, gain, collective_id):
    rows = [s.shape[0] for s in shards]
    count = len(shards)
    sem = pltpu.SemaphoreType.DMA
    anyspec = pl.BlockSpec(memory_space=pl.ANY)
    vm = pl.BlockSpec(memory_space=pltpu.VMEM)
    return pl.pallas_call(
        functools.partial(owner_kernel, rows),
        out_shape=[jax.ShapeDtypeStruct((4 * max(rows), 1024), shards[0].dtype), jax.ShapeDtypeStruct(gain.shape, gain.dtype)],
        in_specs=[anyspec] * count + [vm],
        out_specs=[anyspec, vm],
        scratch_shapes=[pltpu.VMEM((6,) + gain.shape, gain.dtype), sem, sem((count,)), sem((3,))] + [sem((4,))] * 6 + [sem((4, 4))] * 2 + [sem((6,))] * 2,
        compiler_params=pltpu.CompilerParams(collective_id=collective_id, has_side_effects=True),
        name="own_matrix",
    )(*shards, gain)

def return_kernel(rows, *refs):
    count = len(rows)
    steps, outs = refs[0], refs[1 : 1 + count]
    own_sem, send_z, recv_z = refs[1 + count :]
    me = lax.axis_index("dp")
    plane = lax.axis_index("tensor")
    planes = [lax.rem(plane + offset, 4) for offset in (1, 2, 3)]
    greet(plane, (), planes)
    wait = lambda view, sem: pltpu.make_async_copy(view, view, sem).wait()
    for part in range(count):
        @pl.when(plane == part)
        def _():
            for slot in range(4):
                view = steps.at[pl.ds(slot * rows[part], rows[part]), :]
                if slot == part:
                    pltpu.make_async_copy(view, outs[part], own_sem).start()
                else:
                    pltpu.make_async_remote_copy(view, outs[part], send_z.at[slot], recv_z.at[part], device_id=(me, slot), device_id_type=MESH).start()
    for part in range(count):
        @pl.when(plane == part)
        def _():
            wait(outs[part], own_sem)
            for slot in range(4):
                if slot != part:
                    wait(outs[part], send_z.at[slot])
        @pl.when(plane != part)
        def _():
            wait(outs[part], recv_z.at[part])

def return_steps(steps, rows, collective_id):
    sem = pltpu.SemaphoreType.DMA
    anyspec = pl.BlockSpec(memory_space=pl.ANY)
    return pl.pallas_call(
        functools.partial(return_kernel, rows),
        out_shape=[jax.ShapeDtypeStruct((r, 128), steps.dtype) for r in rows],
        in_specs=[anyspec],
        out_specs=[anyspec] * len(rows),
        scratch_shapes=[sem, sem((4,)), sem((4,))],
        compiler_params=pltpu.CompilerParams(collective_id=collective_id, has_side_effects=True),
        name="return_steps",
    )(steps)

def product_of(left, right, dims):
    return lax.dot_general(left, right, (dims, ((), ())), preferred_element_type=jnp.float32)

def iterate_kernel(rows, whole, steps, iterate, poly, product, total, iterate_low, poly_low, other_low, total_low):
    size, tile = iterate.shape[0], 256
    plane = lax.axis_index("tensor")
    me = lax.axis_index("dp")
    f32, bf16 = jnp.float32, jnp.bfloat16
    windows = [pl.ds(first, tile) for first in range(0, size, tile)]
    zero = jnp.zeros((1, 1), f32)
    corner = lax.broadcasted_iota(jnp.int32, (tile, tile), 0) == lax.broadcasted_iota(jnp.int32, (tile, tile), 1)

    def store(window, result, shift, full, low_copy):
        fixed = [
            result[:, columns.start : columns.start + tile]
            - (jnp.where(corner, shift, 0.0) if columns.start == window.start else 0.0)
            for columns in windows
        ]
        result = jnp.concatenate(fixed, axis=1)
        full[window] = result
        low_copy[window] = result.astype(bf16)
        return result

    def fold(values):
        return jnp.sum(values, axis=0, keepdims=True)

    def finish(row):
        return jnp.sum(row, axis=1, keepdims=True) / size

    for part, height in enumerate(rows):
        @pl.when(plane == part)
        def _():
            @pl.loop(0, size // tile)
            def _(index):
                window = pl.ds(pl.multiple_of(index * tile, tile), tile)
                block = whole[0 : 4 * height, window]
                iterate[window] = product_of(block, whole[0 : 4 * height, :], ((0,), (0,)))
    trace = zero
    for window in windows:
        block = jnp.where(corner, iterate[window, window], 0.0)
        trace = trace + jnp.sum(fold(block), axis=1, keepdims=True)
    factor = 1.0 / (jnp.sqrt(trace) + NORM_FLOOR)
    squared = factor * factor
    mean = trace * squared / size
    row = jnp.zeros((1, size), f32)
    for window in windows:
        rest = store(window, iterate[window] * squared, mean, iterate, iterate_low)
        row = row + fold(rest * rest)
    square = finish(row)
    total_mean = None
    for sweep in range(NS_ITERS):
        first_sweep = sweep == 0
        linear = QUINTIC_THREE + 2.0 * QUINTIC_FIVE * mean
        shift = QUINTIC_FIVE * square
        poly_mean = QUINTIC_ONE + QUINTIC_THREE * mean + QUINTIC_FIVE * (mean * mean) + shift
        row = jnp.zeros((1, size), f32)
        total_row = row
        for window in windows:
            mine = iterate[window]
            rest = linear * mine + QUINTIC_FIVE * product_of(iterate_low[window], iterate_low[...], ((1,), (0,)))
            rest = store(window, rest, shift, poly, poly_low)
            row = row + fold(rest * mine)
            if not first_sweep:
                total_row = total_row + fold(rest * total[window])
        cross, cross_total = finish(row), finish(total_row)
        if first_sweep:
            total_mean = poly_mean
            source, source_low = poly, poly_low
            for window in windows:
                total[window] = poly[window]
                total_low[window] = poly_low[window]
        else:
            results = []
            for window in windows:
                result = poly_mean * total[window] + total_mean * poly[window]
                result = result + product_of(poly_low[window], total_low[...], ((1,), (0,)))
                store(window, result, cross_total, total, other_low)
            for window in windows:
                total_low[window] = other_low[window]
            total_mean = poly_mean * total_mean + cross_total
        if sweep == NS_ITERS - 1:
            break
        row = jnp.zeros((1, size), f32)
        for window in windows:
            rest = poly[window]
            result = poly_mean * iterate[window] + mean * rest
            result = result + product_of(poly_low[window], iterate_low[...], ((1,), (0,)))
            result = store(window, result, cross, product, other_low)
            row = row + fold(result * rest)
        product_mean = poly_mean * mean + cross
        cross = finish(row)
        row = jnp.zeros((1, size), f32)
        for window in windows:
            result = poly_mean * product[window] + product_mean * poly[window]
            result = result + product_of(poly_low[window], other_low[...], ((1,), (0,)))
            result = store(window, result, cross, iterate, iterate_low)
            row = row + fold(result * result)
        square = finish(row)
        mean = poly_mean * product_mean + cross

    mine = pl.ds(pl.multiple_of(me * 128, 128), 128)
    columns = total_low[:, mine]
    for part, height in enumerate(rows):
        @pl.when(plane == part)
        def _():
            @pl.loop(0, 4)
            def _(slot):
                window = pl.ds(pl.multiple_of(slot * height, 16), height)
                result = product_of(whole[window, :], columns, ((1,), (0,)))
                result = result + total_mean * whole[window, mine].astype(f32)
                steps[window, :] = (factor * result).astype(bf16)

def iterate_owned(whole, rows):
    size = whole.shape[1]
    f32, bf16 = jnp.float32, jnp.bfloat16
    return pl.pallas_call(
        functools.partial(iterate_kernel, rows),
        out_shape=jax.ShapeDtypeStruct((whole.shape[0], 128), bf16),
        in_specs=[pl.BlockSpec(memory_space=pltpu.VMEM)],
        out_specs=pl.BlockSpec(memory_space=pltpu.VMEM),
        scratch_shapes=[pltpu.VMEM((size, size), f32)] * 4 + [pltpu.VMEM((size, size), bf16)] * 4,
        compiler_params=pltpu.CompilerParams(vmem_limit_bytes=58 * 1024 * 1024),
        name="iterate_owned",
    )(whole)


def gather_weights(weights):
    tensor_count, dp_count = lax.axis_size("tensor"), lax.axis_size("dp")
    shards = [turn(weight) for weight in weights]
    if (tensor_count, dp_count, shards[0].shape[1]) == (4, 8, 128):
        return gather_blocks(shards, 1)
    wholes = [lax.all_gather(shard, ("tensor", "dp")) for shard in shards]
    wholes = [
        whole.reshape(tensor_count, dp_count, *whole.shape[1:]).transpose(0, 2, 1, 3)
        for whole in wholes
    ]
    return [whole.reshape(*whole.shape[:2], -1) for whole in wholes]


def reduce_grads(grads):
    tensor_count, dp_count = lax.axis_size("tensor"), lax.axis_size("dp")
    if (tensor_count, dp_count, grads[0].shape[2]) == (4, 8, 1024):
        return scatter_grads(grads, 2)
    sums = []
    for grad in grads:
        blocks = grad.reshape(*grad.shape[:2], dp_count, -1).transpose(0, 2, 1, 3)
        blocks = blocks.reshape(-1, *blocks.shape[2:])
        part = lax.psum_scatter(blocks, ("tensor", "dp"), scatter_dimension=0, tiled=True)
        sums.append(part[0].astype(jnp.float32))
    return sums


def turn(block):
    return block.transpose(*range(1, block.ndim), 0).reshape(-1, block.shape[0])


def turn_back(rows, like):
    rows = rows.reshape(*like.shape[1:], like.shape[0])
    return rows.transpose(rows.ndim - 1, *range(rows.ndim - 1))


def orthogonal_steps(blocks, gain_part):
    tensor_count, dp_count = lax.axis_size("tensor"), lax.axis_size("dp")
    heights = [block.shape[0] for block in blocks]
    if (tensor_count, dp_count, blocks[0].shape[1]) == (4, 8, 128):
        whole, gain_grad = own_matrix(blocks, gain_part, 3)
        steps = iterate_owned(whole, heights)
        return (return_steps(steps, heights, 4), gain_grad)
    row_count = blocks[0].shape[1]
    first_row = lax.axis_index("dp") * row_count
    gain_grad = lax.psum(gain_part, BOTH)
    widest = max(heights)
    stacked = jnp.stack(
        [jnp.pad(block.T, ((0, 0), (0, widest - block.shape[0]))) for block in blocks]
    )
    owned = lax.all_to_all(stacked, "tensor", split_axis=0, concat_axis=0, tiled=True)
    whole = lax.all_gather(owned, "dp", axis=1, tiled=True)
    mean, rest = newton_schulz(einsum("tik,tjk->ij", whole, whole))
    own_rows = lax.dynamic_slice_in_dim(rest, first_row, row_count, 0)
    own_whole = lax.dynamic_slice_in_dim(whole, first_row, row_count, 1)
    step_rows = low(einsum("ij,tjk->tik", low(own_rows), whole) + mean * own_whole)
    returned = lax.all_to_all(step_rows, "tensor", split_axis=0, concat_axis=0, tiled=True)
    return ([returned[index, :, :height].T for index, height in enumerate(heights)], gain_grad)


def on_device(
    inputs,
    cotangent,
    lengths,
    qkv_weight,
    attn_out_weight,
    ffn_in_weight,
    ffn_out_weight,
    norm_gains,
    qkv_moment,
    attn_out_moment,
    ffn_in_moment,
    ffn_out_moment,
    gain_first,
    gain_second,
):
    tensor_count = lax.axis_size("tensor")
    dp_count = lax.axis_size("dp")
    dp_index = lax.axis_index("dp")
    tensor_index = lax.axis_index("tensor")
    core = dp_index % 2
    odd = tensor_index % 2 == 1
    upper = tensor_index >= tensor_count // 2
    lists = exchange_lists(dp_count // 2, tensor_count)
    weights = (qkv_weight, attn_out_weight, ffn_in_weight, ffn_out_weight)
    row_count = qkv_weight.shape[0]

    rows_low = to_sequences(inputs[:, 0], lists, odd, upper)
    qkv_all, attn_all, ffn_in_all, ffn_out_all = gather_weights(weights)
    cotangent_low = to_sequences(cotangent[:, 0], lists, odd, upper)
    rows_in = rows_low.astype(jnp.float32)
    grad_rows = cotangent_low.astype(jnp.float32)
    local_rows = rows_in.shape[0]
    own_lengths = swap_partner(lengths)
    both_lengths = jnp.where(
        core == 0,
        jnp.concatenate([lengths, own_lengths], 1),
        jnp.concatenate([own_lengths, lengths], 1),
    )
    length = lax.dynamic_index_in_dim(both_lengths.reshape(-1), tensor_index, 0, keepdims=False)
    first_row = core * local_rows
    cosine_table, sine_table = rotary(first_row, local_rows)
    own_positions = first_row + jnp.arange(local_rows)
    other_positions = (1 - core) * local_rows + jnp.arange(local_rows)
    key_valid = (jnp.concatenate([own_positions, other_positions]) < length)[None, None, :]

    normed_one, inverse_one, scaled_one = layer_norm_parts(rows_in, norm_gains[0])
    low_one = low(scaled_one)
    width = rows_in.shape[1]
    heads = width // HEAD_DIM
    qkv_rows = qkv_all.reshape(-1, width)
    attn_rows = attn_all.reshape(-1, width)
    ffn_in_rows = ffn_in_all.reshape(-1, width)
    ffn_out_rows = ffn_out_all.reshape(-1, width)
    projected = einsum("sk,nk->sn", low_one, qkv_rows)
    projected = projected.reshape(local_rows, tensor_count, 3, -1, HEAD_DIM)
    projected = projected.transpose(2, 0, 1, 3, 4).reshape(3, local_rows, heads, HEAD_DIM)
    queries = low(rotate(projected[0], cosine_table, sine_table))
    own_keys = low(rotate(projected[1], cosine_table, sine_table))
    own_values = low(projected[2])
    own_pair = jnp.stack([own_keys, own_values])
    pair = jnp.concatenate([own_pair, swap_partner(own_pair)], axis=1)
    context, log_total = attention_forward(queries, pair[0], pair[1], key_valid)
    context_low = low(context).reshape(local_rows, width)
    middle = rows_in + einsum("sk,kn->sn", context_low, attn_rows)
    normed_two, inverse_two, scaled_two = layer_norm_parts(middle, norm_gains[1])
    low_two = low(scaled_two)
    gate_up = einsum("kn,sn->ks", ffn_in_rows, low_two)
    gate_up = gate_up.reshape(tensor_count, 2, -1, local_rows)

    def activate(gate_part, up_part):
        return jax.nn.gelu(gate_part, approximate=False) * up_part

    hidden, activate_back = jax.vjp(activate, gate_up[:, 0], gate_up[:, 1])
    hidden_low = low(hidden).reshape(-1, local_rows)
    result = low(middle + einsum("ks,kn->sn", hidden_low, ffn_out_rows))
    outputs = from_sequences(result, lists, odd, upper)[:, None]

    grad_hidden = einsum("kn,sn->ks", ffn_out_rows, cotangent_low)
    grad_ffn_out = low(einsum("ks,sn->kn", hidden_low, cotangent_low))
    grad_gate, grad_up = activate_back(grad_hidden.reshape(hidden.shape))
    grad_gate_up = low(jnp.stack([grad_gate, grad_up], axis=1)).reshape(-1, local_rows)
    grad_ffn_in = low(einsum("ks,sn->kn", grad_gate_up, low_two))
    grad_scaled_two = einsum("ks,kn->sn", grad_gate_up, ffn_in_rows)
    grad_from_two, gain_two = layer_norm_back(
        grad_scaled_two, normed_two, inverse_two, norm_gains[1]
    )
    grad_middle = grad_rows + grad_from_two
    grad_branch = low(grad_middle)
    grad_context = low(einsum("sn,kn->sk", grad_branch, attn_rows))
    grad_attn_out = low(einsum("sk,sn->kn", context_low, grad_branch))
    grad_query, grad_keys, grad_values = attention_backward(
        queries,
        pair[0],
        pair[1],
        log_total,
        grad_context.reshape(local_rows, heads, HEAD_DIM),
        key_valid,
    )
    grad_pair = jnp.stack([grad_keys, grad_values])
    grad_pair = grad_pair[:, :local_rows] + swap_partner(low(grad_pair[:, local_rows:])).astype(
        jnp.float32
    )
    grad_projected = jnp.stack(
        [
            rotate(grad_query, cosine_table, -sine_table),
            rotate(grad_pair[0], cosine_table, -sine_table),
            grad_pair[1],
        ]
    )
    grad_projected = low(grad_projected).reshape(3, local_rows, tensor_count, -1)
    grad_projected = grad_projected.transpose(1, 2, 0, 3).reshape(local_rows, -1)
    grad_qkv = low(einsum("sk,sn->kn", grad_projected, low_one))
    grads = (grad_qkv, grad_attn_out, grad_ffn_in, grad_ffn_out)
    grads = [grad.reshape(tensor_count, -1, width) for grad in grads]
    sums = reduce_grads(grads[::-1])[::-1]
    grad_scaled_one = einsum("sk,kn->sn", grad_projected, qkv_rows)
    grad_from_one, gain_one = layer_norm_back(
        grad_scaled_one, normed_one, inverse_one, norm_gains[0]
    )
    grad_input = grad_middle + grad_from_one
    input_grad = from_sequences(low(grad_input), lists, odd, upper)[:, None].astype(jnp.float32)

    moments = (qkv_moment, attn_out_moment, ffn_in_moment, ffn_out_moment)
    gain_part = jnp.stack([gain_one, gain_two])
    turned = [turn(moment) for moment in moments]
    turned = [MOMENTUM * moment + part for moment, part in zip(turned, sums)]
    new_moments = [turn_back(part, moment) for part, moment in zip(turned, moments)]
    steps, gain_grad = orthogonal_steps([low(part) for part in turned], gain_part)
    new_weights = [
        weight.astype(jnp.float32) * (1.0 - MUON_RATE * DECAY_RATE)
        - MUON_RATE
        * 0.2
        * math.sqrt(step.shape[0] * tensor_count)
        * turn_back(step, weight).astype(jnp.float32)
        for weight, step in zip(weights, steps)
    ]
    gain_first_new = BETA_ONE * gain_first + (1.0 - BETA_ONE) * gain_grad
    gain_second_new = BETA_TWO * gain_second + (1.0 - BETA_TWO) * gain_grad * gain_grad
    first_hat = gain_first_new / (1.0 - BETA_ONE**STEP)
    second_hat = gain_second_new / (1.0 - BETA_TWO**STEP)
    norm_gains_new = norm_gains - ADAM_RATE * (
        first_hat / (jnp.sqrt(second_hat) + ADAM_EPS) + DECAY_RATE * norm_gains
    )
    return (
        outputs,
        input_grad,
        new_moments[0],
        new_weights[0],
        new_moments[1],
        new_weights[1],
        new_moments[2],
        new_weights[2],
        new_moments[3],
        new_weights[3],
        gain_first_new,
        gain_second_new,
        norm_gains_new,
    )


def solution(mesh):
    in_specs = (
        P(None, "dp", "tensor", None),
        P(None, "dp", "tensor", None),
        P(None, "dp"),
        P("dp", None, "tensor"),
        P("dp", "tensor"),
        P("dp", None, "tensor"),
        P("dp", "tensor"),
        P(),
        P("dp", None, "tensor"),
        P("dp", "tensor"),
        P("dp", None, "tensor"),
        P("dp", "tensor"),
        P(),
        P(),
    )
    out_specs = (
        P(None, "dp", "tensor", None),
        P(None, "dp", "tensor", None),
        P("dp", None, "tensor"),
        P("dp", None, "tensor"),
        P("dp", "tensor"),
        P("dp", "tensor"),
        P("dp", None, "tensor"),
        P("dp", None, "tensor"),
        P("dp", "tensor"),
        P("dp", "tensor"),
        P(),
        P(),
        P(),
    )
    return jax.shard_map(
        on_device, mesh=mesh, in_specs=in_specs, out_specs=out_specs, check_vma=False
    )
```

```python
import functools
import math

import jax
import jax.numpy as jnp
from jax import lax
from jax.experimental import pallas as pl
from jax.experimental.pallas import tpu as pltpu
from jax.sharding import PartitionSpec as P

HEAD_DIM = 64
NS_ITERS = 5
STEP = 10
SCORE_SCALE = 1.0 / math.sqrt(HEAD_DIM)


ROPE_BASE = 160000.0
NORM_EPS = 1e-05
MASK_VALUE = -1e30
MOMENTUM = 0.95
MUON_RATE = 0.1
DECAY_RATE = 0.01
QUINTIC_ONE = 3.4445
QUINTIC_THREE = -4.775
QUINTIC_FIVE = 2.0315
NORM_FLOOR = 1e-07
BETA_ONE = 0.9
BETA_TWO = 0.95
ADAM_RATE = 0.2
ADAM_EPS = 1e-08
BOTH = ("dp", "tensor")
MESH = pl.DeviceIdType.MESH


def rotary(positions):
    half_size = HEAD_DIM // 2
    exponents = jnp.arange(half_size).astype(jnp.float32) / half_size
    frequency = jnp.power(ROPE_BASE, -exponents)
    angles = positions.astype(jnp.float32)[:, None] * frequency[None, :]
    cosine, sine = jnp.cos(angles), jnp.sin(angles)
    return (
        jnp.concatenate([cosine] * 4, axis=1),
        jnp.concatenate([-sine, sine, -sine, sine], axis=1),
    )


def layer_norm_parts(vectors, gain):
    centre = vectors - jnp.mean(vectors, axis=-1, keepdims=True)
    inverse = lax.rsqrt(jnp.mean(centre * centre, axis=-1, keepdims=True) + NORM_EPS)
    normed = centre * inverse
    return (normed, inverse, normed * gain)


def layer_norm_back(grad_out, normed, inverse, gain):
    grad_normed = grad_out * gain
    mean_grad = jnp.mean(grad_normed, axis=-1, keepdims=True)
    mean_cross = jnp.mean(grad_normed * normed, axis=-1, keepdims=True)
    return (
        inverse * (grad_normed - mean_grad - normed * mean_cross),
        jnp.sum(grad_out * normed, axis=0),
    )


def einsum(spec, *operands):
    return jnp.einsum(spec, *operands, preferred_element_type=jnp.float32)


def low(values):
    return values.astype(jnp.bfloat16)


def exchange_lists(chip_count, tensor_count):
    first_list, second_list = [], []
    for chip in range(chip_count):
        for core in range(2):
            for slot in range(tensor_count):
                for micro in range(2):
                    source = (2 * chip + core) * tensor_count + slot
                    target = (2 * chip + slot // 2) * tensor_count + 2 * micro + core
                    pair = (source, target)
                    (first_list if slot % 2 == micro else second_list).append(pair)
    return (first_list, second_list)


def to_sequences(blocks, lists, odd, upper):
    first = lax.ppermute(jnp.where(odd, blocks[1], blocks[0]), BOTH, lists[0])
    second = lax.ppermute(jnp.where(odd, blocks[0], blocks[1]), BOTH, lists[1])
    return jnp.where(
        upper, jnp.concatenate([second, first]), jnp.concatenate([first, second])
    )


def from_sequences(rows, lists, odd, upper):
    half = rows.shape[0] // 2
    top, bottom = rows[:half], rows[half:]
    back = [[(target, source) for source, target in pairs] for pairs in lists]
    first = lax.ppermute(jnp.where(upper, bottom, top), BOTH, back[0])
    second = lax.ppermute(jnp.where(upper, top, bottom), BOTH, back[1])
    return jnp.where(odd, jnp.stack([second, first]), jnp.stack([first, second]))


def swap_partner(values):
    count = lax.axis_size("dp")
    return lax.ppermute(values, "dp", [(index, index ^ 1) for index in range(count)])


def mean_split(matrix):
    mean = jnp.trace(matrix) / matrix.shape[0]
    return (mean, matrix - mean * jnp.eye(matrix.shape[0], dtype=jnp.float32))


def split_product(left, right):
    left_mean, left_rest = left
    right_mean, right_rest = right
    product = einsum("ij,jk->ik", low(left_rest), low(right_rest))
    product = product + left_mean * right_rest + right_mean * left_rest
    mean, rest = mean_split(product)
    return (mean + left_mean * right_mean, rest)


def newton_schulz(gram):
    factor = 1.0 / (jnp.sqrt(jnp.trace(gram)) + NORM_FLOOR)
    iterate = mean_split(gram * (factor * factor))
    whole = None
    for sweep_index in range(NS_ITERS):
        square = split_product(iterate, iterate)
        poly = (
            QUINTIC_ONE + QUINTIC_THREE * iterate[0] + QUINTIC_FIVE * square[0],
            QUINTIC_THREE * iterate[1] + QUINTIC_FIVE * square[1],
        )
        whole = poly if whole is None else split_product(poly, whole)
        if sweep_index < NS_ITERS - 1:
            iterate = split_product(poly, split_product(poly, iterate))
    return (whole[0] * factor, whole[1] * factor)


def step_of(rows):
    return next(step for step in (128, 64, 32, 16) if rows % step == 0)


def lanes(block):
    return pl.ds(pl.multiple_of(block * 128, 128), 128)

def neighbours():
    me = lax.axis_index("dp")
    core, across, down = lax.rem(me, 2), lax.rem(lax.div(me, 2), 2), lax.div(me, 4)
    return (me, me + 1 - 2 * core, me + 2 - 4 * across, me + 4 - 8 * down)

def greet(plane, others, planes):
    barrier = pltpu.get_barrier_semaphore()
    me = lax.axis_index("dp")
    crossed = list(others[:1])
    for other in others:
        pl.semaphore_signal(barrier, inc=1, device_id=(other, plane), device_id_type=MESH)
    for other in planes:
        for same_place in [me] + crossed:
            pl.semaphore_signal(barrier, inc=1, device_id=(same_place, other), device_id_type=MESH)
    pl.semaphore_wait(barrier, len(others) + len(planes) * (1 + len(crossed)))

def gather_kernel(count, *refs):
    shards, wholes = refs[:count], refs[count : 2 * count]
    (own_sem, send_z, recv_z, send_x, recv_x, send_y, recv_y, send_d, recv_d, send_c, recv_c) = refs[2 * count :]
    me, partner, across, down = neighbours()
    plane = lax.axis_index("tensor")
    diagonal = across + down - me
    planes = [lax.rem(plane + offset, 4) for offset in (1, 2, 3)]
    greet(plane, (partner, across, down), planes)
    started = []

    def remote(source, target, send, recv, device):
        copy = pltpu.make_async_remote_copy(source, target, send, recv, device_id=device, device_id_type=MESH)
        copy.start()
        started.append(copy)

    def spread(part, source, slot, block):
        view = wholes[part].at[slot, :, lanes(block)]
        remote(source, view, send_x.at[part, slot], recv_x.at[part, slot], (across, plane))
        remote(source, view, send_y.at[part, slot], recv_y.at[part, slot], (down, plane))
        remote(source, view, send_c.at[part, slot, 0], recv_c.at[part, slot, 0], (partner, plane))

    def landed(part, slot, block, sem):
        view = wholes[part].at[slot, :, lanes(block)]
        pltpu.make_async_copy(view, view, sem).wait()
        return view

    locals_ = []
    def stage_first(part):
        view = wholes[part].at[plane, :, lanes(me)]
        copy = pltpu.make_async_copy(shards[part], view, own_sem.at[part])
        copy.start()
        locals_.append(copy)
        for index, other in enumerate(planes):
            remote(shards[part], view, send_z.at[part, index], recv_z.at[part, index], (me, other))
        spread(part, shards[part], plane, me)

    def stage_z(part):
        for index, offset in enumerate((1, 2, 3)):
            slot = lax.rem(plane + 4 - offset, 4)
            view = landed(part, slot, me, recv_z.at[part, index])
            spread(part, view, slot, me)

    def stage_xy(part):
        for slot in range(4):
            view = landed(part, slot, across, recv_x.at[part, slot])
            remote(view, view, send_c.at[part, slot, 1], recv_c.at[part, slot, 1], (partner, plane))
            if slot < 2:
                remote(view, view, send_d.at[part, slot], recv_d.at[part, slot], (down, plane))
            view = landed(part, slot, down, recv_y.at[part, slot])
            remote(view, view, send_c.at[part, slot, 2], recv_c.at[part, slot, 2], (partner, plane))
            if slot >= 2:
                remote(view, view, send_d.at[part, slot], recv_d.at[part, slot], (across, plane))

    def stage_diagonal(part):
        for slot in range(4):
            view = landed(part, slot, diagonal, recv_d.at[part, slot])
            remote(view, view, send_c.at[part, slot, 3], recv_c.at[part, slot, 3], (partner, plane))

    stages = (stage_first, stage_z, stage_xy, stage_diagonal)
    for part in range(count):
        stage_first(part)
    for step in range(count + 2):
        for stage in (3, 2, 1):
            part = step - (stage - 1)
            if 0 <= part < count:
                stages[stage](part)
    flip = lambda block: block + 1 - 2 * lax.rem(block, 2)
    for part in range(count):
        for slot in range(4):
            for index, block in enumerate((me, across, down, diagonal)):
                landed(part, slot, flip(block), recv_c.at[part, slot, index])
    for copy in locals_:
        copy.wait()
    for copy in started:
        copy.wait_send()

def gather_blocks(shards, collective_id):
    count = len(shards)
    sem = pltpu.SemaphoreType.DMA
    return pl.pallas_call(
        functools.partial(gather_kernel, count),
        out_shape=[jax.ShapeDtypeStruct((4, s.shape[0], 1024), s.dtype) for s in shards],
        in_specs=[pl.BlockSpec(memory_space=pl.ANY)] * count,
        out_specs=[pl.BlockSpec(memory_space=pl.ANY)] * count,
        scratch_shapes=[sem((count,)), sem((count, 3)), sem((count, 3))] + [sem((count, 4))] * 6 + [sem((count, 4, 4))] * 2,
        compiler_params=pltpu.CompilerParams(collective_id=collective_id, has_side_effects=True),
        name="gather_blocks",
    )(*shards)


def add_into(target, source, rows, step):
    @pl.loop(0, rows // step)
    def _(index):
        window = pl.ds(pl.multiple_of(index * step, step), step)
        total = target[:, window].astype(jnp.float32) + source[:, window].astype(jnp.float32)
        target[:, window] = total.astype(jnp.bfloat16)


def send_to(source, target, send, recv, device):
    pltpu.make_async_remote_copy(
        source, target, send, recv, device_id=device, device_id_type=MESH
    ).start()


def wait_for(view, sem):
    pltpu.make_async_copy(view, view, sem).wait()


def move_plan(outward, source, target, send, recv, own):
    me, partner, _, _ = neighbours()
    plane = lax.axis_index("tensor")
    core = lax.rem(me, 2)
    column = me - core
    high, parity = lax.div(plane, 2), lax.rem(plane, 2)
    height = target.shape[1] if outward else source.shape[1]

    def owner_of(slot):
        return (column + parity, 2 * core + slot)

    def keeper_of(micro):
        return (column + high, 2 * micro + core)

    def same(device):
        return jnp.logical_and(device[0] == me, device[1] == plane)

    def half(rows, index):
        return rows.at[pl.ds(pl.multiple_of(index * height, height), height), :]

    def start():
        for index in range(2):
            if outward:
                device = owner_of(index)
                piece, goal, arrival = half(source, index), target.at[high], high
            else:
                device = keeper_of(index)
                piece, goal, arrival = source.at[index], half(target, parity), parity

            @pl.when(same(device))
            def _():
                pltpu.make_async_copy(piece, goal, own).start()

            @pl.when(jnp.logical_not(same(device)))
            def _():
                send_to(piece, goal, send.at[index], recv.at[arrival], device)

    def finish():
        for index in range(2):
            if outward:
                sent_to, came_from = owner_of(index), keeper_of(index)
                piece, goal = half(source, index), target.at[index]
            else:
                sent_to, came_from = keeper_of(index), owner_of(index)
                piece, goal = source.at[index], half(target, index)

            @pl.when(same(sent_to))
            def _():
                wait_for(piece, own)

            @pl.when(jnp.logical_not(same(sent_to)))
            def _():
                wait_for(piece, send.at[index])

            @pl.when(jnp.logical_not(same(came_from)))
            def _():
                wait_for(goal, recv.at[index])

    return (start, finish)


def scatter_plan(grads, sums, buffers, sems):
    held, from_x, from_y, from_yx, from_xy, from_z = buffers[:6]
    staging = buffers[6][0]
    (load_sem, send_c, recv_c, send_x, recv_x, send_y, recv_y, send_yx, recv_yx, send_xy, recv_xy, send_z, recv_z) = sems
    me, partner, across, down = neighbours()
    plane = lax.axis_index("tensor")
    planes = [lax.rem(plane + offset, 4) for offset in (1, 2, 3)]
    flip = lambda block: block + 1 - 2 * lax.rem(block, 2)
    blocks = (me, across, down, across + down - me)
    order = (3, 1, 2, 0)

    def view(part, block):
        ref, first, rows = grads[part]
        return ref.at[:, pl.ds(first, rows), lanes(block)]

    def slot(part, index):
        return staging.at[index, :, pl.ds(0, grads[part][2])]

    def stage_core(part):
        for index in order:
            send_to(view(part, flip(blocks[index])), held[part].at[index], send_c.at[part, index], recv_c.at[part, index], (partner, plane))

    def load(part):
        for index in order:
            pltpu.make_async_copy(view(part, blocks[index]), slot(part, index), load_sem.at[part, index]).start()

    def stage_first(part):
        rows = grads[part][2]
        load(part)
        for index in order:
            wait_for(slot(part, index), load_sem.at[part, index])
            wait_for(held[part].at[index], recv_c.at[part, index])
            add_into(held[part].at[index], slot(part, index), rows, step_of(rows))
            if index % 2 == 1:
                send_to(held[part].at[index, 0:2], from_x[part].at[index // 2], send_x.at[part, index // 2], recv_x.at[part, index // 2], (across, plane))
            if index // 2 == 1:
                send_to(held[part].at[index, 2:4], from_y[part].at[index % 2], send_y.at[part, index % 2], recv_y.at[part, index % 2], (down, plane))

    def stage_second(part):
        rows = grads[part][2]
        for side in (1, 0):
            wait_for(from_x[part].at[side], recv_x.at[part, side])
            add_into(held[part].at[2 * side, 0:2], from_x[part].at[side], rows, step_of(rows))
            if side == 1:
                send_to(held[part].at[2, 0:2], from_yx[part], send_yx.at[part], recv_yx.at[part], (down, plane))
            wait_for(from_y[part].at[side], recv_y.at[part, side])
            add_into(held[part].at[side, 2:4], from_y[part].at[side], rows, step_of(rows))
            if side == 1:
                send_to(held[part].at[1, 2:4], from_xy[part], send_xy.at[part], recv_xy.at[part], (across, plane))

    def stage_third(part):
        rows = grads[part][2]
        wait_for(from_yx[part], recv_yx.at[part])
        add_into(held[part].at[0, 0:2], from_yx[part], rows, step_of(rows))
        wait_for(from_xy[part], recv_xy.at[part])
        add_into(held[part].at[0, 2:4], from_xy[part], rows, step_of(rows))
        for index, other in enumerate(planes):
            send_to(held[part].at[0, other], from_z[part].at[index], send_z.at[part, index], recv_z.at[part, index], (me, other))

    def stage_last(part):
        rows = grads[part][2]
        step = step_of(rows)
        target, first = sums[part]
        for index in range(3):
            wait_for(from_z[part].at[index], recv_z.at[part, index])

        @pl.loop(0, rows // step)
        def _(index):
            offset = pl.multiple_of(index * step, step)
            window = pl.ds(offset, step)
            total = held[part][0, plane, window].astype(jnp.float32)
            for other in range(3):
                total = total + from_z[part][other, window].astype(jnp.float32)
            target[pl.ds(pl.multiple_of(first + offset, 16), step)] = total

    def finish(part):
        for index in range(4):
            wait_for(held[part].at[index], send_c.at[part, index])
        for side in range(2):
            wait_for(from_x[part].at[side], send_x.at[part, side])
            wait_for(from_y[part].at[side], send_y.at[part, side])
        wait_for(from_yx[part], send_yx.at[part])
        wait_for(from_xy[part], send_xy.at[part])
        for index in range(3):
            wait_for(from_z[part].at[index], send_z.at[part, index])

    return ((stage_core, stage_first, stage_second, stage_third, stage_last), finish)


def scatter_scratch(heights):
    sem = pltpu.SemaphoreType.DMA
    count = len(heights)
    leads = ((4, 4), (2, 2), (2, 2), (2,), (2,), (3,))
    buffers = [pltpu.VMEM(lead + (rows, 128), jnp.bfloat16) for lead in leads for rows in heights]
    buffers.append(pltpu.VMEM((4, 4, max(heights), 128), jnp.bfloat16))
    sems = [sem((count, 4))] * 3 + [sem((count, 2))] * 4 + [sem((count,))] * 4 + [sem((count, 3))] * 2
    return (buffers, sems)


def take(refs, count):
    taken, refs[:] = refs[:count], refs[count:]
    return taken


def backward_kernel(*refs):
    refs = list(refs)
    grad_out, grad_in, grad_attn, rows_in = take(refs, 4)
    low_rows, queries, own, other, bias, grad, context, log_total, cosine, sine = take(refs, 10)
    sums, (grad_query, grad_pair), (rows_out,) = take(refs, 4), take(refs, 2), take(refs, 1)
    weight_grads = take(refs, 3)
    grad_other, arrived, staged = take(refs, 3)
    buffers = [take(refs, 7) for _ in range(6)] + [take(refs, 1)]
    sems = take(refs, 13)
    pair_send, pair_recv, stage_sem, move_send, move_recv, move_own = refs
    me, partner, across, down = neighbours()
    plane = lax.axis_index("tensor")
    height, third = grad_out.shape[1], grad_attn.shape[1]
    parts = [(grad_out, 0, height), (grad_in, 0, height), (grad_in, height, height)]
    parts += [(grad_attn, 0, third)] + [(ref, 0, third) for ref in weight_grads]
    sum_qkv, sum_attn, sum_in, sum_out = sums
    targets = [(sum_out, 0), (sum_in, 0), (sum_in, height), (sum_attn, 0)]
    targets += [(sum_qkv, third * index) for index in range(3)]
    stages, finish = scatter_plan(parts, targets, buffers, sems)
    start_move, finish_move = move_plan(True, rows_in, rows_out, move_send, move_recv, move_own)
    greet(plane, (partner, across, down), [lax.rem(plane + offset, 4) for offset in (1, 2, 3)])
    stages[0](0)
    schedule = {0: ((0, 1),), 1: ((1, 0), (0, 2)), 3: ((1, 1), (0, 3)), 6: ((2, 0),), 7: ((1, 2),)}

    @pl.loop(0, queries.shape[1] // 128)
    def _(index):
        for position, calls in schedule.items():
            @pl.when(index == position)
            def _():
                for stage, part in calls:
                    stages[stage](part)

        attend_back_pair(lanes(index), queries, own, other, bias, grad, context, log_total.at[index], cosine, sine, grad_query, grad_pair, grad_other)

    send_to(grad_other, arrived, pair_send, pair_recv, (partner, plane))
    start_move()

    def weight_grad(which, values):
        target = weight_grads[which]
        for group in range(4):
            slot = staged.at[group % 2]
            if group >= 2:
                wait_for(slot, stage_sem.at[group % 2])
            block = values[:, third * group : third * group + third]
            slot[...] = low(product_of(block, low_rows[...], ((0,), (0,))))
            pltpu.make_async_copy(slot, target.at[group], stage_sem.at[group % 2]).start()
        for group in range(2):
            wait_for(staged.at[group], stage_sem.at[group])

    weight_grad(0, grad_query)
    stages[0](4)
    stages[2](1)
    wait_for(arrived, pair_recv)
    step = 128

    @pl.loop(0, grad_pair.shape[1] // step)
    def _(index):
        window = pl.ds(pl.multiple_of(index * step, step), step)
        total = grad_pair[:, window].astype(jnp.float32) + arrived[:, window].astype(jnp.float32)
        grad_pair[:, window] = low(total)

    weight_grad(1, grad_pair.at[0])
    stages[0](5)
    stages[1](3)
    weight_grad(2, grad_pair.at[1])
    stages[0](6)
    calls = [(stage, step - (stage - 1)) for step in range(10) for stage in (4, 3, 2, 1)]
    done = {(1, 0), (1, 1), (1, 2), (1, 3), (2, 0), (2, 1)}
    for stage, part in calls:
        if 0 <= part < 7 and (stage, part) not in done:
            stages[stage](part)
    for part in range(7):
        finish(part)
    wait_for(grad_other, pair_send)
    finish_move()


def backward(grad_out, grad_in, grad_attn, rows_in, low_rows, queries, own, other, bias, grad, context, log_total, cosine, sine, collective_id):
    height, third = grad_out.shape[1], grad_attn.shape[1]
    count, width = queries.shape
    buffers, sems = scatter_scratch([height] * 3 + [third] * 4)
    sem = pltpu.SemaphoreType.DMA
    anywhere = pl.BlockSpec(memory_space=pl.ANY)
    local = pl.BlockSpec(memory_space=pltpu.VMEM)
    bf16 = jnp.bfloat16
    outs = pl.pallas_call(
        backward_kernel,
        out_shape=[
            jax.ShapeDtypeStruct((rows, 128), jnp.float32)
            for rows in (3 * third, third, 2 * height, height)
        ]
        + [
            jax.ShapeDtypeStruct((count, width), bf16),
            jax.ShapeDtypeStruct((2, count, width), bf16),
            jax.ShapeDtypeStruct((2, count // 2, width), rows_in.dtype),
        ]
        + [jax.ShapeDtypeStruct(grad_attn.shape, bf16)] * 3,
        in_specs=[anywhere] * 4 + [local] * 10,
        out_specs=[local] * 6 + [anywhere] * 4,
        scratch_shapes=[
            pltpu.VMEM((2, count, width), bf16),
            pltpu.VMEM((2, count, width), bf16),
            pltpu.VMEM((2, third, width), bf16),
        ]
        + buffers
        + sems
        + [sem, sem, sem((2,)), sem((2,)), sem((2,)), sem],
        compiler_params=pltpu.CompilerParams(
            collective_id=collective_id, has_side_effects=True, vmem_limit_bytes=60 * 1024 * 1024
        ),
        name="backward",
    )(grad_out, grad_in, grad_attn, rows_in, low_rows, queries, own, other, bias, grad, context, log_total, cosine, sine)
    return outs[:7]


def attend_back_pair(columns, queries, own, other, bias, grad, context, log_total, cosine, sine, grad_query, grad_own, grad_other):
    count = queries.shape[0]
    query_rows, grad_rows = queries[:, columns], grad[:, columns]
    query_turned, grad_turned = query_rows.T, grad_rows.T
    inner = (grad_rows.astype(jnp.float32) * context[:, columns].astype(jnp.float32)).T
    query_parts = [None, None]
    for half, (pair, result) in enumerate(((own, grad_own), (other, grad_other))):
        keys, values = pair[0, :, columns], pair[1, :, columns]
        key_turned = keys.T
        grad_keys, grad_values = None, None
        window = pl.ds(half * count, count)
        for head in range(2):
            lanes_of_head = slice(64 * head, 64 * head + 64)
            scores = scores_of(keys, head_rows(query_turned, head), bias[window])
            weights = jnp.exp(scores - log_total[head : head + 1])
            grad_weights = product_of(values, head_rows(grad_turned, head), ((1,), (0,)))
            inner_row = jnp.sum(inner[lanes_of_head], axis=0, keepdims=True)
            grad_scores = low(weights * (grad_weights - inner_row))
            value_part = product_of(low(weights), head_lanes(grad_rows, head), ((1,), (0,)))
            key_part = product_of(grad_scores, head_lanes(query_rows, head), ((1,), (0,)))
            query_part = product_of(key_turned[lanes_of_head], grad_scores, ((1,), (0,)))
            grad_values = value_part if head == 0 else grad_values + value_part
            grad_keys = key_part if head == 0 else grad_keys + key_part
            query_parts[head] = query_part if half == 0 else query_parts[head] + query_part
        result[0, :, columns] = turned(grad_keys, cosine[window], -sine[window]).astype(result.dtype)
        result[1, :, columns] = grad_values.astype(result.dtype)
    query_rows = jnp.concatenate(query_parts, axis=0).T * SCORE_SCALE
    own_rows = pl.ds(0, count)
    grad_query[:, columns] = low(turned(query_rows, cosine[own_rows], -sine[own_rows]))


def owner_kernel(rows, *refs):
    count = len(rows)
    shards, gain, whole, gain_out = refs[:count], refs[count], refs[count + 1], refs[count + 2]
    (gain_parts, own_sem, send_z, recv_z, send_x, recv_x, send_y, recv_y, send_d, recv_d, send_c, recv_c, send_g, recv_g) = refs[count + 3 :]
    me, partner, across, down = neighbours()
    plane = lax.axis_index("tensor")
    diagonal = across + down - me
    planes = [lax.rem(plane + offset, 4) for offset in (1, 2, 3)]
    greet(plane, (partner, across, down), planes)
    flip = lambda block: block + 1 - 2 * lax.rem(block, 2)

    def remote(source, target, send, recv, device):
        copy = pltpu.make_async_remote_copy(source, target, send, recv, device_id=device, device_id_type=MESH)
        copy.start()
        return copy

    def wait(view, sem):
        pltpu.make_async_copy(view, view, sem).wait()

    def place(part, slot, block):
        height = rows[part]
        first = pl.multiple_of(slot * height, 16)
        return whole.at[pl.ds(first, height), lanes(block)]

    for part in range(count):
        @pl.when(plane != part)
        def _():
            offset = lax.rem(plane + 3 - part, 4)
            remote(shards[part], place(part, plane, me), send_z.at[part], recv_z.at[offset], (me, part))
    gain_copies = [
        remote(gain, gain_parts.at[index], send_g.at[index], recv_g.at[index], (me, other))
        for index, other in enumerate(planes)
    ]

    def spread(part, source, slot):
        view = place(part, slot, me)
        remote(source, view, send_x.at[slot], recv_x.at[slot], (across, plane))
        remote(source, view, send_y.at[slot], recv_y.at[slot], (down, plane))
        remote(source, view, send_c.at[slot, 0], recv_c.at[slot, 0], (partner, plane))

    for part in range(count):
        @pl.when(plane == part)
        def _():
            pltpu.make_async_copy(shards[part], place(part, part, me), own_sem).start()
            spread(part, shards[part], part)
            for distance in (1, 3, 2):
                slot = (part + distance) % 4
                view = place(part, slot, me)
                wait(view, recv_z.at[(slot + 3 - part) % 4])
                spread(part, view, slot)
            for slot in range(4):
                view = place(part, slot, across)
                wait(view, recv_x.at[slot])
                remote(view, view, send_c.at[slot, 1], recv_c.at[slot, 1], (partner, plane))
                if slot < 2:
                    remote(view, view, send_d.at[slot], recv_d.at[slot], (down, plane))
                view = place(part, slot, down)
                wait(view, recv_y.at[slot])
                remote(view, view, send_c.at[slot, 2], recv_c.at[slot, 2], (partner, plane))
                if slot >= 2:
                    remote(view, view, send_d.at[slot], recv_d.at[slot], (across, plane))

    total = gain[...]
    for index in range(3):
        gain_copies[index].wait()
        total = total + gain_parts[index]
    gain_out[...] = total
    for index, other in ((3, across), (4, down), (5, partner)):
        copy = remote(gain_out, gain_parts.at[index], send_g.at[index], recv_g.at[index], (other, plane))
        copy.wait()
        gain_out[...] = gain_out[...] + gain_parts[index]

    for part in range(count):
        @pl.when(plane == part)
        def _():
            for slot in range(4):
                view = place(part, slot, diagonal)
                wait(view, recv_d.at[slot])
                remote(view, view, send_c.at[slot, 3], recv_c.at[slot, 3], (partner, plane))
            for slot in range(4):
                for index, block in enumerate((me, across, down, diagonal)):
                    wait(place(part, slot, flip(block)), recv_c.at[slot, index])
            wait(place(part, part, me), own_sem)
            for slot in range(4):
                view = place(part, slot, me)
                for sem in (send_x.at[slot], send_y.at[slot], send_d.at[slot]):
                    wait(view, sem)
                for index in range(4):
                    wait(view, send_c.at[slot, index])
        @pl.when(plane != part)
        def _():
            wait(shards[part], send_z.at[part])

def own_matrix(shards, gain, collective_id):
    rows = [s.shape[0] for s in shards]
    count = len(shards)
    sem = pltpu.SemaphoreType.DMA
    anyspec = pl.BlockSpec(memory_space=pl.ANY)
    vm = pl.BlockSpec(memory_space=pltpu.VMEM)
    return pl.pallas_call(
        functools.partial(owner_kernel, rows),
        out_shape=[jax.ShapeDtypeStruct((4 * max(rows), 1024), shards[0].dtype), jax.ShapeDtypeStruct(gain.shape, gain.dtype)],
        in_specs=[anyspec] * count + [vm],
        out_specs=[anyspec, vm],
        scratch_shapes=[pltpu.VMEM((6,) + gain.shape, gain.dtype), sem, sem((count,)), sem((3,))] + [sem((4,))] * 6 + [sem((4, 4))] * 2 + [sem((6,))] * 2,
        compiler_params=pltpu.CompilerParams(collective_id=collective_id, has_side_effects=True),
        name="own_matrix",
    )(*shards, gain)

def return_kernel(rows, *refs):
    count = len(rows)
    steps, outs = refs[0], refs[1 : 1 + count]
    own_sem, send_z, recv_z = refs[1 + count :]
    me = lax.axis_index("dp")
    plane = lax.axis_index("tensor")
    planes = [lax.rem(plane + offset, 4) for offset in (1, 2, 3)]
    greet(plane, (), planes)
    wait = lambda view, sem: pltpu.make_async_copy(view, view, sem).wait()
    for part in range(count):
        @pl.when(plane == part)
        def _():
            for slot in range(4):
                view = steps.at[pl.ds(slot * rows[part], rows[part]), :]
                if slot == part:
                    pltpu.make_async_copy(view, outs[part], own_sem).start()
                else:
                    pltpu.make_async_remote_copy(view, outs[part], send_z.at[slot], recv_z.at[part], device_id=(me, slot), device_id_type=MESH).start()
    for part in range(count):
        @pl.when(plane == part)
        def _():
            wait(outs[part], own_sem)
            for slot in range(4):
                if slot != part:
                    wait(outs[part], send_z.at[slot])
        @pl.when(plane != part)
        def _():
            wait(outs[part], recv_z.at[part])

def return_steps(steps, rows, collective_id):
    sem = pltpu.SemaphoreType.DMA
    anyspec = pl.BlockSpec(memory_space=pl.ANY)
    return pl.pallas_call(
        functools.partial(return_kernel, rows),
        out_shape=[jax.ShapeDtypeStruct((r, 128), steps.dtype) for r in rows],
        in_specs=[anyspec],
        out_specs=[anyspec] * len(rows),
        scratch_shapes=[sem, sem((4,)), sem((4,))],
        compiler_params=pltpu.CompilerParams(collective_id=collective_id, has_side_effects=True),
        name="return_steps",
    )(steps)

def product_of(left, right, dims):
    return lax.dot_general(left, right, (dims, ((), ())), preferred_element_type=jnp.float32)

def iterate_kernel(rows, whole, steps, iterate, poly, product, total, iterate_low, poly_low, other_low, total_low):
    size, tile = iterate.shape[0], 256
    plane = lax.axis_index("tensor")
    me = lax.axis_index("dp")
    f32, bf16 = jnp.float32, jnp.bfloat16
    windows = [pl.ds(first, tile) for first in range(0, size, tile)]
    zero = jnp.zeros((1, 1), f32)
    corner = lax.broadcasted_iota(jnp.int32, (tile, tile), 0) == lax.broadcasted_iota(jnp.int32, (tile, tile), 1)

    def store(window, result, shift, full, low_copy):
        fixed = [
            result[:, columns.start : columns.start + tile]
            - (jnp.where(corner, shift, 0.0) if columns.start == window.start else 0.0)
            for columns in windows
        ]
        result = jnp.concatenate(fixed, axis=1)
        full[window] = result
        low_copy[window] = result.astype(bf16)
        return result

    def fold(values):
        return jnp.sum(values, axis=0, keepdims=True)

    def finish(row):
        return jnp.sum(row, axis=1, keepdims=True) / size

    for part, height in enumerate(rows):
        @pl.when(plane == part)
        def _():
            @pl.loop(0, size // tile)
            def _(index):
                window = pl.ds(pl.multiple_of(index * tile, tile), tile)
                block = whole[0 : 4 * height, window]
                iterate[window] = product_of(block, whole[0 : 4 * height, :], ((0,), (0,)))
    trace = zero
    for window in windows:
        block = jnp.where(corner, iterate[window, window], 0.0)
        trace = trace + jnp.sum(fold(block), axis=1, keepdims=True)
    factor = 1.0 / (jnp.sqrt(trace) + NORM_FLOOR)
    squared = factor * factor
    mean = trace * squared / size
    row = jnp.zeros((1, size), f32)
    for window in windows:
        rest = store(window, iterate[window] * squared, mean, iterate, iterate_low)
        row = row + fold(rest * rest)
    square = finish(row)
    blank = jnp.zeros((1, size), f32)

    def polynomial(mean, square, with_total):
        linear = QUINTIC_THREE + 2.0 * QUINTIC_FIVE * mean
        shift = QUINTIC_FIVE * square
        poly_mean = QUINTIC_ONE + QUINTIC_THREE * mean + QUINTIC_FIVE * (mean * mean) + shift
        row, total_row = blank, blank
        for window in windows:
            mine = iterate[window]
            rest = product_of(iterate_low[window], iterate_low[...], ((1,), (0,)))
            rest = linear * mine + QUINTIC_FIVE * rest
            rest = store(window, rest, shift, poly, poly_low)
            row = row + fold(rest * mine)
            if with_total:
                total_row = total_row + fold(rest * total[window])
        return (poly_mean, finish(row), finish(total_row))

    def grow_total(poly_mean, total_mean, cross):
        for window in windows:
            result = poly_mean * total[window] + total_mean * poly[window]
            result = result + product_of(poly_low[window], total_low[...], ((1,), (0,)))
            store(window, result, cross, total, other_low)
        for window in windows:
            total_low[window] = other_low[window]
        return poly_mean * total_mean + cross

    def advance(poly_mean, mean, cross):
        row = blank
        for window in windows:
            rest = poly[window]
            result = poly_mean * iterate[window] + mean * rest
            result = result + product_of(poly_low[window], iterate_low[...], ((1,), (0,)))
            result = store(window, result, cross, product, other_low)
            row = row + fold(result * rest)
        product_mean = poly_mean * mean + cross
        cross = finish(row)
        row = blank
        for window in windows:
            result = poly_mean * product[window] + product_mean * poly[window]
            result = result + product_of(poly_low[window], other_low[...], ((1,), (0,)))
            result = store(window, result, cross, iterate, iterate_low)
            row = row + fold(result * result)
        return (poly_mean * product_mean + cross, finish(row))

    total_mean, cross, _ = polynomial(mean, square, False)
    for window in windows:
        total[window] = poly[window]
        total_low[window] = poly_low[window]
    mean, square = advance(total_mean, mean, cross)

    def sweep(_, carry):
        mean, square, total_mean = carry
        poly_mean, cross, cross_total = polynomial(mean, square, True)
        total_mean = grow_total(poly_mean, total_mean, cross_total)
        return advance(poly_mean, mean, cross) + (total_mean,)

    mean, square, total_mean = lax.fori_loop(0, NS_ITERS - 2, sweep, (mean, square, total_mean))
    poly_mean, _, cross_total = polynomial(mean, square, True)
    total_mean = grow_total(poly_mean, total_mean, cross_total)

    mine = pl.ds(pl.multiple_of(me * 128, 128), 128)
    columns = total_low[:, mine]
    for part, height in enumerate(rows):
        @pl.when(plane == part)
        def _():
            @pl.loop(0, 4)
            def _(slot):
                window = pl.ds(pl.multiple_of(slot * height, 16), height)
                result = product_of(whole[window, :], columns, ((1,), (0,)))
                result = result + total_mean * whole[window, mine].astype(f32)
                steps[window, :] = (factor * result).astype(bf16)

def iterate_owned(whole, rows):
    size = whole.shape[1]
    f32, bf16 = jnp.float32, jnp.bfloat16
    return pl.pallas_call(
        functools.partial(iterate_kernel, rows),
        out_shape=jax.ShapeDtypeStruct((whole.shape[0], 128), bf16),
        in_specs=[pl.BlockSpec(memory_space=pltpu.VMEM)],
        out_specs=pl.BlockSpec(memory_space=pltpu.VMEM),
        scratch_shapes=[pltpu.VMEM((size, size), f32)] * 4 + [pltpu.VMEM((size, size), bf16)] * 4,
        compiler_params=pltpu.CompilerParams(vmem_limit_bytes=58 * 1024 * 1024),
        name="iterate_owned",
    )(whole)


def gather_weights(weights):
    tensor_count, dp_count = lax.axis_size("tensor"), lax.axis_size("dp")
    shards = [turn(weight) for weight in weights]
    third = shards[0].shape[0] // 3
    shards = [shards[0][third * part : third * part + third] for part in range(3)] + shards[1:]
    if (tensor_count, dp_count, shards[0].shape[1]) == (4, 8, 128):
        return gather_blocks(shards, 1)
    wholes = [lax.all_gather(shard, ("tensor", "dp")) for shard in shards]
    wholes = [
        whole.reshape(tensor_count, dp_count, *whole.shape[1:]).transpose(0, 2, 1, 3)
        for whole in wholes
    ]
    return [whole.reshape(*whole.shape[:2], -1) for whole in wholes]


def reduce_grads(grads):
    tensor_count, dp_count = lax.axis_size("tensor"), lax.axis_size("dp")
    sums = []
    for grad in grads:
        blocks = grad.reshape(*grad.shape[:2], dp_count, -1).transpose(0, 2, 1, 3)
        blocks = blocks.reshape(-1, *blocks.shape[2:])
        part = lax.psum_scatter(blocks, ("tensor", "dp"), scatter_dimension=0, tiled=True)
        sums.append(part[0].astype(jnp.float32))
    return sums


def lane_of(shape):
    return lax.broadcasted_iota(jnp.int32, shape, 1)

def turned(vectors, cosine, sine):
    lane = lax.rem(lane_of(vectors.shape), 64)
    swapped = jnp.where(lane < 32, pltpu.roll(vectors, 96, 1), pltpu.roll(vectors, 32, 1))
    return vectors * cosine + swapped * sine

def project_kernel(rows, query_weight, key_weight, value_weight, cosine, sine, queries, pair):
    rows = rows[...]
    for weight, target in ((query_weight, 0), (key_weight, 1)):
        result = product_of(rows, weight[0], ((1,), (1,)))
        for first in range(0, result.shape[1], 128):
            part = turned(result[:, first : first + 128], cosine[...], sine[...])
            if target == 0:
                queries[:, first : first + 128] = low(part * SCORE_SCALE)
            else:
                pair[0, :, first : first + 128] = low(part)
    pair[1] = low(product_of(rows, value_weight[0], ((1,), (1,))))

def project(rows, query_weight, key_weight, value_weight, cosine, sine):
    count, width = rows.shape
    groups, height, _ = query_weight.shape
    whole = lambda *shape: pl.BlockSpec(shape, lambda i: (0,) * len(shape))
    weight = pl.BlockSpec((1, height, width), lambda i: (i, 0, 0))
    return pl.pallas_call(
        project_kernel,
        grid=(groups,),
        out_shape=[jax.ShapeDtypeStruct((count, width), jnp.bfloat16), jax.ShapeDtypeStruct((2, count, width), jnp.bfloat16)],
        in_specs=[whole(count, width), weight, weight, weight, whole(count, 128), whole(count, 128)],
        out_specs=[pl.BlockSpec((count, height), lambda i: (0, i)), pl.BlockSpec((2, count, height), lambda i: (0, 0, i))],
        compiler_params=pltpu.CompilerParams(vmem_limit_bytes=40 * 1024 * 1024),
        name="project",
    )(rows, query_weight, key_weight, value_weight, cosine, sine)

def head_rows(transposed, head):
    rows = lax.broadcasted_iota(jnp.int32, transposed.shape, 0)
    return jnp.where(lax.div(rows, 64) == head, transposed, jnp.zeros_like(transposed))

def head_lanes(values, head):
    return jnp.where(lax.div(lane_of(values.shape), 64) == head, values, jnp.zeros_like(values))

def scores_of(keys, queries_turned, bias):
    scores = product_of(keys, queries_turned, ((1,), (0,)))
    return scores + jnp.concatenate([bias] * (scores.shape[1] // 128), axis=1)

def attend_kernel(queries, own, other, bias, context, log_total):
    query_turned = queries[...].T
    keys = jnp.concatenate([own[0], other[0]], axis=0)
    value_turned = jnp.concatenate([own[1].T, other[1].T], axis=1)
    parts, logs = [], []
    for head in range(2):
        scores = scores_of(keys, head_rows(query_turned, head), bias[...])
        highest = jnp.max(scores, axis=0, keepdims=True)
        weights = jnp.exp(scores - highest)
        total = jnp.sum(weights, axis=0, keepdims=True)
        part = product_of(value_turned[64 * head : 64 * head + 64], low(weights), ((1,), (0,)))
        parts.append(part / total)
        logs.append(highest + jnp.log(total))
    context[...] = low(jnp.concatenate(parts, axis=0)).T
    log_total[0] = jnp.concatenate(logs + logs * 3, axis=0)

def attend(queries, own, other, bias):
    count, width = queries.shape
    pairs = width // 128
    column = pl.BlockSpec((count, 128), lambda i: (0, i))
    double = pl.BlockSpec((2, count, 128), lambda i: (0, 0, i))
    return pl.pallas_call(
        attend_kernel,
        grid=(pairs,),
        out_shape=[jax.ShapeDtypeStruct((count, width), jnp.bfloat16), jax.ShapeDtypeStruct((pairs, 8, count), jnp.float32)],
        in_specs=[column, double, double, pl.BlockSpec((2 * count, 128), lambda i: (0, 0))],
        out_specs=[column, pl.BlockSpec((1, 8, count), lambda i: (i, 0, 0))],
        compiler_params=pltpu.CompilerParams(vmem_limit_bytes=40 * 1024 * 1024),
        name="attend",
    )(queries, own, other, bias)

def attend_back_kernel(queries, own, other, bias, grad, context, log_total, cosine, sine, grad_query, grad_own, grad_other):
    count = queries.shape[0]
    query_turned, grad_turned = queries[...].T, grad[...].T
    inner = (grad[...].astype(jnp.float32) * context[...].astype(jnp.float32)).T
    query_parts = [None, None]
    for half, (pair, result) in enumerate(((own, grad_own), (other, grad_other))):
        keys, values = pair[0], pair[1]
        key_turned = keys.T
        grad_keys, grad_values = None, None
        window = pl.ds(half * count, count)
        for head in range(2):
            lanes_of_head = slice(64 * head, 64 * head + 64)
            scores = scores_of(keys, head_rows(query_turned, head), bias[window])
            weights = jnp.exp(scores - log_total[0, head : head + 1])
            grad_weights = product_of(values, head_rows(grad_turned, head), ((1,), (0,)))
            inner_row = jnp.sum(inner[lanes_of_head], axis=0, keepdims=True)
            grad_scores = low(weights * (grad_weights - inner_row))
            value_part = product_of(low(weights), head_lanes(grad[...], head), ((1,), (0,)))
            key_part = product_of(grad_scores, head_lanes(queries[...], head), ((1,), (0,)))
            query_part = product_of(key_turned[lanes_of_head], grad_scores, ((1,), (0,)))
            grad_values = value_part if head == 0 else grad_values + value_part
            grad_keys = key_part if head == 0 else grad_keys + key_part
            query_parts[head] = query_part if half == 0 else query_parts[head] + query_part
        result[0] = turned(grad_keys, cosine[window], -sine[window]).astype(result.dtype)
        result[1] = grad_values.astype(result.dtype)
    grad_rows = jnp.concatenate(query_parts, axis=0).T * SCORE_SCALE
    own_rows = pl.ds(0, count)
    grad_query[...] = low(turned(grad_rows, cosine[own_rows], -sine[own_rows]))

def attend_back(queries, own, other, bias, grad, context, log_total, cosine, sine):
    count, width = queries.shape
    pairs = width // 128
    column = pl.BlockSpec((count, 128), lambda i: (0, i))
    double = pl.BlockSpec((2, count, 128), lambda i: (0, 0, i))
    table = pl.BlockSpec((2 * count, 128), lambda i: (0, 0))
    return pl.pallas_call(
        attend_back_kernel,
        grid=(pairs,),
        out_shape=[
            jax.ShapeDtypeStruct((count, width), jnp.bfloat16),
            jax.ShapeDtypeStruct((2, count, width), jnp.float32),
            jax.ShapeDtypeStruct((2, count, width), jnp.bfloat16),
        ],
        in_specs=[column, double, double, table, column, column, pl.BlockSpec((1, 8, count), lambda i: (i, 0, 0)), table, table],
        out_specs=[column, double, double],
        compiler_params=pltpu.CompilerParams(vmem_limit_bytes=48 * 1024 * 1024),
        name="attend_back",
    )(queries, own, other, bias, grad, context, log_total, cosine, sine)

def feed_kernel(rows, cotangent, in_weight, out_weight, result, grad_rows, grad_in, grad_out):
    height = out_weight.shape[1]
    @pl.when(pl.program_id(0) == 0)
    def _():
        result[...] = jnp.zeros_like(result)
        grad_rows[...] = jnp.zeros_like(grad_rows)
    gate = product_of(in_weight[0, 0:height], rows[...], ((1,), (1,)))
    up = product_of(in_weight[0, height:], rows[...], ((1,), (1,)))
    grad_hidden = product_of(out_weight[0], cotangent[...], ((1,), (1,)))
    below = 0.5 + 0.5 * lax.erf(gate * math.sqrt(0.5))
    active = gate * below
    hidden = low(active * up)
    slope = below + gate * jnp.exp(-0.5 * gate * gate) * (1.0 / math.sqrt(2.0 * math.pi))
    grad_gate = low(grad_hidden * up * slope)
    grad_up = low(grad_hidden * active)
    grad_out[0] = low(product_of(hidden, cotangent[...], ((1,), (0,))))
    grad_in[0, 0:height] = low(product_of(grad_gate, rows[...], ((1,), (0,))))
    grad_in[0, height:] = low(product_of(grad_up, rows[...], ((1,), (0,))))
    result[...] += product_of(hidden, out_weight[0], ((0,), (0,)))
    grad_rows[...] += product_of(grad_gate, in_weight[0, 0:height], ((0,), (0,)))
    grad_rows[...] += product_of(grad_up, in_weight[0, height:], ((0,), (0,)))

def feed(rows, cotangent, in_weight, out_weight):
    count, width = rows.shape
    groups, height, _ = out_weight.shape
    whole = pl.BlockSpec((count, width), lambda i: (0, 0))
    block = lambda size: pl.BlockSpec((1, size, width), lambda i: (i, 0, 0))
    return pl.pallas_call(
        feed_kernel,
        grid=(groups,),
        out_shape=[
            jax.ShapeDtypeStruct((count, width), jnp.float32),
            jax.ShapeDtypeStruct((count, width), jnp.float32),
            jax.ShapeDtypeStruct(in_weight.shape, jnp.bfloat16),
            jax.ShapeDtypeStruct(out_weight.shape, jnp.bfloat16),
        ],
        in_specs=[whole, whole, block(2 * height), block(height)],
        out_specs=[whole, whole, block(2 * height), block(height)],
        compiler_params=pltpu.CompilerParams(vmem_limit_bytes=60 * 1024 * 1024),
        name="feed",
    )(rows, cotangent, in_weight, out_weight)


def turn(block):
    return block.transpose(*range(1, block.ndim), 0).reshape(-1, block.shape[0])


def turn_back(rows, like):
    rows = rows.reshape(*like.shape[1:], like.shape[0])
    return rows.transpose(rows.ndim - 1, *range(rows.ndim - 1))


def orthogonal_steps(blocks, gain_part):
    tensor_count, dp_count = lax.axis_size("tensor"), lax.axis_size("dp")
    heights = [block.shape[0] for block in blocks]
    if (tensor_count, dp_count, blocks[0].shape[1]) == (4, 8, 128):
        whole, gain_grad = own_matrix(blocks, gain_part, 3)
        steps = iterate_owned(whole, heights)
        return (return_steps(steps, heights, 4), gain_grad)
    row_count = blocks[0].shape[1]
    first_row = lax.axis_index("dp") * row_count
    gain_grad = lax.psum(gain_part, BOTH)
    widest = max(heights)
    stacked = jnp.stack(
        [jnp.pad(block.T, ((0, 0), (0, widest - block.shape[0]))) for block in blocks]
    )
    owned = lax.all_to_all(stacked, "tensor", split_axis=0, concat_axis=0, tiled=True)
    whole = lax.all_gather(owned, "dp", axis=1, tiled=True)
    mean, rest = newton_schulz(einsum("tik,tjk->ij", whole, whole))
    own_rows = lax.dynamic_slice_in_dim(rest, first_row, row_count, 0)
    own_whole = lax.dynamic_slice_in_dim(whole, first_row, row_count, 1)
    step_rows = low(einsum("ij,tjk->tik", low(own_rows), whole) + mean * own_whole)
    returned = lax.all_to_all(step_rows, "tensor", split_axis=0, concat_axis=0, tiled=True)
    return ([returned[index, :, :height].T for index, height in enumerate(heights)], gain_grad)


def on_device(
    inputs,
    cotangent,
    lengths,
    qkv_weight,
    attn_out_weight,
    ffn_in_weight,
    ffn_out_weight,
    norm_gains,
    qkv_moment,
    attn_out_moment,
    ffn_in_moment,
    ffn_out_moment,
    gain_first,
    gain_second,
):
    tensor_count = lax.axis_size("tensor")
    dp_count = lax.axis_size("dp")
    dp_index = lax.axis_index("dp")
    tensor_index = lax.axis_index("tensor")
    core = dp_index % 2
    odd = tensor_index % 2 == 1
    upper = tensor_index >= tensor_count // 2
    lists = exchange_lists(dp_count // 2, tensor_count)
    weights = (qkv_weight, attn_out_weight, ffn_in_weight, ffn_out_weight)
    row_count = qkv_weight.shape[0]

    rows_low = to_sequences(inputs[:, 0], lists, odd, upper)
    query_all, key_all, value_all, attn_all, ffn_in_all, ffn_out_all = gather_weights(weights)
    cotangent_low = to_sequences(cotangent[:, 0], lists, odd, upper)
    rows_in = rows_low.astype(jnp.float32)
    grad_rows = cotangent_low.astype(jnp.float32)
    local_rows = rows_in.shape[0]
    own_lengths = swap_partner(lengths)
    both_lengths = jnp.where(
        core == 0,
        jnp.concatenate([lengths, own_lengths], 1),
        jnp.concatenate([own_lengths, lengths], 1),
    )
    length = lax.dynamic_index_in_dim(both_lengths.reshape(-1), tensor_index, 0, keepdims=False)
    positions = jnp.concatenate(
        [core * local_rows + jnp.arange(local_rows), (1 - core) * local_rows + jnp.arange(local_rows)]
    )
    cosine, sine = rotary(positions)
    bias = jnp.where(positions < length, 0.0, MASK_VALUE).astype(jnp.float32)
    bias = jnp.broadcast_to(bias[:, None], (positions.shape[0], 128))

    normed_one, inverse_one, scaled_one = layer_norm_parts(rows_in, norm_gains[0])
    low_one = low(scaled_one)
    width = rows_in.shape[1]
    attn_rows = attn_all.reshape(-1, width)
    queries, own = project(
        low_one, query_all, key_all, value_all, cosine[:local_rows], sine[:local_rows]
    )
    other = swap_partner(own)
    context, log_total = attend(queries, own, other, bias)
    middle = rows_in + einsum("sk,kn->sn", context, attn_rows)
    normed_two, inverse_two, scaled_two = layer_norm_parts(middle, norm_gains[1])
    low_two = low(scaled_two)
    ffn_branch, grad_scaled_two, grad_ffn_in, grad_ffn_out = feed(
        low_two, cotangent_low, ffn_in_all, ffn_out_all
    )
    result = low(middle + ffn_branch)
    grad_from_two, gain_two = layer_norm_back(
        grad_scaled_two, normed_two, inverse_two, norm_gains[1]
    )
    grad_middle = grad_rows + grad_from_two
    grad_branch = low(grad_middle)
    grad_context = low(einsum("sn,kn->sk", grad_branch, attn_rows))
    grad_attn_out = low(einsum("sk,sn->kn", context, grad_branch)).reshape(attn_all.shape)
    fits = (tensor_count, dp_count, row_count, width) == (4, 8, 128, 1024)
    attention = (queries, own, other, bias, grad_context, context, log_total, cosine, sine)
    if fits:
        outs = backward(grad_ffn_out, grad_ffn_in, grad_attn_out, result, low_one, *attention, 2)
        sums, (grad_query, grad_pair, outputs) = outs[:4], outs[4:]
    else:
        grad_query, grad_own, grad_other = attend_back(*attention)
        grad_pair = low(grad_own + swap_partner(grad_other).astype(jnp.float32))
    grad_parts = (grad_query, grad_pair[0], grad_pair[1])
    grad_scaled_one = sum(
        einsum("sk,kn->sn", part, weight.reshape(-1, width))
        for part, weight in zip(grad_parts, (query_all, key_all, value_all))
    )
    grad_from_one, gain_one = layer_norm_back(
        grad_scaled_one, normed_one, inverse_one, norm_gains[0]
    )
    input_low = low(grad_middle + grad_from_one)
    if not fits:
        grads = [low(einsum("sk,sn->kn", part, low_one)) for part in grad_parts]
        grads = [grad.reshape(query_all.shape) for grad in grads]
        sums = reduce_grads(grads + [grad_attn_out, grad_ffn_in, grad_ffn_out])
        outputs = from_sequences(result, lists, odd, upper)
        sums = [jnp.concatenate(sums[:3])] + list(sums[3:])
    input_grad = from_sequences(input_low, lists, odd, upper)
    outputs, input_grad = outputs[:, None], input_grad[:, None].astype(jnp.float32)

    moments = (qkv_moment, attn_out_moment, ffn_in_moment, ffn_out_moment)
    gain_part = jnp.stack([gain_one, gain_two])
    turned = [turn(moment) for moment in moments]
    turned = [MOMENTUM * moment + part for moment, part in zip(turned, sums)]
    new_moments = [turn_back(part, moment) for part, moment in zip(turned, moments)]
    steps, gain_grad = orthogonal_steps([low(part) for part in turned], gain_part)
    new_weights = [
        weight.astype(jnp.float32) * (1.0 - MUON_RATE * DECAY_RATE)
        - MUON_RATE
        * 0.2
        * math.sqrt(step.shape[0] * tensor_count)
        * turn_back(step, weight).astype(jnp.float32)
        for weight, step in zip(weights, steps)
    ]
    gain_first_new = BETA_ONE * gain_first + (1.0 - BETA_ONE) * gain_grad
    gain_second_new = BETA_TWO * gain_second + (1.0 - BETA_TWO) * gain_grad * gain_grad
    first_hat = gain_first_new / (1.0 - BETA_ONE**STEP)
    second_hat = gain_second_new / (1.0 - BETA_TWO**STEP)
    norm_gains_new = norm_gains - ADAM_RATE * (
        first_hat / (jnp.sqrt(second_hat) + ADAM_EPS) + DECAY_RATE * norm_gains
    )
    return (
        outputs,
        input_grad,
        new_moments[0],
        new_weights[0],
        new_moments[1],
        new_weights[1],
        new_moments[2],
        new_weights[2],
        new_moments[3],
        new_weights[3],
        gain_first_new,
        gain_second_new,
        norm_gains_new,
    )


def solution(mesh):
    in_specs = (
        P(None, "dp", "tensor", None),
        P(None, "dp", "tensor", None),
        P(None, "dp"),
        P("dp", None, "tensor"),
        P("dp", "tensor"),
        P("dp", None, "tensor"),
        P("dp", "tensor"),
        P(),
        P("dp", None, "tensor"),
        P("dp", "tensor"),
        P("dp", None, "tensor"),
        P("dp", "tensor"),
        P(),
        P(),
    )
    out_specs = (
        P(None, "dp", "tensor", None),
        P(None, "dp", "tensor", None),
        P("dp", None, "tensor"),
        P("dp", None, "tensor"),
        P("dp", "tensor"),
        P("dp", "tensor"),
        P("dp", None, "tensor"),
        P("dp", None, "tensor"),
        P("dp", "tensor"),
        P("dp", "tensor"),
        P(),
        P(),
        P(),
    )
    return jax.shard_map(
        on_device, mesh=mesh, in_specs=in_specs, out_specs=out_specs, check_vma=False
    )
```

```python
import functools
import math

import jax
import jax.numpy as jnp
from jax import lax
from jax.experimental import pallas as pl
from jax.experimental.pallas import tpu as pltpu
from jax.sharding import PartitionSpec as P

HEAD_DIM = 64
NS_ITERS = 5
STEP = 10
SCORE_SCALE = 1.0 / math.sqrt(HEAD_DIM)


ROPE_BASE = 160000.0
NORM_EPS = 1e-05
MASK_VALUE = -1e30
MOMENTUM = 0.95
MUON_RATE = 0.1
DECAY_RATE = 0.01
QUINTIC_ONE = 3.4445
QUINTIC_THREE = -4.775
QUINTIC_FIVE = 2.0315
NORM_FLOOR = 1e-07
BETA_ONE = 0.9
BETA_TWO = 0.95
ADAM_RATE = 0.2
ADAM_EPS = 1e-08
BOTH = ("dp", "tensor")
MESH = pl.DeviceIdType.MESH


def rotary(positions):
    half_size = HEAD_DIM // 2
    exponents = jnp.arange(half_size).astype(jnp.float32) / half_size
    frequency = jnp.power(ROPE_BASE, -exponents)
    angles = positions.astype(jnp.float32)[:, None] * frequency[None, :]
    cosine, sine = jnp.cos(angles), jnp.sin(angles)
    return (
        jnp.concatenate([cosine] * 4, axis=1),
        jnp.concatenate([-sine, sine, -sine, sine], axis=1),
    )


def layer_norm_parts(vectors, gain):
    centre = vectors - jnp.mean(vectors, axis=-1, keepdims=True)
    inverse = lax.rsqrt(jnp.mean(centre * centre, axis=-1, keepdims=True) + NORM_EPS)
    normed = centre * inverse
    return (normed, inverse, normed * gain)


def layer_norm_back(grad_out, normed, inverse, gain):
    grad_normed = grad_out * gain
    mean_grad = jnp.mean(grad_normed, axis=-1, keepdims=True)
    mean_cross = jnp.mean(grad_normed * normed, axis=-1, keepdims=True)
    return (
        inverse * (grad_normed - mean_grad - normed * mean_cross),
        jnp.sum(grad_out * normed, axis=0),
    )


def einsum(spec, *operands):
    return jnp.einsum(spec, *operands, preferred_element_type=jnp.float32)


def low(values):
    return values.astype(jnp.bfloat16)


def exchange_lists(chip_count, tensor_count):
    first_list, second_list = [], []
    for chip in range(chip_count):
        for core in range(2):
            for slot in range(tensor_count):
                for micro in range(2):
                    source = (2 * chip + core) * tensor_count + slot
                    target = (2 * chip + slot // 2) * tensor_count + 2 * micro + core
                    pair = (source, target)
                    (first_list if slot % 2 == micro else second_list).append(pair)
    return (first_list, second_list)


def to_sequences(blocks, lists, odd, upper):
    first = lax.ppermute(jnp.where(odd, blocks[1], blocks[0]), BOTH, lists[0])
    second = lax.ppermute(jnp.where(odd, blocks[0], blocks[1]), BOTH, lists[1])
    return jnp.where(
        upper, jnp.concatenate([second, first]), jnp.concatenate([first, second])
    )


def from_sequences(rows, lists, odd, upper):
    half = rows.shape[0] // 2
    top, bottom = rows[:half], rows[half:]
    back = [[(target, source) for source, target in pairs] for pairs in lists]
    first = lax.ppermute(jnp.where(upper, bottom, top), BOTH, back[0])
    second = lax.ppermute(jnp.where(upper, top, bottom), BOTH, back[1])
    return jnp.where(odd, jnp.stack([second, first]), jnp.stack([first, second]))


def swap_partner(values):
    count = lax.axis_size("dp")
    return lax.ppermute(values, "dp", [(index, index ^ 1) for index in range(count)])


def mean_split(matrix):
    mean = jnp.trace(matrix) / matrix.shape[0]
    return (mean, matrix - mean * jnp.eye(matrix.shape[0], dtype=jnp.float32))


def split_product(left, right):
    left_mean, left_rest = left
    right_mean, right_rest = right
    product = einsum("ij,jk->ik", low(left_rest), low(right_rest))
    product = product + left_mean * right_rest + right_mean * left_rest
    mean, rest = mean_split(product)
    return (mean + left_mean * right_mean, rest)


def newton_schulz(gram):
    factor = 1.0 / (jnp.sqrt(jnp.trace(gram)) + NORM_FLOOR)
    iterate = mean_split(gram * (factor * factor))
    whole = None
    for sweep_index in range(NS_ITERS):
        square = split_product(iterate, iterate)
        poly = (
            QUINTIC_ONE + QUINTIC_THREE * iterate[0] + QUINTIC_FIVE * square[0],
            QUINTIC_THREE * iterate[1] + QUINTIC_FIVE * square[1],
        )
        whole = poly if whole is None else split_product(poly, whole)
        if sweep_index < NS_ITERS - 1:
            iterate = split_product(poly, split_product(poly, iterate))
    return (whole[0] * factor, whole[1] * factor)


def step_of(rows):
    return next(step for step in (128, 64, 32, 16) if rows % step == 0)


def lanes(block):
    return pl.ds(pl.multiple_of(block * 128, 128), 128)

def neighbours():
    me = lax.axis_index("dp")
    core, across, down = lax.rem(me, 2), lax.rem(lax.div(me, 2), 2), lax.div(me, 4)
    return (me, me + 1 - 2 * core, me + 2 - 4 * across, me + 4 - 8 * down)

def greet(plane, others, planes):
    barrier = pltpu.get_barrier_semaphore()
    me = lax.axis_index("dp")
    crossed = list(others[:1])
    for other in others:
        pl.semaphore_signal(barrier, inc=1, device_id=(other, plane), device_id_type=MESH)
    for other in planes:
        for same_place in [me] + crossed:
            pl.semaphore_signal(barrier, inc=1, device_id=(same_place, other), device_id_type=MESH)
    pl.semaphore_wait(barrier, len(others) + len(planes) * (1 + len(crossed)))

def add_into(target, source, rows, step):
    @pl.loop(0, rows // step)
    def _(index):
        window = pl.ds(pl.multiple_of(index * step, step), step)
        total = target[:, window].astype(jnp.float32) + source[:, window].astype(jnp.float32)
        target[:, window] = total.astype(jnp.bfloat16)


def send_to(source, target, send, recv, device):
    pltpu.make_async_remote_copy(
        source, target, send, recv, device_id=device, device_id_type=MESH
    ).start()


def wait_for(view, sem):
    pltpu.make_async_copy(view, view, sem).wait()


def move_plan(outward, source, target, send, recv, own):
    me, partner, _, _ = neighbours()
    plane = lax.axis_index("tensor")
    core = lax.rem(me, 2)
    column = me - core
    high, parity = lax.div(plane, 2), lax.rem(plane, 2)
    height = target.shape[1] if outward else source.shape[1]

    def owner_of(slot):
        return (column + parity, 2 * core + slot)

    def keeper_of(micro):
        return (column + high, 2 * micro + core)

    def same(device):
        return jnp.logical_and(device[0] == me, device[1] == plane)

    def half(rows, index):
        return rows.at[pl.ds(pl.multiple_of(index * height, height), height), :]

    def start():
        for index in range(2):
            if outward:
                device = owner_of(index)
                piece, goal, arrival = half(source, index), target.at[high], high
            else:
                device = keeper_of(index)
                piece, goal, arrival = source.at[index], half(target, parity), parity

            @pl.when(same(device))
            def _():
                pltpu.make_async_copy(piece, goal, own).start()

            @pl.when(jnp.logical_not(same(device)))
            def _():
                send_to(piece, goal, send.at[index], recv.at[arrival], device)

    def finish():
        for index in range(2):
            if outward:
                sent_to, came_from = owner_of(index), keeper_of(index)
                piece, goal = half(source, index), target.at[index]
            else:
                sent_to, came_from = keeper_of(index), owner_of(index)
                piece, goal = source.at[index], half(target, index)

            @pl.when(same(sent_to))
            def _():
                wait_for(piece, own)

            @pl.when(jnp.logical_not(same(sent_to)))
            def _():
                wait_for(piece, send.at[index])

            @pl.when(jnp.logical_not(same(came_from)))
            def _():
                wait_for(goal, recv.at[index])

    return (start, finish)


def scatter_plan(grads, sums, buffers, sems):
    held, from_x, from_y, from_yx, from_xy, from_z = buffers[:6]
    staging = buffers[6][0]
    (load_sem, send_c, recv_c, send_x, recv_x, send_y, recv_y, send_yx, recv_yx, send_xy, recv_xy, send_z, recv_z) = sems
    me, partner, across, down = neighbours()
    plane = lax.axis_index("tensor")
    planes = [lax.rem(plane + offset, 4) for offset in (1, 2, 3)]
    flip = lambda block: block + 1 - 2 * lax.rem(block, 2)
    blocks = (me, across, down, across + down - me)
    order = (3, 1, 2, 0)

    def view(part, block):
        ref, first, rows = grads[part]
        return ref.at[:, pl.ds(first, rows), lanes(block)]

    def slot(part, index):
        return staging.at[index, :, pl.ds(0, grads[part][2])]

    def stage_core(part):
        for index in order:
            send_to(view(part, flip(blocks[index])), held[part].at[index], send_c.at[part, index], recv_c.at[part, index], (partner, plane))

    def load(part):
        for index in order:
            pltpu.make_async_copy(view(part, blocks[index]), slot(part, index), load_sem.at[part, index]).start()

    def stage_first(part):
        rows = grads[part][2]
        load(part)
        for index in order:
            wait_for(slot(part, index), load_sem.at[part, index])
            wait_for(held[part].at[index], recv_c.at[part, index])
            add_into(held[part].at[index], slot(part, index), rows, step_of(rows))
            if index % 2 == 1:
                send_to(held[part].at[index, 0:2], from_x[part].at[index // 2], send_x.at[part, index // 2], recv_x.at[part, index // 2], (across, plane))
            if index // 2 == 1:
                send_to(held[part].at[index, 2:4], from_y[part].at[index % 2], send_y.at[part, index % 2], recv_y.at[part, index % 2], (down, plane))

    def stage_second(part):
        rows = grads[part][2]
        for side in (1, 0):
            wait_for(from_x[part].at[side], recv_x.at[part, side])
            add_into(held[part].at[2 * side, 0:2], from_x[part].at[side], rows, step_of(rows))
            if side == 1:
                send_to(held[part].at[2, 0:2], from_yx[part], send_yx.at[part], recv_yx.at[part], (down, plane))
            wait_for(from_y[part].at[side], recv_y.at[part, side])
            add_into(held[part].at[side, 2:4], from_y[part].at[side], rows, step_of(rows))
            if side == 1:
                send_to(held[part].at[1, 2:4], from_xy[part], send_xy.at[part], recv_xy.at[part], (across, plane))

    def stage_third(part):
        rows = grads[part][2]
        wait_for(from_yx[part], recv_yx.at[part])
        add_into(held[part].at[0, 0:2], from_yx[part], rows, step_of(rows))
        wait_for(from_xy[part], recv_xy.at[part])
        add_into(held[part].at[0, 2:4], from_xy[part], rows, step_of(rows))
        for index, other in enumerate(planes):
            send_to(held[part].at[0, other], from_z[part].at[index], send_z.at[part, index], recv_z.at[part, index], (me, other))

    def stage_last(part):
        rows = grads[part][2]
        step = step_of(rows)
        target, first = sums[part]
        for index in range(3):
            wait_for(from_z[part].at[index], recv_z.at[part, index])

        @pl.loop(0, rows // step)
        def _(index):
            offset = pl.multiple_of(index * step, step)
            window = pl.ds(offset, step)
            total = held[part][0, plane, window].astype(jnp.float32)
            for other in range(3):
                total = total + from_z[part][other, window].astype(jnp.float32)
            target[pl.ds(pl.multiple_of(first + offset, 16), step)] = total

    def finish(part):
        for index in range(4):
            wait_for(held[part].at[index], send_c.at[part, index])
        for side in range(2):
            wait_for(from_x[part].at[side], send_x.at[part, side])
            wait_for(from_y[part].at[side], send_y.at[part, side])
        wait_for(from_yx[part], send_yx.at[part])
        wait_for(from_xy[part], send_xy.at[part])
        for index in range(3):
            wait_for(from_z[part].at[index], send_z.at[part, index])

    return ((stage_core, stage_first, stage_second, stage_third, stage_last), finish)


def scatter_scratch(heights):
    sem = pltpu.SemaphoreType.DMA
    count = len(heights)
    leads = ((4, 4), (2, 2), (2, 2), (2,), (2,), (3,))
    buffers = [pltpu.VMEM(lead + (rows, 128), jnp.bfloat16) for lead in leads for rows in heights]
    buffers.append(pltpu.VMEM((4, 4, max(heights), 128), jnp.bfloat16))
    sems = [sem((count, 4))] * 3 + [sem((count, 2))] * 4 + [sem((count,))] * 4 + [sem((count, 3))] * 2
    return (buffers, sems)


def take(refs, count):
    taken, refs[:] = refs[:count], refs[count:]
    return taken


def gather_plan(shards, wholes, sems):
    own_sem, send_up, send_down, recv_z, send_x, recv_x, send_y, recv_y, send_d, recv_d, send_c, recv_c = sems
    me, partner, across, down = neighbours()
    plane = lax.axis_index("tensor")
    diagonal = across + down - me
    flip = lambda block: block + 1 - 2 * lax.rem(block, 2)

    def place(part, slot, block):
        return wholes[part].at[slot, :, lanes(block)]

    def spread(part, source, slot):
        view = place(part, slot, me)
        send_to(source, view, send_x.at[part, slot], recv_x.at[part, slot], (across, plane))
        send_to(source, view, send_y.at[part, slot], recv_y.at[part, slot], (down, plane))
        send_to(source, view, send_c.at[part, slot, 0], recv_c.at[part, slot, 0], (partner, plane))

    def pass_on(part, source, slot, upward):
        view = place(part, slot, me)
        sem = (send_up if upward else send_down).at[part, slot]
        send_to(source, view, sem, recv_z.at[part, slot], (me, plane + 1 if upward else plane - 1))

    def stage_own(part):
        pltpu.make_async_copy(shards[part], place(part, plane, me), own_sem.at[part]).start()

        @pl.when(plane < 3)
        def _():
            pass_on(part, shards[part], plane, True)

        @pl.when(plane > 0)
        def _():
            pass_on(part, shards[part], plane, False)

        spread(part, shards[part], plane)

    def stage_z(part):
        for distance in (1, 2, 3):
            for upward in (True, False):
                slot = plane - distance if upward else plane + distance

                @pl.when(slot >= 0 if upward else slot <= 3)
                def _():
                    view = place(part, slot, me)
                    wait_for(view, recv_z.at[part, slot])

                    @pl.when(plane < 3 if upward else plane > 0)
                    def _():
                        pass_on(part, view, slot, upward)

                    spread(part, view, slot)

    def stage_xy(part):
        for slot in range(4):
            view = place(part, slot, across)
            wait_for(view, recv_x.at[part, slot])
            if slot < 2:
                send_to(view, view, send_d.at[part, slot], recv_d.at[part, slot], (down, plane))
            send_to(view, view, send_c.at[part, slot, 1], recv_c.at[part, slot, 1], (partner, plane))
            view = place(part, slot, down)
            wait_for(view, recv_y.at[part, slot])
            if slot >= 2:
                send_to(view, view, send_d.at[part, slot], recv_d.at[part, slot], (across, plane))
            send_to(view, view, send_c.at[part, slot, 2], recv_c.at[part, slot, 2], (partner, plane))

    def stage_diagonal(part):
        for slot in range(4):
            view = place(part, slot, diagonal)
            wait_for(view, recv_d.at[part, slot])
            send_to(view, view, send_c.at[part, slot, 3], recv_c.at[part, slot, 3], (partner, plane))

    def arrive(part):
        wait_for(shards[part], own_sem.at[part])
        for slot in range(4):
            for index, block in enumerate((me, across, down, diagonal)):
                wait_for(place(part, slot, flip(block)), recv_c.at[part, slot, index])

    def finish(part):
        for slot in range(4):
            @pl.when(jnp.logical_and(slot <= plane, plane < 3))
            def _():
                wait_for(shards[part], send_up.at[part, slot])

            @pl.when(jnp.logical_and(slot >= plane, plane > 0))
            def _():
                wait_for(shards[part], send_down.at[part, slot])

            for sem in (send_x, send_y, send_d):
                wait_for(shards[part], sem.at[part, slot])
            for index in range(4):
                wait_for(shards[part], send_c.at[part, slot, index])

    return (stage_own, stage_z, stage_xy, stage_diagonal, arrive, finish)


def normed_rows(rows, gain):
    centre = rows - jnp.mean(rows, axis=1, keepdims=True)
    inverse = lax.rsqrt(jnp.mean(centre * centre, axis=1, keepdims=True) + NORM_EPS)
    return centre * inverse * gain


def forward_kernel(*refs):
    refs = list(refs)
    shards, (inputs, cotangent, lengths, gains, cosine, sine) = take(refs, 6), take(refs, 6)
    wholes, (rows_low, grad_rows) = take(refs, 6), take(refs, 2)
    low_one, queries, own, other, context, log_total, bias, middle, low_two = take(refs, 9)
    other_lengths, weight, attn_weight = take(refs, 3)
    sems = take(refs, 12)
    pair_send, pair_recv, length_send, length_recv, weight_sem, attn_sem = take(refs, 6)
    move_send, move_recv, move_own = refs
    me, partner, across, down = neighbours()
    plane = lax.axis_index("tensor")
    core = lax.rem(me, 2)
    stage_own, stage_z, stage_xy, stage_diagonal, arrive, finish = gather_plan(shards, wholes, sems)
    moves = [
        move_plan(False, source, target, move_send.at[index], move_recv.at[index], move_own.at[index])
        for index, (source, target) in enumerate(((inputs, rows_low), (cotangent, grad_rows)))
    ]
    greet(plane, (partner, across, down), [lax.rem(plane + offset, 4) for offset in (1, 2, 3)])
    count, width = rows_low.shape
    third = shards[0].shape[0]
    step = 64

    stage_own(0)
    stage_own(1)
    send_to(lengths, other_lengths, length_send, length_recv, (partner, plane))
    stage_z(0)
    stage_own(2)
    stage_z(1)
    stage_xy(0)
    stage_own(3)
    stage_z(2)
    stage_xy(1)
    stage_diagonal(0)
    stage_own(4)
    stage_z(3)
    stage_xy(2)
    stage_diagonal(1)
    stage_own(5)
    stage_z(4)
    moves[0][0]()
    stage_xy(3)
    stage_diagonal(2)
    stage_z(5)
    moves[1][0]()
    stage_diagonal(3)
    stage_xy(4)
    wait_for(other_lengths, length_recv)
    mine = core == lax.rem(plane, 2)
    both = jnp.where(mine, lengths[...], other_lengths[...])
    length = jnp.where(plane < 2, both[0:1], both[1:2])
    position = lax.broadcasted_iota(jnp.int32, bias.shape, 0)
    position = lax.rem(position + core * count, 2 * count).astype(jnp.float32)
    bias[...] = jnp.where(position < length, 0.0, MASK_VALUE)
    moves[0][1]()

    @pl.loop(0, count // step)
    def _(index):
        window = pl.ds(pl.multiple_of(index * step, step), step)
        low_one[window] = low(normed_rows(rows_low[window].astype(jnp.float32), gains[0:1]))

    for part in range(3):
        arrive(part)

    def load(group):
        for part in range(3):
            slot = lax.rem(group, 2)
            pltpu.make_async_copy(wholes[part].at[group], weight.at[slot, part], weight_sem.at[slot, part]).start()

    load(0)

    @pl.loop(0, 4)
    def _(group):
        @pl.when(group < 3)
        def _():
            load(group + 1)

        slot = lax.rem(group, 2)
        for part in range(3):
            wait_for(weight.at[slot, part], weight_sem.at[slot, part])
            result = product_of(low_one[...], weight[slot, part], ((1,), (1,)))
            for first in range(0, third, 128):
                columns = pl.ds(pl.multiple_of(group * third + first, 128), 128)
                piece = result[:, first : first + 128]
                if part < 2:
                    piece = turned(piece, cosine[0:count], sine[0:count])
                if part == 0:
                    queries[:, columns] = low(piece * SCORE_SCALE)
                else:
                    own[part - 1, :, columns] = low(piece)

    send_to(own, other, pair_send, pair_recv, (partner, plane))
    wait_for(other, pair_recv)
    arrive(3)
    attn_copy = pltpu.make_async_copy(wholes[3], attn_weight, attn_sem)
    attn_copy.start()
    schedule = {3: (stage_xy, 5), 6: (stage_diagonal, 4)}

    @pl.loop(0, width // 128)
    def _(index):
        for place, (stage, part) in schedule.items():
            @pl.when(index == place)
            def _():
                stage(part)

        attend_pair(lanes(index), queries, own, other, bias, context, log_total.at[index])

    attn_copy.wait()

    @pl.loop(0, count // 128)
    def _(index):
        window = pl.ds(pl.multiple_of(index * 128, 128), 128)
        rows = rows_low[window].astype(jnp.float32)
        for group in range(4):
            piece = context[window, third * group : third * group + third]
            rows = rows + product_of(piece, attn_weight[group], ((1,), (0,)))
        middle[window] = rows
        low_two[window] = low(normed_rows(rows, gains[1:2]))

    stage_diagonal(5)
    for part in (4, 5):
        arrive(part)
    for part in range(6):
        finish(part)
    wait_for(own, pair_send)
    wait_for(lengths, length_send)
    moves[1][1]()


def forward(shards, inputs, cotangent, lengths, gains, cosine, sine, collective_id):
    sem = pltpu.SemaphoreType.DMA
    anywhere = pl.BlockSpec(memory_space=pl.ANY)
    local = pl.BlockSpec(memory_space=pltpu.VMEM)
    bf16, f32 = jnp.bfloat16, jnp.float32
    count, width = 2 * inputs.shape[1], inputs.shape[2]
    third = shards[0].shape[0]
    shape = jax.ShapeDtypeStruct
    return pl.pallas_call(
        forward_kernel,
        out_shape=[shape((4, shard.shape[0], width), bf16) for shard in shards]
        + [
            shape((count, width), bf16),
            shape((count, width), bf16),
            shape((count, width), bf16),
            shape((count, width), bf16),
            shape((2, count, width), bf16),
            shape((2, count, width), bf16),
            shape((count, width), bf16),
            shape((width // 128, 8, count), f32),
            shape((2 * count, 128), f32),
            shape((count, width), f32),
            shape((count, width), bf16),
        ],
        in_specs=[anywhere] * 8 + [local] * 4,
        out_specs=[anywhere] * 6 + [local, anywhere] + [local] * 9,
        scratch_shapes=[
            pltpu.VMEM(lengths.shape, f32),
            pltpu.VMEM((2, 3, third, width), bf16),
            pltpu.VMEM((4, third, width), bf16),
            sem((6,)),
        ]
        + [sem((6, 4))] * 9
        + [sem((6, 4, 4))] * 2
        + [sem, sem, sem, sem, sem((2, 3)), sem]
        + [sem((2, 2)), sem((2, 2)), sem((2,))],
        compiler_params=pltpu.CompilerParams(
            collective_id=collective_id, has_side_effects=True, vmem_limit_bytes=58 * 1024 * 1024
        ),
        name="forward",
    )(*shards, inputs, cotangent, lengths, gains, cosine, sine)


def attend_pair(columns, queries, own, other, bias, context, log_total):
    query_turned = queries[:, columns].T
    keys = jnp.concatenate([own[0, :, columns], other[0, :, columns]], axis=0)
    value_turned = jnp.concatenate([own[1, :, columns].T, other[1, :, columns].T], axis=1)
    parts, logs = [], []
    for head in range(2):
        scores = scores_of(keys, head_rows(query_turned, head), bias[...])
        highest = jnp.max(scores, axis=0, keepdims=True)
        weights = jnp.exp(scores - highest)
        total = jnp.sum(weights, axis=0, keepdims=True)
        part = product_of(value_turned[64 * head : 64 * head + 64], low(weights), ((1,), (0,)))
        parts.append(part / total)
        logs.append(highest + jnp.log(total))
    context[:, columns] = low(jnp.concatenate(parts, axis=0)).T
    log_total[...] = jnp.concatenate(logs + logs * 3, axis=0)


def backward_kernel(*refs):
    refs = list(refs)
    grad_out, grad_in, grad_attn, rows_in = take(refs, 4)
    far, (bias, log_total, cosine, sine) = take(refs, 6), take(refs, 4)
    sums, (far_query, far_pair), (rows_out,) = take(refs, 4), take(refs, 2), take(refs, 1)
    weight_grads = take(refs, 3)
    near, (grad_query, grad_pair) = take(refs, 6), take(refs, 2)
    low_rows, queries, own, other, grad, context = near
    grad_other, arrived, staged = take(refs, 3)
    buffers = [take(refs, 7) for _ in range(6)] + [take(refs, 1)]
    sems = take(refs, 13)
    pair_send, pair_recv, stage_sem, load_sem, out_sem, move_send, move_recv, move_own = refs
    me, partner, across, down = neighbours()
    plane = lax.axis_index("tensor")
    height, third = grad_out.shape[1], grad_attn.shape[1]
    parts = [(grad_out, 0, height), (grad_in, 0, height), (grad_in, height, height)]
    parts += [(grad_attn, 0, third)] + [(ref, 0, third) for ref in weight_grads]
    sum_qkv, sum_attn, sum_in, sum_out = sums
    targets = [(sum_out, 0), (sum_in, 0), (sum_in, height), (sum_attn, 0)]
    targets += [(sum_qkv, third * index) for index in range(3)]
    stages, finish = scatter_plan(parts, targets, buffers, sems)
    start_move, finish_move = move_plan(True, rows_in, rows_out, move_send, move_recv, move_own)
    greet(plane, (partner, across, down), [lax.rem(plane + offset, 4) for offset in (1, 2, 3)])
    copies = [
        pltpu.make_async_copy(source, target, load_sem.at[index])
        for index, (source, target) in enumerate(zip(far, near))
    ]
    stages[0](0)
    for copy in copies:
        copy.start()
    start_move()
    schedule = {
        0: ((1, 0), (0, 1)),
        4: ((2, 0), (1, 1), (0, 2), (0, 3)),
        7: ((3, 0),),
    }
    for copy in copies[1:]:
        copy.wait()

    def exchanged(index):
        return (arrived.at[:, :, lanes(index)], pair_recv.at[index])

    def add_pair(index):
        wait_for(*exchanged(index))
        columns = lanes(index)
        for which in range(2):
            total = grad_pair[which, :, columns].astype(jnp.float32)
            total = total + arrived[which, :, columns].astype(jnp.float32)
            grad_pair[which, :, columns] = low(total)

    last_pair = queries.shape[1] // 128 - 1

    @pl.loop(0, last_pair + 1)
    def _(index):
        for position, calls in schedule.items():
            @pl.when(index == position)
            def _():
                for stage, part in calls:
                    stages[stage](part)

        attend_back_pair(lanes(index), queries, own, other, bias, grad, context, log_total.at[index], cosine, sine, grad_query, grad_pair, grad_other)
        target, sem = exchanged(index)
        send_to(grad_other.at[:, :, lanes(index)], target, pair_send.at[index], sem, (partner, plane))

        @pl.when(index > 0)
        def _():
            add_pair(index - 1)

    copies[0].wait()
    query_copy = pltpu.make_async_copy(grad_query, far_query, out_sem.at[0])
    query_copy.start()

    def weight_grad(which, values):
        target = weight_grads[which]
        for group in range(4):
            slot = staged.at[group % 2]
            if group >= 2:
                wait_for(slot, stage_sem.at[group % 2])
            block = values[:, third * group : third * group + third]
            slot[...] = low(product_of(block, low_rows[...], ((0,), (0,))))
            pltpu.make_async_copy(slot, target.at[group], stage_sem.at[group % 2]).start()
        for group in range(2):
            wait_for(staged.at[group], stage_sem.at[group])

    weight_grad(0, grad_query)
    stages[0](4)
    add_pair(last_pair)
    pair_copy = pltpu.make_async_copy(grad_pair, far_pair, out_sem.at[1])
    pair_copy.start()
    weight_grad(1, grad_pair.at[0])
    stages[0](5)
    weight_grad(2, grad_pair.at[1])
    stages[0](6)
    calls = [(stage, step - (stage - 1)) for step in range(10) for stage in (4, 3, 2, 1)]
    done = {(1, 0), (2, 0), (1, 1), (3, 0)}
    for stage, part in calls:
        if 0 <= part < 7 and (stage, part) not in done:
            stages[stage](part)
    for part in range(7):
        finish(part)
    for index in range(last_pair + 1):
        wait_for(arrived.at[:, :, lanes(index)], pair_send.at[index])
    query_copy.wait()
    pair_copy.wait()
    finish_move()


def backward(grad_out, grad_in, grad_attn, rows_in, low_rows, queries, own, other, bias, grad, context, log_total, cosine, sine, collective_id):
    height, third = grad_out.shape[1], grad_attn.shape[1]
    count, width = queries.shape
    buffers, sems = scatter_scratch([height] * 3 + [third] * 4)
    sem = pltpu.SemaphoreType.DMA
    anywhere = pl.BlockSpec(memory_space=pl.ANY)
    local = pl.BlockSpec(memory_space=pltpu.VMEM)
    bf16 = jnp.bfloat16
    outs = pl.pallas_call(
        backward_kernel,
        out_shape=[
            jax.ShapeDtypeStruct((rows, 128), jnp.float32)
            for rows in (3 * third, third, 2 * height, height)
        ]
        + [
            jax.ShapeDtypeStruct((count, width), bf16),
            jax.ShapeDtypeStruct((2, count, width), bf16),
            jax.ShapeDtypeStruct((2, count // 2, width), rows_in.dtype),
        ]
        + [jax.ShapeDtypeStruct(grad_attn.shape, bf16)] * 3,
        in_specs=[anywhere] * 10 + [local] * 4,
        out_specs=[local] * 4 + [anywhere] * 6,
        scratch_shapes=[
            pltpu.VMEM(rows.shape, bf16) for rows in (low_rows, queries, own, other, grad, context)
        ]
        + [
            pltpu.VMEM((count, width), bf16),
            pltpu.VMEM((2, count, width), bf16),
            pltpu.VMEM((2, count, width), bf16),
            pltpu.VMEM((2, count, width), bf16),
            pltpu.VMEM((2, third, width), bf16),
        ]
        + buffers
        + sems
        + [sem((8,)), sem((8,)), sem((2,)), sem((6,)), sem((2,)), sem((2,)), sem((2,)), sem],
        compiler_params=pltpu.CompilerParams(
            collective_id=collective_id, has_side_effects=True, vmem_limit_bytes=60 * 1024 * 1024
        ),
        name="backward",
    )(grad_out, grad_in, grad_attn, rows_in, low_rows, queries, own, other, grad, context, bias, log_total, cosine, sine)
    return outs[:7]


def attend_back_pair(columns, queries, own, other, bias, grad, context, log_total, cosine, sine, grad_query, grad_own, grad_other):
    count = queries.shape[0]
    query_rows, grad_rows = queries[:, columns], grad[:, columns]
    query_turned, grad_turned = query_rows.T, grad_rows.T
    inner = (grad_rows.astype(jnp.float32) * context[:, columns].astype(jnp.float32)).T
    query_parts = [None, None]
    for half, (pair, result) in enumerate(((own, grad_own), (other, grad_other))):
        keys, values = pair[0, :, columns], pair[1, :, columns]
        key_turned = keys.T
        grad_keys, grad_values = None, None
        window = pl.ds(half * count, count)
        for head in range(2):
            lanes_of_head = slice(64 * head, 64 * head + 64)
            scores = scores_of(keys, head_rows(query_turned, head), bias[window])
            weights = jnp.exp(scores - log_total[head : head + 1])
            grad_weights = product_of(values, head_rows(grad_turned, head), ((1,), (0,)))
            inner_row = jnp.sum(inner[lanes_of_head], axis=0, keepdims=True)
            grad_scores = low(weights * (grad_weights - inner_row))
            value_part = product_of(low(weights), head_lanes(grad_rows, head), ((1,), (0,)))
            key_part = product_of(grad_scores, head_lanes(query_rows, head), ((1,), (0,)))
            query_part = product_of(key_turned[lanes_of_head], grad_scores, ((1,), (0,)))
            grad_values = value_part if head == 0 else grad_values + value_part
            grad_keys = key_part if head == 0 else grad_keys + key_part
            query_parts[head] = query_part if half == 0 else query_parts[head] + query_part
        result[0, :, columns] = turned(grad_keys, cosine[window], -sine[window]).astype(result.dtype)
        result[1, :, columns] = grad_values.astype(result.dtype)
    query_rows = jnp.concatenate(query_parts, axis=0).T * SCORE_SCALE
    own_rows = pl.ds(0, count)
    grad_query[:, columns] = low(turned(query_rows, cosine[own_rows], -sine[own_rows]))


def owner_kernel(rows, *refs):
    count = len(rows)
    shards, gain, whole, gain_out = refs[:count], refs[count], refs[count + 1], refs[count + 2]
    (gain_parts, own_sem, send_z, recv_z, send_x, recv_x, send_y, recv_y, send_d, recv_d, send_c, recv_c, send_g, recv_g) = refs[count + 3 :]
    me, partner, across, down = neighbours()
    plane = lax.axis_index("tensor")
    diagonal = across + down - me
    planes = [lax.rem(plane + offset, 4) for offset in (1, 2, 3)]
    greet(plane, (partner, across, down), planes)
    flip = lambda block: block + 1 - 2 * lax.rem(block, 2)

    def remote(source, target, send, recv, device):
        copy = pltpu.make_async_remote_copy(source, target, send, recv, device_id=device, device_id_type=MESH)
        copy.start()
        return copy

    def wait(view, sem):
        pltpu.make_async_copy(view, view, sem).wait()

    def place(part, slot, block):
        height = rows[part]
        first = pl.multiple_of(slot * height, 16)
        return whole.at[pl.ds(first, height), lanes(block)]

    for part in range(count):
        @pl.when(plane != part)
        def _():
            offset = lax.rem(plane + 3 - part, 4)
            remote(shards[part], place(part, plane, me), send_z.at[part], recv_z.at[offset], (me, part))
    gain_copies = [
        remote(gain, gain_parts.at[index], send_g.at[index], recv_g.at[index], (me, other))
        for index, other in enumerate(planes)
    ]

    def spread(part, source, slot):
        view = place(part, slot, me)
        remote(source, view, send_x.at[slot], recv_x.at[slot], (across, plane))
        remote(source, view, send_y.at[slot], recv_y.at[slot], (down, plane))
        remote(source, view, send_c.at[slot, 0], recv_c.at[slot, 0], (partner, plane))

    for part in range(count):
        @pl.when(plane == part)
        def _():
            pltpu.make_async_copy(shards[part], place(part, part, me), own_sem).start()
            spread(part, shards[part], part)
            for distance in (1, 3, 2):
                slot = (part + distance) % 4
                view = place(part, slot, me)
                wait(view, recv_z.at[(slot + 3 - part) % 4])
                spread(part, view, slot)
            for slot in range(4):
                view = place(part, slot, across)
                wait(view, recv_x.at[slot])
                remote(view, view, send_c.at[slot, 1], recv_c.at[slot, 1], (partner, plane))
                if slot < 2:
                    remote(view, view, send_d.at[slot], recv_d.at[slot], (down, plane))
                view = place(part, slot, down)
                wait(view, recv_y.at[slot])
                remote(view, view, send_c.at[slot, 2], recv_c.at[slot, 2], (partner, plane))
                if slot >= 2:
                    remote(view, view, send_d.at[slot], recv_d.at[slot], (across, plane))

    total = gain[...]
    for index in range(3):
        gain_copies[index].wait()
        total = total + gain_parts[index]
    gain_out[...] = total
    for index, other in ((3, across), (4, down), (5, partner)):
        copy = remote(gain_out, gain_parts.at[index], send_g.at[index], recv_g.at[index], (other, plane))
        copy.wait()
        gain_out[...] = gain_out[...] + gain_parts[index]

    for part in range(count):
        @pl.when(plane == part)
        def _():
            for slot in range(4):
                view = place(part, slot, diagonal)
                wait(view, recv_d.at[slot])
                remote(view, view, send_c.at[slot, 3], recv_c.at[slot, 3], (partner, plane))
            for slot in range(4):
                for index, block in enumerate((me, across, down, diagonal)):
                    wait(place(part, slot, flip(block)), recv_c.at[slot, index])
            wait(place(part, part, me), own_sem)
            for slot in range(4):
                view = place(part, slot, me)
                for sem in (send_x.at[slot], send_y.at[slot], send_d.at[slot]):
                    wait(view, sem)
                for index in range(4):
                    wait(view, send_c.at[slot, index])
        @pl.when(plane != part)
        def _():
            wait(shards[part], send_z.at[part])

def own_matrix(shards, gain, collective_id):
    rows = [s.shape[0] for s in shards]
    count = len(shards)
    sem = pltpu.SemaphoreType.DMA
    anyspec = pl.BlockSpec(memory_space=pl.ANY)
    vm = pl.BlockSpec(memory_space=pltpu.VMEM)
    return pl.pallas_call(
        functools.partial(owner_kernel, rows),
        out_shape=[jax.ShapeDtypeStruct((4 * max(rows), 1024), shards[0].dtype), jax.ShapeDtypeStruct(gain.shape, gain.dtype)],
        in_specs=[anyspec] * count + [vm],
        out_specs=[anyspec, vm],
        scratch_shapes=[pltpu.VMEM((6,) + gain.shape, gain.dtype), sem, sem((count,)), sem((3,))] + [sem((4,))] * 6 + [sem((4, 4))] * 2 + [sem((6,))] * 2,
        compiler_params=pltpu.CompilerParams(collective_id=collective_id, has_side_effects=True),
        name="own_matrix",
    )(*shards, gain)

def return_kernel(rows, *refs):
    count = len(rows)
    steps, outs = refs[0], refs[1 : 1 + count]
    own_sem, send_z, recv_z = refs[1 + count :]
    me = lax.axis_index("dp")
    plane = lax.axis_index("tensor")
    planes = [lax.rem(plane + offset, 4) for offset in (1, 2, 3)]
    greet(plane, (), planes)
    wait = lambda view, sem: pltpu.make_async_copy(view, view, sem).wait()
    for part in range(count):
        @pl.when(plane == part)
        def _():
            for slot in range(4):
                view = steps.at[pl.ds(slot * rows[part], rows[part]), :]
                if slot == part:
                    pltpu.make_async_copy(view, outs[part], own_sem).start()
                else:
                    pltpu.make_async_remote_copy(view, outs[part], send_z.at[slot], recv_z.at[part], device_id=(me, slot), device_id_type=MESH).start()
    for part in range(count):
        @pl.when(plane == part)
        def _():
            wait(outs[part], own_sem)
            for slot in range(4):
                if slot != part:
                    wait(outs[part], send_z.at[slot])
        @pl.when(plane != part)
        def _():
            wait(outs[part], recv_z.at[part])

def return_steps(steps, rows, collective_id):
    sem = pltpu.SemaphoreType.DMA
    anyspec = pl.BlockSpec(memory_space=pl.ANY)
    return pl.pallas_call(
        functools.partial(return_kernel, rows),
        out_shape=[jax.ShapeDtypeStruct((r, 128), steps.dtype) for r in rows],
        in_specs=[anyspec],
        out_specs=[anyspec] * len(rows),
        scratch_shapes=[sem, sem((4,)), sem((4,))],
        compiler_params=pltpu.CompilerParams(collective_id=collective_id, has_side_effects=True),
        name="return_steps",
    )(steps)

def product_of(left, right, dims):
    return lax.dot_general(left, right, (dims, ((), ())), preferred_element_type=jnp.float32)

def iterate_kernel(rows, whole, steps, iterate, poly, product, total, iterate_low, poly_low, other_low, total_low):
    size, tile = iterate.shape[0], 256
    plane = lax.axis_index("tensor")
    me = lax.axis_index("dp")
    f32, bf16 = jnp.float32, jnp.bfloat16
    windows = [pl.ds(first, tile) for first in range(0, size, tile)]
    zero = jnp.zeros((1, 1), f32)
    corner = lax.broadcasted_iota(jnp.int32, (tile, tile), 0) == lax.broadcasted_iota(jnp.int32, (tile, tile), 1)

    def store(window, result, shift, full, low_copy):
        fixed = [
            result[:, columns.start : columns.start + tile]
            - (jnp.where(corner, shift, 0.0) if columns.start == window.start else 0.0)
            for columns in windows
        ]
        result = jnp.concatenate(fixed, axis=1)
        full[window] = result
        low_copy[window] = result.astype(bf16)
        return result

    def fold(values):
        return jnp.sum(values, axis=0, keepdims=True)

    def finish(row):
        return jnp.sum(row, axis=1, keepdims=True) / size

    for part, height in enumerate(rows):
        @pl.when(plane == part)
        def _():
            @pl.loop(0, size // tile)
            def _(index):
                window = pl.ds(pl.multiple_of(index * tile, tile), tile)
                block = whole[0 : 4 * height, window]
                iterate[window] = product_of(block, whole[0 : 4 * height, :], ((0,), (0,)))
    trace = zero
    for window in windows:
        block = jnp.where(corner, iterate[window, window], 0.0)
        trace = trace + jnp.sum(fold(block), axis=1, keepdims=True)
    factor = 1.0 / (jnp.sqrt(trace) + NORM_FLOOR)
    squared = factor * factor
    mean = trace * squared / size
    row = jnp.zeros((1, size), f32)
    for window in windows:
        rest = store(window, iterate[window] * squared, mean, iterate, iterate_low)
        row = row + fold(rest * rest)
    square = finish(row)
    blank = jnp.zeros((1, size), f32)

    def polynomial(mean, square, with_total):
        linear = QUINTIC_THREE + 2.0 * QUINTIC_FIVE * mean
        shift = QUINTIC_FIVE * square
        poly_mean = QUINTIC_ONE + QUINTIC_THREE * mean + QUINTIC_FIVE * (mean * mean) + shift
        row, total_row = blank, blank
        for window in windows:
            mine = iterate[window]
            rest = product_of(iterate_low[window], iterate_low[...], ((1,), (0,)))
            rest = linear * mine + QUINTIC_FIVE * rest
            rest = store(window, rest, shift, poly, poly_low)
            row = row + fold(rest * mine)
            if with_total:
                total_row = total_row + fold(rest * total[window])
        return (poly_mean, finish(row), finish(total_row))

    def grow_total(poly_mean, total_mean, cross):
        for window in windows:
            result = poly_mean * total[window] + total_mean * poly[window]
            result = result + product_of(poly_low[window], total_low[...], ((1,), (0,)))
            store(window, result, cross, total, other_low)
        for window in windows:
            total_low[window] = other_low[window]
        return poly_mean * total_mean + cross

    def advance(poly_mean, mean, cross):
        row = blank
        for window in windows:
            rest = poly[window]
            result = poly_mean * iterate[window] + mean * rest
            result = result + product_of(poly_low[window], iterate_low[...], ((1,), (0,)))
            result = store(window, result, cross, product, other_low)
            row = row + fold(result * rest)
        product_mean = poly_mean * mean + cross
        cross = finish(row)
        row = blank
        for window in windows:
            result = poly_mean * product[window] + product_mean * poly[window]
            result = result + product_of(poly_low[window], other_low[...], ((1,), (0,)))
            result = store(window, result, cross, iterate, iterate_low)
            row = row + fold(result * result)
        return (poly_mean * product_mean + cross, finish(row))

    total_mean, cross, _ = polynomial(mean, square, False)
    for window in windows:
        total[window] = poly[window]
        total_low[window] = poly_low[window]
    mean, square = advance(total_mean, mean, cross)

    def sweep(_, carry):
        mean, square, total_mean = carry
        poly_mean, cross, cross_total = polynomial(mean, square, True)
        total_mean = grow_total(poly_mean, total_mean, cross_total)
        return advance(poly_mean, mean, cross) + (total_mean,)

    mean, square, total_mean = lax.fori_loop(0, NS_ITERS - 2, sweep, (mean, square, total_mean))
    poly_mean, _, cross_total = polynomial(mean, square, True)
    total_mean = grow_total(poly_mean, total_mean, cross_total)

    mine = pl.ds(pl.multiple_of(me * 128, 128), 128)
    columns = total_low[:, mine]
    for part, height in enumerate(rows):
        @pl.when(plane == part)
        def _():
            @pl.loop(0, 4)
            def _(slot):
                window = pl.ds(pl.multiple_of(slot * height, 16), height)
                result = product_of(whole[window, :], columns, ((1,), (0,)))
                result = result + total_mean * whole[window, mine].astype(f32)
                steps[window, :] = (factor * result).astype(bf16)

def iterate_owned(whole, rows):
    size = whole.shape[1]
    f32, bf16 = jnp.float32, jnp.bfloat16
    return pl.pallas_call(
        functools.partial(iterate_kernel, rows),
        out_shape=jax.ShapeDtypeStruct((whole.shape[0], 128), bf16),
        in_specs=[pl.BlockSpec(memory_space=pltpu.VMEM)],
        out_specs=pl.BlockSpec(memory_space=pltpu.VMEM),
        scratch_shapes=[pltpu.VMEM((size, size), f32)] * 4 + [pltpu.VMEM((size, size), bf16)] * 4,
        compiler_params=pltpu.CompilerParams(vmem_limit_bytes=58 * 1024 * 1024),
        name="iterate_owned",
    )(whole)


def weight_shards(weights):
    shards = [turn(weight) for weight in weights]
    third = shards[0].shape[0] // 3
    return [shards[0][third * part : third * part + third] for part in range(3)] + shards[1:]


def gather_weights(shards):
    tensor_count, dp_count = lax.axis_size("tensor"), lax.axis_size("dp")
    wholes = [lax.all_gather(shard, ("tensor", "dp")) for shard in shards]
    wholes = [
        whole.reshape(tensor_count, dp_count, *whole.shape[1:]).transpose(0, 2, 1, 3)
        for whole in wholes
    ]
    return [whole.reshape(*whole.shape[:2], -1) for whole in wholes]


def reduce_grads(grads):
    tensor_count, dp_count = lax.axis_size("tensor"), lax.axis_size("dp")
    sums = []
    for grad in grads:
        blocks = grad.reshape(*grad.shape[:2], dp_count, -1).transpose(0, 2, 1, 3)
        blocks = blocks.reshape(-1, *blocks.shape[2:])
        part = lax.psum_scatter(blocks, ("tensor", "dp"), scatter_dimension=0, tiled=True)
        sums.append(part[0].astype(jnp.float32))
    return sums


def lane_of(shape):
    return lax.broadcasted_iota(jnp.int32, shape, 1)

def turned(vectors, cosine, sine):
    lane = lax.rem(lane_of(vectors.shape), 64)
    swapped = jnp.where(lane < 32, pltpu.roll(vectors, 96, 1), pltpu.roll(vectors, 32, 1))
    return vectors * cosine + swapped * sine

def project_kernel(rows, query_weight, key_weight, value_weight, cosine, sine, queries, pair):
    rows = rows[...]
    for weight, target in ((query_weight, 0), (key_weight, 1)):
        result = product_of(rows, weight[0], ((1,), (1,)))
        for first in range(0, result.shape[1], 128):
            part = turned(result[:, first : first + 128], cosine[...], sine[...])
            if target == 0:
                queries[:, first : first + 128] = low(part * SCORE_SCALE)
            else:
                pair[0, :, first : first + 128] = low(part)
    pair[1] = low(product_of(rows, value_weight[0], ((1,), (1,))))

def project(rows, query_weight, key_weight, value_weight, cosine, sine):
    count, width = rows.shape
    groups, height, _ = query_weight.shape
    whole = lambda *shape: pl.BlockSpec(shape, lambda i: (0,) * len(shape))
    weight = pl.BlockSpec((1, height, width), lambda i: (i, 0, 0))
    return pl.pallas_call(
        project_kernel,
        grid=(groups,),
        out_shape=[jax.ShapeDtypeStruct((count, width), jnp.bfloat16), jax.ShapeDtypeStruct((2, count, width), jnp.bfloat16)],
        in_specs=[whole(count, width), weight, weight, weight, whole(count, 128), whole(count, 128)],
        out_specs=[pl.BlockSpec((count, height), lambda i: (0, i)), pl.BlockSpec((2, count, height), lambda i: (0, 0, i))],
        compiler_params=pltpu.CompilerParams(vmem_limit_bytes=40 * 1024 * 1024),
        name="project",
    )(rows, query_weight, key_weight, value_weight, cosine, sine)

def head_rows(transposed, head):
    rows = lax.broadcasted_iota(jnp.int32, transposed.shape, 0)
    return jnp.where(lax.div(rows, 64) == head, transposed, jnp.zeros_like(transposed))

def head_lanes(values, head):
    return jnp.where(lax.div(lane_of(values.shape), 64) == head, values, jnp.zeros_like(values))

def scores_of(keys, queries_turned, bias):
    scores = product_of(keys, queries_turned, ((1,), (0,)))
    return scores + jnp.concatenate([bias] * (scores.shape[1] // 128), axis=1)

def attend_kernel(queries, own, other, bias, context, log_total):
    query_turned = queries[...].T
    keys = jnp.concatenate([own[0], other[0]], axis=0)
    value_turned = jnp.concatenate([own[1].T, other[1].T], axis=1)
    parts, logs = [], []
    for head in range(2):
        scores = scores_of(keys, head_rows(query_turned, head), bias[...])
        highest = jnp.max(scores, axis=0, keepdims=True)
        weights = jnp.exp(scores - highest)
        total = jnp.sum(weights, axis=0, keepdims=True)
        part = product_of(value_turned[64 * head : 64 * head + 64], low(weights), ((1,), (0,)))
        parts.append(part / total)
        logs.append(highest + jnp.log(total))
    context[...] = low(jnp.concatenate(parts, axis=0)).T
    log_total[0] = jnp.concatenate(logs + logs * 3, axis=0)

def attend(queries, own, other, bias):
    count, width = queries.shape
    pairs = width // 128
    column = pl.BlockSpec((count, 128), lambda i: (0, i))
    double = pl.BlockSpec((2, count, 128), lambda i: (0, 0, i))
    return pl.pallas_call(
        attend_kernel,
        grid=(pairs,),
        out_shape=[jax.ShapeDtypeStruct((count, width), jnp.bfloat16), jax.ShapeDtypeStruct((pairs, 8, count), jnp.float32)],
        in_specs=[column, double, double, pl.BlockSpec((2 * count, 128), lambda i: (0, 0))],
        out_specs=[column, pl.BlockSpec((1, 8, count), lambda i: (i, 0, 0))],
        compiler_params=pltpu.CompilerParams(vmem_limit_bytes=40 * 1024 * 1024),
        name="attend",
    )(queries, own, other, bias)

def attend_back_kernel(queries, own, other, bias, grad, context, log_total, cosine, sine, grad_query, grad_own, grad_other):
    count = queries.shape[0]
    query_turned, grad_turned = queries[...].T, grad[...].T
    inner = (grad[...].astype(jnp.float32) * context[...].astype(jnp.float32)).T
    query_parts = [None, None]
    for half, (pair, result) in enumerate(((own, grad_own), (other, grad_other))):
        keys, values = pair[0], pair[1]
        key_turned = keys.T
        grad_keys, grad_values = None, None
        window = pl.ds(half * count, count)
        for head in range(2):
            lanes_of_head = slice(64 * head, 64 * head + 64)
            scores = scores_of(keys, head_rows(query_turned, head), bias[window])
            weights = jnp.exp(scores - log_total[0, head : head + 1])
            grad_weights = product_of(values, head_rows(grad_turned, head), ((1,), (0,)))
            inner_row = jnp.sum(inner[lanes_of_head], axis=0, keepdims=True)
            grad_scores = low(weights * (grad_weights - inner_row))
            value_part = product_of(low(weights), head_lanes(grad[...], head), ((1,), (0,)))
            key_part = product_of(grad_scores, head_lanes(queries[...], head), ((1,), (0,)))
            query_part = product_of(key_turned[lanes_of_head], grad_scores, ((1,), (0,)))
            grad_values = value_part if head == 0 else grad_values + value_part
            grad_keys = key_part if head == 0 else grad_keys + key_part
            query_parts[head] = query_part if half == 0 else query_parts[head] + query_part
        result[0] = turned(grad_keys, cosine[window], -sine[window]).astype(result.dtype)
        result[1] = grad_values.astype(result.dtype)
    grad_rows = jnp.concatenate(query_parts, axis=0).T * SCORE_SCALE
    own_rows = pl.ds(0, count)
    grad_query[...] = low(turned(grad_rows, cosine[own_rows], -sine[own_rows]))

def attend_back(queries, own, other, bias, grad, context, log_total, cosine, sine):
    count, width = queries.shape
    pairs = width // 128
    column = pl.BlockSpec((count, 128), lambda i: (0, i))
    double = pl.BlockSpec((2, count, 128), lambda i: (0, 0, i))
    table = pl.BlockSpec((2 * count, 128), lambda i: (0, 0))
    return pl.pallas_call(
        attend_back_kernel,
        grid=(pairs,),
        out_shape=[
            jax.ShapeDtypeStruct((count, width), jnp.bfloat16),
            jax.ShapeDtypeStruct((2, count, width), jnp.float32),
            jax.ShapeDtypeStruct((2, count, width), jnp.bfloat16),
        ],
        in_specs=[column, double, double, table, column, column, pl.BlockSpec((1, 8, count), lambda i: (i, 0, 0)), table, table],
        out_specs=[column, double, double],
        compiler_params=pltpu.CompilerParams(vmem_limit_bytes=48 * 1024 * 1024),
        name="attend_back",
    )(queries, own, other, bias, grad, context, log_total, cosine, sine)

def feed_kernel(rows, cotangent, in_weight, out_weight, result, grad_rows, grad_in, grad_out):
    height = out_weight.shape[1]
    @pl.when(pl.program_id(0) == 0)
    def _():
        result[...] = jnp.zeros_like(result)
        grad_rows[...] = jnp.zeros_like(grad_rows)
    gate = product_of(in_weight[0, 0:height], rows[...], ((1,), (1,)))
    up = product_of(in_weight[0, height:], rows[...], ((1,), (1,)))
    grad_hidden = product_of(out_weight[0], cotangent[...], ((1,), (1,)))
    below = 0.5 + 0.5 * lax.erf(gate * math.sqrt(0.5))
    active = gate * below
    hidden = low(active * up)
    slope = below + gate * jnp.exp(-0.5 * gate * gate) * (1.0 / math.sqrt(2.0 * math.pi))
    grad_gate = low(grad_hidden * up * slope)
    grad_up = low(grad_hidden * active)
    grad_out[0] = low(product_of(hidden, cotangent[...], ((1,), (0,))))
    grad_in[0, 0:height] = low(product_of(grad_gate, rows[...], ((1,), (0,))))
    grad_in[0, height:] = low(product_of(grad_up, rows[...], ((1,), (0,))))
    result[...] += product_of(hidden, out_weight[0], ((0,), (0,)))
    grad_rows[...] += product_of(grad_gate, in_weight[0, 0:height], ((0,), (0,)))
    grad_rows[...] += product_of(grad_up, in_weight[0, height:], ((0,), (0,)))

def feed(rows, cotangent, in_weight, out_weight):
    count, width = rows.shape
    groups, height, _ = out_weight.shape
    whole = pl.BlockSpec((count, width), lambda i: (0, 0))
    block = lambda size: pl.BlockSpec((1, size, width), lambda i: (i, 0, 0))
    return pl.pallas_call(
        feed_kernel,
        grid=(groups,),
        out_shape=[
            jax.ShapeDtypeStruct((count, width), jnp.float32),
            jax.ShapeDtypeStruct((count, width), jnp.float32),
            jax.ShapeDtypeStruct(in_weight.shape, jnp.bfloat16),
            jax.ShapeDtypeStruct(out_weight.shape, jnp.bfloat16),
        ],
        in_specs=[whole, whole, block(2 * height), block(height)],
        out_specs=[whole, whole, block(2 * height), block(height)],
        compiler_params=pltpu.CompilerParams(vmem_limit_bytes=60 * 1024 * 1024),
        name="feed",
    )(rows, cotangent, in_weight, out_weight)


def turn(block):
    return block.transpose(*range(1, block.ndim), 0).reshape(-1, block.shape[0])


def turn_back(rows, like):
    rows = rows.reshape(*like.shape[1:], like.shape[0])
    return rows.transpose(rows.ndim - 1, *range(rows.ndim - 1))


def orthogonal_steps(blocks, gain_part):
    tensor_count, dp_count = lax.axis_size("tensor"), lax.axis_size("dp")
    heights = [block.shape[0] for block in blocks]
    if (tensor_count, dp_count, blocks[0].shape[1]) == (4, 8, 128):
        whole, gain_grad = own_matrix(blocks, gain_part, 3)
        steps = iterate_owned(whole, heights)
        return (return_steps(steps, heights, 4), gain_grad)
    row_count = blocks[0].shape[1]
    first_row = lax.axis_index("dp") * row_count
    gain_grad = lax.psum(gain_part, BOTH)
    widest = max(heights)
    stacked = jnp.stack(
        [jnp.pad(block.T, ((0, 0), (0, widest - block.shape[0]))) for block in blocks]
    )
    owned = lax.all_to_all(stacked, "tensor", split_axis=0, concat_axis=0, tiled=True)
    whole = lax.all_gather(owned, "dp", axis=1, tiled=True)
    mean, rest = newton_schulz(einsum("tik,tjk->ij", whole, whole))
    own_rows = lax.dynamic_slice_in_dim(rest, first_row, row_count, 0)
    own_whole = lax.dynamic_slice_in_dim(whole, first_row, row_count, 1)
    step_rows = low(einsum("ij,tjk->tik", low(own_rows), whole) + mean * own_whole)
    returned = lax.all_to_all(step_rows, "tensor", split_axis=0, concat_axis=0, tiled=True)
    return ([returned[index, :, :height].T for index, height in enumerate(heights)], gain_grad)


def on_device(
    inputs,
    cotangent,
    lengths,
    qkv_weight,
    attn_out_weight,
    ffn_in_weight,
    ffn_out_weight,
    norm_gains,
    qkv_moment,
    attn_out_moment,
    ffn_in_moment,
    ffn_out_moment,
    gain_first,
    gain_second,
):
    tensor_count = lax.axis_size("tensor")
    dp_count = lax.axis_size("dp")
    dp_index = lax.axis_index("dp")
    tensor_index = lax.axis_index("tensor")
    core = dp_index % 2
    odd = tensor_index % 2 == 1
    upper = tensor_index >= tensor_count // 2
    lists = exchange_lists(dp_count // 2, tensor_count)
    weights = (qkv_weight, attn_out_weight, ffn_in_weight, ffn_out_weight)
    row_count = qkv_weight.shape[0]

    width = inputs.shape[3]
    local_rows = 2 * inputs.shape[2]
    fits = (tensor_count, dp_count, row_count, width) == (4, 8, 128, 1024)
    positions = jnp.concatenate(
        [core * local_rows + jnp.arange(local_rows), (1 - core) * local_rows + jnp.arange(local_rows)]
    )
    cosine, sine = rotary(positions)
    shards = weight_shards(weights)
    if fits:
        sizes = lengths.astype(jnp.float32)
        sizes = jnp.broadcast_to(jnp.pad(sizes, ((0, 6), (0, 0))), (8, 128))
        outs = forward(shards, inputs[:, 0], cotangent[:, 0], sizes, norm_gains, cosine, sine, 1)
        wholes, (rows_low, cotangent_low) = outs[:6], outs[6:8]
        low_one, queries, own, other, context, log_total, bias, middle, low_two = outs[8:]
    else:
        wholes = gather_weights(shards)
        rows_low = to_sequences(inputs[:, 0], lists, odd, upper)
        cotangent_low = to_sequences(cotangent[:, 0], lists, odd, upper)
    query_all, key_all, value_all, attn_all, ffn_in_all, ffn_out_all = wholes
    attn_rows = attn_all.reshape(-1, width)
    rows_in = rows_low.astype(jnp.float32)
    grad_rows = cotangent_low.astype(jnp.float32)
    normed_one, inverse_one, scaled_one = layer_norm_parts(rows_in, norm_gains[0])
    if not fits:
        own_lengths = swap_partner(lengths)
        both_lengths = jnp.where(
            core == 0,
            jnp.concatenate([lengths, own_lengths], 1),
            jnp.concatenate([own_lengths, lengths], 1),
        )
        length = lax.dynamic_index_in_dim(both_lengths.reshape(-1), tensor_index, 0, keepdims=False)
        bias = jnp.where(positions < length, 0.0, MASK_VALUE).astype(jnp.float32)
        bias = jnp.broadcast_to(bias[:, None], (positions.shape[0], 128))
        low_one = low(scaled_one)
        queries, own = project(
            low_one, query_all, key_all, value_all, cosine[:local_rows], sine[:local_rows]
        )
        other = swap_partner(own)
        context, log_total = attend(queries, own, other, bias)
        middle = rows_in + einsum("sk,kn->sn", context, attn_rows)
    normed_two, inverse_two, scaled_two = layer_norm_parts(middle, norm_gains[1])
    if not fits:
        low_two = low(scaled_two)
    ffn_branch, grad_scaled_two, grad_ffn_in, grad_ffn_out = feed(
        low_two, cotangent_low, ffn_in_all, ffn_out_all
    )
    result = low(middle + ffn_branch)
    grad_from_two, gain_two = layer_norm_back(
        grad_scaled_two, normed_two, inverse_two, norm_gains[1]
    )
    grad_middle = grad_rows + grad_from_two
    grad_branch = low(grad_middle)
    grad_context = low(einsum("sn,kn->sk", grad_branch, attn_rows))
    grad_attn_out = low(einsum("sk,sn->kn", context, grad_branch)).reshape(attn_all.shape)
    attention = (queries, own, other, bias, grad_context, context, log_total, cosine, sine)
    if fits:
        outs = backward(grad_ffn_out, grad_ffn_in, grad_attn_out, result, low_one, *attention, 2)
        sums, (grad_query, grad_pair, outputs) = outs[:4], outs[4:]
    else:
        grad_query, grad_own, grad_other = attend_back(*attention)
        grad_pair = low(grad_own + swap_partner(grad_other).astype(jnp.float32))
    grad_parts = (grad_query, grad_pair[0], grad_pair[1])
    grad_scaled_one = sum(
        einsum("sk,kn->sn", part, weight.reshape(-1, width))
        for part, weight in zip(grad_parts, (query_all, key_all, value_all))
    )
    grad_from_one, gain_one = layer_norm_back(
        grad_scaled_one, normed_one, inverse_one, norm_gains[0]
    )
    input_low = low(grad_middle + grad_from_one)
    if not fits:
        grads = [low(einsum("sk,sn->kn", part, low_one)) for part in grad_parts]
        grads = [grad.reshape(query_all.shape) for grad in grads]
        sums = reduce_grads(grads + [grad_attn_out, grad_ffn_in, grad_ffn_out])
        outputs = from_sequences(result, lists, odd, upper)
        sums = [jnp.concatenate(sums[:3])] + list(sums[3:])
    input_grad = from_sequences(input_low, lists, odd, upper)
    outputs, input_grad = outputs[:, None], input_grad[:, None].astype(jnp.float32)

    moments = (qkv_moment, attn_out_moment, ffn_in_moment, ffn_out_moment)
    gain_part = jnp.stack([gain_one, gain_two])
    turned = [turn(moment) for moment in moments]
    turned = [MOMENTUM * moment + part for moment, part in zip(turned, sums)]
    new_moments = [turn_back(part, moment) for part, moment in zip(turned, moments)]
    steps, gain_grad = orthogonal_steps([low(part) for part in turned], gain_part)
    new_weights = [
        weight.astype(jnp.float32) * (1.0 - MUON_RATE * DECAY_RATE)
        - MUON_RATE
        * 0.2
        * math.sqrt(step.shape[0] * tensor_count)
        * turn_back(step, weight).astype(jnp.float32)
        for weight, step in zip(weights, steps)
    ]
    gain_first_new = BETA_ONE * gain_first + (1.0 - BETA_ONE) * gain_grad
    gain_second_new = BETA_TWO * gain_second + (1.0 - BETA_TWO) * gain_grad * gain_grad
    first_hat = gain_first_new / (1.0 - BETA_ONE**STEP)
    second_hat = gain_second_new / (1.0 - BETA_TWO**STEP)
    norm_gains_new = norm_gains - ADAM_RATE * (
        first_hat / (jnp.sqrt(second_hat) + ADAM_EPS) + DECAY_RATE * norm_gains
    )
    return (
        outputs,
        input_grad,
        new_moments[0],
        new_weights[0],
        new_moments[1],
        new_weights[1],
        new_moments[2],
        new_weights[2],
        new_moments[3],
        new_weights[3],
        gain_first_new,
        gain_second_new,
        norm_gains_new,
    )


def solution(mesh):
    in_specs = (
        P(None, "dp", "tensor", None),
        P(None, "dp", "tensor", None),
        P(None, "dp"),
        P("dp", None, "tensor"),
        P("dp", "tensor"),
        P("dp", None, "tensor"),
        P("dp", "tensor"),
        P(),
        P("dp", None, "tensor"),
        P("dp", "tensor"),
        P("dp", None, "tensor"),
        P("dp", "tensor"),
        P(),
        P(),
    )
    out_specs = (
        P(None, "dp", "tensor", None),
        P(None, "dp", "tensor", None),
        P("dp", None, "tensor"),
        P("dp", None, "tensor"),
        P("dp", "tensor"),
        P("dp", "tensor"),
        P("dp", None, "tensor"),
        P("dp", None, "tensor"),
        P("dp", "tensor"),
        P("dp", "tensor"),
        P(),
        P(),
        P(),
    )
    return jax.shard_map(
        on_device, mesh=mesh, in_specs=in_specs, out_specs=out_specs, check_vma=False
    )
```

```python
import functools
import math

import jax
import jax.numpy as jnp
from jax import lax
from jax.experimental import pallas as pl
from jax.experimental.pallas import tpu as pltpu
from jax.sharding import PartitionSpec as P

HEAD_DIM = 64
NS_ITERS = 5
STEP = 10
SCORE_SCALE = 1.0 / math.sqrt(HEAD_DIM)


ROPE_BASE = 160000.0
NORM_EPS = 1e-05
MASK_VALUE = -1e30
MOMENTUM = 0.95
MUON_RATE = 0.1
DECAY_RATE = 0.01
QUINTIC_ONE = 3.4445
QUINTIC_THREE = -4.775
QUINTIC_FIVE = 2.0315
NORM_FLOOR = 1e-07
BETA_ONE = 0.9
BETA_TWO = 0.95
ADAM_RATE = 0.2
ADAM_EPS = 1e-08
BOTH = ("dp", "tensor")
MESH = pl.DeviceIdType.MESH


def rotary(positions):
    half_size = HEAD_DIM // 2
    exponents = jnp.arange(half_size).astype(jnp.float32) / half_size
    frequency = jnp.power(ROPE_BASE, -exponents)
    angles = positions.astype(jnp.float32)[:, None] * frequency[None, :]
    cosine, sine = jnp.cos(angles), jnp.sin(angles)
    return (
        jnp.concatenate([cosine] * 4, axis=1),
        jnp.concatenate([-sine, sine, -sine, sine], axis=1),
    )


def layer_norm_parts(vectors, gain):
    centre = vectors - jnp.mean(vectors, axis=-1, keepdims=True)
    inverse = lax.rsqrt(jnp.mean(centre * centre, axis=-1, keepdims=True) + NORM_EPS)
    normed = centre * inverse
    return (normed, inverse, normed * gain)


def layer_norm_back(grad_out, normed, inverse, gain):
    grad_normed = grad_out * gain
    mean_grad = jnp.mean(grad_normed, axis=-1, keepdims=True)
    mean_cross = jnp.mean(grad_normed * normed, axis=-1, keepdims=True)
    return (
        inverse * (grad_normed - mean_grad - normed * mean_cross),
        jnp.sum(grad_out * normed, axis=0),
    )


def einsum(spec, *operands):
    return jnp.einsum(spec, *operands, preferred_element_type=jnp.float32)


def low(values):
    return values.astype(jnp.bfloat16)


def exchange_lists(chip_count, tensor_count):
    first_list, second_list = [], []
    for chip in range(chip_count):
        for core in range(2):
            for slot in range(tensor_count):
                for micro in range(2):
                    source = (2 * chip + core) * tensor_count + slot
                    target = (2 * chip + slot // 2) * tensor_count + 2 * micro + core
                    pair = (source, target)
                    (first_list if slot % 2 == micro else second_list).append(pair)
    return (first_list, second_list)


def to_sequences(blocks, lists, odd, upper):
    first = lax.ppermute(jnp.where(odd, blocks[1], blocks[0]), BOTH, lists[0])
    second = lax.ppermute(jnp.where(odd, blocks[0], blocks[1]), BOTH, lists[1])
    return jnp.where(
        upper, jnp.concatenate([second, first]), jnp.concatenate([first, second])
    )


def from_sequences(rows, lists, odd, upper):
    half = rows.shape[0] // 2
    top, bottom = rows[:half], rows[half:]
    back = [[(target, source) for source, target in pairs] for pairs in lists]
    first = lax.ppermute(jnp.where(upper, bottom, top), BOTH, back[0])
    second = lax.ppermute(jnp.where(upper, top, bottom), BOTH, back[1])
    return jnp.where(odd, jnp.stack([second, first]), jnp.stack([first, second]))


def swap_partner(values):
    count = lax.axis_size("dp")
    return lax.ppermute(values, "dp", [(index, index ^ 1) for index in range(count)])


def mean_split(matrix):
    mean = jnp.trace(matrix) / matrix.shape[0]
    return (mean, matrix - mean * jnp.eye(matrix.shape[0], dtype=jnp.float32))


def split_product(left, right):
    left_mean, left_rest = left
    right_mean, right_rest = right
    product = einsum("ij,jk->ik", low(left_rest), low(right_rest))
    product = product + left_mean * right_rest + right_mean * left_rest
    mean, rest = mean_split(product)
    return (mean + left_mean * right_mean, rest)


def newton_schulz(gram):
    factor = 1.0 / (jnp.sqrt(jnp.trace(gram)) + NORM_FLOOR)
    iterate = mean_split(gram * (factor * factor))
    whole = None
    for sweep_index in range(NS_ITERS):
        square = split_product(iterate, iterate)
        poly = (
            QUINTIC_ONE + QUINTIC_THREE * iterate[0] + QUINTIC_FIVE * square[0],
            QUINTIC_THREE * iterate[1] + QUINTIC_FIVE * square[1],
        )
        whole = poly if whole is None else split_product(poly, whole)
        if sweep_index < NS_ITERS - 1:
            iterate = split_product(poly, split_product(poly, iterate))
    return (whole[0] * factor, whole[1] * factor)


def step_of(rows):
    return next(step for step in (128, 64, 32, 16) if rows % step == 0)


def lanes(block):
    return pl.ds(pl.multiple_of(block * 128, 128), 128)

def neighbours():
    me = lax.axis_index("dp")
    core, across, down = lax.rem(me, 2), lax.rem(lax.div(me, 2), 2), lax.div(me, 4)
    return (me, me + 1 - 2 * core, me + 2 - 4 * across, me + 4 - 8 * down)

def greet(plane, others, planes):
    barrier = pltpu.get_barrier_semaphore()
    me = lax.axis_index("dp")
    crossed = list(others[:1])
    for other in others:
        pl.semaphore_signal(barrier, inc=1, device_id=(other, plane), device_id_type=MESH)
    for other in planes:
        for same_place in [me] + crossed:
            pl.semaphore_signal(barrier, inc=1, device_id=(same_place, other), device_id_type=MESH)
    pl.semaphore_wait(barrier, len(others) + len(planes) * (1 + len(crossed)))

def add_into(target, source, rows, step):
    @pl.loop(0, rows // step)
    def _(index):
        window = pl.ds(pl.multiple_of(index * step, step), step)
        total = target[:, window].astype(jnp.float32) + source[:, window].astype(jnp.float32)
        target[:, window] = total.astype(jnp.bfloat16)


def send_to(source, target, send, recv, device):
    pltpu.make_async_remote_copy(
        source, target, send, recv, device_id=device, device_id_type=MESH
    ).start()


def wait_for(view, sem):
    pltpu.make_async_copy(view, view, sem).wait()


def move_plan(outward, source, target, send, recv, own):
    me, partner, _, _ = neighbours()
    plane = lax.axis_index("tensor")
    core = lax.rem(me, 2)
    column = me - core
    high, parity = lax.div(plane, 2), lax.rem(plane, 2)
    height = target.shape[1] if outward else source.shape[1]

    def owner_of(slot):
        return (column + parity, 2 * core + slot)

    def keeper_of(micro):
        return (column + high, 2 * micro + core)

    def same(device):
        return jnp.logical_and(device[0] == me, device[1] == plane)

    def half(rows, index):
        return rows.at[pl.ds(pl.multiple_of(index * height, height), height), :]

    def start():
        for index in range(2):
            if outward:
                device = owner_of(index)
                piece, goal, arrival = half(source, index), target.at[high], high
            else:
                device = keeper_of(index)
                piece, goal, arrival = source.at[index], half(target, parity), parity

            @pl.when(same(device))
            def _():
                pltpu.make_async_copy(piece, goal, own).start()

            @pl.when(jnp.logical_not(same(device)))
            def _():
                send_to(piece, goal, send.at[index], recv.at[arrival], device)

    def finish():
        for index in range(2):
            if outward:
                sent_to, came_from = owner_of(index), keeper_of(index)
                piece, goal = half(source, index), target.at[index]
            else:
                sent_to, came_from = keeper_of(index), owner_of(index)
                piece, goal = source.at[index], half(target, index)

            @pl.when(same(sent_to))
            def _():
                wait_for(piece, own)

            @pl.when(jnp.logical_not(same(sent_to)))
            def _():
                wait_for(piece, send.at[index])

            @pl.when(jnp.logical_not(same(came_from)))
            def _():
                wait_for(goal, recv.at[index])

    return (start, finish)


def scatter_plan(grads, sums, buffers, sems):
    held, from_x, from_y, from_yx, from_xy, from_z = buffers[:6]
    staging = buffers[6][0]
    (load_sem, send_c, recv_c, send_x, recv_x, send_y, recv_y, send_yx, recv_yx, send_xy, recv_xy, send_z, recv_z) = sems
    me, partner, across, down = neighbours()
    plane = lax.axis_index("tensor")
    planes = [lax.rem(plane + offset, 4) for offset in (1, 2, 3)]
    flip = lambda block: block + 1 - 2 * lax.rem(block, 2)
    blocks = (me, across, down, across + down - me)
    order = (3, 1, 2, 0)

    def view(part, block):
        ref, first, rows = grads[part]
        return ref.at[:, pl.ds(first, rows), lanes(block)]

    def slot(part, index):
        return staging.at[index, :, pl.ds(0, grads[part][2])]

    def stage_core(part):
        for index in order:
            send_to(view(part, flip(blocks[index])), held[part].at[index], send_c.at[part, index], recv_c.at[part, index], (partner, plane))

    def load(part):
        for index in order:
            pltpu.make_async_copy(view(part, blocks[index]), slot(part, index), load_sem.at[part, index]).start()

    def stage_first(part):
        rows = grads[part][2]
        load(part)
        for index in order:
            wait_for(slot(part, index), load_sem.at[part, index])
            wait_for(held[part].at[index], recv_c.at[part, index])
            add_into(held[part].at[index], slot(part, index), rows, step_of(rows))
            if index % 2 == 1:
                send_to(held[part].at[index, 0:2], from_x[part].at[index // 2], send_x.at[part, index // 2], recv_x.at[part, index // 2], (across, plane))
            if index // 2 == 1:
                send_to(held[part].at[index, 2:4], from_y[part].at[index % 2], send_y.at[part, index % 2], recv_y.at[part, index % 2], (down, plane))

    def stage_second(part):
        rows = grads[part][2]
        for side in (1, 0):
            wait_for(from_x[part].at[side], recv_x.at[part, side])
            add_into(held[part].at[2 * side, 0:2], from_x[part].at[side], rows, step_of(rows))
            if side == 1:
                send_to(held[part].at[2, 0:2], from_yx[part], send_yx.at[part], recv_yx.at[part], (down, plane))
            wait_for(from_y[part].at[side], recv_y.at[part, side])
            add_into(held[part].at[side, 2:4], from_y[part].at[side], rows, step_of(rows))
            if side == 1:
                send_to(held[part].at[1, 2:4], from_xy[part], send_xy.at[part], recv_xy.at[part], (across, plane))

    def stage_third(part):
        rows = grads[part][2]
        wait_for(from_yx[part], recv_yx.at[part])
        add_into(held[part].at[0, 0:2], from_yx[part], rows, step_of(rows))
        wait_for(from_xy[part], recv_xy.at[part])
        add_into(held[part].at[0, 2:4], from_xy[part], rows, step_of(rows))
        for index, other in enumerate(planes):
            send_to(held[part].at[0, other], from_z[part].at[index], send_z.at[part, index], recv_z.at[part, index], (me, other))

    def stage_last(part):
        rows = grads[part][2]
        step = step_of(rows)
        target, first = sums[part]
        for index in range(3):
            wait_for(from_z[part].at[index], recv_z.at[part, index])

        @pl.loop(0, rows // step)
        def _(index):
            offset = pl.multiple_of(index * step, step)
            window = pl.ds(offset, step)
            total = held[part][0, plane, window].astype(jnp.float32)
            for other in range(3):
                total = total + from_z[part][other, window].astype(jnp.float32)
            target[pl.ds(pl.multiple_of(first + offset, 16), step)] = total

    def finish(part):
        for index in range(4):
            wait_for(held[part].at[index], send_c.at[part, index])
        for side in range(2):
            wait_for(from_x[part].at[side], send_x.at[part, side])
            wait_for(from_y[part].at[side], send_y.at[part, side])
        wait_for(from_yx[part], send_yx.at[part])
        wait_for(from_xy[part], send_xy.at[part])
        for index in range(3):
            wait_for(from_z[part].at[index], send_z.at[part, index])

    return ((stage_core, stage_first, stage_second, stage_third, stage_last), finish)


def scatter_scratch(heights):
    sem = pltpu.SemaphoreType.DMA
    count = len(heights)
    leads = ((4, 4), (2, 2), (2, 2), (2,), (2,), (3,))
    buffers = [pltpu.VMEM(lead + (rows, 128), jnp.bfloat16) for lead in leads for rows in heights]
    buffers.append(pltpu.VMEM((4, 4, max(heights), 128), jnp.bfloat16))
    sems = [sem((count, 4))] * 3 + [sem((count, 2))] * 4 + [sem((count,))] * 4 + [sem((count, 3))] * 2
    return (buffers, sems)


def take(refs, count):
    taken, refs[:] = refs[:count], refs[count:]
    return taken


def gather_plan(shards, wholes, sems):
    own_sem, send_up, send_down, recv_z, send_x, recv_x, send_y, recv_y, send_d, recv_d, send_c, recv_c = sems
    me, partner, across, down = neighbours()
    plane = lax.axis_index("tensor")
    diagonal = across + down - me
    flip = lambda block: block + 1 - 2 * lax.rem(block, 2)

    def place(part, slot, block):
        return wholes[part].at[slot, :, lanes(block)]

    def spread(part, source, slot):
        view = place(part, slot, me)
        send_to(source, view, send_x.at[part, slot], recv_x.at[part, slot], (across, plane))
        send_to(source, view, send_y.at[part, slot], recv_y.at[part, slot], (down, plane))
        send_to(source, view, send_c.at[part, slot, 0], recv_c.at[part, slot, 0], (partner, plane))

    def pass_on(part, source, slot, upward):
        view = place(part, slot, me)
        sem = (send_up if upward else send_down).at[part, slot]
        send_to(source, view, sem, recv_z.at[part, slot], (me, plane + 1 if upward else plane - 1))

    def stage_own(part):
        pltpu.make_async_copy(shards[part], place(part, plane, me), own_sem.at[part]).start()

        @pl.when(plane < 3)
        def _():
            pass_on(part, shards[part], plane, True)

        @pl.when(plane > 0)
        def _():
            pass_on(part, shards[part], plane, False)

        spread(part, shards[part], plane)

    def stage_z(part):
        for distance in (1, 2, 3):
            for upward in (True, False):
                slot = plane - distance if upward else plane + distance

                @pl.when(slot >= 0 if upward else slot <= 3)
                def _():
                    view = place(part, slot, me)
                    wait_for(view, recv_z.at[part, slot])

                    @pl.when(plane < 3 if upward else plane > 0)
                    def _():
                        pass_on(part, view, slot, upward)

                    spread(part, view, slot)

    def stage_xy(part):
        for slot in range(4):
            view = place(part, slot, across)
            wait_for(view, recv_x.at[part, slot])
            if slot < 2:
                send_to(view, view, send_d.at[part, slot], recv_d.at[part, slot], (down, plane))
            send_to(view, view, send_c.at[part, slot, 1], recv_c.at[part, slot, 1], (partner, plane))
            view = place(part, slot, down)
            wait_for(view, recv_y.at[part, slot])
            if slot >= 2:
                send_to(view, view, send_d.at[part, slot], recv_d.at[part, slot], (across, plane))
            send_to(view, view, send_c.at[part, slot, 2], recv_c.at[part, slot, 2], (partner, plane))

    def stage_diagonal(part):
        for slot in range(4):
            view = place(part, slot, diagonal)
            wait_for(view, recv_d.at[part, slot])
            send_to(view, view, send_c.at[part, slot, 3], recv_c.at[part, slot, 3], (partner, plane))

    def arrive(part):
        wait_for(shards[part], own_sem.at[part])
        for slot in range(4):
            for index, block in enumerate((me, across, down, diagonal)):
                wait_for(place(part, slot, flip(block)), recv_c.at[part, slot, index])

    def finish(part):
        for slot in range(4):
            @pl.when(jnp.logical_and(slot <= plane, plane < 3))
            def _():
                wait_for(shards[part], send_up.at[part, slot])

            @pl.when(jnp.logical_and(slot >= plane, plane > 0))
            def _():
                wait_for(shards[part], send_down.at[part, slot])

            for sem in (send_x, send_y, send_d):
                wait_for(shards[part], sem.at[part, slot])
            for index in range(4):
                wait_for(shards[part], send_c.at[part, slot, index])

    return (stage_own, stage_z, stage_xy, stage_diagonal, arrive, finish)


def normed_rows(rows, gain):
    centre = rows - jnp.mean(rows, axis=1, keepdims=True)
    inverse = lax.rsqrt(jnp.mean(centre * centre, axis=1, keepdims=True) + NORM_EPS)
    return centre * inverse * gain


def forward_kernel(*refs):
    refs = list(refs)
    shards, (inputs, cotangent, lengths, gains, cosine, sine) = take(refs, 6), take(refs, 6)
    wholes, (rows_low, grad_rows) = take(refs, 6), take(refs, 2)
    low_one, queries, own, other, context, log_total, bias, middle, low_two = take(refs, 9)
    other_lengths, weight, attn_weight = take(refs, 3)
    sems = take(refs, 12)
    pair_send, pair_recv, length_send, length_recv, weight_sem, attn_sem = take(refs, 6)
    move_send, move_recv, move_own = refs
    me, partner, across, down = neighbours()
    plane = lax.axis_index("tensor")
    core = lax.rem(me, 2)
    stage_own, stage_z, stage_xy, stage_diagonal, arrive, finish = gather_plan(shards, wholes, sems)
    moves = [
        move_plan(False, source, target, move_send.at[index], move_recv.at[index], move_own.at[index])
        for index, (source, target) in enumerate(((inputs, rows_low), (cotangent, grad_rows)))
    ]
    greet(plane, (partner, across, down), [lax.rem(plane + offset, 4) for offset in (1, 2, 3)])
    count, width = rows_low.shape
    third = shards[0].shape[0]
    step = 64

    stage_own(0)
    stage_own(1)
    send_to(lengths, other_lengths, length_send, length_recv, (partner, plane))
    stage_z(0)
    stage_own(2)
    stage_z(1)
    stage_xy(0)
    stage_own(3)
    stage_z(2)
    stage_xy(1)
    stage_diagonal(0)
    stage_own(4)
    stage_z(3)
    stage_xy(2)
    stage_diagonal(1)
    stage_own(5)
    stage_z(4)
    moves[0][0]()
    stage_xy(3)
    stage_diagonal(2)
    stage_z(5)
    moves[1][0]()
    stage_diagonal(3)
    stage_xy(4)
    wait_for(other_lengths, length_recv)
    mine = core == lax.rem(plane, 2)
    both = jnp.where(mine, lengths[...], other_lengths[...])
    length = jnp.where(plane < 2, both[0:1], both[1:2])
    position = lax.broadcasted_iota(jnp.int32, bias.shape, 0)
    position = lax.rem(position + core * count, 2 * count).astype(jnp.float32)
    bias[...] = jnp.where(position < length, 0.0, MASK_VALUE)
    moves[0][1]()

    @pl.loop(0, count // step)
    def _(index):
        window = pl.ds(pl.multiple_of(index * step, step), step)
        low_one[window] = low(normed_rows(rows_low[window].astype(jnp.float32), gains[0:1]))

    for part in range(3):
        arrive(part)

    def load(group):
        for part in range(3):
            slot = lax.rem(group, 2)
            pltpu.make_async_copy(wholes[part].at[group], weight.at[slot, part], weight_sem.at[slot, part]).start()

    load(0)

    @pl.loop(0, 4)
    def _(group):
        @pl.when(group < 3)
        def _():
            load(group + 1)

        slot = lax.rem(group, 2)
        for part in range(3):
            wait_for(weight.at[slot, part], weight_sem.at[slot, part])
            result = product_of(low_one[...], weight[slot, part], ((1,), (1,)))
            for first in range(0, third, 128):
                columns = pl.ds(pl.multiple_of(group * third + first, 128), 128)
                piece = result[:, first : first + 128]
                if part < 2:
                    piece = turned(piece, cosine[0:count], sine[0:count])
                if part == 0:
                    queries[:, columns] = low(piece * SCORE_SCALE)
                else:
                    own[part - 1, :, columns] = low(piece)

    send_to(own, other, pair_send, pair_recv, (partner, plane))
    wait_for(other, pair_recv)
    arrive(3)
    attn_copy = pltpu.make_async_copy(wholes[3], attn_weight, attn_sem)
    attn_copy.start()
    schedule = {3: (stage_xy, 5), 6: (stage_diagonal, 4)}

    @pl.loop(0, width // 128)
    def _(index):
        for place, (stage, part) in schedule.items():
            @pl.when(index == place)
            def _():
                stage(part)

        attend_pair(lanes(index), queries, own, other, bias, context, log_total.at[index])

    attn_copy.wait()

    @pl.loop(0, count // 128)
    def _(index):
        window = pl.ds(pl.multiple_of(index * 128, 128), 128)
        rows = rows_low[window].astype(jnp.float32)
        for group in range(4):
            piece = context[window, third * group : third * group + third]
            rows = rows + product_of(piece, attn_weight[group], ((1,), (0,)))
        middle[window] = rows
        low_two[window] = low(normed_rows(rows, gains[1:2]))

    stage_diagonal(5)
    for part in (4, 5):
        arrive(part)
    for part in range(6):
        finish(part)
    wait_for(own, pair_send)
    wait_for(lengths, length_send)
    moves[1][1]()


def forward(shards, inputs, cotangent, lengths, gains, cosine, sine, collective_id):
    sem = pltpu.SemaphoreType.DMA
    anywhere = pl.BlockSpec(memory_space=pl.ANY)
    local = pl.BlockSpec(memory_space=pltpu.VMEM)
    bf16, f32 = jnp.bfloat16, jnp.float32
    count, width = 2 * inputs.shape[1], inputs.shape[2]
    third = shards[0].shape[0]
    shape = jax.ShapeDtypeStruct
    return pl.pallas_call(
        forward_kernel,
        out_shape=[shape((4, shard.shape[0], width), bf16) for shard in shards]
        + [
            shape((count, width), bf16),
            shape((count, width), bf16),
            shape((count, width), bf16),
            shape((count, width), bf16),
            shape((2, count, width), bf16),
            shape((2, count, width), bf16),
            shape((count, width), bf16),
            shape((width // 128, 8, count), f32),
            shape((2 * count, 128), f32),
            shape((count, width), f32),
            shape((count, width), bf16),
        ],
        in_specs=[anywhere] * 8 + [local] * 4,
        out_specs=[anywhere] * 6 + [local, anywhere] + [local] * 9,
        scratch_shapes=[
            pltpu.VMEM(lengths.shape, f32),
            pltpu.VMEM((2, 3, third, width), bf16),
            pltpu.VMEM((4, third, width), bf16),
            sem((6,)),
        ]
        + [sem((6, 4))] * 9
        + [sem((6, 4, 4))] * 2
        + [sem, sem, sem, sem, sem((2, 3)), sem]
        + [sem((2, 2)), sem((2, 2)), sem((2,))],
        compiler_params=pltpu.CompilerParams(
            collective_id=collective_id, has_side_effects=True, vmem_limit_bytes=58 * 1024 * 1024
        ),
        name="forward",
    )(*shards, inputs, cotangent, lengths, gains, cosine, sine)


def attend_pair(columns, queries, own, other, bias, context, log_total):
    query_turned = queries[:, columns].T
    keys = jnp.concatenate([own[0, :, columns], other[0, :, columns]], axis=0)
    value_turned = jnp.concatenate([own[1, :, columns].T, other[1, :, columns].T], axis=1)
    parts, logs = [], []
    for head in range(2):
        scores = scores_of(keys, head_rows(query_turned, head), bias[...])
        highest = jnp.max(scores, axis=0, keepdims=True)
        weights = jnp.exp(scores - highest)
        total = jnp.sum(weights, axis=0, keepdims=True)
        part = product_of(value_turned[64 * head : 64 * head + 64], low(weights), ((1,), (0,)))
        parts.append(part / total)
        logs.append(highest + jnp.log(total))
    context[:, columns] = low(jnp.concatenate(parts, axis=0)).T
    log_total[...] = jnp.concatenate(logs + logs * 3, axis=0)


def backward_kernel(*refs):
    refs = list(refs)
    grad_out, grad_in, grad_attn, rows_in = take(refs, 4)
    far, (bias, log_total, cosine, sine) = take(refs, 6), take(refs, 4)
    sums, (far_query, far_pair), (rows_out,) = take(refs, 4), take(refs, 2), take(refs, 1)
    weight_grads = take(refs, 3)
    near, (grad_query, grad_pair) = take(refs, 6), take(refs, 2)
    low_rows, queries, own, other, grad, context = near
    grad_other, arrived, staged = take(refs, 3)
    buffers = [take(refs, 7) for _ in range(6)] + [take(refs, 1)]
    sems = take(refs, 13)
    pair_send, pair_recv, stage_sem, load_sem, out_sem, move_send, move_recv, move_own = refs
    me, partner, across, down = neighbours()
    plane = lax.axis_index("tensor")
    height, third = grad_out.shape[1], grad_attn.shape[1]
    parts = [(grad_out, 0, height), (grad_in, 0, height), (grad_in, height, height)]
    parts += [(grad_attn, 0, third)] + [(ref, 0, third) for ref in weight_grads]
    sum_qkv, sum_attn, sum_in, sum_out = sums
    targets = [(sum_out, 0), (sum_in, 0), (sum_in, height), (sum_attn, 0)]
    targets += [(sum_qkv, third * index) for index in range(3)]
    stages, finish = scatter_plan(parts, targets, buffers, sems)
    start_move, finish_move = move_plan(True, rows_in, rows_out, move_send, move_recv, move_own)
    greet(plane, (partner, across, down), [lax.rem(plane + offset, 4) for offset in (1, 2, 3)])
    copies = [
        pltpu.make_async_copy(source, target, load_sem.at[index])
        for index, (source, target) in enumerate(zip(far, near))
    ]
    stages[0](0)
    for copy in copies:
        copy.start()
    start_move()
    schedule = {
        0: ((1, 0), (0, 1)),
        4: ((2, 0), (1, 1), (0, 2), (0, 3)),
        7: ((3, 0),),
    }
    for copy in copies[1:]:
        copy.wait()

    def exchanged(index):
        return (arrived.at[:, :, lanes(index)], pair_recv.at[index])

    def add_pair(index):
        wait_for(*exchanged(index))
        columns = lanes(index)
        for which in range(2):
            total = grad_pair[which, :, columns].astype(jnp.float32)
            total = total + arrived[which, :, columns].astype(jnp.float32)
            grad_pair[which, :, columns] = low(total)

    last_pair = queries.shape[1] // 128 - 1

    @pl.loop(0, last_pair + 1)
    def _(index):
        for position, calls in schedule.items():
            @pl.when(index == position)
            def _():
                for stage, part in calls:
                    stages[stage](part)

        attend_back_pair(lanes(index), queries, own, other, bias, grad, context, log_total.at[index], cosine, sine, grad_query, grad_pair, grad_other)
        target, sem = exchanged(index)
        send_to(grad_other.at[:, :, lanes(index)], target, pair_send.at[index], sem, (partner, plane))

        @pl.when(index > 0)
        def _():
            add_pair(index - 1)

    copies[0].wait()
    query_copy = pltpu.make_async_copy(grad_query, far_query, out_sem.at[0])
    query_copy.start()

    def weight_grad(which, values):
        target = weight_grads[which]
        for group in range(4):
            slot = staged.at[group % 2]
            if group >= 2:
                wait_for(slot, stage_sem.at[group % 2])
            block = values[:, third * group : third * group + third]
            slot[...] = low(product_of(block, low_rows[...], ((0,), (0,))))
            pltpu.make_async_copy(slot, target.at[group], stage_sem.at[group % 2]).start()
        for group in range(2):
            wait_for(staged.at[group], stage_sem.at[group])

    weight_grad(0, grad_query)
    stages[0](4)
    add_pair(last_pair)
    pair_copy = pltpu.make_async_copy(grad_pair, far_pair, out_sem.at[1])
    pair_copy.start()
    weight_grad(1, grad_pair.at[0])
    stages[0](5)
    weight_grad(2, grad_pair.at[1])
    stages[0](6)
    calls = [(stage, step - (stage - 1)) for step in range(10) for stage in (4, 3, 2, 1)]
    done = {(1, 0), (2, 0), (1, 1), (3, 0)}
    for stage, part in calls:
        if 0 <= part < 7 and (stage, part) not in done:
            stages[stage](part)
    for part in range(7):
        finish(part)
    for index in range(last_pair + 1):
        wait_for(arrived.at[:, :, lanes(index)], pair_send.at[index])
    query_copy.wait()
    pair_copy.wait()
    finish_move()


def backward(grad_out, grad_in, grad_attn, rows_in, low_rows, queries, own, other, bias, grad, context, log_total, cosine, sine, collective_id):
    height, third = grad_out.shape[1], grad_attn.shape[1]
    count, width = queries.shape
    buffers, sems = scatter_scratch([height] * 3 + [third] * 4)
    sem = pltpu.SemaphoreType.DMA
    anywhere = pl.BlockSpec(memory_space=pl.ANY)
    local = pl.BlockSpec(memory_space=pltpu.VMEM)
    bf16 = jnp.bfloat16
    outs = pl.pallas_call(
        backward_kernel,
        out_shape=[
            jax.ShapeDtypeStruct((rows, 128), jnp.float32)
            for rows in (3 * third, third, 2 * height, height)
        ]
        + [
            jax.ShapeDtypeStruct((count, width), bf16),
            jax.ShapeDtypeStruct((2, count, width), bf16),
            jax.ShapeDtypeStruct((2, count // 2, width), rows_in.dtype),
        ]
        + [jax.ShapeDtypeStruct(grad_attn.shape, bf16)] * 3,
        in_specs=[anywhere] * 10 + [local] * 4,
        out_specs=[local] * 4 + [anywhere] * 6,
        scratch_shapes=[
            pltpu.VMEM(rows.shape, bf16) for rows in (low_rows, queries, own, other, grad, context)
        ]
        + [
            pltpu.VMEM((count, width), bf16),
            pltpu.VMEM((2, count, width), bf16),
            pltpu.VMEM((2, count, width), bf16),
            pltpu.VMEM((2, count, width), bf16),
            pltpu.VMEM((2, third, width), bf16),
        ]
        + buffers
        + sems
        + [sem((8,)), sem((8,)), sem((2,)), sem((6,)), sem((2,)), sem((2,)), sem((2,)), sem],
        compiler_params=pltpu.CompilerParams(
            collective_id=collective_id, has_side_effects=True, vmem_limit_bytes=60 * 1024 * 1024
        ),
        name="backward",
    )(grad_out, grad_in, grad_attn, rows_in, low_rows, queries, own, other, grad, context, bias, log_total, cosine, sine)
    return outs[:7]


def attend_back_pair(columns, queries, own, other, bias, grad, context, log_total, cosine, sine, grad_query, grad_own, grad_other):
    count = queries.shape[0]
    query_rows, grad_rows = queries[:, columns], grad[:, columns]
    query_turned, grad_turned = query_rows.T, grad_rows.T
    inner = (grad_rows.astype(jnp.float32) * context[:, columns].astype(jnp.float32)).T
    query_parts = [None, None]
    for half, (pair, result) in enumerate(((own, grad_own), (other, grad_other))):
        keys, values = pair[0, :, columns], pair[1, :, columns]
        key_turned = keys.T
        grad_keys, grad_values = None, None
        window = pl.ds(half * count, count)
        for head in range(2):
            lanes_of_head = slice(64 * head, 64 * head + 64)
            scores = scores_of(keys, head_rows(query_turned, head), bias[window])
            weights = jnp.exp(scores - log_total[head : head + 1])
            grad_weights = product_of(values, head_rows(grad_turned, head), ((1,), (0,)))
            inner_row = jnp.sum(inner[lanes_of_head], axis=0, keepdims=True)
            grad_scores = low(weights * (grad_weights - inner_row))
            value_part = product_of(low(weights), head_lanes(grad_rows, head), ((1,), (0,)))
            key_part = product_of(grad_scores, head_lanes(query_rows, head), ((1,), (0,)))
            query_part = product_of(key_turned[lanes_of_head], grad_scores, ((1,), (0,)))
            grad_values = value_part if head == 0 else grad_values + value_part
            grad_keys = key_part if head == 0 else grad_keys + key_part
            query_parts[head] = query_part if half == 0 else query_parts[head] + query_part
        result[0, :, columns] = turned(grad_keys, cosine[window], -sine[window]).astype(result.dtype)
        result[1, :, columns] = grad_values.astype(result.dtype)
    query_rows = jnp.concatenate(query_parts, axis=0).T * SCORE_SCALE
    own_rows = pl.ds(0, count)
    grad_query[:, columns] = low(turned(query_rows, cosine[own_rows], -sine[own_rows]))


def product_of(left, right, dims):
    return lax.dot_general(left, right, (dims, ((), ())), preferred_element_type=jnp.float32)

def optimize_kernel(heights, *refs):
    refs = list(refs)
    count, size, tile = len(heights), 1024, 256
    f32, bf16 = jnp.float32, jnp.bfloat16
    sums, moments, weights = take(refs, count), take(refs, count), take(refs, count)
    (gain_two, gains), far = take(refs, 2), take(refs, 8)
    new_moments, new_weights = take(refs, count), take(refs, count)
    gain_out, rows_out = take(refs, 2)
    blocks, backs = take(refs, count), take(refs, count)
    whole, steps, gain_parts = take(refs, 3)
    iterate, poly, product, total = take(refs, 4)
    iterate_low, poly_low, other_low, total_low = take(refs, 4)
    value_rows, rows_in, rows_low = take(refs, 3)
    load_sem, own_sem, send_z, recv_z, send_x, recv_x, send_y, recv_y, send_d, recv_d, send_c, recv_c = take(refs, 12)
    send_g, recv_g, back_sem, send_b, recv_b, move_send, move_recv, move_own = refs
    me, partner, across, down = neighbours()
    plane = lax.axis_index("tensor")
    diagonal = across + down - me
    planes = [lax.rem(plane + offset, 4) for offset in (1, 2, 3)]
    flip = lambda block: block + 1 - 2 * lax.rem(block, 2)
    half = rows_low.shape[0]
    start_move, finish_move = move_plan(True, rows_low, rows_out, move_send, move_recv, move_own)
    near = (
        poly_low, other_low, total_low, iterate_low.at[0:half], iterate_low.at[half : 2 * half],
        value_rows, rows_in, poly.at[0:half],
    )
    loads = [
        pltpu.make_async_copy(source, target, load_sem.at[index])
        for index, (source, target) in enumerate(zip(far, near))
    ]
    for load in loads:
        load.start()

    def place(part, slot, block):
        height = heights[part]
        return whole.at[pl.ds(pl.multiple_of(slot * height, 16), height), lanes(block)]

    def spread(part, source, slot):
        view = place(part, slot, me)
        send_to(source, view, send_x.at[slot], recv_x.at[slot], (across, plane))
        send_to(source, view, send_y.at[slot], recv_y.at[slot], (down, plane))
        send_to(source, view, send_c.at[slot, 0], recv_c.at[slot, 0], (partner, plane))

    def on_plane(body):
        for part in range(count):
            @pl.when(plane == part)
            def _():
                body(part)

    def off_plane(body):
        for part in range(count):
            @pl.when(plane != part)
            def _():
                body(part)

    def tiles_of(part):
        height = heights[part]
        return [(first, min(128, height - first)) for first in range(0, height, 128)]

    greet(plane, (partner, across, down), planes)
    for part in (2, 0, 3, 1):
        for first, extent in tiles_of(part):
            rows, columns = pl.ds(first, extent), slice(first, first + extent)
            added = MOMENTUM * moments[part][:, columns] + sums[part][rows].T
            new_moments[part][:, columns] = added
            blocks[part][rows] = low(added.T)

        @pl.when(plane != part)
        def _():
            offset = lax.rem(plane + 3 - part, 4)
            send_to(blocks[part], place(part, plane, me), send_z.at[part], recv_z.at[offset], (me, part))

        @pl.when(plane == part)
        def _():
            pltpu.make_async_copy(blocks[part], place(part, part, me), own_sem).start()
            spread(part, blocks[part], part)

    def pass_z(part):
        for distance in (1, 3, 2):
            slot = (part + distance) % 4
            view = place(part, slot, me)
            wait_for(view, recv_z.at[(slot + 3 - part) % 4])
            spread(part, view, slot)

    on_plane(pass_z)

    for load in loads:
        load.wait()
    gain_out[1:2] = gain_two[...]
    gain_out[0:1] = jnp.zeros((1, size), f32)

    @pl.loop(0, half // 64)
    def _(index):
        first = pl.multiple_of(index * 64, 64)
        window = pl.ds(first, 64)
        other_window = pl.ds(pl.multiple_of(first + half, 64), 64)
        grad = product_of(iterate_low[window], poly_low[...], ((1,), (0,)))
        grad = grad + product_of(iterate_low[other_window], other_low[...], ((1,), (0,)))
        grad = grad + product_of(value_rows[window], total_low[...], ((1,), (0,)))
        rows = rows_in[window].astype(f32)
        centre = rows - jnp.mean(rows, axis=1, keepdims=True)
        inverse = lax.rsqrt(jnp.mean(centre * centre, axis=1, keepdims=True) + NORM_EPS)
        normed = centre * inverse
        scaled = grad * gains[0:1]
        mean_grad = jnp.mean(scaled, axis=1, keepdims=True)
        mean_cross = jnp.mean(scaled * normed, axis=1, keepdims=True)
        back = inverse * (scaled - mean_grad - normed * mean_cross)
        rows_low[window] = low(poly[window] + back)
        gain_out[0:1] += jnp.sum(grad * normed, axis=0, keepdims=True)

    start_move()
    for index, other in enumerate(planes):
        send_to(gain_out, gain_parts.at[index], send_g.at[index], recv_g.at[index], (me, other))

    def pass_xy(part):
        for slot in range(4):
            view = place(part, slot, across)
            wait_for(view, recv_x.at[slot])
            if slot < 2:
                send_to(view, view, send_d.at[slot], recv_d.at[slot], (down, plane))
            send_to(view, view, send_c.at[slot, 1], recv_c.at[slot, 1], (partner, plane))
            view = place(part, slot, down)
            wait_for(view, recv_y.at[slot])
            if slot >= 2:
                send_to(view, view, send_d.at[slot], recv_d.at[slot], (across, plane))
            send_to(view, view, send_c.at[slot, 2], recv_c.at[slot, 2], (partner, plane))

    on_plane(pass_xy)

    def pass_diagonal(part):
        for slot in range(4):
            view = place(part, slot, diagonal)
            wait_for(view, recv_d.at[slot])
            send_to(view, view, send_c.at[slot, 3], recv_c.at[slot, 3], (partner, plane))
        for slot in range(4):
            for index, block in enumerate((me, across, down, diagonal)):
                wait_for(place(part, slot, flip(block)), recv_c.at[slot, index])
        wait_for(blocks[part], own_sem)

    on_plane(pass_diagonal)

    windows = [pl.ds(first, tile) for first in range(0, size, tile)]
    zero = jnp.zeros((1, 1), f32)
    blank = jnp.zeros((1, size), f32)
    corner = lax.broadcasted_iota(jnp.int32, (tile, tile), 0) == lax.broadcasted_iota(jnp.int32, (tile, tile), 1)

    def gram(part):
        rows = slice(0, 4 * heights[part])
        for group in range(2):
            edge = group * size // 2

            @pl.loop(0, 2)
            def _(index):
                window = pl.ds(pl.multiple_of(edge + index * tile, tile), tile)
                iterate[window, edge:] = product_of(whole[rows, window], whole[rows, edge:], ((0,), (0,)))

    on_plane(gram)

    def upper(window):
        return slice(window.start, size)

    def store(window, result, shift, full, low_copy):
        corner_block = result[:, :tile] - jnp.where(corner, shift, 0.0)
        result = jnp.concatenate([corner_block, result[:, tile:]], axis=1) if result.shape[1] > tile else corner_block
        full[window, upper(window)] = result
        result_low = low(result)
        low_copy[window, upper(window)] = result_low
        for first in range(tile, result.shape[1], tile):
            low_copy[pl.ds(window.start + first, tile), window] = result_low[:, first : first + tile].T
        return result

    def fold(left, right, window):
        sums_of = jnp.sum(left * right, axis=0, keepdims=True)
        weighted = jnp.concatenate([sums_of[:, :tile], 2.0 * sums_of[:, tile:]], axis=1) if sums_of.shape[1] > tile else sums_of
        return jnp.concatenate([blank[:, : window.start], weighted], axis=1) if window.start else weighted

    def finish(row):
        return jnp.sum(row, axis=1, keepdims=True) / size

    def multiply(left, right, window):
        return product_of(left[window], right[:, upper(window)], ((1,), (0,)))

    trace = zero
    for window in windows:
        block = jnp.where(corner, iterate[window, window], 0.0)
        trace = trace + jnp.sum(jnp.sum(block, axis=0, keepdims=True), axis=1, keepdims=True)
    factor = 1.0 / (jnp.sqrt(trace) + NORM_FLOOR)
    squared = factor * factor
    mean = trace * squared / size
    row = blank
    for window in windows:
        rest = store(window, iterate[window, upper(window)] * squared, mean, iterate, iterate_low)
        row = row + fold(rest, rest, window)
    square = finish(row)

    def polynomial(mean, square, with_total):
        linear = QUINTIC_THREE + 2.0 * QUINTIC_FIVE * mean
        shift = QUINTIC_FIVE * square
        poly_mean = QUINTIC_ONE + QUINTIC_THREE * mean + QUINTIC_FIVE * (mean * mean) + shift
        row, total_row = blank, blank
        for window in windows:
            mine = iterate[window, upper(window)]
            rest = linear * mine + QUINTIC_FIVE * multiply(iterate_low, iterate_low, window)
            rest = store(window, rest, shift, poly, poly_low)
            row = row + fold(rest, mine, window)
            if with_total:
                total_row = total_row + fold(rest, total[window, upper(window)], window)
        return (poly_mean, finish(row), finish(total_row))

    def grow_total(poly_mean, total_mean, cross):
        for window in windows:
            result = poly_mean * total[window, upper(window)] + total_mean * poly[window, upper(window)]
            result = result + multiply(poly_low, total_low, window)
            store(window, result, cross, total, other_low)
        total_low[...] = other_low[...]
        return poly_mean * total_mean + cross

    def advance(poly_mean, mean, cross):
        row = blank
        for window in windows:
            rest = poly[window, upper(window)]
            result = poly_mean * iterate[window, upper(window)] + mean * rest
            result = result + multiply(poly_low, iterate_low, window)
            result = store(window, result, cross, product, other_low)
            row = row + fold(result, rest, window)
        product_mean = poly_mean * mean + cross
        cross = finish(row)
        row = blank
        for window in windows:
            result = poly_mean * product[window, upper(window)] + product_mean * poly[window, upper(window)]
            result = result + multiply(poly_low, other_low, window)
            result = store(window, result, cross, iterate, iterate_low)
            row = row + fold(result, result, window)
        return (poly_mean * product_mean + cross, finish(row))

    total_mean, cross, _ = polynomial(mean, square, False)
    for window in windows:
        total[window, upper(window)] = poly[window, upper(window)]
    total_low[...] = poly_low[...]
    mean, square = advance(total_mean, mean, cross)

    def sweep(_, carry):
        mean, square, total_mean = carry
        poly_mean, cross, cross_total = polynomial(mean, square, True)
        total_mean = grow_total(poly_mean, total_mean, cross_total)
        return advance(poly_mean, mean, cross) + (total_mean,)

    mean, square, total_mean = lax.fori_loop(0, NS_ITERS - 2, sweep, (mean, square, total_mean))
    poly_mean, _, cross_total = polynomial(mean, square, True)
    total_mean = grow_total(poly_mean, total_mean, cross_total)

    mine = lanes(me)
    columns = total_low[:, mine]

    def step_home(part):
        height = heights[part]

        @pl.loop(0, 4)
        def _(turn_of):
            slot = lax.rem(part + 1 + turn_of, 4)
            window = pl.ds(pl.multiple_of(slot * height, 16), height)
            result = product_of(whole[window, :], columns, ((1,), (0,)))
            result = result + total_mean * whole[window, mine].astype(f32)
            steps[window, :] = low(factor * result)

            @pl.when(turn_of == 3)
            def _():
                pltpu.make_async_copy(steps.at[window, :], backs[part], back_sem).start()

            @pl.when(turn_of < 3)
            def _():
                send_to(steps.at[window, :], backs[part], send_b.at[turn_of], recv_b.at[part], (me, slot))

    on_plane(step_home)

    for index in range(3):
        wait_for(gain_out, send_g.at[index])
        wait_for(gain_parts.at[index], recv_g.at[index])
    gain_out[...] = gain_out[...] + gain_parts[0] + gain_parts[1] + gain_parts[2]
    for index, other in ((3, across), (4, down), (5, partner)):
        send_to(gain_out, gain_parts.at[index], send_g.at[index], recv_g.at[index], (other, plane))
        wait_for(gain_out, send_g.at[index])
        wait_for(gain_parts.at[index], recv_g.at[index])
        gain_out[...] = gain_out[...] + gain_parts[index]

    on_plane(lambda part: wait_for(backs[part], back_sem))
    off_plane(lambda part: wait_for(backs[part], recv_b.at[part]))
    for part in range(count):
        rate = MUON_RATE * 0.2 * math.sqrt(4 * heights[part])
        for first, extent in tiles_of(part):
            rows, columns_of = pl.ds(first, extent), slice(first, first + extent)
            step = backs[part][rows].astype(f32).T
            kept = weights[part][:, columns_of].astype(f32) * (1.0 - MUON_RATE * DECAY_RATE)
            new_weights[part][:, columns_of] = kept - rate * step

    def last_waits(part):
        for slot in range(4):
            for sem in (send_x.at[slot], send_y.at[slot], send_d.at[slot]):
                wait_for(blocks[part], sem)
            for index in range(4):
                wait_for(blocks[part], send_c.at[slot, index])
        for index in range(3):
            wait_for(blocks[part], send_b.at[index])

    on_plane(last_waits)
    off_plane(lambda part: wait_for(blocks[part], send_z.at[part]))
    finish_move()


def optimize(sums, moments, weights, gain_two, gains, far, collective_id):
    heights = [part.shape[0] for part in sums]
    count, size = len(heights), gains.shape[1]
    f32, bf16 = jnp.float32, jnp.bfloat16
    sem = pltpu.SemaphoreType.DMA
    anywhere = pl.BlockSpec(memory_space=pl.ANY)
    local = pl.BlockSpec(memory_space=pltpu.VMEM)
    half = far[6].shape[0]
    outs = pl.pallas_call(
        functools.partial(optimize_kernel, heights),
        out_shape=[jax.ShapeDtypeStruct((128, height), f32) for height in heights] * 2
        + [jax.ShapeDtypeStruct(gains.shape, f32), jax.ShapeDtypeStruct((2, half // 2, size), bf16)],
        in_specs=[local] * (3 * count + 2) + [anywhere] * 8,
        out_specs=[local] * (2 * count + 1) + [anywhere],
        scratch_shapes=[pltpu.VMEM((height, 128), bf16) for height in heights] * 2
        + [pltpu.VMEM((4 * max(heights), size), bf16), pltpu.VMEM((4 * max(heights), 128), bf16)]
        + [pltpu.VMEM((6,) + gains.shape, f32)]
        + [pltpu.VMEM((size, size), f32)] * 4
        + [pltpu.VMEM((size, size), bf16)] * 4
        + [pltpu.VMEM((half, size), bf16)] * 3
        + [sem((8,)), sem, sem((count,)), sem((3,))]
        + [sem((4,))] * 6
        + [sem((4, 4))] * 2
        + [sem((6,))] * 2
        + [sem, sem((3,)), sem((count,)), sem((2,)), sem((2,)), sem],
        compiler_params=pltpu.CompilerParams(
            collective_id=collective_id, has_side_effects=True, vmem_limit_bytes=60 * 1024 * 1024
        ),
        name="optimize",
    )(*sums, *moments, *weights, gain_two, gains, *far)
    return (outs[:count], outs[count : 2 * count], outs[2 * count], outs[2 * count + 1])


def weight_shards(weights):
    shards = [turn(weight) for weight in weights]
    third = shards[0].shape[0] // 3
    return [shards[0][third * part : third * part + third] for part in range(3)] + shards[1:]


def gather_weights(shards):
    tensor_count, dp_count = lax.axis_size("tensor"), lax.axis_size("dp")
    wholes = [lax.all_gather(shard, ("tensor", "dp")) for shard in shards]
    wholes = [
        whole.reshape(tensor_count, dp_count, *whole.shape[1:]).transpose(0, 2, 1, 3)
        for whole in wholes
    ]
    return [whole.reshape(*whole.shape[:2], -1) for whole in wholes]


def reduce_grads(grads):
    tensor_count, dp_count = lax.axis_size("tensor"), lax.axis_size("dp")
    sums = []
    for grad in grads:
        blocks = grad.reshape(*grad.shape[:2], dp_count, -1).transpose(0, 2, 1, 3)
        blocks = blocks.reshape(-1, *blocks.shape[2:])
        part = lax.psum_scatter(blocks, ("tensor", "dp"), scatter_dimension=0, tiled=True)
        sums.append(part[0].astype(jnp.float32))
    return sums


def lane_of(shape):
    return lax.broadcasted_iota(jnp.int32, shape, 1)

def turned(vectors, cosine, sine):
    lane = lax.rem(lane_of(vectors.shape), 64)
    swapped = jnp.where(lane < 32, pltpu.roll(vectors, 96, 1), pltpu.roll(vectors, 32, 1))
    return vectors * cosine + swapped * sine

def project_kernel(rows, query_weight, key_weight, value_weight, cosine, sine, queries, pair):
    rows = rows[...]
    for weight, target in ((query_weight, 0), (key_weight, 1)):
        result = product_of(rows, weight[0], ((1,), (1,)))
        for first in range(0, result.shape[1], 128):
            part = turned(result[:, first : first + 128], cosine[...], sine[...])
            if target == 0:
                queries[:, first : first + 128] = low(part * SCORE_SCALE)
            else:
                pair[0, :, first : first + 128] = low(part)
    pair[1] = low(product_of(rows, value_weight[0], ((1,), (1,))))

def project(rows, query_weight, key_weight, value_weight, cosine, sine):
    count, width = rows.shape
    groups, height, _ = query_weight.shape
    whole = lambda *shape: pl.BlockSpec(shape, lambda i: (0,) * len(shape))
    weight = pl.BlockSpec((1, height, width), lambda i: (i, 0, 0))
    return pl.pallas_call(
        project_kernel,
        grid=(groups,),
        out_shape=[jax.ShapeDtypeStruct((count, width), jnp.bfloat16), jax.ShapeDtypeStruct((2, count, width), jnp.bfloat16)],
        in_specs=[whole(count, width), weight, weight, weight, whole(count, 128), whole(count, 128)],
        out_specs=[pl.BlockSpec((count, height), lambda i: (0, i)), pl.BlockSpec((2, count, height), lambda i: (0, 0, i))],
        compiler_params=pltpu.CompilerParams(vmem_limit_bytes=40 * 1024 * 1024),
        name="project",
    )(rows, query_weight, key_weight, value_weight, cosine, sine)

def head_rows(transposed, head):
    rows = lax.broadcasted_iota(jnp.int32, transposed.shape, 0)
    return jnp.where(lax.div(rows, 64) == head, transposed, jnp.zeros_like(transposed))

def head_lanes(values, head):
    return jnp.where(lax.div(lane_of(values.shape), 64) == head, values, jnp.zeros_like(values))

def scores_of(keys, queries_turned, bias):
    scores = product_of(keys, queries_turned, ((1,), (0,)))
    return scores + jnp.concatenate([bias] * (scores.shape[1] // 128), axis=1)

def attend_kernel(queries, own, other, bias, context, log_total):
    query_turned = queries[...].T
    keys = jnp.concatenate([own[0], other[0]], axis=0)
    value_turned = jnp.concatenate([own[1].T, other[1].T], axis=1)
    parts, logs = [], []
    for head in range(2):
        scores = scores_of(keys, head_rows(query_turned, head), bias[...])
        highest = jnp.max(scores, axis=0, keepdims=True)
        weights = jnp.exp(scores - highest)
        total = jnp.sum(weights, axis=0, keepdims=True)
        part = product_of(value_turned[64 * head : 64 * head + 64], low(weights), ((1,), (0,)))
        parts.append(part / total)
        logs.append(highest + jnp.log(total))
    context[...] = low(jnp.concatenate(parts, axis=0)).T
    log_total[0] = jnp.concatenate(logs + logs * 3, axis=0)

def attend(queries, own, other, bias):
    count, width = queries.shape
    pairs = width // 128
    column = pl.BlockSpec((count, 128), lambda i: (0, i))
    double = pl.BlockSpec((2, count, 128), lambda i: (0, 0, i))
    return pl.pallas_call(
        attend_kernel,
        grid=(pairs,),
        out_shape=[jax.ShapeDtypeStruct((count, width), jnp.bfloat16), jax.ShapeDtypeStruct((pairs, 8, count), jnp.float32)],
        in_specs=[column, double, double, pl.BlockSpec((2 * count, 128), lambda i: (0, 0))],
        out_specs=[column, pl.BlockSpec((1, 8, count), lambda i: (i, 0, 0))],
        compiler_params=pltpu.CompilerParams(vmem_limit_bytes=40 * 1024 * 1024),
        name="attend",
    )(queries, own, other, bias)

def attend_back_kernel(queries, own, other, bias, grad, context, log_total, cosine, sine, grad_query, grad_own, grad_other):
    count = queries.shape[0]
    query_turned, grad_turned = queries[...].T, grad[...].T
    inner = (grad[...].astype(jnp.float32) * context[...].astype(jnp.float32)).T
    query_parts = [None, None]
    for half, (pair, result) in enumerate(((own, grad_own), (other, grad_other))):
        keys, values = pair[0], pair[1]
        key_turned = keys.T
        grad_keys, grad_values = None, None
        window = pl.ds(half * count, count)
        for head in range(2):
            lanes_of_head = slice(64 * head, 64 * head + 64)
            scores = scores_of(keys, head_rows(query_turned, head), bias[window])
            weights = jnp.exp(scores - log_total[0, head : head + 1])
            grad_weights = product_of(values, head_rows(grad_turned, head), ((1,), (0,)))
            inner_row = jnp.sum(inner[lanes_of_head], axis=0, keepdims=True)
            grad_scores = low(weights * (grad_weights - inner_row))
            value_part = product_of(low(weights), head_lanes(grad[...], head), ((1,), (0,)))
            key_part = product_of(grad_scores, head_lanes(queries[...], head), ((1,), (0,)))
            query_part = product_of(key_turned[lanes_of_head], grad_scores, ((1,), (0,)))
            grad_values = value_part if head == 0 else grad_values + value_part
            grad_keys = key_part if head == 0 else grad_keys + key_part
            query_parts[head] = query_part if half == 0 else query_parts[head] + query_part
        result[0] = turned(grad_keys, cosine[window], -sine[window]).astype(result.dtype)
        result[1] = grad_values.astype(result.dtype)
    grad_rows = jnp.concatenate(query_parts, axis=0).T * SCORE_SCALE
    own_rows = pl.ds(0, count)
    grad_query[...] = low(turned(grad_rows, cosine[own_rows], -sine[own_rows]))

def attend_back(queries, own, other, bias, grad, context, log_total, cosine, sine):
    count, width = queries.shape
    pairs = width // 128
    column = pl.BlockSpec((count, 128), lambda i: (0, i))
    double = pl.BlockSpec((2, count, 128), lambda i: (0, 0, i))
    table = pl.BlockSpec((2 * count, 128), lambda i: (0, 0))
    return pl.pallas_call(
        attend_back_kernel,
        grid=(pairs,),
        out_shape=[
            jax.ShapeDtypeStruct((count, width), jnp.bfloat16),
            jax.ShapeDtypeStruct((2, count, width), jnp.float32),
            jax.ShapeDtypeStruct((2, count, width), jnp.bfloat16),
        ],
        in_specs=[column, double, double, table, column, column, pl.BlockSpec((1, 8, count), lambda i: (i, 0, 0)), table, table],
        out_specs=[column, double, double],
        compiler_params=pltpu.CompilerParams(vmem_limit_bytes=48 * 1024 * 1024),
        name="attend_back",
    )(queries, own, other, bias, grad, context, log_total, cosine, sine)

def feed_kernel(rows, cotangent, in_weight, out_weight, result, grad_rows, grad_in, grad_out):
    height = out_weight.shape[1]
    @pl.when(pl.program_id(0) == 0)
    def _():
        result[...] = jnp.zeros_like(result)
        grad_rows[...] = jnp.zeros_like(grad_rows)
    gate = product_of(in_weight[0, 0:height], rows[...], ((1,), (1,)))
    up = product_of(in_weight[0, height:], rows[...], ((1,), (1,)))
    grad_hidden = product_of(out_weight[0], cotangent[...], ((1,), (1,)))
    below = 0.5 + 0.5 * lax.erf(gate * math.sqrt(0.5))
    active = gate * below
    hidden = low(active * up)
    slope = below + gate * jnp.exp(-0.5 * gate * gate) * (1.0 / math.sqrt(2.0 * math.pi))
    grad_gate = low(grad_hidden * up * slope)
    grad_up = low(grad_hidden * active)
    grad_out[0] = low(product_of(hidden, cotangent[...], ((1,), (0,))))
    grad_in[0, 0:height] = low(product_of(grad_gate, rows[...], ((1,), (0,))))
    grad_in[0, height:] = low(product_of(grad_up, rows[...], ((1,), (0,))))
    result[...] += product_of(hidden, out_weight[0], ((0,), (0,)))
    grad_rows[...] += product_of(grad_gate, in_weight[0, 0:height], ((0,), (0,)))
    grad_rows[...] += product_of(grad_up, in_weight[0, height:], ((0,), (0,)))

def feed(rows, cotangent, in_weight, out_weight):
    count, width = rows.shape
    groups, height, _ = out_weight.shape
    whole = pl.BlockSpec((count, width), lambda i: (0, 0))
    block = lambda size: pl.BlockSpec((1, size, width), lambda i: (i, 0, 0))
    return pl.pallas_call(
        feed_kernel,
        grid=(groups,),
        out_shape=[
            jax.ShapeDtypeStruct((count, width), jnp.float32),
            jax.ShapeDtypeStruct((count, width), jnp.float32),
            jax.ShapeDtypeStruct(in_weight.shape, jnp.bfloat16),
            jax.ShapeDtypeStruct(out_weight.shape, jnp.bfloat16),
        ],
        in_specs=[whole, whole, block(2 * height), block(height)],
        out_specs=[whole, whole, block(2 * height), block(height)],
        compiler_params=pltpu.CompilerParams(vmem_limit_bytes=60 * 1024 * 1024),
        name="feed",
    )(rows, cotangent, in_weight, out_weight)


def turn(block):
    return block.transpose(*range(1, block.ndim), 0).reshape(-1, block.shape[0])


def turn_back(rows, like):
    rows = rows.reshape(*like.shape[1:], like.shape[0])
    return rows.transpose(rows.ndim - 1, *range(rows.ndim - 1))


def orthogonal_steps(blocks, gain_part):
    tensor_count = lax.axis_size("tensor")
    heights = [block.shape[0] for block in blocks]
    row_count = blocks[0].shape[1]
    first_row = lax.axis_index("dp") * row_count
    gain_grad = lax.psum(gain_part, BOTH)
    widest = max(heights)
    stacked = jnp.stack(
        [jnp.pad(block.T, ((0, 0), (0, widest - block.shape[0]))) for block in blocks]
    )
    owned = lax.all_to_all(stacked, "tensor", split_axis=0, concat_axis=0, tiled=True)
    whole = lax.all_gather(owned, "dp", axis=1, tiled=True)
    mean, rest = newton_schulz(einsum("tik,tjk->ij", whole, whole))
    own_rows = lax.dynamic_slice_in_dim(rest, first_row, row_count, 0)
    own_whole = lax.dynamic_slice_in_dim(whole, first_row, row_count, 1)
    step_rows = low(einsum("ij,tjk->tik", low(own_rows), whole) + mean * own_whole)
    returned = lax.all_to_all(step_rows, "tensor", split_axis=0, concat_axis=0, tiled=True)
    return ([returned[index, :, :height].T for index, height in enumerate(heights)], gain_grad)


def on_device(
    inputs,
    cotangent,
    lengths,
    qkv_weight,
    attn_out_weight,
    ffn_in_weight,
    ffn_out_weight,
    norm_gains,
    qkv_moment,
    attn_out_moment,
    ffn_in_moment,
    ffn_out_moment,
    gain_first,
    gain_second,
):
    tensor_count = lax.axis_size("tensor")
    dp_count = lax.axis_size("dp")
    dp_index = lax.axis_index("dp")
    tensor_index = lax.axis_index("tensor")
    core = dp_index % 2
    odd = tensor_index % 2 == 1
    upper = tensor_index >= tensor_count // 2
    lists = exchange_lists(dp_count // 2, tensor_count)
    weights = (qkv_weight, attn_out_weight, ffn_in_weight, ffn_out_weight)
    row_count = qkv_weight.shape[0]

    width = inputs.shape[3]
    local_rows = 2 * inputs.shape[2]
    fits = (tensor_count, dp_count, row_count, width) == (4, 8, 128, 1024)
    positions = jnp.concatenate(
        [core * local_rows + jnp.arange(local_rows), (1 - core) * local_rows + jnp.arange(local_rows)]
    )
    cosine, sine = rotary(positions)
    shards = weight_shards(weights)
    if fits:
        sizes = lengths.astype(jnp.float32)
        sizes = jnp.broadcast_to(jnp.pad(sizes, ((0, 6), (0, 0))), (8, 128))
        outs = forward(shards, inputs[:, 0], cotangent[:, 0], sizes, norm_gains, cosine, sine, 1)
        wholes, (rows_low, cotangent_low) = outs[:6], outs[6:8]
        low_one, queries, own, other, context, log_total, bias, middle, low_two = outs[8:]
    else:
        wholes = gather_weights(shards)
        rows_low = to_sequences(inputs[:, 0], lists, odd, upper)
        cotangent_low = to_sequences(cotangent[:, 0], lists, odd, upper)
    query_all, key_all, value_all, attn_all, ffn_in_all, ffn_out_all = wholes
    attn_rows = attn_all.reshape(-1, width)
    rows_in = rows_low.astype(jnp.float32)
    grad_rows = cotangent_low.astype(jnp.float32)
    normed_one, inverse_one, scaled_one = layer_norm_parts(rows_in, norm_gains[0])
    if not fits:
        own_lengths = swap_partner(lengths)
        both_lengths = jnp.where(
            core == 0,
            jnp.concatenate([lengths, own_lengths], 1),
            jnp.concatenate([own_lengths, lengths], 1),
        )
        length = lax.dynamic_index_in_dim(both_lengths.reshape(-1), tensor_index, 0, keepdims=False)
        bias = jnp.where(positions < length, 0.0, MASK_VALUE).astype(jnp.float32)
        bias = jnp.broadcast_to(bias[:, None], (positions.shape[0], 128))
        low_one = low(scaled_one)
        queries, own = project(
            low_one, query_all, key_all, value_all, cosine[:local_rows], sine[:local_rows]
        )
        other = swap_partner(own)
        context, log_total = attend(queries, own, other, bias)
        middle = rows_in + einsum("sk,kn->sn", context, attn_rows)
    normed_two, inverse_two, scaled_two = layer_norm_parts(middle, norm_gains[1])
    if not fits:
        low_two = low(scaled_two)
    ffn_branch, grad_scaled_two, grad_ffn_in, grad_ffn_out = feed(
        low_two, cotangent_low, ffn_in_all, ffn_out_all
    )
    result = low(middle + ffn_branch)
    grad_from_two, gain_two = layer_norm_back(
        grad_scaled_two, normed_two, inverse_two, norm_gains[1]
    )
    grad_middle = grad_rows + grad_from_two
    grad_branch = low(grad_middle)
    grad_context = low(einsum("sn,kn->sk", grad_branch, attn_rows))
    grad_attn_out = low(einsum("sk,sn->kn", context, grad_branch)).reshape(attn_all.shape)
    attention = (queries, own, other, bias, grad_context, context, log_total, cosine, sine)
    if fits:
        outs = backward(grad_ffn_out, grad_ffn_in, grad_attn_out, result, low_one, *attention, 2)
        sums, (grad_query, grad_pair, outputs) = outs[:4], outs[4:]
    else:
        grad_query, grad_own, grad_other = attend_back(*attention)
        grad_pair = low(grad_own + swap_partner(grad_other).astype(jnp.float32))
    moments = (qkv_moment, attn_out_moment, ffn_in_moment, ffn_out_moment)
    grad_parts = (grad_query, grad_pair[0], grad_pair[1])
    weight_parts = [part.reshape(-1, width) for part in (query_all, key_all, value_all)]
    if fits:
        far = (*weight_parts, *grad_parts, rows_low, grad_middle)
        new_moments, new_weights, gain_grad, input_grad = optimize(
            sums,
            [moment.reshape(row_count, -1) for moment in moments],
            [weight.reshape(row_count, -1) for weight in weights],
            gain_two[None],
            norm_gains,
            far,
            3,
        )
        new_moments = [part.reshape(like.shape) for part, like in zip(new_moments, moments)]
        new_weights = [part.reshape(like.shape) for part, like in zip(new_weights, moments)]
    else:
        grad_scaled_one = sum(
            einsum("sk,kn->sn", part, weight) for part, weight in zip(grad_parts, weight_parts)
        )
        grad_from_one, gain_one = layer_norm_back(
            grad_scaled_one, normed_one, inverse_one, norm_gains[0]
        )
        grads = [low(einsum("sk,sn->kn", part, low_one)) for part in grad_parts]
        grads = [grad.reshape(query_all.shape) for grad in grads]
        sums = reduce_grads(grads + [grad_attn_out, grad_ffn_in, grad_ffn_out])
        sums = [jnp.concatenate(sums[:3])] + list(sums[3:])
        outputs = from_sequences(result, lists, odd, upper)
        input_grad = from_sequences(low(grad_middle + grad_from_one), lists, odd, upper)
        turned_sums = [turn_back(part, moment) for part, moment in zip(sums, moments)]
        new_moments = [MOMENTUM * moment + part for moment, part in zip(moments, turned_sums)]
        steps, gain_grad = orthogonal_steps(
            [low(turn(moment)) for moment in new_moments], jnp.stack([gain_one, gain_two])
        )
        new_weights = [
            weight.astype(jnp.float32) * (1.0 - MUON_RATE * DECAY_RATE)
            - MUON_RATE
            * 0.2
            * math.sqrt(step.shape[0] * tensor_count)
            * turn_back(step, weight).astype(jnp.float32)
            for weight, step in zip(weights, steps)
        ]
    outputs, input_grad = outputs[:, None], input_grad[:, None].astype(jnp.float32)
    gain_first_new = BETA_ONE * gain_first + (1.0 - BETA_ONE) * gain_grad
    gain_second_new = BETA_TWO * gain_second + (1.0 - BETA_TWO) * gain_grad * gain_grad
    first_hat = gain_first_new / (1.0 - BETA_ONE**STEP)
    second_hat = gain_second_new / (1.0 - BETA_TWO**STEP)
    norm_gains_new = norm_gains - ADAM_RATE * (
        first_hat / (jnp.sqrt(second_hat) + ADAM_EPS) + DECAY_RATE * norm_gains
    )
    return (
        outputs,
        input_grad,
        new_moments[0],
        new_weights[0],
        new_moments[1],
        new_weights[1],
        new_moments[2],
        new_weights[2],
        new_moments[3],
        new_weights[3],
        gain_first_new,
        gain_second_new,
        norm_gains_new,
    )


def solution(mesh):
    in_specs = (
        P(None, "dp", "tensor", None),
        P(None, "dp", "tensor", None),
        P(None, "dp"),
        P("dp", None, "tensor"),
        P("dp", "tensor"),
        P("dp", None, "tensor"),
        P("dp", "tensor"),
        P(),
        P("dp", None, "tensor"),
        P("dp", "tensor"),
        P("dp", None, "tensor"),
        P("dp", "tensor"),
        P(),
        P(),
    )
    out_specs = (
        P(None, "dp", "tensor", None),
        P(None, "dp", "tensor", None),
        P("dp", None, "tensor"),
        P("dp", None, "tensor"),
        P("dp", "tensor"),
        P("dp", "tensor"),
        P("dp", None, "tensor"),
        P("dp", None, "tensor"),
        P("dp", "tensor"),
        P("dp", "tensor"),
        P(),
        P(),
        P(),
    )
    return jax.shard_map(
        on_device, mesh=mesh, in_specs=in_specs, out_specs=out_specs, check_vma=False
    )
```

```python
import functools
import math

import jax
import jax.numpy as jnp
from jax import lax
from jax.experimental import pallas as pl
from jax.experimental.pallas import tpu as pltpu
from jax.sharding import PartitionSpec as P

HEAD_DIM = 64
NS_ITERS = 5
STEP = 10
SCORE_SCALE = 1.0 / math.sqrt(HEAD_DIM)


ROPE_BASE = 160000.0
NORM_EPS = 1e-05
MASK_VALUE = -1e30
MOMENTUM = 0.95
MUON_RATE = 0.1
DECAY_RATE = 0.01
QUINTIC_ONE = 3.4445
QUINTIC_THREE = -4.775
QUINTIC_FIVE = 2.0315
NORM_FLOOR = 1e-07
BETA_ONE = 0.9
BETA_TWO = 0.95
ADAM_RATE = 0.2
ADAM_EPS = 1e-08
BOTH = ("dp", "tensor")
MESH = pl.DeviceIdType.MESH


def rotary(positions):
    half_size = HEAD_DIM // 2
    exponents = jnp.arange(half_size).astype(jnp.float32) / half_size
    frequency = jnp.power(ROPE_BASE, -exponents)
    angles = positions.astype(jnp.float32)[:, None] * frequency[None, :]
    cosine, sine = jnp.cos(angles), jnp.sin(angles)
    return (
        jnp.concatenate([cosine] * 4, axis=1),
        jnp.concatenate([-sine, sine, -sine, sine], axis=1),
    )


def layer_norm_parts(vectors, gain):
    centre = vectors - jnp.mean(vectors, axis=-1, keepdims=True)
    inverse = lax.rsqrt(jnp.mean(centre * centre, axis=-1, keepdims=True) + NORM_EPS)
    normed = centre * inverse
    return (normed, inverse, normed * gain)


def layer_norm_back(grad_out, normed, inverse, gain):
    grad_normed = grad_out * gain
    mean_grad = jnp.mean(grad_normed, axis=-1, keepdims=True)
    mean_cross = jnp.mean(grad_normed * normed, axis=-1, keepdims=True)
    return (
        inverse * (grad_normed - mean_grad - normed * mean_cross),
        jnp.sum(grad_out * normed, axis=0),
    )


def einsum(spec, *operands):
    return jnp.einsum(spec, *operands, preferred_element_type=jnp.float32)


def low(values):
    return values.astype(jnp.bfloat16)


def exchange_lists(chip_count, tensor_count):
    first_list, second_list = [], []
    for chip in range(chip_count):
        for core in range(2):
            for slot in range(tensor_count):
                for micro in range(2):
                    source = (2 * chip + core) * tensor_count + slot
                    target = (2 * chip + slot // 2) * tensor_count + 2 * micro + core
                    pair = (source, target)
                    (first_list if slot % 2 == micro else second_list).append(pair)
    return (first_list, second_list)


def to_sequences(blocks, lists, odd, upper):
    first = lax.ppermute(jnp.where(odd, blocks[1], blocks[0]), BOTH, lists[0])
    second = lax.ppermute(jnp.where(odd, blocks[0], blocks[1]), BOTH, lists[1])
    return jnp.where(
        upper, jnp.concatenate([second, first]), jnp.concatenate([first, second])
    )


def from_sequences(rows, lists, odd, upper):
    half = rows.shape[0] // 2
    top, bottom = rows[:half], rows[half:]
    back = [[(target, source) for source, target in pairs] for pairs in lists]
    first = lax.ppermute(jnp.where(upper, bottom, top), BOTH, back[0])
    second = lax.ppermute(jnp.where(upper, top, bottom), BOTH, back[1])
    return jnp.where(odd, jnp.stack([second, first]), jnp.stack([first, second]))


def swap_partner(values):
    count = lax.axis_size("dp")
    return lax.ppermute(values, "dp", [(index, index ^ 1) for index in range(count)])


def mean_split(matrix):
    mean = jnp.trace(matrix) / matrix.shape[0]
    return (mean, matrix - mean * jnp.eye(matrix.shape[0], dtype=jnp.float32))


def split_product(left, right):
    left_mean, left_rest = left
    right_mean, right_rest = right
    product = einsum("ij,jk->ik", low(left_rest), low(right_rest))
    product = product + left_mean * right_rest + right_mean * left_rest
    mean, rest = mean_split(product)
    return (mean + left_mean * right_mean, rest)


def newton_schulz(gram):
    factor = 1.0 / (jnp.sqrt(jnp.trace(gram)) + NORM_FLOOR)
    iterate = mean_split(gram * (factor * factor))
    whole = None
    for sweep_index in range(NS_ITERS):
        square = split_product(iterate, iterate)
        poly = (
            QUINTIC_ONE + QUINTIC_THREE * iterate[0] + QUINTIC_FIVE * square[0],
            QUINTIC_THREE * iterate[1] + QUINTIC_FIVE * square[1],
        )
        whole = poly if whole is None else split_product(poly, whole)
        if sweep_index < NS_ITERS - 1:
            iterate = split_product(poly, split_product(poly, iterate))
    return (whole[0] * factor, whole[1] * factor)


def step_of(rows):
    return next(step for step in (128, 64, 48, 32, 16) if rows % step == 0)


def lanes(block):
    return pl.ds(pl.multiple_of(block * 128, 128), 128)

def neighbours():
    me = lax.axis_index("dp")
    core, across, down = lax.rem(me, 2), lax.rem(lax.div(me, 2), 2), lax.div(me, 4)
    return (me, me + 1 - 2 * core, me + 2 - 4 * across, me + 4 - 8 * down)

def greet(plane, others, planes):
    barrier = pltpu.get_barrier_semaphore()
    me = lax.axis_index("dp")
    crossed = list(others[:1])
    for other in others:
        pl.semaphore_signal(barrier, inc=1, device_id=(other, plane), device_id_type=MESH)
    for other in planes:
        for same_place in [me] + crossed:
            pl.semaphore_signal(barrier, inc=1, device_id=(same_place, other), device_id_type=MESH)
    pl.semaphore_wait(barrier, len(others) + len(planes) * (1 + len(crossed)))

def add_into(target, source, rows, step):
    @pl.loop(0, rows // step)
    def _(index):
        window = pl.ds(pl.multiple_of(index * step, step), step)
        total = target[:, window].astype(jnp.float32) + source[:, window].astype(jnp.float32)
        target[:, window] = total.astype(jnp.bfloat16)


def send_to(source, target, send, recv, device):
    pltpu.make_async_remote_copy(
        source, target, send, recv, device_id=device, device_id_type=MESH
    ).start()


def wait_for(view, sem):
    pltpu.make_async_copy(view, view, sem).wait()


def move_plan(outward, source, target, send, recv, own):
    me, partner, _, _ = neighbours()
    plane = lax.axis_index("tensor")
    core = lax.rem(me, 2)
    column = me - core
    high, parity = lax.div(plane, 2), lax.rem(plane, 2)
    height = target.shape[1] if outward else source.shape[1]

    def owner_of(slot):
        return (column + parity, 2 * core + slot)

    def keeper_of(micro):
        return (column + high, 2 * micro + core)

    def same(device):
        return jnp.logical_and(device[0] == me, device[1] == plane)

    def half(rows, index):
        return rows.at[pl.ds(pl.multiple_of(index * height, height), height), :]

    def start():
        for index in range(2):
            if outward:
                device = owner_of(index)
                piece, goal, arrival = half(source, index), target.at[high], high
            else:
                device = keeper_of(index)
                piece, goal, arrival = source.at[index], half(target, parity), parity

            @pl.when(same(device))
            def _():
                pltpu.make_async_copy(piece, goal, own).start()

            @pl.when(jnp.logical_not(same(device)))
            def _():
                send_to(piece, goal, send.at[index], recv.at[arrival], device)

    def finish():
        for index in range(2):
            if outward:
                sent_to, came_from = owner_of(index), keeper_of(index)
                piece, goal = half(source, index), target.at[index]
            else:
                sent_to, came_from = keeper_of(index), owner_of(index)
                piece, goal = source.at[index], half(target, index)

            @pl.when(same(sent_to))
            def _():
                wait_for(piece, own)

            @pl.when(jnp.logical_not(same(sent_to)))
            def _():
                wait_for(piece, send.at[index])

            @pl.when(jnp.logical_not(same(came_from)))
            def _():
                wait_for(goal, recv.at[index])

    return (start, finish)


def scatter_plan(grads, sums, buffers, sems):
    held, from_x, from_y, from_yx, from_xy, from_z = buffers[:6]
    staging = buffers[6][0]
    (load_sem, send_c, recv_c, send_x, recv_x, send_y, recv_y, send_yx, recv_yx, send_xy, recv_xy, send_z, recv_z) = sems
    me, partner, across, down = neighbours()
    plane = lax.axis_index("tensor")
    planes = [lax.rem(plane + offset, 4) for offset in (1, 2, 3)]
    flip = lambda block: block + 1 - 2 * lax.rem(block, 2)
    blocks = (me, across, down, across + down - me)
    order = (3, 1, 2, 0)

    def view(part, block):
        ref, first, rows = grads[part]
        return ref.at[:, pl.ds(first, rows), lanes(block)]

    def slot(part, index):
        return staging.at[index, :, pl.ds(0, grads[part][2])]

    def stage_core(part):
        for index in order:
            send_to(view(part, flip(blocks[index])), held[part].at[index], send_c.at[part, index], recv_c.at[part, index], (partner, plane))

    def load(part):
        for index in order:
            pltpu.make_async_copy(view(part, blocks[index]), slot(part, index), load_sem.at[part, index]).start()

    def stage_first(part):
        rows = grads[part][2]
        load(part)
        for index in order:
            wait_for(slot(part, index), load_sem.at[part, index])
            wait_for(held[part].at[index], recv_c.at[part, index])
            add_into(held[part].at[index], slot(part, index), rows, step_of(rows))
            if index % 2 == 1:
                send_to(held[part].at[index, 0:2], from_x[part].at[index // 2], send_x.at[part, index // 2], recv_x.at[part, index // 2], (across, plane))
            if index // 2 == 1:
                send_to(held[part].at[index, 2:4], from_y[part].at[index % 2], send_y.at[part, index % 2], recv_y.at[part, index % 2], (down, plane))

    def stage_second(part):
        rows = grads[part][2]
        for side in (1, 0):
            wait_for(from_x[part].at[side], recv_x.at[part, side])
            add_into(held[part].at[2 * side, 0:2], from_x[part].at[side], rows, step_of(rows))
            if side == 1:
                send_to(held[part].at[2, 0:2], from_yx[part], send_yx.at[part], recv_yx.at[part], (down, plane))
            wait_for(from_y[part].at[side], recv_y.at[part, side])
            add_into(held[part].at[side, 2:4], from_y[part].at[side], rows, step_of(rows))
            if side == 1:
                send_to(held[part].at[1, 2:4], from_xy[part], send_xy.at[part], recv_xy.at[part], (across, plane))

    def stage_third(part):
        rows = grads[part][2]
        wait_for(from_yx[part], recv_yx.at[part])
        add_into(held[part].at[0, 0:2], from_yx[part], rows, step_of(rows))
        wait_for(from_xy[part], recv_xy.at[part])
        add_into(held[part].at[0, 2:4], from_xy[part], rows, step_of(rows))
        for index, other in enumerate(planes):
            send_to(held[part].at[0, other], from_z[part].at[index], send_z.at[part, index], recv_z.at[part, index], (me, other))

    def stage_last(part):
        rows = grads[part][2]
        step = step_of(rows)
        target, first = sums[part]
        for index in range(3):
            wait_for(from_z[part].at[index], recv_z.at[part, index])

        @pl.loop(0, rows // step)
        def _(index):
            offset = pl.multiple_of(index * step, step)
            window = pl.ds(offset, step)
            total = held[part][0, plane, window].astype(jnp.float32)
            for other in range(3):
                total = total + from_z[part][other, window].astype(jnp.float32)
            target[pl.ds(pl.multiple_of(first + offset, 16), step)] = total

    def finish(part):
        for index in range(4):
            wait_for(held[part].at[index], send_c.at[part, index])
        for side in range(2):
            wait_for(from_x[part].at[side], send_x.at[part, side])
            wait_for(from_y[part].at[side], send_y.at[part, side])
        wait_for(from_yx[part], send_yx.at[part])
        wait_for(from_xy[part], send_xy.at[part])
        for index in range(3):
            wait_for(from_z[part].at[index], send_z.at[part, index])

    return ((stage_core, stage_first, stage_second, stage_third, stage_last), finish)


def scatter_scratch(heights):
    sem = pltpu.SemaphoreType.DMA
    count = len(heights)
    leads = ((4, 4), (2, 2), (2, 2), (2,), (2,), (3,))
    buffers = [pltpu.VMEM(lead + (rows, 128), jnp.bfloat16) for lead in leads for rows in heights]
    buffers.append(pltpu.VMEM((4, 4, max(heights), 128), jnp.bfloat16))
    sems = [sem((count, 4))] * 3 + [sem((count, 2))] * 4 + [sem((count,))] * 4 + [sem((count, 3))] * 2
    return (buffers, sems)


def take(refs, count):
    taken, refs[:] = refs[:count], refs[count:]
    return taken


def gather_plan(shards, wholes, sems):
    own_sem, send_up, send_down, recv_z, send_x, recv_x, send_y, recv_y, send_d, recv_d, send_c, recv_c = sems
    me, partner, across, down = neighbours()
    plane = lax.axis_index("tensor")
    diagonal = across + down - me
    flip = lambda block: block + 1 - 2 * lax.rem(block, 2)

    def place(part, slot, block):
        return wholes[part].at[slot, :, lanes(block)]

    def spread(part, source, slot):
        view = place(part, slot, me)
        send_to(source, view, send_x.at[part, slot], recv_x.at[part, slot], (across, plane))
        send_to(source, view, send_y.at[part, slot], recv_y.at[part, slot], (down, plane))
        send_to(source, view, send_c.at[part, slot, 0], recv_c.at[part, slot, 0], (partner, plane))

    def pass_on(part, source, slot, upward):
        view = place(part, slot, me)
        sem = (send_up if upward else send_down).at[part, slot]
        send_to(source, view, sem, recv_z.at[part, slot], (me, plane + 1 if upward else plane - 1))

    def stage_own(part):
        pltpu.make_async_copy(shards[part], place(part, plane, me), own_sem.at[part]).start()

        @pl.when(plane < 3)
        def _():
            pass_on(part, shards[part], plane, True)

        @pl.when(plane > 0)
        def _():
            pass_on(part, shards[part], plane, False)

        spread(part, shards[part], plane)

    def stage_z(part):
        for distance in (1, 2, 3):
            for upward in (True, False):
                slot = plane - distance if upward else plane + distance

                @pl.when(slot >= 0 if upward else slot <= 3)
                def _():
                    view = place(part, slot, me)
                    wait_for(view, recv_z.at[part, slot])

                    @pl.when(plane < 3 if upward else plane > 0)
                    def _():
                        pass_on(part, view, slot, upward)

                    spread(part, view, slot)

    def stage_xy(part):
        for slot in range(4):
            view = place(part, slot, across)
            wait_for(view, recv_x.at[part, slot])
            if slot < 2:
                send_to(view, view, send_d.at[part, slot], recv_d.at[part, slot], (down, plane))
            send_to(view, view, send_c.at[part, slot, 1], recv_c.at[part, slot, 1], (partner, plane))
            view = place(part, slot, down)
            wait_for(view, recv_y.at[part, slot])
            if slot >= 2:
                send_to(view, view, send_d.at[part, slot], recv_d.at[part, slot], (across, plane))
            send_to(view, view, send_c.at[part, slot, 2], recv_c.at[part, slot, 2], (partner, plane))

    def stage_diagonal(part):
        for slot in range(4):
            view = place(part, slot, diagonal)
            wait_for(view, recv_d.at[part, slot])
            send_to(view, view, send_c.at[part, slot, 3], recv_c.at[part, slot, 3], (partner, plane))

    def arrive(part):
        wait_for(shards[part], own_sem.at[part])
        for slot in range(4):
            for index, block in enumerate((me, across, down, diagonal)):
                wait_for(place(part, slot, flip(block)), recv_c.at[part, slot, index])

    def finish(part):
        for slot in range(4):
            @pl.when(jnp.logical_and(slot <= plane, plane < 3))
            def _():
                wait_for(shards[part], send_up.at[part, slot])

            @pl.when(jnp.logical_and(slot >= plane, plane > 0))
            def _():
                wait_for(shards[part], send_down.at[part, slot])

            for sem in (send_x, send_y, send_d):
                wait_for(shards[part], sem.at[part, slot])
            for index in range(4):
                wait_for(shards[part], send_c.at[part, slot, index])

    return (stage_own, stage_z, stage_xy, stage_diagonal, arrive, finish)


def normed_rows(rows, gain):
    centre = rows - jnp.mean(rows, axis=1, keepdims=True)
    inverse = lax.rsqrt(jnp.mean(centre * centre, axis=1, keepdims=True) + NORM_EPS)
    return centre * inverse * gain


def forward_kernel(*refs):
    refs = list(refs)
    shards, (inputs, cotangent, lengths, gains, cosine, sine) = take(refs, 6), take(refs, 6)
    wholes, (rows_low, grad_rows) = take(refs, 6), take(refs, 2)
    low_one, queries, own, other, context, log_total, bias, middle, low_two = take(refs, 9)
    other_lengths, weight, attn_weight = take(refs, 3)
    sems = take(refs, 12)
    pair_send, pair_recv, length_send, length_recv, weight_sem, attn_sem = take(refs, 6)
    move_send, move_recv, move_own = refs
    me, partner, across, down = neighbours()
    plane = lax.axis_index("tensor")
    core = lax.rem(me, 2)
    stage_own, stage_z, stage_xy, stage_diagonal, arrive, finish = gather_plan(shards, wholes, sems)
    moves = [
        move_plan(False, source, target, move_send.at[index], move_recv.at[index], move_own.at[index])
        for index, (source, target) in enumerate(((inputs, rows_low), (cotangent, grad_rows)))
    ]
    greet(plane, (partner, across, down), [lax.rem(plane + offset, 4) for offset in (1, 2, 3)])
    count, width = rows_low.shape
    third = shards[0].shape[0]
    step = 64

    stage_own(0)
    stage_own(1)
    send_to(lengths, other_lengths, length_send, length_recv, (partner, plane))
    stage_z(0)
    stage_own(2)
    stage_z(1)
    stage_xy(0)
    stage_own(3)
    stage_z(2)
    stage_xy(1)
    stage_diagonal(0)
    stage_own(4)
    stage_z(3)
    stage_xy(2)
    stage_diagonal(1)
    stage_own(5)
    stage_z(4)
    moves[0][0]()
    stage_xy(3)
    stage_diagonal(2)
    stage_z(5)
    moves[1][0]()
    stage_diagonal(3)
    stage_xy(4)
    wait_for(other_lengths, length_recv)
    mine = core == lax.rem(plane, 2)
    both = jnp.where(mine, lengths[...], other_lengths[...])
    length = jnp.where(plane < 2, both[0:1], both[1:2])
    position = lax.broadcasted_iota(jnp.int32, bias.shape, 0)
    position = lax.rem(position + core * count, 2 * count).astype(jnp.float32)
    bias[...] = jnp.where(position < length, 0.0, MASK_VALUE)
    moves[0][1]()

    @pl.loop(0, count // step)
    def _(index):
        window = pl.ds(pl.multiple_of(index * step, step), step)
        low_one[window] = low(normed_rows(rows_low[window].astype(jnp.float32), gains[0:1]))

    for part in range(3):
        arrive(part)

    def load(group):
        for part in range(3):
            slot = lax.rem(group, 2)
            pltpu.make_async_copy(wholes[part].at[group], weight.at[slot, part], weight_sem.at[slot, part]).start()

    load(0)

    @pl.loop(0, 4)
    def _(group):
        @pl.when(group < 3)
        def _():
            load(group + 1)

        slot = lax.rem(group, 2)
        for part in range(3):
            wait_for(weight.at[slot, part], weight_sem.at[slot, part])
            result = product_of(low_one[...], weight[slot, part], ((1,), (1,)))
            for first in range(0, third, 128):
                columns = pl.ds(pl.multiple_of(group * third + first, 128), 128)
                piece = result[:, first : first + 128]
                if part < 2:
                    piece = turned(piece, cosine[0:count], sine[0:count])
                if part == 0:
                    queries[:, columns] = low(piece * SCORE_SCALE)
                else:
                    own[part - 1, :, columns] = low(piece)

    send_to(own, other, pair_send, pair_recv, (partner, plane))
    wait_for(other, pair_recv)
    arrive(3)
    attn_copy = pltpu.make_async_copy(wholes[3], attn_weight, attn_sem)
    attn_copy.start()
    schedule = {3: (stage_xy, 5), 6: (stage_diagonal, 4)}

    @pl.loop(0, width // 128)
    def _(index):
        for place, (stage, part) in schedule.items():
            @pl.when(index == place)
            def _():
                stage(part)

        attend_pair(lanes(index), queries, own, other, bias, context, log_total.at[index])

    attn_copy.wait()

    @pl.loop(0, count // 128)
    def _(index):
        window = pl.ds(pl.multiple_of(index * 128, 128), 128)
        rows = rows_low[window].astype(jnp.float32)
        for group in range(4):
            piece = context[window, third * group : third * group + third]
            rows = rows + product_of(piece, attn_weight[group], ((1,), (0,)))
        middle[window] = rows
        low_two[window] = low(normed_rows(rows, gains[1:2]))

    stage_diagonal(5)
    for part in (4, 5):
        arrive(part)
    for part in range(6):
        finish(part)
    wait_for(own, pair_send)
    wait_for(lengths, length_send)
    moves[1][1]()


def forward(shards, inputs, cotangent, lengths, gains, cosine, sine, collective_id):
    sem = pltpu.SemaphoreType.DMA
    anywhere = pl.BlockSpec(memory_space=pl.ANY)
    local = pl.BlockSpec(memory_space=pltpu.VMEM)
    bf16, f32 = jnp.bfloat16, jnp.float32
    count, width = 2 * inputs.shape[1], inputs.shape[2]
    third = shards[0].shape[0]
    shape = jax.ShapeDtypeStruct
    return pl.pallas_call(
        forward_kernel,
        out_shape=[shape((4, shard.shape[0], width), bf16) for shard in shards]
        + [
            shape((count, width), bf16),
            shape((count, width), bf16),
            shape((count, width), bf16),
            shape((count, width), bf16),
            shape((2, count, width), bf16),
            shape((2, count, width), bf16),
            shape((count, width), bf16),
            shape((width // 128, 8, count), f32),
            shape((2 * count, 128), f32),
            shape((count, width), f32),
            shape((count, width), bf16),
        ],
        in_specs=[anywhere] * 8 + [local] * 4,
        out_specs=[anywhere] * 6 + [local, anywhere] + [local] * 9,
        scratch_shapes=[
            pltpu.VMEM(lengths.shape, f32),
            pltpu.VMEM((2, 3, third, width), bf16),
            pltpu.VMEM((4, third, width), bf16),
            sem((6,)),
        ]
        + [sem((6, 4))] * 9
        + [sem((6, 4, 4))] * 2
        + [sem, sem, sem, sem, sem((2, 3)), sem]
        + [sem((2, 2)), sem((2, 2)), sem((2,))],
        compiler_params=pltpu.CompilerParams(
            collective_id=collective_id, has_side_effects=True, vmem_limit_bytes=58 * 1024 * 1024
        ),
        name="forward",
    )(*shards, inputs, cotangent, lengths, gains, cosine, sine)


def attend_pair(columns, queries, own, other, bias, context, log_total):
    query_turned = queries[:, columns].T
    keys = jnp.concatenate([own[0, :, columns], other[0, :, columns]], axis=0)
    value_turned = jnp.concatenate([own[1, :, columns].T, other[1, :, columns].T], axis=1)
    parts, logs = [], []
    for head in range(2):
        scores = scores_of(keys, head_rows(query_turned, head), bias[...])
        highest = jnp.max(scores, axis=0, keepdims=True)
        weights = jnp.exp(scores - highest)
        total = jnp.sum(weights, axis=0, keepdims=True)
        part = product_of(value_turned[64 * head : 64 * head + 64], low(weights), ((1,), (0,)))
        parts.append(part / total)
        logs.append(highest + jnp.log(total))
    context[:, columns] = low(jnp.concatenate(parts, axis=0)).T
    log_total[...] = jnp.concatenate(logs + logs * 3, axis=0)


def add_rows(target, source, extent):
    step = step_of(extent)

    @pl.loop(0, extent // step)
    def _(index):
        window = pl.ds(pl.multiple_of(index * step, step), step)
        target[window] = low(target[window].astype(jnp.float32) + source[window].astype(jnp.float32))


def slot_of(part):
    return (4 - part) % 4


def slot_plan(grads, sums, buffers, sems):
    held, from_x, from_y, from_yx, from_xy = buffers[:5]
    from_z, staging = buffers[5][0], buffers[6][0]
    (load_sem, send_c, recv_c, send_x, recv_x, send_y, recv_y, send_yx, recv_yx, send_xy, recv_xy, send_z, recv_z) = sems
    me, partner, across, down = neighbours()
    plane = lax.axis_index("tensor")
    flip = lambda block: block + 1 - 2 * lax.rem(block, 2)
    blocks = (me, across, down, across + down - me)
    order = (3, 1, 2, 0)
    rows, early = grads.shape[1], from_x[0].shape[1]
    late = rows - early
    one, two = pl.ds(0, early), pl.ds(early, late)

    def stage_core(part):
        for index in order:
            send_to(grads.at[slot_of(part), :, lanes(flip(blocks[index]))], held[part].at[index], send_c.at[part, index], recv_c.at[part, index], (partner, plane))

    def stage_first(part):
        for index in order:
            pltpu.make_async_copy(grads.at[slot_of(part), :, lanes(blocks[index])], staging.at[index], load_sem.at[part, index]).start()
        for index in order:
            wait_for(staging.at[index], load_sem.at[part, index])
            wait_for(held[part].at[index], recv_c.at[part, index])
            add_rows(held[part].at[index], staging.at[index], rows)
            if index % 2 == 1:
                send_to(held[part].at[index, one], from_x[part].at[index // 2], send_x.at[part, index // 2], recv_x.at[part, index // 2], (across, plane))
            if index // 2 == 1:
                send_to(held[part].at[index, two], from_y[part].at[index % 2], send_y.at[part, index % 2], recv_y.at[part, index % 2], (down, plane))

    def stage_second(part):
        for side in (1, 0):
            wait_for(from_x[part].at[side], recv_x.at[part, side])
            add_rows(held[part].at[2 * side, one], from_x[part].at[side], early)
            if side == 1:
                send_to(held[part].at[2, one], from_yx[part], send_yx.at[part], recv_yx.at[part], (down, plane))
            wait_for(from_y[part].at[side], recv_y.at[part, side])
            add_rows(held[part].at[side, two], from_y[part].at[side], late)
            if side == 1:
                send_to(held[part].at[1, two], from_xy[part], send_xy.at[part], recv_xy.at[part], (across, plane))

    def stage_third(part):
        wait_for(from_yx[part], recv_yx.at[part])
        add_rows(held[part].at[0, one], from_yx[part], early)
        wait_for(from_xy[part], recv_xy.at[part])
        add_rows(held[part].at[0, two], from_xy[part], late)

        @pl.when(plane != slot_of(part))
        def _():
            offset = lax.rem(plane + 3 - slot_of(part), 4)
            send_to(held[part].at[0], from_z.at[offset], send_z.at[part], recv_z.at[offset], (me, slot_of(part)))

    def stage_last(part):
        @pl.when(plane == slot_of(part))
        def _():
            for offset in range(3):
                wait_for(from_z.at[offset], recv_z.at[offset])
            for target, first, extent in sums:
                step = step_of(extent)

                @pl.loop(0, extent // step)
                def _(index):
                    offset = pl.multiple_of(index * step, step)
                    window = pl.ds(pl.multiple_of(first + offset, 16), step)
                    total = held[part][0, window].astype(jnp.float32)
                    for other in range(3):
                        total = total + from_z[other, window].astype(jnp.float32)
                    target[pl.ds(offset, step)] = total

    def finish(part):
        for index in range(4):
            wait_for(held[part].at[index], send_c.at[part, index])
        for side in range(2):
            wait_for(from_x[part].at[side], send_x.at[part, side])
            wait_for(from_y[part].at[side], send_y.at[part, side])
        wait_for(from_yx[part], send_yx.at[part])
        wait_for(from_xy[part], send_xy.at[part])

        @pl.when(plane != slot_of(part))
        def _():
            wait_for(from_z.at[0], send_z.at[part])

    return ((stage_core, stage_first, stage_second, stage_third, stage_last), finish)


def slot_scratch(rows, early):
    sem = pltpu.SemaphoreType.DMA
    late = rows - early
    shapes = [(4, rows)] * 4 + [(2, early)] * 4 + [(2, late)] * 4 + [(early,)] * 4 + [(late,)] * 4
    shapes += [(3, rows), (4, rows)]
    buffers = [pltpu.VMEM(shape + (128,), jnp.bfloat16) for shape in shapes]
    sems = [sem((4, 4))] * 3 + [sem((4, 2))] * 4 + [sem((4,))] * 4 + [sem((4,)), sem((3,))]
    return (buffers, sems)


def backward_kernel(*refs):
    refs = list(refs)
    f32, bf16 = jnp.float32, jnp.bfloat16
    in_weight, out_weight, attn_weight, far_two, far_cot, far_middle = take(refs, 6)
    far_query, far_own, far_other, far_context, far_one = take(refs, 5)
    bias, log_total, cosine, sine, gains = take(refs, 5)
    sums, (far_grad_query, far_pair, rows_out, far_grad_middle, gain_two) = take(refs, 4), take(refs, 5)
    grad_feed, weight_grads = take(refs, 1)[0], take(refs, 4)
    branch, cotangent, low_rows, queries, own, other, grad, context = take(refs, 8)
    grad_query, grad_pair, grad_other, arrived, staged = take(refs, 5)
    result, grad_rows, middle = take(refs, 3)
    slot_buffers = [take(refs, 4) for _ in range(5)] + [take(refs, 1), take(refs, 1)]
    slot_sems = take(refs, 13)
    buffers = [take(refs, 4) for _ in range(6)] + [take(refs, 1)]
    sems = take(refs, 13)
    pair_send, pair_recv, stage_sem, load_sem, out_sem, weight_sem, feed_sem, middle_sem = take(refs, 8)
    move_send, move_recv, move_own = refs
    me, partner, across, down = neighbours()
    plane = lax.axis_index("tensor")
    height, third = out_weight.shape[1], attn_weight.shape[1]
    count, width = cotangent.shape
    sum_qkv, sum_attn, sum_in, sum_out = sums
    feed_sums = [(sum_in, 0, 2 * height), (sum_out, 2 * height, height)]
    feed_stages, feed_finish = slot_plan(grad_feed, feed_sums, slot_buffers, slot_sems)
    parts = [(ref, 0, third) for ref in weight_grads]
    targets = [(sum_attn, 0)] + [(sum_qkv, third * index) for index in range(3)]
    stages, finish = scatter_plan(parts, targets, buffers, sems)
    start_move, finish_move = move_plan(True, cotangent, rows_out, move_send, move_recv, move_own)

    def call(stage, part):
        if part < 4:
            feed_stages[stage](part)
        else:
            stages[stage](part - 4)

    pieces = ((0, 336), (336, height - 336))
    weight_slots = (
        (own.at[0], own.at[1], grad_pair.at[0]),
        (other.at[0], other.at[1], grad_pair.at[1]),
    )
    grad_slots = ((grad_other.at[0], grad_other.at[1], grad_query), (queries, context, grad))

    def weight_copies(group, piece):
        first, extent = pieces[piece]
        sources = ((in_weight, first), (in_weight, height + first), (out_weight, first))
        return [
            pltpu.make_async_copy(source.at[lax.rem(4 - group, 4), pl.ds(offset, extent)], target.at[pl.ds(0, extent)], weight_sem.at[piece, index])
            for index, ((source, offset), target) in enumerate(zip(sources, weight_slots[piece]))
        ]

    def grad_copies(group, piece):
        first, extent = pieces[piece]
        return [
            pltpu.make_async_copy(source.at[pl.ds(0, extent)], grad_feed.at[lax.rem(4 - group, 4), pl.ds(index * height + first, extent)], feed_sem.at[piece, index])
            for index, source in enumerate(grad_slots[piece])
        ]

    def start_all(copies):
        for copy in copies:
            copy.start()

    def wait_all(copies):
        for copy in copies:
            copy.wait()

    first_loads = [
        pltpu.make_async_copy(far_two, branch, load_sem.at[0]),
        pltpu.make_async_copy(far_cot, cotangent, load_sem.at[1]),
    ]
    start_all(first_loads)
    start_all(weight_copies(0, 0))
    start_all(weight_copies(0, 1))
    greet(plane, (partner, across, down), [lax.rem(plane + offset, 4) for offset in (1, 2, 3)])
    result[...] = jnp.zeros_like(result)
    grad_rows[...] = jnp.zeros_like(grad_rows)
    wait_all(first_loads)
    feed_calls = {(1, 1): ((1, 0),), (2, 1): ((1, 1),), (3, 0): ((2, 0),), (3, 1): ((1, 2),)}

    @pl.loop(0, 4)
    def _(group):
        @pl.when(group > 0)
        def _():
            for piece in range(2):
                wait_all(grad_copies(group - 1, piece))
            for part in range(3):
                @pl.when(group == part + 1)
                def _():
                    call(0, part)

        for piece, (_, extent) in enumerate(pieces):
            for (when, place), calls in feed_calls.items():
                if place == piece:
                    @pl.when(group == when)
                    def _():
                        for stage, part in calls:
                            call(stage, part)

            window = pl.ds(0, extent)
            wait_all(weight_copies(group, piece))
            gate_weight, up_weight, down_weight = (ref[window] for ref in weight_slots[piece])
            gate = product_of(gate_weight, branch[...], ((1,), (1,)))
            up = product_of(up_weight, branch[...], ((1,), (1,)))
            grad_hidden = product_of(down_weight, cotangent[...], ((1,), (1,)))
            below = 0.5 + 0.5 * lax.erf(gate * math.sqrt(0.5))
            active = gate * below
            hidden = low(active * up)
            slope = below + gate * jnp.exp(-0.5 * gate * gate) * (1.0 / math.sqrt(2.0 * math.pi))
            grad_gate = low(grad_hidden * up * slope)
            grad_up = low(grad_hidden * active)
            grad_slots[piece][2][window] = low(product_of(hidden, cotangent[...], ((1,), (0,))))
            grad_slots[piece][0][window] = low(product_of(grad_gate, branch[...], ((1,), (0,))))
            grad_slots[piece][1][window] = low(product_of(grad_up, branch[...], ((1,), (0,))))
            start_all(grad_copies(group, piece))
            result[...] += product_of(hidden, down_weight, ((0,), (0,)))
            grad_rows[...] += product_of(grad_gate, gate_weight, ((0,), (0,)))
            grad_rows[...] += product_of(grad_up, up_weight, ((0,), (0,)))

            @pl.when(group < 3)
            def _():
                start_all(weight_copies(group + 1, piece))

    step = 64

    def middle_copy(index):
        window = pl.ds(pl.multiple_of(index * step, step), step)
        slot = lax.rem(index, 2)
        return pltpu.make_async_copy(far_middle.at[window], middle.at[slot], middle_sem.at[slot])

    middle_copy(0).start()
    for piece in range(2):
        wait_all(grad_copies(3, piece))
    call(0, 3)
    near = (queries, own, other, context, low_rows)
    loads = [
        pltpu.make_async_copy(source, target, load_sem.at[index])
        for index, (source, target) in enumerate(zip((far_query, far_own, far_other, far_context, far_one), near))
    ]
    start_all(loads)
    attn_loads = [
        pltpu.make_async_copy(
            attn_weight.at[group], grad_other.at[group // 2, pl.ds(group % 2 * third, third)], weight_sem.at[group // 2, group % 2]
        )
        for group in range(4)
    ]
    start_all(attn_loads)
    gain_two[...] = jnp.zeros_like(gain_two)

    @pl.loop(0, count // step)
    def _(index):
        @pl.when(index < count // step - 1)
        def _():
            middle_copy(index + 1).start()

        middle_copy(index).wait()
        window = pl.ds(pl.multiple_of(index * step, step), step)
        rows = middle[lax.rem(index, 2)]
        centre = rows - jnp.mean(rows, axis=1, keepdims=True)
        inverse = lax.rsqrt(jnp.mean(centre * centre, axis=1, keepdims=True) + NORM_EPS)
        normed = centre * inverse
        scaled = grad_rows[window] * gains[1:2]
        mean_grad = jnp.mean(scaled, axis=1, keepdims=True)
        mean_cross = jnp.mean(scaled * normed, axis=1, keepdims=True)
        gain_two[...] += jnp.sum(grad_rows[window] * normed, axis=0, keepdims=True)
        total = cotangent[window].astype(f32) + inverse * (scaled - mean_grad - normed * mean_cross)
        grad_rows[window] = total
        branch[window] = low(total)
        cotangent[window] = low(rows + result[window])

    call(3, 0)
    call(2, 1)
    start_move()
    middle_out = pltpu.make_async_copy(grad_rows, far_grad_middle, out_sem.at[2])
    middle_out.start()
    wait_all(attn_loads)

    @pl.loop(0, count // 128)
    def _(index):
        window = pl.ds(pl.multiple_of(index * 128, 128), 128)
        for part in range(2):
            columns = slice(part * count, part * count + count)
            grad[window, columns] = low(product_of(branch[window], grad_other[part], ((1,), (1,))))

    wait_all(loads)

    def weight_grad(which, values, rows):
        target = weight_grads[which]
        for group in range(4):
            slot = staged.at[group % 2]
            if group >= 2:
                wait_for(slot, stage_sem.at[group % 2])
            block = values[:, third * group : third * group + third]
            slot[...] = low(product_of(block, rows[...], ((0,), (0,))))
            pltpu.make_async_copy(slot, target.at[group], stage_sem.at[group % 2]).start()
        for group in range(2):
            wait_for(staged.at[group], stage_sem.at[group])

    weight_grad(0, context, branch)
    call(0, 4)

    def exchanged(index):
        return (arrived.at[:, :, lanes(index)], pair_recv.at[index])

    def add_pair(index):
        wait_for(*exchanged(index))
        columns = lanes(index)
        for which in range(2):
            total = grad_pair[which, :, columns].astype(f32)
            total = total + arrived[which, :, columns].astype(f32)
            grad_pair[which, :, columns] = low(total)

    last_pair = width // 128 - 1
    schedule = {0: ((1, 3),), 2: ((3, 1), (2, 2)), 5: ((3, 2), (1, 4)), 7: ((2, 3),)}

    @pl.loop(0, last_pair + 1)
    def _(index):
        for position, calls in schedule.items():
            @pl.when(index == position)
            def _():
                for stage, part in calls:
                    call(stage, part)

        attend_back_pair(lanes(index), queries, own, other, bias, grad, context, log_total.at[index], cosine, sine, grad_query, grad_pair, grad_other)
        target, sem = exchanged(index)
        send_to(grad_other.at[:, :, lanes(index)], target, pair_send.at[index], sem, (partner, plane))

        @pl.when(index > 0)
        def _():
            add_pair(index - 1)

    query_copy = pltpu.make_async_copy(grad_query, far_grad_query, out_sem.at[0])
    query_copy.start()
    weight_grad(1, grad_query, low_rows)
    call(0, 5)
    add_pair(last_pair)
    pair_copy = pltpu.make_async_copy(grad_pair, far_pair, out_sem.at[1])
    pair_copy.start()
    weight_grad(2, grad_pair.at[0], low_rows)
    call(0, 6)
    weight_grad(3, grad_pair.at[1], low_rows)
    call(0, 7)
    done = {(1, 4), (3, 2), (2, 3), (1, 0), (2, 0), (1, 1), (3, 0), (2, 1), (1, 2), (3, 1), (2, 2), (1, 3)}
    for turn_of in range(10):
        for stage in (3, 2, 1):
            part = turn_of - (stage - 1)
            if 0 <= part < 8 and (stage, part) not in done:
                call(stage, part)
    for part in range(8):
        call(4, part)
    for part in range(4):
        feed_finish(part)
        finish(part)
    for index in range(last_pair + 1):
        wait_for(arrived.at[:, :, lanes(index)], pair_send.at[index])
    query_copy.wait()
    pair_copy.wait()
    middle_out.wait()
    finish_move()


def backward(wholes, low_two, cotangent, middle, queries, own, other, context, low_one, bias, log_total, cosine, sine, gains, collective_id):
    attn_all, in_all, out_all = wholes
    height, third = out_all.shape[1], attn_all.shape[1]
    count, width = queries.shape
    early = 3 * height // 32 * 16 + 16
    slot_buffers, slot_sems = slot_scratch(3 * height, early)
    buffers, sems = scatter_scratch([third] * 4)
    sem = pltpu.SemaphoreType.DMA
    anywhere = pl.BlockSpec(memory_space=pl.ANY)
    local = pl.BlockSpec(memory_space=pltpu.VMEM)
    bf16, f32 = jnp.bfloat16, jnp.float32
    shape, vmem = jax.ShapeDtypeStruct, pltpu.VMEM
    outs = pl.pallas_call(
        backward_kernel,
        out_shape=[shape((rows, 128), f32) for rows in (3 * third, third, 2 * height, height)]
        + [
            shape((count, width), bf16),
            shape((2, count, width), bf16),
            shape((2, count // 2, width), bf16),
            shape((count, width), f32),
            shape((1, width), f32),
            shape((4, 3 * height, width), bf16),
        ]
        + [shape(attn_all.shape, bf16)] * 4,
        in_specs=[anywhere] * 11 + [local] * 5,
        out_specs=[local] * 4 + [anywhere] * 4 + [local] + [anywhere] * 5,
        scratch_shapes=[vmem((count, width), bf16)] * 4
        + [vmem((2, count, width), bf16)] * 2
        + [vmem((count, width), bf16)] * 3
        + [vmem((2, count, width), bf16)] * 3
        + [vmem((2, third, width), bf16)]
        + [vmem((count, width), f32)] * 2
        + [vmem((2, 64, width), f32)]
        + slot_buffers
        + slot_sems
        + buffers
        + sems
        + [sem((8,)), sem((8,)), sem((2,)), sem((5,)), sem((3,)), sem((2, 3)), sem((2, 3)), sem((2,))]
        + [sem((2,)), sem((2,)), sem],
        compiler_params=pltpu.CompilerParams(
            collective_id=collective_id, has_side_effects=True, vmem_limit_bytes=62 * 1024 * 1024
        ),
        name="backward",
    )(in_all, out_all, attn_all, low_two, cotangent, middle, queries, own, other, context, low_one, bias, log_total, cosine, sine, gains)
    return outs[:9]


def attend_back_pair(columns, queries, own, other, bias, grad, context, log_total, cosine, sine, grad_query, grad_own, grad_other):
    count = queries.shape[0]
    query_rows, grad_rows = queries[:, columns], grad[:, columns]
    query_turned, grad_turned = query_rows.T, grad_rows.T
    inner = (grad_rows.astype(jnp.float32) * context[:, columns].astype(jnp.float32)).T
    query_parts = [None, None]
    for half, (pair, result) in enumerate(((own, grad_own), (other, grad_other))):
        keys, values = pair[0, :, columns], pair[1, :, columns]
        key_turned = keys.T
        grad_keys, grad_values = None, None
        window = pl.ds(half * count, count)
        for head in range(2):
            lanes_of_head = slice(64 * head, 64 * head + 64)
            scores = scores_of(keys, head_rows(query_turned, head), bias[window])
            weights = jnp.exp(scores - log_total[head : head + 1])
            grad_weights = product_of(values, head_rows(grad_turned, head), ((1,), (0,)))
            inner_row = jnp.sum(inner[lanes_of_head], axis=0, keepdims=True)
            grad_scores = low(weights * (grad_weights - inner_row))
            value_part = product_of(low(weights), head_lanes(grad_rows, head), ((1,), (0,)))
            key_part = product_of(grad_scores, head_lanes(query_rows, head), ((1,), (0,)))
            query_part = product_of(key_turned[lanes_of_head], grad_scores, ((1,), (0,)))
            grad_values = value_part if head == 0 else grad_values + value_part
            grad_keys = key_part if head == 0 else grad_keys + key_part
            query_parts[head] = query_part if half == 0 else query_parts[head] + query_part
        result[0, :, columns] = turned(grad_keys, cosine[window], -sine[window]).astype(result.dtype)
        result[1, :, columns] = grad_values.astype(result.dtype)
    query_rows = jnp.concatenate(query_parts, axis=0).T * SCORE_SCALE
    own_rows = pl.ds(0, count)
    grad_query[:, columns] = low(turned(query_rows, cosine[own_rows], -sine[own_rows]))


def product_of(left, right, dims):
    return lax.dot_general(left, right, (dims, ((), ())), preferred_element_type=jnp.float32)

def optimize_kernel(heights, *refs):
    refs = list(refs)
    count, size, tile = len(heights), 1024, 256
    f32, bf16 = jnp.float32, jnp.bfloat16
    sums, moments, weights = take(refs, count), take(refs, count), take(refs, count)
    (gain_two, gains), far = take(refs, 2), take(refs, 8)
    new_moments, new_weights = take(refs, count), take(refs, count)
    gain_out, rows_out = take(refs, 2)
    blocks, backs = take(refs, count), take(refs, count)
    whole, steps, gain_parts = take(refs, 3)
    iterate, poly, product, total = take(refs, 4)
    iterate_low, poly_low, other_low, total_low = take(refs, 4)
    value_rows, rows_in, rows_low = take(refs, 3)
    load_sem, own_sem, send_z, recv_z, send_x, recv_x, send_y, recv_y, send_d, recv_d, send_c, recv_c = take(refs, 12)
    send_g, recv_g, back_sem, send_b, recv_b, move_send, move_recv, move_own = refs
    me, partner, across, down = neighbours()
    plane = lax.axis_index("tensor")
    diagonal = across + down - me
    planes = [lax.rem(plane + offset, 4) for offset in (1, 2, 3)]
    flip = lambda block: block + 1 - 2 * lax.rem(block, 2)
    half = rows_low.shape[0]
    start_move, finish_move = move_plan(True, rows_low, rows_out, move_send, move_recv, move_own)
    near = (
        poly_low, other_low, total_low, iterate_low.at[0:half], iterate_low.at[half : 2 * half],
        value_rows, rows_in, poly.at[0:half],
    )
    loads = [
        pltpu.make_async_copy(source, target, load_sem.at[index])
        for index, (source, target) in enumerate(zip(far, near))
    ]
    for load in loads:
        load.start()

    def place(part, slot, block):
        height = heights[part]
        return whole.at[pl.ds(pl.multiple_of(slot * height, 16), height), lanes(block)]

    def spread(part, source, slot):
        view = place(part, slot, me)
        send_to(source, view, send_x.at[slot], recv_x.at[slot], (across, plane))
        send_to(source, view, send_y.at[slot], recv_y.at[slot], (down, plane))
        send_to(source, view, send_c.at[slot, 0], recv_c.at[slot, 0], (partner, plane))

    def on_plane(body):
        for part in range(count):
            @pl.when(plane == part)
            def _():
                body(part)

    def off_plane(body):
        for part in range(count):
            @pl.when(plane != part)
            def _():
                body(part)

    def tiles_of(part):
        height = heights[part]
        return [(first, min(128, height - first)) for first in range(0, height, 128)]

    greet(plane, (partner, across, down), planes)
    for part in (2, 0, 3, 1):
        for first, extent in tiles_of(part):
            rows, columns = pl.ds(first, extent), slice(first, first + extent)
            added = MOMENTUM * moments[part][:, columns] + sums[part][rows].T
            new_moments[part][:, columns] = added
            blocks[part][rows] = low(added.T)

        @pl.when(plane != part)
        def _():
            offset = lax.rem(plane + 3 - part, 4)
            send_to(blocks[part], place(part, plane, me), send_z.at[part], recv_z.at[offset], (me, part))

        @pl.when(plane == part)
        def _():
            pltpu.make_async_copy(blocks[part], place(part, part, me), own_sem).start()
            spread(part, blocks[part], part)

    def pass_z(part):
        for distance in (1, 3, 2):
            slot = (part + distance) % 4
            view = place(part, slot, me)
            wait_for(view, recv_z.at[(slot + 3 - part) % 4])
            spread(part, view, slot)

    on_plane(pass_z)

    for load in loads:
        load.wait()
    gain_out[1:2] = gain_two[...]
    gain_out[0:1] = jnp.zeros((1, size), f32)

    @pl.loop(0, half // 64)
    def _(index):
        first = pl.multiple_of(index * 64, 64)
        window = pl.ds(first, 64)
        other_window = pl.ds(pl.multiple_of(first + half, 64), 64)
        grad = product_of(iterate_low[window], poly_low[...], ((1,), (0,)))
        grad = grad + product_of(iterate_low[other_window], other_low[...], ((1,), (0,)))
        grad = grad + product_of(value_rows[window], total_low[...], ((1,), (0,)))
        rows = rows_in[window].astype(f32)
        centre = rows - jnp.mean(rows, axis=1, keepdims=True)
        inverse = lax.rsqrt(jnp.mean(centre * centre, axis=1, keepdims=True) + NORM_EPS)
        normed = centre * inverse
        scaled = grad * gains[0:1]
        mean_grad = jnp.mean(scaled, axis=1, keepdims=True)
        mean_cross = jnp.mean(scaled * normed, axis=1, keepdims=True)
        back = inverse * (scaled - mean_grad - normed * mean_cross)
        rows_low[window] = low(poly[window] + back)
        gain_out[0:1] += jnp.sum(grad * normed, axis=0, keepdims=True)

    start_move()
    for index, other in enumerate(planes):
        send_to(gain_out, gain_parts.at[index], send_g.at[index], recv_g.at[index], (me, other))

    def pass_xy(part):
        for slot in range(4):
            view = place(part, slot, across)
            wait_for(view, recv_x.at[slot])
            if slot < 2:
                send_to(view, view, send_d.at[slot], recv_d.at[slot], (down, plane))
            send_to(view, view, send_c.at[slot, 1], recv_c.at[slot, 1], (partner, plane))
            view = place(part, slot, down)
            wait_for(view, recv_y.at[slot])
            if slot >= 2:
                send_to(view, view, send_d.at[slot], recv_d.at[slot], (across, plane))
            send_to(view, view, send_c.at[slot, 2], recv_c.at[slot, 2], (partner, plane))

    on_plane(pass_xy)

    def pass_diagonal(part):
        for slot in range(4):
            view = place(part, slot, diagonal)
            wait_for(view, recv_d.at[slot])
            send_to(view, view, send_c.at[slot, 3], recv_c.at[slot, 3], (partner, plane))
        for slot in range(4):
            for index, block in enumerate((me, across, down, diagonal)):
                wait_for(place(part, slot, flip(block)), recv_c.at[slot, index])
        wait_for(blocks[part], own_sem)

    on_plane(pass_diagonal)

    windows = [pl.ds(first, tile) for first in range(0, size, tile)]
    zero = jnp.zeros((1, 1), f32)
    blank = jnp.zeros((1, size), f32)
    corner = lax.broadcasted_iota(jnp.int32, (tile, tile), 0) == lax.broadcasted_iota(jnp.int32, (tile, tile), 1)

    def gram(part):
        rows = slice(0, 4 * heights[part])
        for group in range(2):
            edge = group * size // 2

            @pl.loop(0, 2)
            def _(index):
                window = pl.ds(pl.multiple_of(edge + index * tile, tile), tile)
                iterate[window, edge:] = product_of(whole[rows, window], whole[rows, edge:], ((0,), (0,)))

    on_plane(gram)

    def upper(window):
        return slice(window.start, size)

    def store(window, result, shift, full, low_copy):
        corner_block = result[:, :tile] - jnp.where(corner, shift, 0.0)
        result = jnp.concatenate([corner_block, result[:, tile:]], axis=1) if result.shape[1] > tile else corner_block
        full[window, upper(window)] = result
        result_low = low(result)
        low_copy[window, upper(window)] = result_low
        for first in range(tile, result.shape[1], tile):
            low_copy[pl.ds(window.start + first, tile), window] = result_low[:, first : first + tile].T
        return result

    def fold(left, right, window):
        sums_of = jnp.sum(left * right, axis=0, keepdims=True)
        weighted = jnp.concatenate([sums_of[:, :tile], 2.0 * sums_of[:, tile:]], axis=1) if sums_of.shape[1] > tile else sums_of
        return jnp.concatenate([blank[:, : window.start], weighted], axis=1) if window.start else weighted

    def finish(row):
        return jnp.sum(row, axis=1, keepdims=True) / size

    def multiply(left, right, window):
        return product_of(left[window], right[:, upper(window)], ((1,), (0,)))

    trace = zero
    for window in windows:
        block = jnp.where(corner, iterate[window, window], 0.0)
        trace = trace + jnp.sum(jnp.sum(block, axis=0, keepdims=True), axis=1, keepdims=True)
    factor = 1.0 / (jnp.sqrt(trace) + NORM_FLOOR)
    squared = factor * factor
    mean = trace * squared / size
    row = blank
    for window in windows:
        rest = store(window, iterate[window, upper(window)] * squared, mean, iterate, iterate_low)
        row = row + fold(rest, rest, window)
    square = finish(row)

    def polynomial(mean, square, with_total):
        linear = QUINTIC_THREE + 2.0 * QUINTIC_FIVE * mean
        shift = QUINTIC_FIVE * square
        poly_mean = QUINTIC_ONE + QUINTIC_THREE * mean + QUINTIC_FIVE * (mean * mean) + shift
        row, total_row = blank, blank
        for window in windows:
            mine = iterate[window, upper(window)]
            rest = linear * mine + QUINTIC_FIVE * multiply(iterate_low, iterate_low, window)
            rest = store(window, rest, shift, poly, poly_low)
            row = row + fold(rest, mine, window)
            if with_total:
                total_row = total_row + fold(rest, total[window, upper(window)], window)
        return (poly_mean, finish(row), finish(total_row))

    def grow_total(poly_mean, total_mean, cross):
        for window in windows:
            result = poly_mean * total[window, upper(window)] + total_mean * poly[window, upper(window)]
            result = result + multiply(poly_low, total_low, window)
            store(window, result, cross, total, other_low)
        total_low[...] = other_low[...]
        return poly_mean * total_mean + cross

    def advance(poly_mean, mean, cross):
        row = blank
        for window in windows:
            rest = poly[window, upper(window)]
            result = poly_mean * iterate[window, upper(window)] + mean * rest
            result = result + multiply(poly_low, iterate_low, window)
            result = store(window, result, cross, product, other_low)
            row = row + fold(result, rest, window)
        product_mean = poly_mean * mean + cross
        cross = finish(row)
        row = blank
        for window in windows:
            result = poly_mean * product[window, upper(window)] + product_mean * poly[window, upper(window)]
            result = result + multiply(poly_low, other_low, window)
            result = store(window, result, cross, iterate, iterate_low)
            row = row + fold(result, result, window)
        return (poly_mean * product_mean + cross, finish(row))

    total_mean, cross, _ = polynomial(mean, square, False)
    for window in windows:
        total[window, upper(window)] = poly[window, upper(window)]
    total_low[...] = poly_low[...]
    mean, square = advance(total_mean, mean, cross)

    def sweep(_, carry):
        mean, square, total_mean = carry
        poly_mean, cross, cross_total = polynomial(mean, square, True)
        total_mean = grow_total(poly_mean, total_mean, cross_total)
        return advance(poly_mean, mean, cross) + (total_mean,)

    mean, square, total_mean = lax.fori_loop(0, NS_ITERS - 2, sweep, (mean, square, total_mean))
    poly_mean, _, cross_total = polynomial(mean, square, True)
    total_mean = grow_total(poly_mean, total_mean, cross_total)

    mine = lanes(me)
    columns = total_low[:, mine]

    def step_home(part):
        height = heights[part]

        @pl.loop(0, 4)
        def _(turn_of):
            slot = lax.rem(part + 1 + turn_of, 4)
            window = pl.ds(pl.multiple_of(slot * height, 16), height)
            result = product_of(whole[window, :], columns, ((1,), (0,)))
            result = result + total_mean * whole[window, mine].astype(f32)
            steps[window, :] = low(factor * result)

            @pl.when(turn_of == 3)
            def _():
                pltpu.make_async_copy(steps.at[window, :], backs[part], back_sem).start()

            @pl.when(turn_of < 3)
            def _():
                send_to(steps.at[window, :], backs[part], send_b.at[turn_of], recv_b.at[part], (me, slot))

    on_plane(step_home)

    for index in range(3):
        wait_for(gain_out, send_g.at[index])
        wait_for(gain_parts.at[index], recv_g.at[index])
    gain_out[...] = gain_out[...] + gain_parts[0] + gain_parts[1] + gain_parts[2]
    for index, other in ((3, across), (4, down), (5, partner)):
        send_to(gain_out, gain_parts.at[index], send_g.at[index], recv_g.at[index], (other, plane))
        wait_for(gain_out, send_g.at[index])
        wait_for(gain_parts.at[index], recv_g.at[index])
        gain_out[...] = gain_out[...] + gain_parts[index]

    on_plane(lambda part: wait_for(backs[part], back_sem))
    off_plane(lambda part: wait_for(backs[part], recv_b.at[part]))
    for part in range(count):
        rate = MUON_RATE * 0.2 * math.sqrt(4 * heights[part])
        for first, extent in tiles_of(part):
            rows, columns_of = pl.ds(first, extent), slice(first, first + extent)
            step = backs[part][rows].astype(f32).T
            kept = weights[part][:, columns_of].astype(f32) * (1.0 - MUON_RATE * DECAY_RATE)
            new_weights[part][:, columns_of] = kept - rate * step

    def last_waits(part):
        for slot in range(4):
            for sem in (send_x.at[slot], send_y.at[slot], send_d.at[slot]):
                wait_for(blocks[part], sem)
            for index in range(4):
                wait_for(blocks[part], send_c.at[slot, index])
        for index in range(3):
            wait_for(blocks[part], send_b.at[index])

    on_plane(last_waits)
    off_plane(lambda part: wait_for(blocks[part], send_z.at[part]))
    finish_move()


def optimize(sums, moments, weights, gain_two, gains, far, collective_id):
    heights = [part.shape[0] for part in sums]
    count, size = len(heights), gains.shape[1]
    f32, bf16 = jnp.float32, jnp.bfloat16
    sem = pltpu.SemaphoreType.DMA
    anywhere = pl.BlockSpec(memory_space=pl.ANY)
    local = pl.BlockSpec(memory_space=pltpu.VMEM)
    half = far[6].shape[0]
    outs = pl.pallas_call(
        functools.partial(optimize_kernel, heights),
        out_shape=[jax.ShapeDtypeStruct((128, height), f32) for height in heights] * 2
        + [jax.ShapeDtypeStruct(gains.shape, f32), jax.ShapeDtypeStruct((2, half // 2, size), bf16)],
        in_specs=[local] * (3 * count + 2) + [anywhere] * 8,
        out_specs=[local] * (2 * count + 1) + [anywhere],
        scratch_shapes=[pltpu.VMEM((height, 128), bf16) for height in heights] * 2
        + [pltpu.VMEM((4 * max(heights), size), bf16), pltpu.VMEM((4 * max(heights), 128), bf16)]
        + [pltpu.VMEM((6,) + gains.shape, f32)]
        + [pltpu.VMEM((size, size), f32)] * 4
        + [pltpu.VMEM((size, size), bf16)] * 4
        + [pltpu.VMEM((half, size), bf16)] * 3
        + [sem((8,)), sem, sem((count,)), sem((3,))]
        + [sem((4,))] * 6
        + [sem((4, 4))] * 2
        + [sem((6,))] * 2
        + [sem, sem((3,)), sem((count,)), sem((2,)), sem((2,)), sem],
        compiler_params=pltpu.CompilerParams(
            collective_id=collective_id, has_side_effects=True, vmem_limit_bytes=60 * 1024 * 1024
        ),
        name="optimize",
    )(*sums, *moments, *weights, gain_two, gains, *far)
    return (outs[:count], outs[count : 2 * count], outs[2 * count], outs[2 * count + 1])


def weight_shards(weights):
    shards = [turn(weight) for weight in weights]
    third = shards[0].shape[0] // 3
    return [shards[0][third * part : third * part + third] for part in range(3)] + shards[1:]


def gather_weights(shards):
    tensor_count, dp_count = lax.axis_size("tensor"), lax.axis_size("dp")
    wholes = [lax.all_gather(shard, ("tensor", "dp")) for shard in shards]
    wholes = [
        whole.reshape(tensor_count, dp_count, *whole.shape[1:]).transpose(0, 2, 1, 3)
        for whole in wholes
    ]
    return [whole.reshape(*whole.shape[:2], -1) for whole in wholes]


def reduce_grads(grads):
    tensor_count, dp_count = lax.axis_size("tensor"), lax.axis_size("dp")
    sums = []
    for grad in grads:
        blocks = grad.reshape(*grad.shape[:2], dp_count, -1).transpose(0, 2, 1, 3)
        blocks = blocks.reshape(-1, *blocks.shape[2:])
        part = lax.psum_scatter(blocks, ("tensor", "dp"), scatter_dimension=0, tiled=True)
        sums.append(part[0].astype(jnp.float32))
    return sums


def lane_of(shape):
    return lax.broadcasted_iota(jnp.int32, shape, 1)

def turned(vectors, cosine, sine):
    lane = lax.rem(lane_of(vectors.shape), 64)
    swapped = jnp.where(lane < 32, pltpu.roll(vectors, 96, 1), pltpu.roll(vectors, 32, 1))
    return vectors * cosine + swapped * sine

def project_kernel(rows, query_weight, key_weight, value_weight, cosine, sine, queries, pair):
    rows = rows[...]
    for weight, target in ((query_weight, 0), (key_weight, 1)):
        result = product_of(rows, weight[0], ((1,), (1,)))
        for first in range(0, result.shape[1], 128):
            part = turned(result[:, first : first + 128], cosine[...], sine[...])
            if target == 0:
                queries[:, first : first + 128] = low(part * SCORE_SCALE)
            else:
                pair[0, :, first : first + 128] = low(part)
    pair[1] = low(product_of(rows, value_weight[0], ((1,), (1,))))

def project(rows, query_weight, key_weight, value_weight, cosine, sine):
    count, width = rows.shape
    groups, height, _ = query_weight.shape
    whole = lambda *shape: pl.BlockSpec(shape, lambda i: (0,) * len(shape))
    weight = pl.BlockSpec((1, height, width), lambda i: (i, 0, 0))
    return pl.pallas_call(
        project_kernel,
        grid=(groups,),
        out_shape=[jax.ShapeDtypeStruct((count, width), jnp.bfloat16), jax.ShapeDtypeStruct((2, count, width), jnp.bfloat16)],
        in_specs=[whole(count, width), weight, weight, weight, whole(count, 128), whole(count, 128)],
        out_specs=[pl.BlockSpec((count, height), lambda i: (0, i)), pl.BlockSpec((2, count, height), lambda i: (0, 0, i))],
        compiler_params=pltpu.CompilerParams(vmem_limit_bytes=40 * 1024 * 1024),
        name="project",
    )(rows, query_weight, key_weight, value_weight, cosine, sine)

def head_rows(transposed, head):
    rows = lax.broadcasted_iota(jnp.int32, transposed.shape, 0)
    return jnp.where(lax.div(rows, 64) == head, transposed, jnp.zeros_like(transposed))

def head_lanes(values, head):
    return jnp.where(lax.div(lane_of(values.shape), 64) == head, values, jnp.zeros_like(values))

def scores_of(keys, queries_turned, bias):
    scores = product_of(keys, queries_turned, ((1,), (0,)))
    return scores + jnp.concatenate([bias] * (scores.shape[1] // 128), axis=1)

def attend_kernel(queries, own, other, bias, context, log_total):
    query_turned = queries[...].T
    keys = jnp.concatenate([own[0], other[0]], axis=0)
    value_turned = jnp.concatenate([own[1].T, other[1].T], axis=1)
    parts, logs = [], []
    for head in range(2):
        scores = scores_of(keys, head_rows(query_turned, head), bias[...])
        highest = jnp.max(scores, axis=0, keepdims=True)
        weights = jnp.exp(scores - highest)
        total = jnp.sum(weights, axis=0, keepdims=True)
        part = product_of(value_turned[64 * head : 64 * head + 64], low(weights), ((1,), (0,)))
        parts.append(part / total)
        logs.append(highest + jnp.log(total))
    context[...] = low(jnp.concatenate(parts, axis=0)).T
    log_total[0] = jnp.concatenate(logs + logs * 3, axis=0)

def attend(queries, own, other, bias):
    count, width = queries.shape
    pairs = width // 128
    column = pl.BlockSpec((count, 128), lambda i: (0, i))
    double = pl.BlockSpec((2, count, 128), lambda i: (0, 0, i))
    return pl.pallas_call(
        attend_kernel,
        grid=(pairs,),
        out_shape=[jax.ShapeDtypeStruct((count, width), jnp.bfloat16), jax.ShapeDtypeStruct((pairs, 8, count), jnp.float32)],
        in_specs=[column, double, double, pl.BlockSpec((2 * count, 128), lambda i: (0, 0))],
        out_specs=[column, pl.BlockSpec((1, 8, count), lambda i: (i, 0, 0))],
        compiler_params=pltpu.CompilerParams(vmem_limit_bytes=40 * 1024 * 1024),
        name="attend",
    )(queries, own, other, bias)

def attend_back_kernel(queries, own, other, bias, grad, context, log_total, cosine, sine, grad_query, grad_own, grad_other):
    count = queries.shape[0]
    query_turned, grad_turned = queries[...].T, grad[...].T
    inner = (grad[...].astype(jnp.float32) * context[...].astype(jnp.float32)).T
    query_parts = [None, None]
    for half, (pair, result) in enumerate(((own, grad_own), (other, grad_other))):
        keys, values = pair[0], pair[1]
        key_turned = keys.T
        grad_keys, grad_values = None, None
        window = pl.ds(half * count, count)
        for head in range(2):
            lanes_of_head = slice(64 * head, 64 * head + 64)
            scores = scores_of(keys, head_rows(query_turned, head), bias[window])
            weights = jnp.exp(scores - log_total[0, head : head + 1])
            grad_weights = product_of(values, head_rows(grad_turned, head), ((1,), (0,)))
            inner_row = jnp.sum(inner[lanes_of_head], axis=0, keepdims=True)
            grad_scores = low(weights * (grad_weights - inner_row))
            value_part = product_of(low(weights), head_lanes(grad[...], head), ((1,), (0,)))
            key_part = product_of(grad_scores, head_lanes(queries[...], head), ((1,), (0,)))
            query_part = product_of(key_turned[lanes_of_head], grad_scores, ((1,), (0,)))
            grad_values = value_part if head == 0 else grad_values + value_part
            grad_keys = key_part if head == 0 else grad_keys + key_part
            query_parts[head] = query_part if half == 0 else query_parts[head] + query_part
        result[0] = turned(grad_keys, cosine[window], -sine[window]).astype(result.dtype)
        result[1] = grad_values.astype(result.dtype)
    grad_rows = jnp.concatenate(query_parts, axis=0).T * SCORE_SCALE
    own_rows = pl.ds(0, count)
    grad_query[...] = low(turned(grad_rows, cosine[own_rows], -sine[own_rows]))

def attend_back(queries, own, other, bias, grad, context, log_total, cosine, sine):
    count, width = queries.shape
    pairs = width // 128
    column = pl.BlockSpec((count, 128), lambda i: (0, i))
    double = pl.BlockSpec((2, count, 128), lambda i: (0, 0, i))
    table = pl.BlockSpec((2 * count, 128), lambda i: (0, 0))
    return pl.pallas_call(
        attend_back_kernel,
        grid=(pairs,),
        out_shape=[
            jax.ShapeDtypeStruct((count, width), jnp.bfloat16),
            jax.ShapeDtypeStruct((2, count, width), jnp.float32),
            jax.ShapeDtypeStruct((2, count, width), jnp.bfloat16),
        ],
        in_specs=[column, double, double, table, column, column, pl.BlockSpec((1, 8, count), lambda i: (i, 0, 0)), table, table],
        out_specs=[column, double, double],
        compiler_params=pltpu.CompilerParams(vmem_limit_bytes=48 * 1024 * 1024),
        name="attend_back",
    )(queries, own, other, bias, grad, context, log_total, cosine, sine)

def feed_kernel(rows, cotangent, in_weight, out_weight, result, grad_rows, grad_in, grad_out):
    height = out_weight.shape[1]
    @pl.when(pl.program_id(0) == 0)
    def _():
        result[...] = jnp.zeros_like(result)
        grad_rows[...] = jnp.zeros_like(grad_rows)
    gate = product_of(in_weight[0, 0:height], rows[...], ((1,), (1,)))
    up = product_of(in_weight[0, height:], rows[...], ((1,), (1,)))
    grad_hidden = product_of(out_weight[0], cotangent[...], ((1,), (1,)))
    below = 0.5 + 0.5 * lax.erf(gate * math.sqrt(0.5))
    active = gate * below
    hidden = low(active * up)
    slope = below + gate * jnp.exp(-0.5 * gate * gate) * (1.0 / math.sqrt(2.0 * math.pi))
    grad_gate = low(grad_hidden * up * slope)
    grad_up = low(grad_hidden * active)
    grad_out[0] = low(product_of(hidden, cotangent[...], ((1,), (0,))))
    grad_in[0, 0:height] = low(product_of(grad_gate, rows[...], ((1,), (0,))))
    grad_in[0, height:] = low(product_of(grad_up, rows[...], ((1,), (0,))))
    result[...] += product_of(hidden, out_weight[0], ((0,), (0,)))
    grad_rows[...] += product_of(grad_gate, in_weight[0, 0:height], ((0,), (0,)))
    grad_rows[...] += product_of(grad_up, in_weight[0, height:], ((0,), (0,)))

def feed(rows, cotangent, in_weight, out_weight):
    count, width = rows.shape
    groups, height, _ = out_weight.shape
    whole = pl.BlockSpec((count, width), lambda i: (0, 0))
    block = lambda size: pl.BlockSpec((1, size, width), lambda i: (i, 0, 0))
    return pl.pallas_call(
        feed_kernel,
        grid=(groups,),
        out_shape=[
            jax.ShapeDtypeStruct((count, width), jnp.float32),
            jax.ShapeDtypeStruct((count, width), jnp.float32),
            jax.ShapeDtypeStruct(in_weight.shape, jnp.bfloat16),
            jax.ShapeDtypeStruct(out_weight.shape, jnp.bfloat16),
        ],
        in_specs=[whole, whole, block(2 * height), block(height)],
        out_specs=[whole, whole, block(2 * height), block(height)],
        compiler_params=pltpu.CompilerParams(vmem_limit_bytes=60 * 1024 * 1024),
        name="feed",
    )(rows, cotangent, in_weight, out_weight)


def turn(block):
    return block.transpose(*range(1, block.ndim), 0).reshape(-1, block.shape[0])


def turn_back(rows, like):
    rows = rows.reshape(*like.shape[1:], like.shape[0])
    return rows.transpose(rows.ndim - 1, *range(rows.ndim - 1))


def orthogonal_steps(blocks, gain_part):
    tensor_count = lax.axis_size("tensor")
    heights = [block.shape[0] for block in blocks]
    row_count = blocks[0].shape[1]
    first_row = lax.axis_index("dp") * row_count
    gain_grad = lax.psum(gain_part, BOTH)
    widest = max(heights)
    stacked = jnp.stack(
        [jnp.pad(block.T, ((0, 0), (0, widest - block.shape[0]))) for block in blocks]
    )
    owned = lax.all_to_all(stacked, "tensor", split_axis=0, concat_axis=0, tiled=True)
    whole = lax.all_gather(owned, "dp", axis=1, tiled=True)
    mean, rest = newton_schulz(einsum("tik,tjk->ij", whole, whole))
    own_rows = lax.dynamic_slice_in_dim(rest, first_row, row_count, 0)
    own_whole = lax.dynamic_slice_in_dim(whole, first_row, row_count, 1)
    step_rows = low(einsum("ij,tjk->tik", low(own_rows), whole) + mean * own_whole)
    returned = lax.all_to_all(step_rows, "tensor", split_axis=0, concat_axis=0, tiled=True)
    return ([returned[index, :, :height].T for index, height in enumerate(heights)], gain_grad)


def on_device(
    inputs,
    cotangent,
    lengths,
    qkv_weight,
    attn_out_weight,
    ffn_in_weight,
    ffn_out_weight,
    norm_gains,
    qkv_moment,
    attn_out_moment,
    ffn_in_moment,
    ffn_out_moment,
    gain_first,
    gain_second,
):
    tensor_count = lax.axis_size("tensor")
    dp_count = lax.axis_size("dp")
    dp_index = lax.axis_index("dp")
    tensor_index = lax.axis_index("tensor")
    core = dp_index % 2
    odd = tensor_index % 2 == 1
    upper = tensor_index >= tensor_count // 2
    lists = exchange_lists(dp_count // 2, tensor_count)
    weights = (qkv_weight, attn_out_weight, ffn_in_weight, ffn_out_weight)
    row_count = qkv_weight.shape[0]

    width = inputs.shape[3]
    local_rows = 2 * inputs.shape[2]
    fits = (tensor_count, dp_count, row_count, width) == (4, 8, 128, 1024)
    positions = jnp.concatenate(
        [core * local_rows + jnp.arange(local_rows), (1 - core) * local_rows + jnp.arange(local_rows)]
    )
    cosine, sine = rotary(positions)
    shards = weight_shards(weights)
    if fits:
        sizes = lengths.astype(jnp.float32)
        sizes = jnp.broadcast_to(jnp.pad(sizes, ((0, 6), (0, 0))), (8, 128))
        outs = forward(shards, inputs[:, 0], cotangent[:, 0], sizes, norm_gains, cosine, sine, 1)
        wholes, (rows_low, cotangent_low) = outs[:6], outs[6:8]
        low_one, queries, own, other, context, log_total, bias, middle, low_two = outs[8:]
    else:
        wholes = gather_weights(shards)
        rows_low = to_sequences(inputs[:, 0], lists, odd, upper)
        cotangent_low = to_sequences(cotangent[:, 0], lists, odd, upper)
    query_all, key_all, value_all, attn_all, ffn_in_all, ffn_out_all = wholes
    attn_rows = attn_all.reshape(-1, width)
    rows_in = rows_low.astype(jnp.float32)
    grad_rows = cotangent_low.astype(jnp.float32)
    normed_one, inverse_one, scaled_one = layer_norm_parts(rows_in, norm_gains[0])
    if not fits:
        own_lengths = swap_partner(lengths)
        both_lengths = jnp.where(
            core == 0,
            jnp.concatenate([lengths, own_lengths], 1),
            jnp.concatenate([own_lengths, lengths], 1),
        )
        length = lax.dynamic_index_in_dim(both_lengths.reshape(-1), tensor_index, 0, keepdims=False)
        bias = jnp.where(positions < length, 0.0, MASK_VALUE).astype(jnp.float32)
        bias = jnp.broadcast_to(bias[:, None], (positions.shape[0], 128))
        low_one = low(scaled_one)
        queries, own = project(
            low_one, query_all, key_all, value_all, cosine[:local_rows], sine[:local_rows]
        )
        other = swap_partner(own)
        context, log_total = attend(queries, own, other, bias)
        middle = rows_in + einsum("sk,kn->sn", context, attn_rows)
    normed_two, inverse_two, scaled_two = layer_norm_parts(middle, norm_gains[1])
    if not fits:
        low_two = low(scaled_two)
    if fits:
        outs = backward(
            (attn_all, ffn_in_all, ffn_out_all),
            low_two,
            cotangent_low,
            middle,
            queries,
            own,
            other,
            context,
            low_one,
            bias,
            log_total,
            cosine,
            sine,
            norm_gains,
            2,
        )
        sums, (grad_query, grad_pair, outputs, grad_middle, gain_two) = outs[:4], outs[4:]
    else:
        ffn_branch, grad_scaled_two, grad_ffn_in, grad_ffn_out = feed(
            low_two, cotangent_low, ffn_in_all, ffn_out_all
        )
        result = low(middle + ffn_branch)
        grad_from_two, gain_two = layer_norm_back(
            grad_scaled_two, normed_two, inverse_two, norm_gains[1]
        )
        grad_middle = grad_rows + grad_from_two
        grad_branch = low(grad_middle)
        grad_context = low(einsum("sn,kn->sk", grad_branch, attn_rows))
        grad_attn_out = low(einsum("sk,sn->kn", context, grad_branch)).reshape(attn_all.shape)
        grad_query, grad_own, grad_other = attend_back(
            queries, own, other, bias, grad_context, context, log_total, cosine, sine
        )
        grad_pair = low(grad_own + swap_partner(grad_other).astype(jnp.float32))
    moments = (qkv_moment, attn_out_moment, ffn_in_moment, ffn_out_moment)
    grad_parts = (grad_query, grad_pair[0], grad_pair[1])
    weight_parts = [part.reshape(-1, width) for part in (query_all, key_all, value_all)]
    if fits:
        far = (*weight_parts, *grad_parts, rows_low, grad_middle)
        new_moments, new_weights, gain_grad, input_grad = optimize(
            sums,
            [moment.reshape(row_count, -1) for moment in moments],
            [weight.reshape(row_count, -1) for weight in weights],
            gain_two,
            norm_gains,
            far,
            3,
        )
        new_moments = [part.reshape(like.shape) for part, like in zip(new_moments, moments)]
        new_weights = [part.reshape(like.shape) for part, like in zip(new_weights, moments)]
    else:
        grad_scaled_one = sum(
            einsum("sk,kn->sn", part, weight) for part, weight in zip(grad_parts, weight_parts)
        )
        grad_from_one, gain_one = layer_norm_back(
            grad_scaled_one, normed_one, inverse_one, norm_gains[0]
        )
        grads = [low(einsum("sk,sn->kn", part, low_one)) for part in grad_parts]
        grads = [grad.reshape(query_all.shape) for grad in grads]
        sums = reduce_grads(grads + [grad_attn_out, grad_ffn_in, grad_ffn_out])
        sums = [jnp.concatenate(sums[:3])] + list(sums[3:])
        outputs = from_sequences(result, lists, odd, upper)
        input_grad = from_sequences(low(grad_middle + grad_from_one), lists, odd, upper)
        turned_sums = [turn_back(part, moment) for part, moment in zip(sums, moments)]
        new_moments = [MOMENTUM * moment + part for moment, part in zip(moments, turned_sums)]
        steps, gain_grad = orthogonal_steps(
            [low(turn(moment)) for moment in new_moments], jnp.stack([gain_one, gain_two])
        )
        new_weights = [
            weight.astype(jnp.float32) * (1.0 - MUON_RATE * DECAY_RATE)
            - MUON_RATE
            * 0.2
            * math.sqrt(step.shape[0] * tensor_count)
            * turn_back(step, weight).astype(jnp.float32)
            for weight, step in zip(weights, steps)
        ]
    outputs, input_grad = outputs[:, None], input_grad[:, None].astype(jnp.float32)
    gain_first_new = BETA_ONE * gain_first + (1.0 - BETA_ONE) * gain_grad
    gain_second_new = BETA_TWO * gain_second + (1.0 - BETA_TWO) * gain_grad * gain_grad
    first_hat = gain_first_new / (1.0 - BETA_ONE**STEP)
    second_hat = gain_second_new / (1.0 - BETA_TWO**STEP)
    norm_gains_new = norm_gains - ADAM_RATE * (
        first_hat / (jnp.sqrt(second_hat) + ADAM_EPS) + DECAY_RATE * norm_gains
    )
    return (
        outputs,
        input_grad,
        new_moments[0],
        new_weights[0],
        new_moments[1],
        new_weights[1],
        new_moments[2],
        new_weights[2],
        new_moments[3],
        new_weights[3],
        gain_first_new,
        gain_second_new,
        norm_gains_new,
    )


def solution(mesh):
    in_specs = (
        P(None, "dp", "tensor", None),
        P(None, "dp", "tensor", None),
        P(None, "dp"),
        P("dp", None, "tensor"),
        P("dp", "tensor"),
        P("dp", None, "tensor"),
        P("dp", "tensor"),
        P(),
        P("dp", None, "tensor"),
        P("dp", "tensor"),
        P("dp", None, "tensor"),
        P("dp", "tensor"),
        P(),
        P(),
    )
    out_specs = (
        P(None, "dp", "tensor", None),
        P(None, "dp", "tensor", None),
        P("dp", None, "tensor"),
        P("dp", None, "tensor"),
        P("dp", "tensor"),
        P("dp", "tensor"),
        P("dp", None, "tensor"),
        P("dp", None, "tensor"),
        P("dp", "tensor"),
        P("dp", "tensor"),
        P(),
        P(),
        P(),
    )
    return jax.shard_map(
        on_device, mesh=mesh, in_specs=in_specs, out_specs=out_specs, check_vma=False
    )
```

```python
import functools
import math

import jax
import jax.numpy as jnp
import numpy as np
from jax import lax
from jax.experimental import pallas as pl
from jax.experimental.pallas import tpu as pltpu
from jax.sharding import PartitionSpec as P

HEAD_DIM = 64
NS_ITERS = 5
STEP = 10
SCORE_SCALE = 1.0 / math.sqrt(HEAD_DIM)


ROPE_BASE = 160000.0
NORM_EPS = 1e-05
MASK_VALUE = -1e30
MOMENTUM = 0.95
MUON_RATE = 0.1
DECAY_RATE = 0.01
QUINTIC_ONE = 3.4445
QUINTIC_THREE = -4.775
QUINTIC_FIVE = 2.0315
NORM_FLOOR = 1e-07
BETA_ONE = 0.9
BETA_TWO = 0.95
ADAM_RATE = 0.2
ADAM_EPS = 1e-08
BOTH = ("dp", "tensor")
MESH = pl.DeviceIdType.MESH


def rotary(positions):
    half_size = HEAD_DIM // 2
    exponents = jnp.arange(half_size).astype(jnp.float32) / half_size
    frequency = jnp.power(ROPE_BASE, -exponents)
    angles = positions.astype(jnp.float32)[:, None] * frequency[None, :]
    cosine, sine = jnp.cos(angles), jnp.sin(angles)
    return (
        jnp.concatenate([cosine] * 4, axis=1),
        jnp.concatenate([-sine, sine, -sine, sine], axis=1),
    )


def layer_norm_parts(vectors, gain):
    centre = vectors - jnp.mean(vectors, axis=-1, keepdims=True)
    inverse = lax.rsqrt(jnp.mean(centre * centre, axis=-1, keepdims=True) + NORM_EPS)
    normed = centre * inverse
    return (normed, inverse, normed * gain)


def layer_norm_back(grad_out, normed, inverse, gain):
    grad_normed = grad_out * gain
    mean_grad = jnp.mean(grad_normed, axis=-1, keepdims=True)
    mean_cross = jnp.mean(grad_normed * normed, axis=-1, keepdims=True)
    return (
        inverse * (grad_normed - mean_grad - normed * mean_cross),
        jnp.sum(grad_out * normed, axis=0),
    )


def einsum(spec, *operands):
    return jnp.einsum(spec, *operands, preferred_element_type=jnp.float32)


def low(values):
    return values.astype(jnp.bfloat16)


def exchange_lists(chip_count, tensor_count):
    first_list, second_list = [], []
    for chip in range(chip_count):
        for core in range(2):
            for slot in range(tensor_count):
                for micro in range(2):
                    source = (2 * chip + core) * tensor_count + slot
                    target = (2 * chip + slot // 2) * tensor_count + 2 * micro + core
                    pair = (source, target)
                    (first_list if slot % 2 == micro else second_list).append(pair)
    return (first_list, second_list)


def to_sequences(blocks, lists, odd, upper):
    first = lax.ppermute(jnp.where(odd, blocks[1], blocks[0]), BOTH, lists[0])
    second = lax.ppermute(jnp.where(odd, blocks[0], blocks[1]), BOTH, lists[1])
    return jnp.where(
        upper, jnp.concatenate([second, first]), jnp.concatenate([first, second])
    )


def from_sequences(rows, lists, odd, upper):
    half = rows.shape[0] // 2
    top, bottom = rows[:half], rows[half:]
    back = [[(target, source) for source, target in pairs] for pairs in lists]
    first = lax.ppermute(jnp.where(upper, bottom, top), BOTH, back[0])
    second = lax.ppermute(jnp.where(upper, top, bottom), BOTH, back[1])
    return jnp.where(odd, jnp.stack([second, first]), jnp.stack([first, second]))


def swap_partner(values):
    count = lax.axis_size("dp")
    return lax.ppermute(values, "dp", [(index, index ^ 1) for index in range(count)])


def mean_split(matrix):
    mean = jnp.trace(matrix) / matrix.shape[0]
    return (mean, matrix - mean * jnp.eye(matrix.shape[0], dtype=jnp.float32))


def split_product(left, right):
    left_mean, left_rest = left
    right_mean, right_rest = right
    product = einsum("ij,jk->ik", low(left_rest), low(right_rest))
    product = product + left_mean * right_rest + right_mean * left_rest
    mean, rest = mean_split(product)
    return (mean + left_mean * right_mean, rest)


def newton_schulz(gram):
    factor = 1.0 / (jnp.sqrt(jnp.trace(gram)) + NORM_FLOOR)
    iterate = mean_split(gram * (factor * factor))
    whole = None
    for sweep_index in range(NS_ITERS):
        square = split_product(iterate, iterate)
        poly = (
            QUINTIC_ONE + QUINTIC_THREE * iterate[0] + QUINTIC_FIVE * square[0],
            QUINTIC_THREE * iterate[1] + QUINTIC_FIVE * square[1],
        )
        whole = poly if whole is None else split_product(poly, whole)
        if sweep_index < NS_ITERS - 1:
            iterate = split_product(poly, split_product(poly, iterate))
    return (whole[0] * factor, whole[1] * factor)


def step_of(rows):
    return next(step for step in (128, 64, 48, 32, 16) if rows % step == 0)


def lanes(block):
    return pl.ds(pl.multiple_of(block * 128, 128), 128)

def neighbours():
    me = lax.axis_index("dp")
    core, across, down = lax.rem(me, 2), lax.rem(lax.div(me, 2), 2), lax.div(me, 4)
    return (me, me + 1 - 2 * core, me + 2 - 4 * across, me + 4 - 8 * down)

def greet(plane, others, planes):
    barrier = pltpu.get_barrier_semaphore()
    me = lax.axis_index("dp")
    crossed = list(others[:1])
    for other in others:
        pl.semaphore_signal(barrier, inc=1, device_id=(other, plane), device_id_type=MESH)
    for other in planes:
        for same_place in [me] + crossed:
            pl.semaphore_signal(barrier, inc=1, device_id=(same_place, other), device_id_type=MESH)
    pl.semaphore_wait(barrier, len(others) + len(planes) * (1 + len(crossed)))

def add_into(target, source, rows, step):
    @pl.loop(0, rows // step)
    def _(index):
        window = pl.ds(pl.multiple_of(index * step, step), step)
        total = target[:, window].astype(jnp.float32) + source[:, window].astype(jnp.float32)
        target[:, window] = total.astype(jnp.bfloat16)


def send_to(source, target, send, recv, device):
    pltpu.make_async_remote_copy(
        source, target, send, recv, device_id=device, device_id_type=MESH
    ).start()


def wait_for(view, sem):
    pltpu.make_async_copy(view, view, sem).wait()


def move_plan(outward, source, target, send, recv, own):
    me, partner, _, _ = neighbours()
    plane = lax.axis_index("tensor")
    core = lax.rem(me, 2)
    column = me - core
    high, parity = lax.div(plane, 2), lax.rem(plane, 2)
    height = target.shape[1] if outward else source.shape[1]

    def owner_of(slot):
        return (column + parity, 2 * core + slot)

    def keeper_of(micro):
        return (column + high, 2 * micro + core)

    def same(device):
        return jnp.logical_and(device[0] == me, device[1] == plane)

    def half(rows, index):
        return rows.at[pl.ds(pl.multiple_of(index * height, height), height), :]

    def start():
        for index in range(2):
            if outward:
                device = owner_of(index)
                piece, goal, arrival = half(source, index), target.at[high], high
            else:
                device = keeper_of(index)
                piece, goal, arrival = source.at[index], half(target, parity), parity

            @pl.when(same(device))
            def _():
                pltpu.make_async_copy(piece, goal, own).start()

            @pl.when(jnp.logical_not(same(device)))
            def _():
                send_to(piece, goal, send.at[index], recv.at[arrival], device)

    def finish():
        for index in range(2):
            if outward:
                sent_to, came_from = owner_of(index), keeper_of(index)
                piece, goal = half(source, index), target.at[index]
            else:
                sent_to, came_from = keeper_of(index), owner_of(index)
                piece, goal = source.at[index], half(target, index)

            @pl.when(same(sent_to))
            def _():
                wait_for(piece, own)

            @pl.when(jnp.logical_not(same(sent_to)))
            def _():
                wait_for(piece, send.at[index])

            @pl.when(jnp.logical_not(same(came_from)))
            def _():
                wait_for(goal, recv.at[index])

    return (start, finish)


def scatter_plan(grads, sums, buffers, sems):
    held, from_x, from_y, from_yx, from_xy, from_z = buffers[:6]
    staging = buffers[6][0]
    (load_sem, send_c, recv_c, send_x, recv_x, send_y, recv_y, send_yx, recv_yx, send_xy, recv_xy, send_z, recv_z) = sems
    me, partner, across, down = neighbours()
    plane = lax.axis_index("tensor")
    planes = [lax.rem(plane + offset, 4) for offset in (1, 2, 3)]
    flip = lambda block: block + 1 - 2 * lax.rem(block, 2)
    blocks = (me, across, down, across + down - me)
    order = (3, 1, 2, 0)

    def view(part, block):
        ref, first, rows = grads[part]
        return ref.at[:, pl.ds(first, rows), lanes(block)]

    def slot(part, index):
        return staging.at[index, :, pl.ds(0, grads[part][2])]

    def stage_core(part):
        for index in order:
            send_to(view(part, flip(blocks[index])), held[part].at[index], send_c.at[part, index], recv_c.at[part, index], (partner, plane))

    def load(part):
        for index in order:
            pltpu.make_async_copy(view(part, blocks[index]), slot(part, index), load_sem.at[part, index]).start()

    def stage_first(part):
        rows = grads[part][2]
        load(part)
        for index in order:
            wait_for(slot(part, index), load_sem.at[part, index])
            wait_for(held[part].at[index], recv_c.at[part, index])
            add_into(held[part].at[index], slot(part, index), rows, step_of(rows))
            if index % 2 == 1:
                send_to(held[part].at[index, 0:2], from_x[part].at[index // 2], send_x.at[part, index // 2], recv_x.at[part, index // 2], (across, plane))
            if index // 2 == 1:
                send_to(held[part].at[index, 2:4], from_y[part].at[index % 2], send_y.at[part, index % 2], recv_y.at[part, index % 2], (down, plane))

    def stage_second(part):
        rows = grads[part][2]
        for side in (1, 0):
            wait_for(from_x[part].at[side], recv_x.at[part, side])
            add_into(held[part].at[2 * side, 0:2], from_x[part].at[side], rows, step_of(rows))
            if side == 1:
                send_to(held[part].at[2, 0:2], from_yx[part], send_yx.at[part], recv_yx.at[part], (down, plane))
            wait_for(from_y[part].at[side], recv_y.at[part, side])
            add_into(held[part].at[side, 2:4], from_y[part].at[side], rows, step_of(rows))
            if side == 1:
                send_to(held[part].at[1, 2:4], from_xy[part], send_xy.at[part], recv_xy.at[part], (across, plane))

    def stage_third(part):
        rows = grads[part][2]
        wait_for(from_yx[part], recv_yx.at[part])
        add_into(held[part].at[0, 0:2], from_yx[part], rows, step_of(rows))
        wait_for(from_xy[part], recv_xy.at[part])
        add_into(held[part].at[0, 2:4], from_xy[part], rows, step_of(rows))
        for index, other in enumerate(planes):
            send_to(held[part].at[0, other], from_z[part].at[index], send_z.at[part, index], recv_z.at[part, index], (me, other))

    def stage_last(part):
        rows = grads[part][2]
        step = step_of(rows)
        target, first = sums[part]
        for index in range(3):
            wait_for(from_z[part].at[index], recv_z.at[part, index])

        @pl.loop(0, rows // step)
        def _(index):
            offset = pl.multiple_of(index * step, step)
            window = pl.ds(offset, step)
            total = held[part][0, plane, window].astype(jnp.float32)
            for other in range(3):
                total = total + from_z[part][other, window].astype(jnp.float32)
            target[pl.ds(pl.multiple_of(first + offset, 16), step)] = total

    def finish(part):
        for index in range(4):
            wait_for(held[part].at[index], send_c.at[part, index])
        for side in range(2):
            wait_for(from_x[part].at[side], send_x.at[part, side])
            wait_for(from_y[part].at[side], send_y.at[part, side])
        wait_for(from_yx[part], send_yx.at[part])
        wait_for(from_xy[part], send_xy.at[part])
        for index in range(3):
            wait_for(from_z[part].at[index], send_z.at[part, index])

    return ((stage_core, stage_first, stage_second, stage_third, stage_last), finish)


def scatter_scratch(heights):
    sem = pltpu.SemaphoreType.DMA
    count = len(heights)
    leads = ((4, 4), (2, 2), (2, 2), (2,), (2,), (3,))
    buffers = [pltpu.VMEM(lead + (rows, 128), jnp.bfloat16) for lead in leads for rows in heights]
    buffers.append(pltpu.VMEM((4, 4, max(heights), 128), jnp.bfloat16))
    sems = [sem((count, 4))] * 3 + [sem((count, 2))] * 4 + [sem((count,))] * 4 + [sem((count, 3))] * 2
    return (buffers, sems)


def take(refs, count):
    taken, refs[:] = refs[:count], refs[count:]
    return taken


def gather_plan(shards, wholes, sems):
    own_sem, send_up, send_down, recv_z, send_x, recv_x, send_y, recv_y, send_d, recv_d, send_c, recv_c = sems
    me, partner, across, down = neighbours()
    plane = lax.axis_index("tensor")
    diagonal = across + down - me
    flip = lambda block: block + 1 - 2 * lax.rem(block, 2)

    def place(part, slot, block):
        return wholes[part].at[slot, :, lanes(block)]

    def spread(part, source, slot):
        view = place(part, slot, me)
        send_to(source, view, send_x.at[part, slot], recv_x.at[part, slot], (across, plane))
        send_to(source, view, send_y.at[part, slot], recv_y.at[part, slot], (down, plane))
        send_to(source, view, send_c.at[part, slot, 0], recv_c.at[part, slot, 0], (partner, plane))

    def pass_on(part, source, slot, upward):
        view = place(part, slot, me)
        sem = (send_up if upward else send_down).at[part, slot]
        send_to(source, view, sem, recv_z.at[part, slot], (me, plane + 1 if upward else plane - 1))

    def stage_own(part):
        pltpu.make_async_copy(shards[part], place(part, plane, me), own_sem.at[part]).start()

        @pl.when(plane < 3)
        def _():
            pass_on(part, shards[part], plane, True)

        @pl.when(plane > 0)
        def _():
            pass_on(part, shards[part], plane, False)

        spread(part, shards[part], plane)

    def stage_z(part):
        for distance in (1, 2, 3):
            for upward in (True, False):
                slot = plane - distance if upward else plane + distance

                @pl.when(slot >= 0 if upward else slot <= 3)
                def _():
                    view = place(part, slot, me)
                    wait_for(view, recv_z.at[part, slot])

                    @pl.when(plane < 3 if upward else plane > 0)
                    def _():
                        pass_on(part, view, slot, upward)

                    spread(part, view, slot)

    def stage_xy(part):
        for slot in range(4):
            view = place(part, slot, across)
            wait_for(view, recv_x.at[part, slot])
            if slot < 2:
                send_to(view, view, send_d.at[part, slot], recv_d.at[part, slot], (down, plane))
            send_to(view, view, send_c.at[part, slot, 1], recv_c.at[part, slot, 1], (partner, plane))
            view = place(part, slot, down)
            wait_for(view, recv_y.at[part, slot])
            if slot >= 2:
                send_to(view, view, send_d.at[part, slot], recv_d.at[part, slot], (across, plane))
            send_to(view, view, send_c.at[part, slot, 2], recv_c.at[part, slot, 2], (partner, plane))

    def stage_diagonal(part):
        for slot in range(4):
            view = place(part, slot, diagonal)
            wait_for(view, recv_d.at[part, slot])
            send_to(view, view, send_c.at[part, slot, 3], recv_c.at[part, slot, 3], (partner, plane))

    def arrive(part):
        wait_for(shards[part], own_sem.at[part])
        for slot in range(4):
            for index, block in enumerate((me, across, down, diagonal)):
                wait_for(place(part, slot, flip(block)), recv_c.at[part, slot, index])

    def finish(part):
        for slot in range(4):
            @pl.when(jnp.logical_and(slot <= plane, plane < 3))
            def _():
                wait_for(shards[part], send_up.at[part, slot])

            @pl.when(jnp.logical_and(slot >= plane, plane > 0))
            def _():
                wait_for(shards[part], send_down.at[part, slot])

            for sem in (send_x, send_y, send_d):
                wait_for(shards[part], sem.at[part, slot])
            for index in range(4):
                wait_for(shards[part], send_c.at[part, slot, index])

    return (stage_own, stage_z, stage_xy, stage_diagonal, arrive, finish)


def normed_rows(rows, gain):
    centre = rows - jnp.mean(rows, axis=1, keepdims=True)
    inverse = lax.rsqrt(jnp.mean(centre * centre, axis=1, keepdims=True) + NORM_EPS)
    return centre * inverse * gain


def forward_kernel(*refs):
    refs = list(refs)
    shards, (inputs, cotangent, lengths, gains, frequency) = take(refs, 6), take(refs, 5)
    wholes, (rows_low, grad_rows) = take(refs, 6), take(refs, 2)
    low_one, queries, own, other, context, log_total, bias, middle, low_two = take(refs, 9)
    cosine, sine = take(refs, 2)
    other_lengths, weight, attn_weight = take(refs, 3)
    sems = take(refs, 12)
    pair_send, pair_recv, length_send, length_recv, weight_sem, attn_sem = take(refs, 6)
    move_send, move_recv, move_own = refs
    me, partner, across, down = neighbours()
    plane = lax.axis_index("tensor")
    core = lax.rem(me, 2)
    stage_own, stage_z, stage_xy, stage_diagonal, arrive, finish = gather_plan(shards, wholes, sems)
    moves = [
        move_plan(False, source, target, move_send.at[index], move_recv.at[index], move_own.at[index])
        for index, (source, target) in enumerate(((inputs, rows_low), (cotangent, grad_rows)))
    ]
    greet(plane, (partner, across, down), [lax.rem(plane + offset, 4) for offset in (1, 2, 3)])
    count, width = rows_low.shape
    third = shards[0].shape[0]
    step = 64

    stage_own(0)
    stage_own(1)
    send_to(lengths, other_lengths, length_send, length_recv, (partner, plane))
    stage_z(0)
    stage_own(2)
    stage_z(1)
    stage_xy(0)
    stage_own(3)
    stage_z(2)
    stage_xy(1)
    stage_diagonal(0)
    stage_own(4)
    stage_z(3)
    stage_xy(2)
    stage_diagonal(1)
    stage_own(5)
    stage_z(4)
    moves[0][0]()
    stage_xy(3)
    stage_diagonal(2)
    stage_z(5)
    moves[1][0]()
    stage_diagonal(3)
    stage_xy(4)
    wait_for(other_lengths, length_recv)
    mine = core == lax.rem(plane, 2)
    both = jnp.where(mine, lengths[...], other_lengths[...])
    length = jnp.where(plane < 2, both[0:1], both[1:2])
    position = lax.broadcasted_iota(jnp.int32, bias.shape, 0)
    position = lax.rem(position + core * count, 2 * count).astype(jnp.float32)
    bias[...] = jnp.where(position < length, 0.0, MASK_VALUE)

    @pl.loop(0, bias.shape[0] // 128)
    def _(index):
        first = pl.multiple_of(index * 128, 128)
        place = lax.broadcasted_iota(jnp.int32, (128, 128), 0) + first + core * count
        angles = lax.rem(place, 2 * count).astype(jnp.float32) * frequency[0:1]
        half_lane = lax.rem(lane_of((128, 128)), HEAD_DIM) < HEAD_DIM // 2
        cosine[pl.ds(first, 128)] = jnp.cos(angles)
        turned_sine = jnp.sin(angles)
        sine[pl.ds(first, 128)] = jnp.where(half_lane, -turned_sine, turned_sine)

    moves[0][1]()

    @pl.loop(0, count // step)
    def _(index):
        window = pl.ds(pl.multiple_of(index * step, step), step)
        low_one[window] = low(normed_rows(rows_low[window].astype(jnp.float32), gains[0:1]))

    for part in range(3):
        arrive(part)

    def load(group):
        for part in range(3):
            slot = lax.rem(group, 2)
            pltpu.make_async_copy(wholes[part].at[group], weight.at[slot, part], weight_sem.at[slot, part]).start()

    load(0)

    @pl.loop(0, 4)
    def _(group):
        @pl.when(group < 3)
        def _():
            load(group + 1)

        slot = lax.rem(group, 2)
        for part in range(3):
            wait_for(weight.at[slot, part], weight_sem.at[slot, part])
            result = product_of(low_one[...], weight[slot, part], ((1,), (1,)))
            for first in range(0, third, 128):
                columns = pl.ds(pl.multiple_of(group * third + first, 128), 128)
                piece = result[:, first : first + 128]
                if part < 2:
                    piece = turned(piece, cosine[0:count], sine[0:count])
                if part == 0:
                    queries[:, columns] = low(piece * SCORE_SCALE)
                else:
                    own[part - 1, :, columns] = low(piece)

    send_to(own, other, pair_send, pair_recv, (partner, plane))
    wait_for(other, pair_recv)
    arrive(3)
    attn_copy = pltpu.make_async_copy(wholes[3], attn_weight, attn_sem)
    attn_copy.start()
    schedule = {3: (stage_xy, 5), 6: (stage_diagonal, 4)}

    @pl.loop(0, width // 128)
    def _(index):
        for place, (stage, part) in schedule.items():
            @pl.when(index == place)
            def _():
                stage(part)

        attend_pair(lanes(index), queries, own, other, bias, context, log_total.at[index])

    attn_copy.wait()

    @pl.loop(0, count // 128)
    def _(index):
        window = pl.ds(pl.multiple_of(index * 128, 128), 128)
        rows = rows_low[window].astype(jnp.float32)
        for group in range(4):
            piece = context[window, third * group : third * group + third]
            rows = rows + product_of(piece, attn_weight[group], ((1,), (0,)))
        middle[window] = rows
        low_two[window] = low(normed_rows(rows, gains[1:2]))

    stage_diagonal(5)
    for part in (4, 5):
        arrive(part)
    for part in range(6):
        finish(part)
    wait_for(own, pair_send)
    wait_for(lengths, length_send)
    moves[1][1]()


def forward(shards, inputs, cotangent, lengths, gains, frequency, collective_id):
    sem = pltpu.SemaphoreType.DMA
    anywhere = pl.BlockSpec(memory_space=pl.ANY)
    local = pl.BlockSpec(memory_space=pltpu.VMEM)
    bf16, f32 = jnp.bfloat16, jnp.float32
    count, width = 2 * inputs.shape[1], inputs.shape[2]
    third = shards[0].shape[0]
    shape = jax.ShapeDtypeStruct
    return pl.pallas_call(
        forward_kernel,
        out_shape=[shape((4, shard.shape[0], width), bf16) for shard in shards]
        + [
            shape((count, width), bf16),
            shape((count, width), bf16),
            shape((count, width), bf16),
            shape((count, width), bf16),
            shape((2, count, width), bf16),
            shape((2, count, width), bf16),
            shape((count, width), bf16),
            shape((width // 128, 8, count), f32),
            shape((2 * count, 128), f32),
            shape((count, width), f32),
            shape((count, width), bf16),
            shape((2 * count, 128), f32),
            shape((2 * count, 128), f32),
        ],
        in_specs=[anywhere] * 8 + [local] * 3,
        out_specs=[anywhere] * 6 + [local, anywhere] + [local] * 11,
        scratch_shapes=[
            pltpu.VMEM(lengths.shape, f32),
            pltpu.VMEM((2, 3, third, width), bf16),
            pltpu.VMEM((4, third, width), bf16),
            sem((6,)),
        ]
        + [sem((6, 4))] * 9
        + [sem((6, 4, 4))] * 2
        + [sem, sem, sem, sem, sem((2, 3)), sem]
        + [sem((2, 2)), sem((2, 2)), sem((2,))],
        compiler_params=pltpu.CompilerParams(
            collective_id=collective_id, has_side_effects=True, vmem_limit_bytes=58 * 1024 * 1024
        ),
        name="forward",
    )(*shards, inputs, cotangent, lengths, gains, frequency)


def attend_pair(columns, queries, own, other, bias, context, log_total):
    query_turned = queries[:, columns].T
    keys = jnp.concatenate([own[0, :, columns], other[0, :, columns]], axis=0)
    value_turned = jnp.concatenate([own[1, :, columns].T, other[1, :, columns].T], axis=1)
    parts, logs = [], []
    for head in range(2):
        scores = scores_of(keys, head_rows(query_turned, head), bias[...])
        highest = jnp.max(scores, axis=0, keepdims=True)
        weights = jnp.exp(scores - highest)
        total = jnp.sum(weights, axis=0, keepdims=True)
        part = product_of(value_turned[64 * head : 64 * head + 64], low(weights), ((1,), (0,)))
        parts.append(part / total)
        logs.append(highest + jnp.log(total))
    context[:, columns] = low(jnp.concatenate(parts, axis=0)).T
    log_total[...] = jnp.concatenate(logs + logs * 3, axis=0)


def add_rows(target, source, extent):
    step = step_of(extent)

    @pl.loop(0, extent // step)
    def _(index):
        window = pl.ds(pl.multiple_of(index * step, step), step)
        target[window] = low(target[window].astype(jnp.float32) + source[window].astype(jnp.float32))


def slot_of(part):
    return (4 - part) % 4


def slot_plan(grads, sums, buffers, sems):
    held, from_x, from_y, from_yx, from_xy = buffers[:5]
    from_z, staging = buffers[5][0], buffers[6][0]
    (load_sem, send_c, recv_c, send_x, recv_x, send_y, recv_y, send_yx, recv_yx, send_xy, recv_xy, send_z, recv_z) = sems
    me, partner, across, down = neighbours()
    plane = lax.axis_index("tensor")
    flip = lambda block: block + 1 - 2 * lax.rem(block, 2)
    blocks = (me, across, down, across + down - me)
    order = (3, 1, 2, 0)
    rows, early = grads.shape[1], from_x[0].shape[1]
    late = rows - early
    one, two = pl.ds(0, early), pl.ds(early, late)

    def stage_core(part):
        for index in order:
            send_to(grads.at[slot_of(part), :, lanes(flip(blocks[index]))], held[part].at[index], send_c.at[part, index], recv_c.at[part, index], (partner, plane))

    def stage_first(part):
        for index in order:
            pltpu.make_async_copy(grads.at[slot_of(part), :, lanes(blocks[index])], staging.at[index], load_sem.at[part, index]).start()
        for index in order:
            wait_for(staging.at[index], load_sem.at[part, index])
            wait_for(held[part].at[index], recv_c.at[part, index])
            add_rows(held[part].at[index], staging.at[index], rows)
            if index % 2 == 1:
                send_to(held[part].at[index, one], from_x[part].at[index // 2], send_x.at[part, index // 2], recv_x.at[part, index // 2], (across, plane))
            if index // 2 == 1:
                send_to(held[part].at[index, two], from_y[part].at[index % 2], send_y.at[part, index % 2], recv_y.at[part, index % 2], (down, plane))

    def stage_second(part):
        for side in (1, 0):
            wait_for(from_x[part].at[side], recv_x.at[part, side])
            add_rows(held[part].at[2 * side, one], from_x[part].at[side], early)
            if side == 1:
                send_to(held[part].at[2, one], from_yx[part], send_yx.at[part], recv_yx.at[part], (down, plane))
            wait_for(from_y[part].at[side], recv_y.at[part, side])
            add_rows(held[part].at[side, two], from_y[part].at[side], late)
            if side == 1:
                send_to(held[part].at[1, two], from_xy[part], send_xy.at[part], recv_xy.at[part], (across, plane))

    def stage_third(part):
        wait_for(from_yx[part], recv_yx.at[part])
        add_rows(held[part].at[0, one], from_yx[part], early)
        wait_for(from_xy[part], recv_xy.at[part])
        add_rows(held[part].at[0, two], from_xy[part], late)

        @pl.when(plane != slot_of(part))
        def _():
            offset = lax.rem(plane + 3 - slot_of(part), 4)
            send_to(held[part].at[0], from_z.at[offset], send_z.at[part], recv_z.at[offset], (me, slot_of(part)))

    def stage_last(part):
        @pl.when(plane == slot_of(part))
        def _():
            for offset in range(3):
                wait_for(from_z.at[offset], recv_z.at[offset])
            for target, first, extent in sums:
                step = step_of(extent)

                @pl.loop(0, extent // step)
                def _(index):
                    offset = pl.multiple_of(index * step, step)
                    window = pl.ds(pl.multiple_of(first + offset, 16), step)
                    total = held[part][0, window].astype(jnp.float32)
                    for other in range(3):
                        total = total + from_z[other, window].astype(jnp.float32)
                    target[pl.ds(offset, step)] = total

    def finish(part):
        for index in range(4):
            wait_for(held[part].at[index], send_c.at[part, index])
        for side in range(2):
            wait_for(from_x[part].at[side], send_x.at[part, side])
            wait_for(from_y[part].at[side], send_y.at[part, side])
        wait_for(from_yx[part], send_yx.at[part])
        wait_for(from_xy[part], send_xy.at[part])

        @pl.when(plane != slot_of(part))
        def _():
            wait_for(from_z.at[0], send_z.at[part])

    return ((stage_core, stage_first, stage_second, stage_third, stage_last), finish)


def slot_scratch(rows, early):
    sem = pltpu.SemaphoreType.DMA
    late = rows - early
    shapes = [(4, rows)] * 4 + [(2, early)] * 4 + [(2, late)] * 4 + [(early,)] * 4 + [(late,)] * 4
    shapes += [(3, rows), (4, rows)]
    buffers = [pltpu.VMEM(shape + (128,), jnp.bfloat16) for shape in shapes]
    sems = [sem((4, 4))] * 3 + [sem((4, 2))] * 4 + [sem((4,))] * 4 + [sem((4,)), sem((3,))]
    return (buffers, sems)


def backward_kernel(*refs):
    refs = list(refs)
    f32, bf16 = jnp.float32, jnp.bfloat16
    in_weight, out_weight, attn_weight, far_two, far_cot, far_middle = take(refs, 6)
    far_query, far_own, far_other, far_context, far_one = take(refs, 5)
    bias, log_total, cosine, sine, gains = take(refs, 5)
    sums, (far_grad_query, far_pair, rows_out, far_grad_middle, gain_two) = take(refs, 4), take(refs, 5)
    grad_feed, weight_grads = take(refs, 1)[0], take(refs, 4)
    branch, cotangent, low_rows, queries, own, other, grad, context = take(refs, 8)
    grad_query, grad_pair, grad_other, arrived, staged = take(refs, 5)
    result, grad_rows, middle = take(refs, 3)
    slot_buffers = [take(refs, 4) for _ in range(5)] + [take(refs, 1), take(refs, 1)]
    slot_sems = take(refs, 13)
    buffers = [take(refs, 4) for _ in range(6)] + [take(refs, 1)]
    sems = take(refs, 13)
    pair_send, pair_recv, stage_sem, load_sem, out_sem, weight_sem, feed_sem, middle_sem = take(refs, 8)
    move_send, move_recv, move_own = refs
    me, partner, across, down = neighbours()
    plane = lax.axis_index("tensor")
    height, third = out_weight.shape[1], attn_weight.shape[1]
    count, width = cotangent.shape
    sum_qkv, sum_attn, sum_in, sum_out = sums
    feed_sums = [(sum_in, 0, 2 * height), (sum_out, 2 * height, height)]
    feed_stages, feed_finish = slot_plan(grad_feed, feed_sums, slot_buffers, slot_sems)
    parts = [(ref, 0, third) for ref in weight_grads]
    targets = [(sum_attn, 0)] + [(sum_qkv, third * index) for index in range(3)]
    stages, finish = scatter_plan(parts, targets, buffers, sems)
    start_move, finish_move = move_plan(True, cotangent, rows_out, move_send, move_recv, move_own)

    def call(stage, part):
        if part < 4:
            feed_stages[stage](part)
        else:
            stages[stage](part - 4)

    pieces = ((0, 336), (336, height - 336))
    weight_slots = (
        (own.at[0], own.at[1], grad_pair.at[0]),
        (other.at[0], other.at[1], grad_pair.at[1]),
    )
    grad_slots = ((grad_other.at[0], grad_other.at[1], grad_query), (queries, context, grad))

    def weight_copies(group, piece):
        first, extent = pieces[piece]
        sources = ((in_weight, first), (in_weight, height + first), (out_weight, first))
        return [
            pltpu.make_async_copy(source.at[lax.rem(4 - group, 4), pl.ds(offset, extent)], target.at[pl.ds(0, extent)], weight_sem.at[piece, index])
            for index, ((source, offset), target) in enumerate(zip(sources, weight_slots[piece]))
        ]

    def grad_copies(group, piece):
        first, extent = pieces[piece]
        return [
            pltpu.make_async_copy(source.at[pl.ds(0, extent)], grad_feed.at[lax.rem(4 - group, 4), pl.ds(index * height + first, extent)], feed_sem.at[piece, index])
            for index, source in enumerate(grad_slots[piece])
        ]

    def start_all(copies):
        for copy in copies:
            copy.start()

    def wait_all(copies):
        for copy in copies:
            copy.wait()

    first_loads = [
        pltpu.make_async_copy(far_two, branch, load_sem.at[0]),
        pltpu.make_async_copy(far_cot, cotangent, load_sem.at[1]),
    ]
    start_all(first_loads)
    start_all(weight_copies(0, 0))
    start_all(weight_copies(0, 1))
    greet(plane, (partner, across, down), [lax.rem(plane + offset, 4) for offset in (1, 2, 3)])
    result[...] = jnp.zeros_like(result)
    grad_rows[...] = jnp.zeros_like(grad_rows)
    wait_all(first_loads)
    feed_calls = {(1, 1): ((1, 0),), (2, 1): ((1, 1),), (3, 0): ((2, 0),), (3, 1): ((1, 2),)}

    @pl.loop(0, 4)
    def _(group):
        @pl.when(group > 0)
        def _():
            for piece in range(2):
                wait_all(grad_copies(group - 1, piece))
            for part in range(3):
                @pl.when(group == part + 1)
                def _():
                    call(0, part)

        for piece, (_, extent) in enumerate(pieces):
            for (when, place), calls in feed_calls.items():
                if place == piece:
                    @pl.when(group == when)
                    def _():
                        for stage, part in calls:
                            call(stage, part)

            window = pl.ds(0, extent)
            wait_all(weight_copies(group, piece))
            gate_weight, up_weight, down_weight = (ref[window] for ref in weight_slots[piece])
            gate = product_of(gate_weight, branch[...], ((1,), (1,)))
            up = product_of(up_weight, branch[...], ((1,), (1,)))
            grad_hidden = product_of(down_weight, cotangent[...], ((1,), (1,)))
            below = 0.5 + 0.5 * lax.erf(gate * math.sqrt(0.5))
            active = gate * below
            hidden = low(active * up)
            slope = below + gate * jnp.exp(-0.5 * gate * gate) * (1.0 / math.sqrt(2.0 * math.pi))
            grad_gate = low(grad_hidden * up * slope)
            grad_up = low(grad_hidden * active)
            grad_slots[piece][2][window] = low(product_of(hidden, cotangent[...], ((1,), (0,))))
            grad_slots[piece][0][window] = low(product_of(grad_gate, branch[...], ((1,), (0,))))
            grad_slots[piece][1][window] = low(product_of(grad_up, branch[...], ((1,), (0,))))
            start_all(grad_copies(group, piece))
            result[...] += product_of(hidden, down_weight, ((0,), (0,)))
            grad_rows[...] += product_of(grad_gate, gate_weight, ((0,), (0,)))
            grad_rows[...] += product_of(grad_up, up_weight, ((0,), (0,)))

            @pl.when(group < 3)
            def _():
                start_all(weight_copies(group + 1, piece))

    step = 64

    def middle_copy(index):
        window = pl.ds(pl.multiple_of(index * step, step), step)
        slot = lax.rem(index, 2)
        return pltpu.make_async_copy(far_middle.at[window], middle.at[slot], middle_sem.at[slot])

    middle_copy(0).start()
    for piece in range(2):
        wait_all(grad_copies(3, piece))
    call(0, 3)
    near = (queries, own, other, context, low_rows)
    loads = [
        pltpu.make_async_copy(source, target, load_sem.at[index])
        for index, (source, target) in enumerate(zip((far_query, far_own, far_other, far_context, far_one), near))
    ]
    start_all(loads)
    attn_loads = [
        pltpu.make_async_copy(
            attn_weight.at[group], grad_other.at[group // 2, pl.ds(group % 2 * third, third)], weight_sem.at[group // 2, group % 2]
        )
        for group in range(4)
    ]
    start_all(attn_loads)
    gain_two[...] = jnp.zeros_like(gain_two)

    @pl.loop(0, count // step)
    def _(index):
        @pl.when(index < count // step - 1)
        def _():
            middle_copy(index + 1).start()

        middle_copy(index).wait()
        window = pl.ds(pl.multiple_of(index * step, step), step)
        rows = middle[lax.rem(index, 2)]
        centre = rows - jnp.mean(rows, axis=1, keepdims=True)
        inverse = lax.rsqrt(jnp.mean(centre * centre, axis=1, keepdims=True) + NORM_EPS)
        normed = centre * inverse
        scaled = grad_rows[window] * gains[1:2]
        mean_grad = jnp.mean(scaled, axis=1, keepdims=True)
        mean_cross = jnp.mean(scaled * normed, axis=1, keepdims=True)
        gain_two[...] += jnp.sum(grad_rows[window] * normed, axis=0, keepdims=True)
        total = cotangent[window].astype(f32) + inverse * (scaled - mean_grad - normed * mean_cross)
        grad_rows[window] = total
        branch[window] = low(total)
        cotangent[window] = low(rows + result[window])

    call(3, 0)
    call(2, 1)
    start_move()
    middle_out = pltpu.make_async_copy(grad_rows, far_grad_middle, out_sem.at[2])
    middle_out.start()
    wait_all(attn_loads)

    @pl.loop(0, count // 128)
    def _(index):
        window = pl.ds(pl.multiple_of(index * 128, 128), 128)
        for part in range(2):
            columns = slice(part * count, part * count + count)
            grad[window, columns] = low(product_of(branch[window], grad_other[part], ((1,), (1,))))

    wait_all(loads)

    def weight_grad(which, values, rows):
        target = weight_grads[which]
        for group in range(4):
            slot = staged.at[group % 2]
            if group >= 2:
                wait_for(slot, stage_sem.at[group % 2])
            block = values[:, third * group : third * group + third]
            slot[...] = low(product_of(block, rows[...], ((0,), (0,))))
            pltpu.make_async_copy(slot, target.at[group], stage_sem.at[group % 2]).start()
        for group in range(2):
            wait_for(staged.at[group], stage_sem.at[group])

    weight_grad(0, context, branch)
    call(0, 4)

    def exchanged(index):
        return (arrived.at[:, :, lanes(index)], pair_recv.at[index])

    def add_pair(index):
        wait_for(*exchanged(index))
        columns = lanes(index)
        for which in range(2):
            total = grad_pair[which, :, columns].astype(f32)
            total = total + arrived[which, :, columns].astype(f32)
            grad_pair[which, :, columns] = low(total)

    last_pair = width // 128 - 1
    schedule = {0: ((1, 3),), 2: ((3, 1), (2, 2)), 5: ((3, 2), (1, 4)), 7: ((2, 3),)}

    @pl.loop(0, last_pair + 1)
    def _(index):
        for position, calls in schedule.items():
            @pl.when(index == position)
            def _():
                for stage, part in calls:
                    call(stage, part)

        attend_back_pair(lanes(index), queries, own, other, bias, grad, context, log_total.at[index], cosine, sine, grad_query, grad_pair, grad_other)
        target, sem = exchanged(index)
        send_to(grad_other.at[:, :, lanes(index)], target, pair_send.at[index], sem, (partner, plane))

        @pl.when(index > 0)
        def _():
            add_pair(index - 1)

    query_copy = pltpu.make_async_copy(grad_query, far_grad_query, out_sem.at[0])
    query_copy.start()
    weight_grad(1, grad_query, low_rows)
    call(0, 5)
    add_pair(last_pair)
    pair_copy = pltpu.make_async_copy(grad_pair, far_pair, out_sem.at[1])
    pair_copy.start()
    weight_grad(2, grad_pair.at[0], low_rows)
    call(0, 6)
    weight_grad(3, grad_pair.at[1], low_rows)
    call(0, 7)
    done = {(1, 4), (3, 2), (2, 3), (1, 0), (2, 0), (1, 1), (3, 0), (2, 1), (1, 2), (3, 1), (2, 2), (1, 3)}
    for turn_of in range(10):
        for stage in (3, 2, 1):
            part = turn_of - (stage - 1)
            if 0 <= part < 8 and (stage, part) not in done:
                call(stage, part)
    for part in range(8):
        call(4, part)
    for part in range(4):
        feed_finish(part)
        finish(part)
    for index in range(last_pair + 1):
        wait_for(arrived.at[:, :, lanes(index)], pair_send.at[index])
    query_copy.wait()
    pair_copy.wait()
    middle_out.wait()
    finish_move()


def backward(wholes, low_two, cotangent, middle, queries, own, other, context, low_one, bias, log_total, cosine, sine, gains, collective_id):
    attn_all, in_all, out_all = wholes
    height, third = out_all.shape[1], attn_all.shape[1]
    count, width = queries.shape
    early = 3 * height // 32 * 16 + 16
    slot_buffers, slot_sems = slot_scratch(3 * height, early)
    buffers, sems = scatter_scratch([third] * 4)
    sem = pltpu.SemaphoreType.DMA
    anywhere = pl.BlockSpec(memory_space=pl.ANY)
    local = pl.BlockSpec(memory_space=pltpu.VMEM)
    bf16, f32 = jnp.bfloat16, jnp.float32
    shape, vmem = jax.ShapeDtypeStruct, pltpu.VMEM
    outs = pl.pallas_call(
        backward_kernel,
        out_shape=[shape((rows, 128), f32) for rows in (3 * third, third, 2 * height, height)]
        + [
            shape((count, width), bf16),
            shape((2, count, width), bf16),
            shape((2, count // 2, width), bf16),
            shape((count, width), f32),
            shape((1, width), f32),
            shape((4, 3 * height, width), bf16),
        ]
        + [shape(attn_all.shape, bf16)] * 4,
        in_specs=[anywhere] * 11 + [local] * 5,
        out_specs=[local] * 4 + [anywhere] * 4 + [local] + [anywhere] * 5,
        scratch_shapes=[vmem((count, width), bf16)] * 4
        + [vmem((2, count, width), bf16)] * 2
        + [vmem((count, width), bf16)] * 3
        + [vmem((2, count, width), bf16)] * 3
        + [vmem((2, third, width), bf16)]
        + [vmem((count, width), f32)] * 2
        + [vmem((2, 64, width), f32)]
        + slot_buffers
        + slot_sems
        + buffers
        + sems
        + [sem((8,)), sem((8,)), sem((2,)), sem((5,)), sem((3,)), sem((2, 3)), sem((2, 3)), sem((2,))]
        + [sem((2,)), sem((2,)), sem],
        compiler_params=pltpu.CompilerParams(
            collective_id=collective_id, has_side_effects=True, vmem_limit_bytes=62 * 1024 * 1024
        ),
        name="backward",
    )(in_all, out_all, attn_all, low_two, cotangent, middle, queries, own, other, context, low_one, bias, log_total, cosine, sine, gains)
    return outs[:9]


def attend_back_pair(columns, queries, own, other, bias, grad, context, log_total, cosine, sine, grad_query, grad_own, grad_other):
    count = queries.shape[0]
    query_rows, grad_rows = queries[:, columns], grad[:, columns]
    query_turned, grad_turned = query_rows.T, grad_rows.T
    inner = (grad_rows.astype(jnp.float32) * context[:, columns].astype(jnp.float32)).T
    query_parts = [None, None]
    for half, (pair, result) in enumerate(((own, grad_own), (other, grad_other))):
        keys, values = pair[0, :, columns], pair[1, :, columns]
        key_turned = keys.T
        grad_keys, grad_values = None, None
        window = pl.ds(half * count, count)
        for head in range(2):
            lanes_of_head = slice(64 * head, 64 * head + 64)
            scores = scores_of(keys, head_rows(query_turned, head), bias[window])
            weights = jnp.exp(scores - log_total[head : head + 1])
            grad_weights = product_of(values, head_rows(grad_turned, head), ((1,), (0,)))
            inner_row = jnp.sum(inner[lanes_of_head], axis=0, keepdims=True)
            grad_scores = low(weights * (grad_weights - inner_row))
            value_part = product_of(low(weights), head_lanes(grad_rows, head), ((1,), (0,)))
            key_part = product_of(grad_scores, head_lanes(query_rows, head), ((1,), (0,)))
            query_part = product_of(key_turned[lanes_of_head], grad_scores, ((1,), (0,)))
            grad_values = value_part if head == 0 else grad_values + value_part
            grad_keys = key_part if head == 0 else grad_keys + key_part
            query_parts[head] = query_part if half == 0 else query_parts[head] + query_part
        result[0, :, columns] = turned(grad_keys, cosine[window], -sine[window]).astype(result.dtype)
        result[1, :, columns] = grad_values.astype(result.dtype)
    query_rows = jnp.concatenate(query_parts, axis=0).T * SCORE_SCALE
    own_rows = pl.ds(0, count)
    grad_query[:, columns] = low(turned(query_rows, cosine[own_rows], -sine[own_rows]))


def product_of(left, right, dims):
    return lax.dot_general(left, right, (dims, ((), ())), preferred_element_type=jnp.float32)

def tiles_of(like):
    if len(like.shape) == 2 and like.shape[1] == 128:
        return [(pl.ds(0, like.shape[0]), (slice(None), slice(None)), True)]
    width = like.shape[-1]
    tiles = []
    for part in range(like.shape[0] if len(like.shape) == 3 else 1):
        for first in range(0, width, 128):
            columns = slice(first, first + 128)
            place = (part, slice(None), columns) if len(like.shape) == 3 else (slice(None), columns)
            tiles.append((pl.ds(part * width + first, 128), place, False))
    return tiles


def optimize_kernel(heights, *refs):
    refs = list(refs)
    count, size, tile = len(heights), 1024, 256
    f32, bf16 = jnp.float32, jnp.bfloat16
    sums, moments = take(refs, count), take(refs, count)
    (gain_two, gains), far = take(refs, 2), take(refs, 7)
    far = far[:4] + [far[4].at[0], far[4].at[1]] + far[5:]
    backs, (gain_out, rows_out), blocks = take(refs, count), take(refs, 2), take(refs, count)
    whole, steps, gain_parts = take(refs, 3)
    iterate, poly, product, total = take(refs, 4)
    iterate_low, poly_low, other_low, total_low = take(refs, 4)
    value_rows, rows_in, rows_low = take(refs, 3)
    load_sem, own_sem, send_z, recv_z, send_x, recv_x, send_y, recv_y, send_d, recv_d, send_c, recv_c = take(refs, 12)
    send_g, recv_g, back_sem, send_b, recv_b, move_send, move_recv, move_own = refs
    me, partner, across, down = neighbours()
    plane = lax.axis_index("tensor")
    diagonal = across + down - me
    planes = [lax.rem(plane + offset, 4) for offset in (1, 2, 3)]
    flip = lambda block: block + 1 - 2 * lax.rem(block, 2)
    half = rows_low.shape[0]
    start_move, finish_move = move_plan(True, rows_low, rows_out, move_send, move_recv, move_own)
    near = (
        poly_low, other_low, total_low, iterate_low.at[0:half], iterate_low.at[half : 2 * half],
        value_rows, rows_in, poly.at[0:half],
    )
    loads = [
        pltpu.make_async_copy(source, target, load_sem.at[index])
        for index, (source, target) in enumerate(zip(far, near))
    ]
    for load in loads:
        load.start()

    def place(part, slot, block):
        height = heights[part]
        return whole.at[pl.ds(pl.multiple_of(slot * height, 16), height), lanes(block)]

    def spread(part, source, slot):
        view = place(part, slot, me)
        send_to(source, view, send_x.at[slot], recv_x.at[slot], (across, plane))
        send_to(source, view, send_y.at[slot], recv_y.at[slot], (down, plane))
        send_to(source, view, send_c.at[slot, 0], recv_c.at[slot, 0], (partner, plane))

    def on_plane(body):
        for part in range(count):
            @pl.when(plane == part)
            def _():
                body(part)

    def off_plane(body):
        for part in range(count):
            @pl.when(plane != part)
            def _():
                body(part)

    greet(plane, (partner, across, down), planes)
    for part in (2, 0, 3, 1):
        for rows, place_of, is_turned in tiles_of(moments[part]):
            moment = moments[part][place_of]
            moment = moment if is_turned else moment.T
            blocks[part][rows] = low(MOMENTUM * moment + sums[part][rows])

        @pl.when(plane != part)
        def _():
            offset = lax.rem(plane + 3 - part, 4)
            send_to(blocks[part], place(part, plane, me), send_z.at[part], recv_z.at[offset], (me, part))

        @pl.when(plane == part)
        def _():
            pltpu.make_async_copy(blocks[part], place(part, part, me), own_sem).start()
            spread(part, blocks[part], part)

    def pass_z(part):
        for distance in (1, 3, 2):
            slot = (part + distance) % 4
            view = place(part, slot, me)
            wait_for(view, recv_z.at[(slot + 3 - part) % 4])
            spread(part, view, slot)

    on_plane(pass_z)

    for load in loads:
        load.wait()
    gain_out[1:2] = gain_two[...]
    gain_out[0:1] = jnp.zeros((1, size), f32)

    @pl.loop(0, half // 64)
    def _(index):
        first = pl.multiple_of(index * 64, 64)
        window = pl.ds(first, 64)
        other_window = pl.ds(pl.multiple_of(first + half, 64), 64)
        grad = product_of(iterate_low[window], poly_low[...], ((1,), (0,)))
        grad = grad + product_of(iterate_low[other_window], other_low[...], ((1,), (0,)))
        grad = grad + product_of(value_rows[window], total_low[...], ((1,), (0,)))
        rows = rows_in[window].astype(f32)
        centre = rows - jnp.mean(rows, axis=1, keepdims=True)
        inverse = lax.rsqrt(jnp.mean(centre * centre, axis=1, keepdims=True) + NORM_EPS)
        normed = centre * inverse
        scaled = grad * gains[0:1]
        mean_grad = jnp.mean(scaled, axis=1, keepdims=True)
        mean_cross = jnp.mean(scaled * normed, axis=1, keepdims=True)
        back = inverse * (scaled - mean_grad - normed * mean_cross)
        rows_low[window] = low(poly[window] + back)
        gain_out[0:1] += jnp.sum(grad * normed, axis=0, keepdims=True)

    start_move()
    for index, other in enumerate(planes):
        send_to(gain_out, gain_parts.at[index], send_g.at[index], recv_g.at[index], (me, other))

    def pass_xy(part):
        for slot in range(4):
            view = place(part, slot, across)
            wait_for(view, recv_x.at[slot])
            if slot < 2:
                send_to(view, view, send_d.at[slot], recv_d.at[slot], (down, plane))
            send_to(view, view, send_c.at[slot, 1], recv_c.at[slot, 1], (partner, plane))
            view = place(part, slot, down)
            wait_for(view, recv_y.at[slot])
            if slot >= 2:
                send_to(view, view, send_d.at[slot], recv_d.at[slot], (across, plane))
            send_to(view, view, send_c.at[slot, 2], recv_c.at[slot, 2], (partner, plane))

    on_plane(pass_xy)

    def pass_diagonal(part):
        for slot in range(4):
            view = place(part, slot, diagonal)
            wait_for(view, recv_d.at[slot])
            send_to(view, view, send_c.at[slot, 3], recv_c.at[slot, 3], (partner, plane))
        for slot in range(4):
            for index, block in enumerate((me, across, down, diagonal)):
                wait_for(place(part, slot, flip(block)), recv_c.at[slot, index])
        wait_for(blocks[part], own_sem)

    on_plane(pass_diagonal)

    windows = [pl.ds(first, tile) for first in range(0, size, tile)]
    zero = jnp.zeros((1, 1), f32)
    blank = jnp.zeros((1, size), f32)
    corner = lax.broadcasted_iota(jnp.int32, (tile, tile), 0) == lax.broadcasted_iota(jnp.int32, (tile, tile), 1)

    def gram(part):
        rows = slice(0, 4 * heights[part])
        for group in range(2):
            edge = group * size // 2

            @pl.loop(0, 2)
            def _(index):
                window = pl.ds(pl.multiple_of(edge + index * tile, tile), tile)
                iterate[window, edge:] = product_of(whole[rows, window], whole[rows, edge:], ((0,), (0,)))

    on_plane(gram)

    def upper(window):
        return slice(window.start, size)

    def store(window, result, shift, full, low_copy):
        corner_block = result[:, :tile] - jnp.where(corner, shift, 0.0)
        result = jnp.concatenate([corner_block, result[:, tile:]], axis=1) if result.shape[1] > tile else corner_block
        full[window, upper(window)] = result
        result_low = low(result)
        low_copy[window, upper(window)] = result_low
        for first in range(tile, result.shape[1], tile):
            low_copy[pl.ds(window.start + first, tile), window] = result_low[:, first : first + tile].T
        return result

    def fold(left, right, window):
        sums_of = jnp.sum(left * right, axis=0, keepdims=True)
        weighted = jnp.concatenate([sums_of[:, :tile], 2.0 * sums_of[:, tile:]], axis=1) if sums_of.shape[1] > tile else sums_of
        return jnp.concatenate([blank[:, : window.start], weighted], axis=1) if window.start else weighted

    def finish(row):
        return jnp.sum(row, axis=1, keepdims=True) / size

    def multiply(left, right, window):
        return product_of(left[window], right[:, upper(window)], ((1,), (0,)))

    trace = zero
    for window in windows:
        block = jnp.where(corner, iterate[window, window], 0.0)
        trace = trace + jnp.sum(jnp.sum(block, axis=0, keepdims=True), axis=1, keepdims=True)
    factor = 1.0 / (jnp.sqrt(trace) + NORM_FLOOR)
    squared = factor * factor
    mean = trace * squared / size
    row = blank
    for window in windows:
        rest = store(window, iterate[window, upper(window)] * squared, mean, iterate, iterate_low)
        row = row + fold(rest, rest, window)
    square = finish(row)

    def polynomial(mean, square, with_total):
        linear = QUINTIC_THREE + 2.0 * QUINTIC_FIVE * mean
        shift = QUINTIC_FIVE * square
        poly_mean = QUINTIC_ONE + QUINTIC_THREE * mean + QUINTIC_FIVE * (mean * mean) + shift
        row, total_row = blank, blank
        for window in windows:
            mine = iterate[window, upper(window)]
            rest = linear * mine + QUINTIC_FIVE * multiply(iterate_low, iterate_low, window)
            rest = store(window, rest, shift, poly, poly_low)
            row = row + fold(rest, mine, window)
            if with_total:
                total_row = total_row + fold(rest, total[window, upper(window)], window)
        return (poly_mean, finish(row), finish(total_row))

    def grow_total(poly_mean, total_mean, cross):
        for window in windows:
            result = poly_mean * total[window, upper(window)] + total_mean * poly[window, upper(window)]
            result = result + multiply(poly_low, total_low, window)
            store(window, result, cross, total, other_low)
        total_low[...] = other_low[...]
        return poly_mean * total_mean + cross

    def advance(poly_mean, mean, cross):
        row = blank
        for window in windows:
            rest = poly[window, upper(window)]
            result = poly_mean * iterate[window, upper(window)] + mean * rest
            result = result + multiply(poly_low, iterate_low, window)
            result = store(window, result, cross, product, other_low)
            row = row + fold(result, rest, window)
        product_mean = poly_mean * mean + cross
        cross = finish(row)
        row = blank
        for window in windows:
            result = poly_mean * product[window, upper(window)] + product_mean * poly[window, upper(window)]
            result = result + multiply(poly_low, other_low, window)
            result = store(window, result, cross, iterate, iterate_low)
            row = row + fold(result, result, window)
        return (poly_mean * product_mean + cross, finish(row))

    total_mean, cross, _ = polynomial(mean, square, False)
    for window in windows:
        total[window, upper(window)] = poly[window, upper(window)]
    total_low[...] = poly_low[...]
    mean, square = advance(total_mean, mean, cross)

    def sweep(_, carry):
        mean, square, total_mean = carry
        poly_mean, cross, cross_total = polynomial(mean, square, True)
        total_mean = grow_total(poly_mean, total_mean, cross_total)
        return advance(poly_mean, mean, cross) + (total_mean,)

    mean, square, total_mean = lax.fori_loop(0, NS_ITERS - 2, sweep, (mean, square, total_mean))
    poly_mean, _, cross_total = polynomial(mean, square, True)
    total_mean = grow_total(poly_mean, total_mean, cross_total)

    mine = lanes(me)
    columns = total_low[:, mine]

    def step_home(part):
        height = heights[part]

        @pl.loop(0, 4)
        def _(turn_of):
            slot = lax.rem(part + 1 + turn_of, 4)
            window = pl.ds(pl.multiple_of(slot * height, 16), height)
            result = product_of(whole[window, :], columns, ((1,), (0,)))
            result = result + total_mean * whole[window, mine].astype(f32)
            steps[window, :] = low(factor * result)

            @pl.when(turn_of == 3)
            def _():
                pltpu.make_async_copy(steps.at[window, :], backs[part], back_sem).start()

            @pl.when(turn_of < 3)
            def _():
                send_to(steps.at[window, :], backs[part], send_b.at[turn_of], recv_b.at[part], (me, slot))

    on_plane(step_home)

    for index in range(3):
        wait_for(gain_out, send_g.at[index])
        wait_for(gain_parts.at[index], recv_g.at[index])
    gain_out[...] = gain_out[...] + gain_parts[0] + gain_parts[1] + gain_parts[2]
    for index, other in ((3, across), (4, down), (5, partner)):
        send_to(gain_out, gain_parts.at[index], send_g.at[index], recv_g.at[index], (other, plane))
        wait_for(gain_out, send_g.at[index])
        wait_for(gain_parts.at[index], recv_g.at[index])
        gain_out[...] = gain_out[...] + gain_parts[index]

    on_plane(lambda part: wait_for(backs[part], back_sem))
    off_plane(lambda part: wait_for(backs[part], recv_b.at[part]))
    def last_waits(part):
        for slot in range(4):
            for sem in (send_x.at[slot], send_y.at[slot], send_d.at[slot]):
                wait_for(blocks[part], sem)
            for index in range(4):
                wait_for(blocks[part], send_c.at[slot, index])
        for index in range(3):
            wait_for(blocks[part], send_b.at[index])

    on_plane(last_waits)
    off_plane(lambda part: wait_for(blocks[part], send_z.at[part]))
    finish_move()


def optimize(sums, moments, gain_two, gains, far, collective_id):
    heights = [part.shape[0] for part in sums]
    count, size = len(heights), gains.shape[1]
    f32, bf16 = jnp.float32, jnp.bfloat16
    sem = pltpu.SemaphoreType.DMA
    anywhere = pl.BlockSpec(memory_space=pl.ANY)
    local = pl.BlockSpec(memory_space=pltpu.VMEM)
    half = far[5].shape[0]
    outs = pl.pallas_call(
        functools.partial(optimize_kernel, heights),
        out_shape=[jax.ShapeDtypeStruct((height, 128), bf16) for height in heights]
        + [jax.ShapeDtypeStruct(gains.shape, f32), jax.ShapeDtypeStruct((2, half // 2, size), bf16)],
        in_specs=[local] * (2 * count + 2) + [anywhere] * 7,
        out_specs=[local] * (count + 1) + [anywhere],
        scratch_shapes=[pltpu.VMEM((height, 128), bf16) for height in heights]
        + [pltpu.VMEM((4 * max(heights), size), bf16), pltpu.VMEM((4 * max(heights), 128), bf16)]
        + [pltpu.VMEM((6,) + gains.shape, f32)]
        + [pltpu.VMEM((size, size), f32)] * 4
        + [pltpu.VMEM((size, size), bf16)] * 4
        + [pltpu.VMEM((half, size), bf16)] * 3
        + [sem((8,)), sem, sem((count,)), sem((3,))]
        + [sem((4,))] * 6
        + [sem((4, 4))] * 2
        + [sem((6,))] * 2
        + [sem, sem((3,)), sem((count,)), sem((2,)), sem((2,)), sem],
        compiler_params=pltpu.CompilerParams(
            collective_id=collective_id, has_side_effects=True, vmem_limit_bytes=60 * 1024 * 1024
        ),
        name="optimize",
    )(*sums, *moments, gain_two, gains, *far)
    return (outs[:count], outs[count], outs[count + 1])


def settle_kernel(*refs):
    refs = list(refs)
    sums, steps, moments, weights = (take(refs, 4) for _ in range(4))
    new_moments, new_weights = take(refs, 4), take(refs, 4)
    for part in range(4):
        rate = MUON_RATE * 0.2 * math.sqrt(4 * sums[part].shape[0])
        for rows, place, is_turned in tiles_of(moments[part]):
            gradient, step = sums[part][rows], steps[part][rows].astype(jnp.float32)
            if not is_turned:
                gradient, step = gradient.T, step.T
            kept = weights[part][place].astype(jnp.float32) * (1.0 - MUON_RATE * DECAY_RATE)
            new_moments[part][place] = MOMENTUM * moments[part][place] + gradient
            new_weights[part][place] = kept - rate * step


def settle(sums, steps, moments, weights):
    local = pl.BlockSpec(memory_space=pltpu.VMEM)
    shapes = [jax.ShapeDtypeStruct(moment.shape, jnp.float32) for moment in moments]
    outs = pl.pallas_call(
        settle_kernel,
        out_shape=shapes * 2,
        in_specs=[local] * 16,
        out_specs=[local] * 8,
        compiler_params=pltpu.CompilerParams(vmem_limit_bytes=48 * 1024 * 1024),
        name="settle",
    )(*sums, *steps, *moments, *weights)
    return (outs[:4], outs[4:])


def weight_shards(weights):
    shards = [turn(weight) for weight in weights]
    third = shards[0].shape[0] // 3
    return [shards[0][third * part : third * part + third] for part in range(3)] + shards[1:]


def gather_weights(shards):
    tensor_count, dp_count = lax.axis_size("tensor"), lax.axis_size("dp")
    wholes = [lax.all_gather(shard, ("tensor", "dp")) for shard in shards]
    wholes = [
        whole.reshape(tensor_count, dp_count, *whole.shape[1:]).transpose(0, 2, 1, 3)
        for whole in wholes
    ]
    return [whole.reshape(*whole.shape[:2], -1) for whole in wholes]


def reduce_grads(grads):
    tensor_count, dp_count = lax.axis_size("tensor"), lax.axis_size("dp")
    sums = []
    for grad in grads:
        blocks = grad.reshape(*grad.shape[:2], dp_count, -1).transpose(0, 2, 1, 3)
        blocks = blocks.reshape(-1, *blocks.shape[2:])
        part = lax.psum_scatter(blocks, ("tensor", "dp"), scatter_dimension=0, tiled=True)
        sums.append(part[0].astype(jnp.float32))
    return sums


def lane_of(shape):
    return lax.broadcasted_iota(jnp.int32, shape, 1)

def turned(vectors, cosine, sine):
    lane = lax.rem(lane_of(vectors.shape), 64)
    swapped = jnp.where(lane < 32, pltpu.roll(vectors, 96, 1), pltpu.roll(vectors, 32, 1))
    return vectors * cosine + swapped * sine

def project_kernel(rows, query_weight, key_weight, value_weight, cosine, sine, queries, pair):
    rows = rows[...]
    for weight, target in ((query_weight, 0), (key_weight, 1)):
        result = product_of(rows, weight[0], ((1,), (1,)))
        for first in range(0, result.shape[1], 128):
            part = turned(result[:, first : first + 128], cosine[...], sine[...])
            if target == 0:
                queries[:, first : first + 128] = low(part * SCORE_SCALE)
            else:
                pair[0, :, first : first + 128] = low(part)
    pair[1] = low(product_of(rows, value_weight[0], ((1,), (1,))))

def project(rows, query_weight, key_weight, value_weight, cosine, sine):
    count, width = rows.shape
    groups, height, _ = query_weight.shape
    whole = lambda *shape: pl.BlockSpec(shape, lambda i: (0,) * len(shape))
    weight = pl.BlockSpec((1, height, width), lambda i: (i, 0, 0))
    return pl.pallas_call(
        project_kernel,
        grid=(groups,),
        out_shape=[jax.ShapeDtypeStruct((count, width), jnp.bfloat16), jax.ShapeDtypeStruct((2, count, width), jnp.bfloat16)],
        in_specs=[whole(count, width), weight, weight, weight, whole(count, 128), whole(count, 128)],
        out_specs=[pl.BlockSpec((count, height), lambda i: (0, i)), pl.BlockSpec((2, count, height), lambda i: (0, 0, i))],
        compiler_params=pltpu.CompilerParams(vmem_limit_bytes=40 * 1024 * 1024),
        name="project",
    )(rows, query_weight, key_weight, value_weight, cosine, sine)

def head_rows(transposed, head):
    rows = lax.broadcasted_iota(jnp.int32, transposed.shape, 0)
    return jnp.where(lax.div(rows, 64) == head, transposed, jnp.zeros_like(transposed))

def head_lanes(values, head):
    return jnp.where(lax.div(lane_of(values.shape), 64) == head, values, jnp.zeros_like(values))

def scores_of(keys, queries_turned, bias):
    scores = product_of(keys, queries_turned, ((1,), (0,)))
    return scores + jnp.concatenate([bias] * (scores.shape[1] // 128), axis=1)

def attend_kernel(queries, own, other, bias, context, log_total):
    query_turned = queries[...].T
    keys = jnp.concatenate([own[0], other[0]], axis=0)
    value_turned = jnp.concatenate([own[1].T, other[1].T], axis=1)
    parts, logs = [], []
    for head in range(2):
        scores = scores_of(keys, head_rows(query_turned, head), bias[...])
        highest = jnp.max(scores, axis=0, keepdims=True)
        weights = jnp.exp(scores - highest)
        total = jnp.sum(weights, axis=0, keepdims=True)
        part = product_of(value_turned[64 * head : 64 * head + 64], low(weights), ((1,), (0,)))
        parts.append(part / total)
        logs.append(highest + jnp.log(total))
    context[...] = low(jnp.concatenate(parts, axis=0)).T
    log_total[0] = jnp.concatenate(logs + logs * 3, axis=0)

def attend(queries, own, other, bias):
    count, width = queries.shape
    pairs = width // 128
    column = pl.BlockSpec((count, 128), lambda i: (0, i))
    double = pl.BlockSpec((2, count, 128), lambda i: (0, 0, i))
    return pl.pallas_call(
        attend_kernel,
        grid=(pairs,),
        out_shape=[jax.ShapeDtypeStruct((count, width), jnp.bfloat16), jax.ShapeDtypeStruct((pairs, 8, count), jnp.float32)],
        in_specs=[column, double, double, pl.BlockSpec((2 * count, 128), lambda i: (0, 0))],
        out_specs=[column, pl.BlockSpec((1, 8, count), lambda i: (i, 0, 0))],
        compiler_params=pltpu.CompilerParams(vmem_limit_bytes=40 * 1024 * 1024),
        name="attend",
    )(queries, own, other, bias)

def attend_back_kernel(queries, own, other, bias, grad, context, log_total, cosine, sine, grad_query, grad_own, grad_other):
    count = queries.shape[0]
    query_turned, grad_turned = queries[...].T, grad[...].T
    inner = (grad[...].astype(jnp.float32) * context[...].astype(jnp.float32)).T
    query_parts = [None, None]
    for half, (pair, result) in enumerate(((own, grad_own), (other, grad_other))):
        keys, values = pair[0], pair[1]
        key_turned = keys.T
        grad_keys, grad_values = None, None
        window = pl.ds(half * count, count)
        for head in range(2):
            lanes_of_head = slice(64 * head, 64 * head + 64)
            scores = scores_of(keys, head_rows(query_turned, head), bias[window])
            weights = jnp.exp(scores - log_total[0, head : head + 1])
            grad_weights = product_of(values, head_rows(grad_turned, head), ((1,), (0,)))
            inner_row = jnp.sum(inner[lanes_of_head], axis=0, keepdims=True)
            grad_scores = low(weights * (grad_weights - inner_row))
            value_part = product_of(low(weights), head_lanes(grad[...], head), ((1,), (0,)))
            key_part = product_of(grad_scores, head_lanes(queries[...], head), ((1,), (0,)))
            query_part = product_of(key_turned[lanes_of_head], grad_scores, ((1,), (0,)))
            grad_values = value_part if head == 0 else grad_values + value_part
            grad_keys = key_part if head == 0 else grad_keys + key_part
            query_parts[head] = query_part if half == 0 else query_parts[head] + query_part
        result[0] = turned(grad_keys, cosine[window], -sine[window]).astype(result.dtype)
        result[1] = grad_values.astype(result.dtype)
    grad_rows = jnp.concatenate(query_parts, axis=0).T * SCORE_SCALE
    own_rows = pl.ds(0, count)
    grad_query[...] = low(turned(grad_rows, cosine[own_rows], -sine[own_rows]))

def attend_back(queries, own, other, bias, grad, context, log_total, cosine, sine):
    count, width = queries.shape
    pairs = width // 128
    column = pl.BlockSpec((count, 128), lambda i: (0, i))
    double = pl.BlockSpec((2, count, 128), lambda i: (0, 0, i))
    table = pl.BlockSpec((2 * count, 128), lambda i: (0, 0))
    return pl.pallas_call(
        attend_back_kernel,
        grid=(pairs,),
        out_shape=[
            jax.ShapeDtypeStruct((count, width), jnp.bfloat16),
            jax.ShapeDtypeStruct((2, count, width), jnp.float32),
            jax.ShapeDtypeStruct((2, count, width), jnp.bfloat16),
        ],
        in_specs=[column, double, double, table, column, column, pl.BlockSpec((1, 8, count), lambda i: (i, 0, 0)), table, table],
        out_specs=[column, double, double],
        compiler_params=pltpu.CompilerParams(vmem_limit_bytes=48 * 1024 * 1024),
        name="attend_back",
    )(queries, own, other, bias, grad, context, log_total, cosine, sine)

def feed_kernel(rows, cotangent, in_weight, out_weight, result, grad_rows, grad_in, grad_out):
    height = out_weight.shape[1]
    @pl.when(pl.program_id(0) == 0)
    def _():
        result[...] = jnp.zeros_like(result)
        grad_rows[...] = jnp.zeros_like(grad_rows)
    gate = product_of(in_weight[0, 0:height], rows[...], ((1,), (1,)))
    up = product_of(in_weight[0, height:], rows[...], ((1,), (1,)))
    grad_hidden = product_of(out_weight[0], cotangent[...], ((1,), (1,)))
    below = 0.5 + 0.5 * lax.erf(gate * math.sqrt(0.5))
    active = gate * below
    hidden = low(active * up)
    slope = below + gate * jnp.exp(-0.5 * gate * gate) * (1.0 / math.sqrt(2.0 * math.pi))
    grad_gate = low(grad_hidden * up * slope)
    grad_up = low(grad_hidden * active)
    grad_out[0] = low(product_of(hidden, cotangent[...], ((1,), (0,))))
    grad_in[0, 0:height] = low(product_of(grad_gate, rows[...], ((1,), (0,))))
    grad_in[0, height:] = low(product_of(grad_up, rows[...], ((1,), (0,))))
    result[...] += product_of(hidden, out_weight[0], ((0,), (0,)))
    grad_rows[...] += product_of(grad_gate, in_weight[0, 0:height], ((0,), (0,)))
    grad_rows[...] += product_of(grad_up, in_weight[0, height:], ((0,), (0,)))

def feed(rows, cotangent, in_weight, out_weight):
    count, width = rows.shape
    groups, height, _ = out_weight.shape
    whole = pl.BlockSpec((count, width), lambda i: (0, 0))
    block = lambda size: pl.BlockSpec((1, size, width), lambda i: (i, 0, 0))
    return pl.pallas_call(
        feed_kernel,
        grid=(groups,),
        out_shape=[
            jax.ShapeDtypeStruct((count, width), jnp.float32),
            jax.ShapeDtypeStruct((count, width), jnp.float32),
            jax.ShapeDtypeStruct(in_weight.shape, jnp.bfloat16),
            jax.ShapeDtypeStruct(out_weight.shape, jnp.bfloat16),
        ],
        in_specs=[whole, whole, block(2 * height), block(height)],
        out_specs=[whole, whole, block(2 * height), block(height)],
        compiler_params=pltpu.CompilerParams(vmem_limit_bytes=60 * 1024 * 1024),
        name="feed",
    )(rows, cotangent, in_weight, out_weight)


def turn(block):
    return block.transpose(*range(1, block.ndim), 0).reshape(-1, block.shape[0])


def turn_back(rows, like):
    rows = rows.reshape(*like.shape[1:], like.shape[0])
    return rows.transpose(rows.ndim - 1, *range(rows.ndim - 1))


def orthogonal_steps(blocks, gain_part):
    tensor_count = lax.axis_size("tensor")
    heights = [block.shape[0] for block in blocks]
    row_count = blocks[0].shape[1]
    first_row = lax.axis_index("dp") * row_count
    gain_grad = lax.psum(gain_part, BOTH)
    widest = max(heights)
    stacked = jnp.stack(
        [jnp.pad(block.T, ((0, 0), (0, widest - block.shape[0]))) for block in blocks]
    )
    owned = lax.all_to_all(stacked, "tensor", split_axis=0, concat_axis=0, tiled=True)
    whole = lax.all_gather(owned, "dp", axis=1, tiled=True)
    mean, rest = newton_schulz(einsum("tik,tjk->ij", whole, whole))
    own_rows = lax.dynamic_slice_in_dim(rest, first_row, row_count, 0)
    own_whole = lax.dynamic_slice_in_dim(whole, first_row, row_count, 1)
    step_rows = low(einsum("ij,tjk->tik", low(own_rows), whole) + mean * own_whole)
    returned = lax.all_to_all(step_rows, "tensor", split_axis=0, concat_axis=0, tiled=True)
    return ([returned[index, :, :height].T for index, height in enumerate(heights)], gain_grad)


def view_of(block):
    if block.shape[-1] % 128:
        return turn(block)
    return block.transpose(1, 0, 2) if block.ndim == 3 else block


def unview(view, like):
    if like.shape[-1] % 128:
        return turn_back(view, like)
    return view.transpose(1, 0, 2) if like.ndim == 3 else view


def on_device(
    inputs,
    cotangent,
    lengths,
    qkv_weight,
    attn_out_weight,
    ffn_in_weight,
    ffn_out_weight,
    norm_gains,
    qkv_moment,
    attn_out_moment,
    ffn_in_moment,
    ffn_out_moment,
    gain_first,
    gain_second,
):
    tensor_count = lax.axis_size("tensor")
    dp_count = lax.axis_size("dp")
    dp_index = lax.axis_index("dp")
    tensor_index = lax.axis_index("tensor")
    core = dp_index % 2
    odd = tensor_index % 2 == 1
    upper = tensor_index >= tensor_count // 2
    lists = exchange_lists(dp_count // 2, tensor_count)
    weights = (qkv_weight, attn_out_weight, ffn_in_weight, ffn_out_weight)
    row_count = qkv_weight.shape[0]

    width = inputs.shape[3]
    local_rows = 2 * inputs.shape[2]
    fits = (tensor_count, dp_count, row_count, width) == (4, 8, 128, 1024)
    positions = jnp.concatenate(
        [core * local_rows + jnp.arange(local_rows), (1 - core) * local_rows + jnp.arange(local_rows)]
    )
    shards = weight_shards(weights)
    if fits:
        sizes = lengths.astype(jnp.float32)
        sizes = jnp.broadcast_to(jnp.pad(sizes, ((0, 6), (0, 0))), (8, 128))
        exponents = np.arange(HEAD_DIM // 2, dtype=np.float32) / np.float32(HEAD_DIM // 2)
        frequency = np.power(np.float32(ROPE_BASE), -exponents).astype(np.float32)
        frequency = jnp.asarray(np.tile(frequency, (8, 4)))
        outs = forward(shards, inputs[:, 0], cotangent[:, 0], sizes, norm_gains, frequency, 1)
        wholes, (rows_low, cotangent_low) = outs[:6], outs[6:8]
        low_one, queries, own, other, context, log_total, bias, middle, low_two = outs[8:17]
        cosine, sine = outs[17:]
    else:
        cosine, sine = rotary(positions)
        wholes = gather_weights(shards)
        rows_low = to_sequences(inputs[:, 0], lists, odd, upper)
        cotangent_low = to_sequences(cotangent[:, 0], lists, odd, upper)
    query_all, key_all, value_all, attn_all, ffn_in_all, ffn_out_all = wholes
    attn_rows = attn_all.reshape(-1, width)
    rows_in = rows_low.astype(jnp.float32)
    grad_rows = cotangent_low.astype(jnp.float32)
    normed_one, inverse_one, scaled_one = layer_norm_parts(rows_in, norm_gains[0])
    if not fits:
        own_lengths = swap_partner(lengths)
        both_lengths = jnp.where(
            core == 0,
            jnp.concatenate([lengths, own_lengths], 1),
            jnp.concatenate([own_lengths, lengths], 1),
        )
        length = lax.dynamic_index_in_dim(both_lengths.reshape(-1), tensor_index, 0, keepdims=False)
        bias = jnp.where(positions < length, 0.0, MASK_VALUE).astype(jnp.float32)
        bias = jnp.broadcast_to(bias[:, None], (positions.shape[0], 128))
        low_one = low(scaled_one)
        queries, own = project(
            low_one, query_all, key_all, value_all, cosine[:local_rows], sine[:local_rows]
        )
        other = swap_partner(own)
        context, log_total = attend(queries, own, other, bias)
        middle = rows_in + einsum("sk,kn->sn", context, attn_rows)
    normed_two, inverse_two, scaled_two = layer_norm_parts(middle, norm_gains[1])
    if not fits:
        low_two = low(scaled_two)
    if fits:
        outs = backward(
            (attn_all, ffn_in_all, ffn_out_all),
            low_two,
            cotangent_low,
            middle,
            queries,
            own,
            other,
            context,
            low_one,
            bias,
            log_total,
            cosine,
            sine,
            norm_gains,
            2,
        )
        sums, (grad_query, grad_pair, outputs, grad_middle, gain_two) = outs[:4], outs[4:]
    else:
        ffn_branch, grad_scaled_two, grad_ffn_in, grad_ffn_out = feed(
            low_two, cotangent_low, ffn_in_all, ffn_out_all
        )
        result = low(middle + ffn_branch)
        grad_from_two, gain_two = layer_norm_back(
            grad_scaled_two, normed_two, inverse_two, norm_gains[1]
        )
        grad_middle = grad_rows + grad_from_two
        grad_branch = low(grad_middle)
        grad_context = low(einsum("sn,kn->sk", grad_branch, attn_rows))
        grad_attn_out = low(einsum("sk,sn->kn", context, grad_branch)).reshape(attn_all.shape)
        grad_query, grad_own, grad_other = attend_back(
            queries, own, other, bias, grad_context, context, log_total, cosine, sine
        )
        grad_pair = low(grad_own + swap_partner(grad_other).astype(jnp.float32))
    moments = (qkv_moment, attn_out_moment, ffn_in_moment, ffn_out_moment)
    grad_parts = (grad_query, grad_pair[0], grad_pair[1])
    weight_parts = [part.reshape(-1, width) for part in (query_all, key_all, value_all)]
    if fits:
        far = (*weight_parts, grad_query, grad_pair, rows_low, grad_middle)
        viewed = [view_of(moment) for moment in moments]
        steps, gain_grad, input_grad = optimize(sums, viewed, gain_two, norm_gains, far, 3)
        outs = settle(sums, steps, viewed, [view_of(weight) for weight in weights])
        new_moments, new_weights = (
            [unview(part, like) for part, like in zip(parts, moments)] for parts in outs
        )
    else:
        grad_scaled_one = sum(
            einsum("sk,kn->sn", part, weight) for part, weight in zip(grad_parts, weight_parts)
        )
        grad_from_one, gain_one = layer_norm_back(
            grad_scaled_one, normed_one, inverse_one, norm_gains[0]
        )
        grads = [low(einsum("sk,sn->kn", part, low_one)) for part in grad_parts]
        grads = [grad.reshape(query_all.shape) for grad in grads]
        sums = reduce_grads(grads + [grad_attn_out, grad_ffn_in, grad_ffn_out])
        sums = [jnp.concatenate(sums[:3])] + list(sums[3:])
        outputs = from_sequences(result, lists, odd, upper)
        input_grad = from_sequences(low(grad_middle + grad_from_one), lists, odd, upper)
        turned_sums = [turn_back(part, moment) for part, moment in zip(sums, moments)]
        new_moments = [MOMENTUM * moment + part for moment, part in zip(moments, turned_sums)]
        steps, gain_grad = orthogonal_steps(
            [low(turn(moment)) for moment in new_moments], jnp.stack([gain_one, gain_two])
        )
        new_weights = [
            weight.astype(jnp.float32) * (1.0 - MUON_RATE * DECAY_RATE)
            - MUON_RATE
            * 0.2
            * math.sqrt(step.shape[0] * tensor_count)
            * turn_back(step, weight).astype(jnp.float32)
            for weight, step in zip(weights, steps)
        ]
    outputs, input_grad = outputs[:, None], input_grad[:, None].astype(jnp.float32)
    gain_first_new = BETA_ONE * gain_first + (1.0 - BETA_ONE) * gain_grad
    gain_second_new = BETA_TWO * gain_second + (1.0 - BETA_TWO) * gain_grad * gain_grad
    first_hat = gain_first_new / (1.0 - BETA_ONE**STEP)
    second_hat = gain_second_new / (1.0 - BETA_TWO**STEP)
    norm_gains_new = norm_gains - ADAM_RATE * (
        first_hat / (jnp.sqrt(second_hat) + ADAM_EPS) + DECAY_RATE * norm_gains
    )
    return (
        outputs,
        input_grad,
        new_moments[0],
        new_weights[0],
        new_moments[1],
        new_weights[1],
        new_moments[2],
        new_weights[2],
        new_moments[3],
        new_weights[3],
        gain_first_new,
        gain_second_new,
        norm_gains_new,
    )


def solution(mesh):
    in_specs = (
        P(None, "dp", "tensor", None),
        P(None, "dp", "tensor", None),
        P(None, "dp"),
        P("dp", None, "tensor"),
        P("dp", "tensor"),
        P("dp", None, "tensor"),
        P("dp", "tensor"),
        P(),
        P("dp", None, "tensor"),
        P("dp", "tensor"),
        P("dp", None, "tensor"),
        P("dp", "tensor"),
        P(),
        P(),
    )
    out_specs = (
        P(None, "dp", "tensor", None),
        P(None, "dp", "tensor", None),
        P("dp", None, "tensor"),
        P("dp", None, "tensor"),
        P("dp", "tensor"),
        P("dp", "tensor"),
        P("dp", None, "tensor"),
        P("dp", None, "tensor"),
        P("dp", "tensor"),
        P("dp", "tensor"),
        P(),
        P(),
        P(),
    )
    return jax.shard_map(
        on_device, mesh=mesh, in_specs=in_specs, out_specs=out_specs, check_vma=False
    )
```

```python
import functools
import math

import jax
import jax.numpy as jnp
import numpy as np
from jax import lax
from jax.experimental import pallas as pl
from jax.experimental.pallas import tpu as pltpu
from jax.sharding import PartitionSpec as P

HEAD_DIM = 64
NS_ITERS = 5
STEP = 10
SCORE_SCALE = 1.0 / math.sqrt(HEAD_DIM)


ROPE_BASE = 160000.0
NORM_EPS = 1e-05
MASK_VALUE = -1e30
MOMENTUM = 0.95
MUON_RATE = 0.1
DECAY_RATE = 0.01
QUINTIC_ONE = 3.4445
QUINTIC_THREE = -4.775
QUINTIC_FIVE = 2.0315
NORM_FLOOR = 1e-07
BETA_ONE = 0.9
BETA_TWO = 0.95
ADAM_RATE = 0.2
ADAM_EPS = 1e-08
BOTH = ("dp", "tensor")
MESH = pl.DeviceIdType.MESH


def rotary(positions):
    half_size = HEAD_DIM // 2
    exponents = jnp.arange(half_size).astype(jnp.float32) / half_size
    frequency = jnp.power(ROPE_BASE, -exponents)
    angles = positions.astype(jnp.float32)[:, None] * frequency[None, :]
    cosine, sine = jnp.cos(angles), jnp.sin(angles)
    return (
        jnp.concatenate([cosine] * 4, axis=1),
        jnp.concatenate([-sine, sine, -sine, sine], axis=1),
    )


def layer_norm_parts(vectors, gain):
    centre = vectors - jnp.mean(vectors, axis=-1, keepdims=True)
    inverse = lax.rsqrt(jnp.mean(centre * centre, axis=-1, keepdims=True) + NORM_EPS)
    normed = centre * inverse
    return (normed, inverse, normed * gain)


def layer_norm_back(grad_out, normed, inverse, gain):
    grad_normed = grad_out * gain
    mean_grad = jnp.mean(grad_normed, axis=-1, keepdims=True)
    mean_cross = jnp.mean(grad_normed * normed, axis=-1, keepdims=True)
    return (
        inverse * (grad_normed - mean_grad - normed * mean_cross),
        jnp.sum(grad_out * normed, axis=0),
    )


def einsum(spec, *operands):
    return jnp.einsum(spec, *operands, preferred_element_type=jnp.float32)


def low(values):
    return values.astype(jnp.bfloat16)


def exchange_lists(chip_count, tensor_count):
    first_list, second_list = [], []
    for chip in range(chip_count):
        for core in range(2):
            for slot in range(tensor_count):
                for micro in range(2):
                    source = (2 * chip + core) * tensor_count + slot
                    target = (2 * chip + slot // 2) * tensor_count + 2 * micro + core
                    pair = (source, target)
                    (first_list if slot % 2 == micro else second_list).append(pair)
    return (first_list, second_list)


def to_sequences(blocks, lists, odd, upper):
    first = lax.ppermute(jnp.where(odd, blocks[1], blocks[0]), BOTH, lists[0])
    second = lax.ppermute(jnp.where(odd, blocks[0], blocks[1]), BOTH, lists[1])
    return jnp.where(
        upper, jnp.concatenate([second, first]), jnp.concatenate([first, second])
    )


def from_sequences(rows, lists, odd, upper):
    half = rows.shape[0] // 2
    top, bottom = rows[:half], rows[half:]
    back = [[(target, source) for source, target in pairs] for pairs in lists]
    first = lax.ppermute(jnp.where(upper, bottom, top), BOTH, back[0])
    second = lax.ppermute(jnp.where(upper, top, bottom), BOTH, back[1])
    return jnp.where(odd, jnp.stack([second, first]), jnp.stack([first, second]))


def swap_partner(values):
    count = lax.axis_size("dp")
    return lax.ppermute(values, "dp", [(index, index ^ 1) for index in range(count)])


def mean_split(matrix):
    mean = jnp.trace(matrix) / matrix.shape[0]
    return (mean, matrix - mean * jnp.eye(matrix.shape[0], dtype=jnp.float32))


def split_product(left, right):
    left_mean, left_rest = left
    right_mean, right_rest = right
    product = einsum("ij,jk->ik", low(left_rest), low(right_rest))
    product = product + left_mean * right_rest + right_mean * left_rest
    mean, rest = mean_split(product)
    return (mean + left_mean * right_mean, rest)


def newton_schulz(gram):
    factor = 1.0 / (jnp.sqrt(jnp.trace(gram)) + NORM_FLOOR)
    iterate = mean_split(gram * (factor * factor))
    whole = None
    for sweep_index in range(NS_ITERS):
        square = split_product(iterate, iterate)
        poly = (
            QUINTIC_ONE + QUINTIC_THREE * iterate[0] + QUINTIC_FIVE * square[0],
            QUINTIC_THREE * iterate[1] + QUINTIC_FIVE * square[1],
        )
        whole = poly if whole is None else split_product(poly, whole)
        if sweep_index < NS_ITERS - 1:
            iterate = split_product(poly, split_product(poly, iterate))
    return (whole[0] * factor, whole[1] * factor)


def step_of(rows):
    return next(step for step in (128, 64, 48, 32, 16) if rows % step == 0)


def lanes(block):
    return pl.ds(pl.multiple_of(block * 128, 128), 128)

def neighbours():
    me = lax.axis_index("dp")
    core, across, down = lax.rem(me, 2), lax.rem(lax.div(me, 2), 2), lax.div(me, 4)
    return (me, me + 1 - 2 * core, me + 2 - 4 * across, me + 4 - 8 * down)

def greet(plane, others, planes):
    barrier = pltpu.get_barrier_semaphore()
    me = lax.axis_index("dp")
    crossed = list(others[:1])
    for other in others:
        pl.semaphore_signal(barrier, inc=1, device_id=(other, plane), device_id_type=MESH)
    for other in planes:
        for same_place in [me] + crossed:
            pl.semaphore_signal(barrier, inc=1, device_id=(same_place, other), device_id_type=MESH)
    pl.semaphore_wait(barrier, len(others) + len(planes) * (1 + len(crossed)))

def add_into(target, source, rows, step):
    @pl.loop(0, rows // step)
    def _(index):
        window = pl.ds(pl.multiple_of(index * step, step), step)
        total = target[:, window].astype(jnp.float32) + source[:, window].astype(jnp.float32)
        target[:, window] = total.astype(jnp.bfloat16)


def send_to(source, target, send, recv, device):
    pltpu.make_async_remote_copy(
        source, target, send, recv, device_id=device, device_id_type=MESH
    ).start()


def wait_for(view, sem):
    pltpu.make_async_copy(view, view, sem).wait()


def move_plan(outward, source, target, send, recv, own):
    me, partner, _, _ = neighbours()
    plane = lax.axis_index("tensor")
    core = lax.rem(me, 2)
    column = me - core
    high, parity = lax.div(plane, 2), lax.rem(plane, 2)
    height = target.shape[1] if outward else source.shape[1]

    def owner_of(slot):
        return (column + parity, 2 * core + slot)

    def keeper_of(micro):
        return (column + high, 2 * micro + core)

    def same(device):
        return jnp.logical_and(device[0] == me, device[1] == plane)

    def half(rows, index):
        return rows.at[pl.ds(pl.multiple_of(index * height, height), height), :]

    def start():
        for index in range(2):
            if outward:
                device = owner_of(index)
                piece, goal, arrival = half(source, index), target.at[high], high
            else:
                device = keeper_of(index)
                piece, goal, arrival = source.at[index], half(target, parity), parity

            @pl.when(same(device))
            def _():
                pltpu.make_async_copy(piece, goal, own).start()

            @pl.when(jnp.logical_not(same(device)))
            def _():
                send_to(piece, goal, send.at[index], recv.at[arrival], device)

    def finish():
        for index in range(2):
            if outward:
                sent_to, came_from = owner_of(index), keeper_of(index)
                piece, goal = half(source, index), target.at[index]
            else:
                sent_to, came_from = keeper_of(index), owner_of(index)
                piece, goal = source.at[index], half(target, index)

            @pl.when(same(sent_to))
            def _():
                wait_for(piece, own)

            @pl.when(jnp.logical_not(same(sent_to)))
            def _():
                wait_for(piece, send.at[index])

            @pl.when(jnp.logical_not(same(came_from)))
            def _():
                wait_for(goal, recv.at[index])

    return (start, finish)


def scatter_plan(grads, sums, buffers, sems):
    held, from_x, from_y, from_yx, from_xy, from_z = buffers[:6]
    staging = buffers[6][0]
    (load_sem, send_c, recv_c, send_x, recv_x, send_y, recv_y, send_yx, recv_yx, send_xy, recv_xy, send_z, recv_z) = sems
    me, partner, across, down = neighbours()
    plane = lax.axis_index("tensor")
    planes = [lax.rem(plane + offset, 4) for offset in (1, 2, 3)]
    flip = lambda block: block + 1 - 2 * lax.rem(block, 2)
    blocks = (me, across, down, across + down - me)
    order = (3, 1, 2, 0)

    def view(part, block):
        ref, first, rows = grads[part]
        return ref.at[:, pl.ds(first, rows), lanes(block)]

    def slot(part, index):
        return staging.at[index, :, pl.ds(0, grads[part][2])]

    def stage_core(part):
        for index in order:
            send_to(view(part, flip(blocks[index])), held[part].at[index], send_c.at[part, index], recv_c.at[part, index], (partner, plane))

    def load(part):
        for index in order:
            pltpu.make_async_copy(view(part, blocks[index]), slot(part, index), load_sem.at[part, index]).start()

    def stage_first(part):
        rows = grads[part][2]
        load(part)
        for index in order:
            wait_for(slot(part, index), load_sem.at[part, index])
            wait_for(held[part].at[index], recv_c.at[part, index])
            add_into(held[part].at[index], slot(part, index), rows, step_of(rows))
            if index % 2 == 1:
                send_to(held[part].at[index, 0:2], from_x[part].at[index // 2], send_x.at[part, index // 2], recv_x.at[part, index // 2], (across, plane))
            if index // 2 == 1:
                send_to(held[part].at[index, 2:4], from_y[part].at[index % 2], send_y.at[part, index % 2], recv_y.at[part, index % 2], (down, plane))

    def stage_second(part):
        rows = grads[part][2]
        for side in (1, 0):
            wait_for(from_x[part].at[side], recv_x.at[part, side])
            add_into(held[part].at[2 * side, 0:2], from_x[part].at[side], rows, step_of(rows))
            if side == 1:
                send_to(held[part].at[2, 0:2], from_yx[part], send_yx.at[part], recv_yx.at[part], (down, plane))
            wait_for(from_y[part].at[side], recv_y.at[part, side])
            add_into(held[part].at[side, 2:4], from_y[part].at[side], rows, step_of(rows))
            if side == 1:
                send_to(held[part].at[1, 2:4], from_xy[part], send_xy.at[part], recv_xy.at[part], (across, plane))

    def stage_third(part):
        rows = grads[part][2]
        wait_for(from_yx[part], recv_yx.at[part])
        add_into(held[part].at[0, 0:2], from_yx[part], rows, step_of(rows))
        wait_for(from_xy[part], recv_xy.at[part])
        add_into(held[part].at[0, 2:4], from_xy[part], rows, step_of(rows))
        for index, other in enumerate(planes):
            send_to(held[part].at[0, other], from_z[part].at[index], send_z.at[part, index], recv_z.at[part, index], (me, other))

    def stage_last(part):
        rows = grads[part][2]
        step = step_of(rows)
        target, first = sums[part]
        for index in range(3):
            wait_for(from_z[part].at[index], recv_z.at[part, index])

        @pl.loop(0, rows // step)
        def _(index):
            offset = pl.multiple_of(index * step, step)
            window = pl.ds(offset, step)
            total = held[part][0, plane, window].astype(jnp.float32)
            for other in range(3):
                total = total + from_z[part][other, window].astype(jnp.float32)
            target[pl.ds(pl.multiple_of(first + offset, 16), step)] = total

    def finish(part):
        for index in range(4):
            wait_for(held[part].at[index], send_c.at[part, index])
        for side in range(2):
            wait_for(from_x[part].at[side], send_x.at[part, side])
            wait_for(from_y[part].at[side], send_y.at[part, side])
        wait_for(from_yx[part], send_yx.at[part])
        wait_for(from_xy[part], send_xy.at[part])
        for index in range(3):
            wait_for(from_z[part].at[index], send_z.at[part, index])

    return ((stage_core, stage_first, stage_second, stage_third, stage_last), finish)


def scatter_scratch(heights):
    sem = pltpu.SemaphoreType.DMA
    count = len(heights)
    leads = ((4, 4), (2, 2), (2, 2), (2,), (2,), (3,))
    buffers = [pltpu.VMEM(lead + (rows, 128), jnp.bfloat16) for lead in leads for rows in heights]
    buffers.append(pltpu.VMEM((4, 4, max(heights), 128), jnp.bfloat16))
    sems = [sem((count, 4))] * 3 + [sem((count, 2))] * 4 + [sem((count,))] * 4 + [sem((count, 3))] * 2
    return (buffers, sems)


def take(refs, count):
    taken, refs[:] = refs[:count], refs[count:]
    return taken


def gather_plan(shards, wholes, sems):
    own_sem, send_up, send_down, recv_z, send_x, recv_x, send_y, recv_y, send_d, recv_d, send_c, recv_c = sems
    me, partner, across, down = neighbours()
    plane = lax.axis_index("tensor")
    diagonal = across + down - me
    flip = lambda block: block + 1 - 2 * lax.rem(block, 2)

    def place(part, slot, block):
        return wholes[part].at[slot, :, lanes(block)]

    def spread(part, source, slot):
        view = place(part, slot, me)
        send_to(source, view, send_x.at[part, slot], recv_x.at[part, slot], (across, plane))
        send_to(source, view, send_y.at[part, slot], recv_y.at[part, slot], (down, plane))
        send_to(source, view, send_c.at[part, slot, 0], recv_c.at[part, slot, 0], (partner, plane))

    def pass_on(part, source, slot, upward):
        view = place(part, slot, me)
        sem = (send_up if upward else send_down).at[part, slot]
        send_to(source, view, sem, recv_z.at[part, slot], (me, plane + 1 if upward else plane - 1))

    def stage_own(part):
        pltpu.make_async_copy(shards[part], place(part, plane, me), own_sem.at[part]).start()

        @pl.when(plane < 3)
        def _():
            pass_on(part, shards[part], plane, True)

        @pl.when(plane > 0)
        def _():
            pass_on(part, shards[part], plane, False)

        spread(part, shards[part], plane)

    def stage_z(part):
        for distance in (1, 2, 3):
            for upward in (True, False):
                slot = plane - distance if upward else plane + distance

                @pl.when(slot >= 0 if upward else slot <= 3)
                def _():
                    view = place(part, slot, me)
                    wait_for(view, recv_z.at[part, slot])

                    @pl.when(plane < 3 if upward else plane > 0)
                    def _():
                        pass_on(part, view, slot, upward)

                    spread(part, view, slot)

    def stage_xy(part):
        for slot in range(4):
            view = place(part, slot, across)
            wait_for(view, recv_x.at[part, slot])
            if slot < 2:
                send_to(view, view, send_d.at[part, slot], recv_d.at[part, slot], (down, plane))
            send_to(view, view, send_c.at[part, slot, 1], recv_c.at[part, slot, 1], (partner, plane))
            view = place(part, slot, down)
            wait_for(view, recv_y.at[part, slot])
            if slot >= 2:
                send_to(view, view, send_d.at[part, slot], recv_d.at[part, slot], (across, plane))
            send_to(view, view, send_c.at[part, slot, 2], recv_c.at[part, slot, 2], (partner, plane))

    def stage_diagonal(part):
        for slot in range(4):
            view = place(part, slot, diagonal)
            wait_for(view, recv_d.at[part, slot])
            send_to(view, view, send_c.at[part, slot, 3], recv_c.at[part, slot, 3], (partner, plane))

    def arrive(part):
        wait_for(shards[part], own_sem.at[part])
        for slot in range(4):
            for index, block in enumerate((me, across, down, diagonal)):
                wait_for(place(part, slot, flip(block)), recv_c.at[part, slot, index])

    def finish(part):
        for slot in range(4):
            @pl.when(jnp.logical_and(slot <= plane, plane < 3))
            def _():
                wait_for(shards[part], send_up.at[part, slot])

            @pl.when(jnp.logical_and(slot >= plane, plane > 0))
            def _():
                wait_for(shards[part], send_down.at[part, slot])

            for sem in (send_x, send_y, send_d):
                wait_for(shards[part], sem.at[part, slot])
            for index in range(4):
                wait_for(shards[part], send_c.at[part, slot, index])

    return (stage_own, stage_z, stage_xy, stage_diagonal, arrive, finish)


def normed_rows(rows, gain):
    centre = rows - jnp.mean(rows, axis=1, keepdims=True)
    inverse = lax.rsqrt(jnp.mean(centre * centre, axis=1, keepdims=True) + NORM_EPS)
    return centre * inverse * gain


def forward_kernel(*refs):
    refs = list(refs)
    shards, (inputs, cotangent, lengths, gains, frequency) = take(refs, 6), take(refs, 5)
    wholes, (far_rows, grad_rows) = take(refs, 6), take(refs, 2)
    far = [far_rows] + take(refs, 4)
    context, log_total, bias, middle, low_two, cosine, sine = take(refs, 7)
    near = take(refs, 5)
    rows_low, low_one, queries, own, other = near
    other_lengths, weight, attn_weight = take(refs, 3)
    sems = take(refs, 12)
    pair_send, pair_recv, length_send, length_recv, weight_sem, attn_sem, out_sem = take(refs, 7)
    move_send, move_recv, move_own = refs
    outward = [
        pltpu.make_async_copy(source, target, out_sem.at[index])
        for index, (source, target) in enumerate(zip(near, far))
    ]
    me, partner, across, down = neighbours()
    plane = lax.axis_index("tensor")
    core = lax.rem(me, 2)
    stage_own, stage_z, stage_xy, stage_diagonal, arrive, finish = gather_plan(shards, wholes, sems)
    moves = [
        move_plan(False, source, target, move_send.at[index], move_recv.at[index], move_own.at[index])
        for index, (source, target) in enumerate(((inputs, rows_low), (cotangent, grad_rows)))
    ]
    greet(plane, (partner, across, down), [lax.rem(plane + offset, 4) for offset in (1, 2, 3)])
    count, width = rows_low.shape
    third = shards[0].shape[0]
    step = 64

    stage_own(0)
    stage_own(1)
    send_to(lengths, other_lengths, length_send, length_recv, (partner, plane))
    stage_z(0)
    stage_own(2)
    stage_z(1)
    stage_xy(0)
    stage_own(3)
    stage_z(2)
    stage_xy(1)
    stage_diagonal(0)
    stage_own(4)
    stage_z(3)
    stage_xy(2)
    stage_diagonal(1)
    stage_own(5)
    stage_z(4)
    moves[0][0]()
    stage_xy(3)
    stage_diagonal(2)
    stage_z(5)
    moves[1][0]()
    stage_diagonal(3)
    stage_xy(4)
    wait_for(other_lengths, length_recv)
    mine = core == lax.rem(plane, 2)
    both = jnp.where(mine, lengths[...], other_lengths[...])
    length = jnp.where(plane < 2, both[0:1], both[1:2])
    position = lax.broadcasted_iota(jnp.int32, bias.shape, 0)
    position = lax.rem(position + core * count, 2 * count).astype(jnp.float32)
    bias[...] = jnp.where(position < length, 0.0, MASK_VALUE)

    @pl.loop(0, bias.shape[0] // 128)
    def _(index):
        first = pl.multiple_of(index * 128, 128)
        place = lax.broadcasted_iota(jnp.int32, (128, 128), 0) + first + core * count
        angles = lax.rem(place, 2 * count).astype(jnp.float32) * frequency[0:1]
        half_lane = lax.rem(lane_of((128, 128)), HEAD_DIM) < HEAD_DIM // 2
        cosine[pl.ds(first, 128)] = jnp.cos(angles)
        turned_sine = jnp.sin(angles)
        sine[pl.ds(first, 128)] = jnp.where(half_lane, -turned_sine, turned_sine)

    moves[0][1]()

    @pl.loop(0, count // step)
    def _(index):
        window = pl.ds(pl.multiple_of(index * step, step), step)
        low_one[window] = low(normed_rows(rows_low[window].astype(jnp.float32), gains[0:1]))

    outward[0].start()
    outward[1].start()
    for part in range(3):
        arrive(part)

    def load(group):
        for part in range(3):
            slot = lax.rem(group, 2)
            pltpu.make_async_copy(wholes[part].at[group], weight.at[slot, part], weight_sem.at[slot, part]).start()

    load(0)

    @pl.loop(0, 4)
    def _(group):
        @pl.when(group < 3)
        def _():
            load(group + 1)

        slot = lax.rem(group, 2)
        for part in range(3):
            wait_for(weight.at[slot, part], weight_sem.at[slot, part])
            result = product_of(low_one[...], weight[slot, part], ((1,), (1,)))
            for first in range(0, third, 128):
                columns = pl.ds(pl.multiple_of(group * third + first, 128), 128)
                piece = result[:, first : first + 128]
                if part < 2:
                    piece = turned(piece, cosine[0:count], sine[0:count])
                if part == 0:
                    queries[:, columns] = low(piece * SCORE_SCALE)
                else:
                    own[part - 1, :, columns] = low(piece)

    send_to(own, other, pair_send, pair_recv, (partner, plane))
    outward[2].start()
    outward[3].start()
    wait_for(other, pair_recv)
    outward[4].start()
    arrive(3)
    attn_copy = pltpu.make_async_copy(wholes[3], attn_weight, attn_sem)
    attn_copy.start()
    schedule = {3: (stage_xy, 5), 6: (stage_diagonal, 4)}

    @pl.loop(0, width // 128)
    def _(index):
        for place, (stage, part) in schedule.items():
            @pl.when(index == place)
            def _():
                stage(part)

        attend_pair(lanes(index), queries, own, other, bias, context, log_total.at[index])

    attn_copy.wait()

    @pl.loop(0, count // 128)
    def _(index):
        window = pl.ds(pl.multiple_of(index * 128, 128), 128)
        rows = rows_low[window].astype(jnp.float32)
        for group in range(4):
            piece = context[window, third * group : third * group + third]
            rows = rows + product_of(piece, attn_weight[group], ((1,), (0,)))
        middle[window] = rows
        low_two[window] = low(normed_rows(rows, gains[1:2]))

    stage_diagonal(5)
    for part in (4, 5):
        arrive(part)
    for part in range(6):
        finish(part)
    for copy in outward:
        copy.wait()
    wait_for(own, pair_send)
    wait_for(lengths, length_send)
    moves[1][1]()


def forward(shards, inputs, cotangent, lengths, gains, frequency, collective_id):
    sem = pltpu.SemaphoreType.DMA
    anywhere = pl.BlockSpec(memory_space=pl.ANY)
    local = pl.BlockSpec(memory_space=pltpu.VMEM)
    bf16, f32 = jnp.bfloat16, jnp.float32
    count, width = 2 * inputs.shape[1], inputs.shape[2]
    third = shards[0].shape[0]
    shape = jax.ShapeDtypeStruct
    return pl.pallas_call(
        forward_kernel,
        out_shape=[shape((4, shard.shape[0], width), bf16) for shard in shards]
        + [
            shape((count, width), bf16),
            shape((count, width), bf16),
            shape((count, width), bf16),
            shape((count, width), bf16),
            shape((2, count, width), bf16),
            shape((2, count, width), bf16),
            shape((count, width), bf16),
            shape((width // 128, 8, count), f32),
            shape((2 * count, 128), f32),
            shape((count, width), f32),
            shape((count, width), bf16),
            shape((2 * count, 128), f32),
            shape((2 * count, 128), f32),
        ],
        in_specs=[anywhere] * 8 + [local] * 3,
        out_specs=[anywhere] * 12 + [local] * 7,
        scratch_shapes=[
            pltpu.VMEM((count, width), bf16),
            pltpu.VMEM((count, width), bf16),
            pltpu.VMEM((count, width), bf16),
            pltpu.VMEM((2, count, width), bf16),
            pltpu.VMEM((2, count, width), bf16),
            pltpu.VMEM(lengths.shape, f32),
            pltpu.VMEM((2, 3, third, width), bf16),
            pltpu.VMEM((4, third, width), bf16),
            sem((6,)),
        ]
        + [sem((6, 4))] * 9
        + [sem((6, 4, 4))] * 2
        + [sem, sem, sem, sem, sem((2, 3)), sem, sem((5,))]
        + [sem((2, 2)), sem((2, 2)), sem((2,))],
        compiler_params=pltpu.CompilerParams(
            collective_id=collective_id, has_side_effects=True, vmem_limit_bytes=58 * 1024 * 1024
        ),
        name="forward",
    )(*shards, inputs, cotangent, lengths, gains, frequency)


def attend_pair(columns, queries, own, other, bias, context, log_total):
    query_turned = queries[:, columns].T
    keys = jnp.concatenate([own[0, :, columns], other[0, :, columns]], axis=0)
    value_turned = jnp.concatenate([own[1, :, columns].T, other[1, :, columns].T], axis=1)
    parts, logs = [], []
    for head in range(2):
        scores = scores_of(keys, head_rows(query_turned, head), bias[...])
        highest = jnp.max(scores, axis=0, keepdims=True)
        weights = jnp.exp(scores - highest)
        total = jnp.sum(weights, axis=0, keepdims=True)
        part = product_of(value_turned[64 * head : 64 * head + 64], low(weights), ((1,), (0,)))
        parts.append(part / total)
        logs.append(highest + jnp.log(total))
    context[:, columns] = low(jnp.concatenate(parts, axis=0)).T
    log_total[...] = jnp.concatenate(logs + logs * 3, axis=0)


def add_rows(target, source, extent):
    step = step_of(extent)

    @pl.loop(0, extent // step)
    def _(index):
        window = pl.ds(pl.multiple_of(index * step, step), step)
        target[window] = low(target[window].astype(jnp.float32) + source[window].astype(jnp.float32))


def slot_of(part):
    return (4 - part) % 4


def slot_plan(grads, sums, buffers, sems):
    held, from_x, from_y, from_yx, from_xy = buffers[:5]
    from_z, staging = buffers[5][0], buffers[6][0]
    (load_sem, send_c, recv_c, send_x, recv_x, send_y, recv_y, send_yx, recv_yx, send_xy, recv_xy, send_z, recv_z) = sems
    me, partner, across, down = neighbours()
    plane = lax.axis_index("tensor")
    flip = lambda block: block + 1 - 2 * lax.rem(block, 2)
    blocks = (me, across, down, across + down - me)
    order = (3, 1, 2, 0)
    rows, early = grads.shape[1], from_x[0].shape[1]
    late = rows - early
    one, two = pl.ds(0, early), pl.ds(early, late)

    def stage_core(part):
        for index in order:
            send_to(grads.at[slot_of(part), :, lanes(flip(blocks[index]))], held[part].at[index], send_c.at[part, index], recv_c.at[part, index], (partner, plane))

    def stage_first(part):
        for index in order:
            pltpu.make_async_copy(grads.at[slot_of(part), :, lanes(blocks[index])], staging.at[index], load_sem.at[part, index]).start()
        for index in order:
            wait_for(staging.at[index], load_sem.at[part, index])
            wait_for(held[part].at[index], recv_c.at[part, index])
            add_rows(held[part].at[index], staging.at[index], rows)
            if index % 2 == 1:
                send_to(held[part].at[index, one], from_x[part].at[index // 2], send_x.at[part, index // 2], recv_x.at[part, index // 2], (across, plane))
            if index // 2 == 1:
                send_to(held[part].at[index, two], from_y[part].at[index % 2], send_y.at[part, index % 2], recv_y.at[part, index % 2], (down, plane))

    def stage_second(part):
        for side in (1, 0):
            wait_for(from_x[part].at[side], recv_x.at[part, side])
            add_rows(held[part].at[2 * side, one], from_x[part].at[side], early)
            if side == 1:
                send_to(held[part].at[2, one], from_yx[part], send_yx.at[part], recv_yx.at[part], (down, plane))
            wait_for(from_y[part].at[side], recv_y.at[part, side])
            add_rows(held[part].at[side, two], from_y[part].at[side], late)
            if side == 1:
                send_to(held[part].at[1, two], from_xy[part], send_xy.at[part], recv_xy.at[part], (across, plane))

    def stage_third(part):
        wait_for(from_yx[part], recv_yx.at[part])
        add_rows(held[part].at[0, one], from_yx[part], early)
        wait_for(from_xy[part], recv_xy.at[part])
        add_rows(held[part].at[0, two], from_xy[part], late)

        @pl.when(plane != slot_of(part))
        def _():
            offset = lax.rem(plane + 3 - slot_of(part), 4)
            send_to(held[part].at[0], from_z.at[offset], send_z.at[part], recv_z.at[offset], (me, slot_of(part)))

    def stage_last(part):
        @pl.when(plane == slot_of(part))
        def _():
            for offset in range(3):
                wait_for(from_z.at[offset], recv_z.at[offset])
            for target, first, extent in sums:
                step = step_of(extent)

                @pl.loop(0, extent // step)
                def _(index):
                    offset = pl.multiple_of(index * step, step)
                    window = pl.ds(pl.multiple_of(first + offset, 16), step)
                    total = held[part][0, window].astype(jnp.float32)
                    for other in range(3):
                        total = total + from_z[other, window].astype(jnp.float32)
                    target[pl.ds(offset, step)] = total

    def finish(part):
        for index in range(4):
            wait_for(held[part].at[index], send_c.at[part, index])
        for side in range(2):
            wait_for(from_x[part].at[side], send_x.at[part, side])
            wait_for(from_y[part].at[side], send_y.at[part, side])
        wait_for(from_yx[part], send_yx.at[part])
        wait_for(from_xy[part], send_xy.at[part])

        @pl.when(plane != slot_of(part))
        def _():
            wait_for(from_z.at[0], send_z.at[part])

    return ((stage_core, stage_first, stage_second, stage_third, stage_last), finish)


def slot_scratch(rows, early):
    sem = pltpu.SemaphoreType.DMA
    late = rows - early
    shapes = [(4, rows)] * 4 + [(2, early)] * 4 + [(2, late)] * 4 + [(early,)] * 4 + [(late,)] * 4
    shapes += [(3, rows), (4, rows)]
    buffers = [pltpu.VMEM(shape + (128,), jnp.bfloat16) for shape in shapes]
    sems = [sem((4, 4))] * 3 + [sem((4, 2))] * 4 + [sem((4,))] * 4 + [sem((4,)), sem((3,))]
    return (buffers, sems)


def backward_kernel(*refs):
    refs = list(refs)
    f32, bf16 = jnp.float32, jnp.bfloat16
    in_weight, out_weight, attn_weight, far_two, far_cot, far_middle = take(refs, 6)
    far_query, far_own, far_other, far_context, far_one = take(refs, 5)
    bias, log_total, cosine, sine, gains = take(refs, 5)
    sums, (far_grad_query, far_pair, rows_out, far_grad_middle, gain_two) = take(refs, 4), take(refs, 5)
    grad_feed, weight_grads = take(refs, 1)[0], take(refs, 4)
    branch, cotangent, low_rows, queries, own, other, grad, context = take(refs, 8)
    grad_query, grad_pair, grad_other, arrived, staged = take(refs, 5)
    result, grad_rows, middle = take(refs, 3)
    slot_buffers = [take(refs, 4) for _ in range(5)] + [take(refs, 1), take(refs, 1)]
    slot_sems = take(refs, 13)
    buffers = [take(refs, 4) for _ in range(6)] + [take(refs, 1)]
    sems = take(refs, 13)
    pair_send, pair_recv, stage_sem, load_sem, out_sem, weight_sem, feed_sem, middle_sem = take(refs, 8)
    move_send, move_recv, move_own = refs
    me, partner, across, down = neighbours()
    plane = lax.axis_index("tensor")
    height, third = out_weight.shape[1], attn_weight.shape[1]
    count, width = cotangent.shape
    sum_qkv, sum_attn, sum_in, sum_out = sums
    feed_sums = [(sum_in, 0, 2 * height), (sum_out, 2 * height, height)]
    feed_stages, feed_finish = slot_plan(grad_feed, feed_sums, slot_buffers, slot_sems)
    parts = [(ref, 0, third) for ref in weight_grads]
    targets = [(sum_attn, 0)] + [(sum_qkv, third * index) for index in range(3)]
    stages, finish = scatter_plan(parts, targets, buffers, sems)
    start_move, finish_move = move_plan(True, cotangent, rows_out, move_send, move_recv, move_own)

    def call(stage, part):
        if part < 4:
            feed_stages[stage](part)
        else:
            stages[stage](part - 4)

    pieces = ((0, 336), (336, height - 336))
    weight_slots = (
        (own.at[0], own.at[1], grad_pair.at[0]),
        (other.at[0], other.at[1], grad_pair.at[1]),
    )
    grad_slots = ((grad_other.at[0], grad_other.at[1], grad_query), (queries, context, grad))

    def weight_copies(group, piece):
        first, extent = pieces[piece]
        sources = ((in_weight, first), (in_weight, height + first), (out_weight, first))
        return [
            pltpu.make_async_copy(source.at[lax.rem(4 - group, 4), pl.ds(offset, extent)], target.at[pl.ds(0, extent)], weight_sem.at[piece, index])
            for index, ((source, offset), target) in enumerate(zip(sources, weight_slots[piece]))
        ]

    def grad_copies(group, piece):
        first, extent = pieces[piece]
        return [
            pltpu.make_async_copy(source.at[pl.ds(0, extent)], grad_feed.at[lax.rem(4 - group, 4), pl.ds(index * height + first, extent)], feed_sem.at[piece, index])
            for index, source in enumerate(grad_slots[piece])
        ]

    def start_all(copies):
        for copy in copies:
            copy.start()

    def wait_all(copies):
        for copy in copies:
            copy.wait()

    first_loads = [
        pltpu.make_async_copy(far_two, branch, load_sem.at[0]),
        pltpu.make_async_copy(far_cot, cotangent, load_sem.at[1]),
    ]
    start_all(first_loads)
    start_all(weight_copies(0, 0))
    start_all(weight_copies(0, 1))
    greet(plane, (partner, across, down), [lax.rem(plane + offset, 4) for offset in (1, 2, 3)])
    result[...] = jnp.zeros_like(result)
    grad_rows[...] = jnp.zeros_like(grad_rows)
    wait_all(first_loads)
    feed_calls = {(1, 1): ((1, 0),), (2, 1): ((1, 1),), (3, 0): ((2, 0),), (3, 1): ((1, 2),)}

    @pl.loop(0, 4)
    def _(group):
        @pl.when(group > 0)
        def _():
            for piece in range(2):
                wait_all(grad_copies(group - 1, piece))
            for part in range(3):
                @pl.when(group == part + 1)
                def _():
                    call(0, part)

        for piece, (_, extent) in enumerate(pieces):
            for (when, place), calls in feed_calls.items():
                if place == piece:
                    @pl.when(group == when)
                    def _():
                        for stage, part in calls:
                            call(stage, part)

            window = pl.ds(0, extent)
            wait_all(weight_copies(group, piece))
            gate_weight, up_weight, down_weight = (ref[window] for ref in weight_slots[piece])
            gate = product_of(gate_weight, branch[...], ((1,), (1,)))
            up = product_of(up_weight, branch[...], ((1,), (1,)))
            grad_hidden = product_of(down_weight, cotangent[...], ((1,), (1,)))
            below = 0.5 + 0.5 * lax.erf(gate * math.sqrt(0.5))
            active = gate * below
            hidden = low(active * up)
            slope = below + gate * jnp.exp(-0.5 * gate * gate) * (1.0 / math.sqrt(2.0 * math.pi))
            grad_gate = low(grad_hidden * up * slope)
            grad_up = low(grad_hidden * active)
            grad_slots[piece][2][window] = low(product_of(hidden, cotangent[...], ((1,), (0,))))
            grad_slots[piece][0][window] = low(product_of(grad_gate, branch[...], ((1,), (0,))))
            grad_slots[piece][1][window] = low(product_of(grad_up, branch[...], ((1,), (0,))))
            start_all(grad_copies(group, piece))
            result[...] += product_of(hidden, down_weight, ((0,), (0,)))
            grad_rows[...] += product_of(grad_gate, gate_weight, ((0,), (0,)))
            grad_rows[...] += product_of(grad_up, up_weight, ((0,), (0,)))

            @pl.when(group < 3)
            def _():
                start_all(weight_copies(group + 1, piece))

    step = 64

    def middle_copy(index):
        window = pl.ds(pl.multiple_of(index * step, step), step)
        slot = lax.rem(index, 2)
        return pltpu.make_async_copy(far_middle.at[window], middle.at[slot], middle_sem.at[slot])

    middle_copy(0).start()
    for piece in range(2):
        wait_all(grad_copies(3, piece))
    call(0, 3)
    near = (queries, own, other, context, low_rows)
    loads = [
        pltpu.make_async_copy(source, target, load_sem.at[index])
        for index, (source, target) in enumerate(zip((far_query, far_own, far_other, far_context, far_one), near))
    ]
    start_all(loads)
    attn_loads = [
        pltpu.make_async_copy(
            attn_weight.at[group], grad_other.at[group // 2, pl.ds(group % 2 * third, third)], weight_sem.at[group // 2, group % 2]
        )
        for group in range(4)
    ]
    start_all(attn_loads)
    gain_two[...] = jnp.zeros_like(gain_two)

    @pl.loop(0, count // step)
    def _(index):
        @pl.when(index < count // step - 1)
        def _():
            middle_copy(index + 1).start()

        middle_copy(index).wait()
        window = pl.ds(pl.multiple_of(index * step, step), step)
        rows = middle[lax.rem(index, 2)]
        centre = rows - jnp.mean(rows, axis=1, keepdims=True)
        inverse = lax.rsqrt(jnp.mean(centre * centre, axis=1, keepdims=True) + NORM_EPS)
        normed = centre * inverse
        scaled = grad_rows[window] * gains[1:2]
        mean_grad = jnp.mean(scaled, axis=1, keepdims=True)
        mean_cross = jnp.mean(scaled * normed, axis=1, keepdims=True)
        gain_two[...] += jnp.sum(grad_rows[window] * normed, axis=0, keepdims=True)
        total = cotangent[window].astype(f32) + inverse * (scaled - mean_grad - normed * mean_cross)
        grad_rows[window] = total
        branch[window] = low(total)
        cotangent[window] = low(rows + result[window])

    call(3, 0)
    call(2, 1)
    start_move()
    middle_out = pltpu.make_async_copy(grad_rows, far_grad_middle, out_sem.at[2])
    middle_out.start()
    wait_all(attn_loads)

    @pl.loop(0, count // 128)
    def _(index):
        window = pl.ds(pl.multiple_of(index * 128, 128), 128)
        for part in range(2):
            columns = slice(part * count, part * count + count)
            grad[window, columns] = low(product_of(branch[window], grad_other[part], ((1,), (1,))))

    wait_all(loads)

    def weight_grad(which, values, rows):
        target = weight_grads[which]
        for group in range(4):
            slot = staged.at[group % 2]
            if group >= 2:
                wait_for(slot, stage_sem.at[group % 2])
            block = values[:, third * group : third * group + third]
            slot[...] = low(product_of(block, rows[...], ((0,), (0,))))
            pltpu.make_async_copy(slot, target.at[group], stage_sem.at[group % 2]).start()
        for group in range(2):
            wait_for(staged.at[group], stage_sem.at[group])

    weight_grad(0, context, branch)
    call(0, 4)

    def exchanged(index):
        return (arrived.at[:, :, lanes(index)], pair_recv.at[index])

    def add_pair(index):
        wait_for(*exchanged(index))
        columns = lanes(index)
        for which in range(2):
            total = grad_pair[which, :, columns].astype(f32)
            total = total + arrived[which, :, columns].astype(f32)
            grad_pair[which, :, columns] = low(total)

    last_pair = width // 128 - 1
    schedule = {0: ((1, 3),), 2: ((3, 1), (2, 2)), 5: ((3, 2), (1, 4)), 7: ((2, 3),)}

    @pl.loop(0, last_pair + 1)
    def _(index):
        for position, calls in schedule.items():
            @pl.when(index == position)
            def _():
                for stage, part in calls:
                    call(stage, part)

        attend_back_pair(lanes(index), queries, own, other, bias, grad, context, log_total.at[index], cosine, sine, grad_query, grad_pair, grad_other)
        target, sem = exchanged(index)
        send_to(grad_other.at[:, :, lanes(index)], target, pair_send.at[index], sem, (partner, plane))

        @pl.when(index > 0)
        def _():
            add_pair(index - 1)

    query_copy = pltpu.make_async_copy(grad_query, far_grad_query, out_sem.at[0])
    query_copy.start()
    weight_grad(1, grad_query, low_rows)
    call(0, 5)
    call(3, 3)
    add_pair(last_pair)
    pair_copy = pltpu.make_async_copy(grad_pair, far_pair, out_sem.at[1])
    pair_copy.start()
    weight_grad(2, grad_pair.at[0], low_rows)
    call(0, 6)
    weight_grad(3, grad_pair.at[1], low_rows)
    call(0, 7)
    done = {(3, 3), (1, 4), (3, 2), (2, 3), (1, 0), (2, 0), (1, 1), (3, 0), (2, 1), (1, 2), (3, 1), (2, 2), (1, 3)}
    for turn_of in range(10):
        for stage in (3, 2, 1):
            part = turn_of - (stage - 1)
            if 0 <= part < 8 and (stage, part) not in done:
                call(stage, part)
    for part in range(8):
        call(4, part)
    for part in range(4):
        feed_finish(part)
        finish(part)
    for index in range(last_pair + 1):
        wait_for(arrived.at[:, :, lanes(index)], pair_send.at[index])
    query_copy.wait()
    pair_copy.wait()
    middle_out.wait()
    finish_move()


def backward(wholes, low_two, cotangent, middle, queries, own, other, context, low_one, bias, log_total, cosine, sine, gains, collective_id):
    attn_all, in_all, out_all = wholes
    height, third = out_all.shape[1], attn_all.shape[1]
    count, width = queries.shape
    early = 3 * height // 32 * 16 + 16
    slot_buffers, slot_sems = slot_scratch(3 * height, early)
    buffers, sems = scatter_scratch([third] * 4)
    sem = pltpu.SemaphoreType.DMA
    anywhere = pl.BlockSpec(memory_space=pl.ANY)
    local = pl.BlockSpec(memory_space=pltpu.VMEM)
    bf16, f32 = jnp.bfloat16, jnp.float32
    shape, vmem = jax.ShapeDtypeStruct, pltpu.VMEM
    outs = pl.pallas_call(
        backward_kernel,
        out_shape=[shape((rows, 128), f32) for rows in (3 * third, third, 2 * height, height)]
        + [
            shape((count, width), bf16),
            shape((2, count, width), bf16),
            shape((2, count // 2, width), bf16),
            shape((count, width), f32),
            shape((1, width), f32),
            shape((4, 3 * height, width), bf16),
        ]
        + [shape(attn_all.shape, bf16)] * 4,
        in_specs=[anywhere] * 11 + [local] * 5,
        out_specs=[local] * 4 + [anywhere] * 4 + [local] + [anywhere] * 5,
        scratch_shapes=[vmem((count, width), bf16)] * 4
        + [vmem((2, count, width), bf16)] * 2
        + [vmem((count, width), bf16)] * 3
        + [vmem((2, count, width), bf16)] * 3
        + [vmem((2, third, width), bf16)]
        + [vmem((count, width), f32)] * 2
        + [vmem((2, 64, width), f32)]
        + slot_buffers
        + slot_sems
        + buffers
        + sems
        + [sem((8,)), sem((8,)), sem((2,)), sem((5,)), sem((3,)), sem((2, 3)), sem((2, 3)), sem((2,))]
        + [sem((2,)), sem((2,)), sem],
        compiler_params=pltpu.CompilerParams(
            collective_id=collective_id, has_side_effects=True, vmem_limit_bytes=62 * 1024 * 1024
        ),
        name="backward",
    )(in_all, out_all, attn_all, low_two, cotangent, middle, queries, own, other, context, low_one, bias, log_total, cosine, sine, gains)
    return outs[:9]


def attend_back_pair(columns, queries, own, other, bias, grad, context, log_total, cosine, sine, grad_query, grad_own, grad_other):
    count = queries.shape[0]
    query_rows, grad_rows = queries[:, columns], grad[:, columns]
    query_turned, grad_turned = query_rows.T, grad_rows.T
    inner = (grad_rows.astype(jnp.float32) * context[:, columns].astype(jnp.float32)).T
    query_parts = [None, None]
    for half, (pair, result) in enumerate(((own, grad_own), (other, grad_other))):
        keys, values = pair[0, :, columns], pair[1, :, columns]
        key_turned = keys.T
        grad_keys, grad_values = None, None
        window = pl.ds(half * count, count)
        for head in range(2):
            lanes_of_head = slice(64 * head, 64 * head + 64)
            scores = scores_of(keys, head_rows(query_turned, head), bias[window])
            weights = jnp.exp(scores - log_total[head : head + 1])
            grad_weights = product_of(values, head_rows(grad_turned, head), ((1,), (0,)))
            inner_row = jnp.sum(inner[lanes_of_head], axis=0, keepdims=True)
            grad_scores = low(weights * (grad_weights - inner_row))
            value_part = product_of(low(weights), head_lanes(grad_rows, head), ((1,), (0,)))
            key_part = product_of(grad_scores, head_lanes(query_rows, head), ((1,), (0,)))
            query_part = product_of(key_turned[lanes_of_head], grad_scores, ((1,), (0,)))
            grad_values = value_part if head == 0 else grad_values + value_part
            grad_keys = key_part if head == 0 else grad_keys + key_part
            query_parts[head] = query_part if half == 0 else query_parts[head] + query_part
        result[0, :, columns] = turned(grad_keys, cosine[window], -sine[window]).astype(result.dtype)
        result[1, :, columns] = grad_values.astype(result.dtype)
    query_rows = jnp.concatenate(query_parts, axis=0).T * SCORE_SCALE
    own_rows = pl.ds(0, count)
    grad_query[:, columns] = low(turned(query_rows, cosine[own_rows], -sine[own_rows]))


def product_of(left, right, dims):
    return lax.dot_general(left, right, (dims, ((), ())), preferred_element_type=jnp.float32)

def tiles_of(like):
    if len(like.shape) == 2 and like.shape[1] == 128:
        return [(pl.ds(0, like.shape[0]), (slice(None), slice(None)), True)]
    width = like.shape[-1]
    tiles = []
    for part in range(like.shape[0] if len(like.shape) == 3 else 1):
        for first in range(0, width, 128):
            columns = slice(first, first + 128)
            place = (part, slice(None), columns) if len(like.shape) == 3 else (slice(None), columns)
            tiles.append((pl.ds(part * width + first, 128), place, False))
    return tiles


def optimize_kernel(heights, *refs):
    refs = list(refs)
    count, size, tile = len(heights), 1024, 256
    f32, bf16 = jnp.float32, jnp.bfloat16
    sums, moments = take(refs, count), take(refs, count)
    (gain_two, gains), far = take(refs, 2), take(refs, 7)
    far = far[:4] + [far[4].at[0], far[4].at[1]] + far[5:]
    backs, (gain_out, rows_out), blocks = take(refs, count), take(refs, 2), take(refs, count)
    whole, steps, gain_parts = take(refs, 3)
    iterate, poly, product, total = take(refs, 4)
    iterate_low, poly_low, other_low, total_low = take(refs, 4)
    value_rows, rows_in, rows_low = take(refs, 3)
    load_sem, own_sem, send_z, recv_z, send_x, recv_x, send_y, recv_y, send_d, recv_d, send_c, recv_c = take(refs, 12)
    send_g, recv_g, back_sem, send_b, recv_b, move_send, move_recv, move_own = refs
    me, partner, across, down = neighbours()
    plane = lax.axis_index("tensor")
    diagonal = across + down - me
    planes = [lax.rem(plane + offset, 4) for offset in (1, 2, 3)]
    flip = lambda block: block + 1 - 2 * lax.rem(block, 2)
    half = rows_low.shape[0]
    start_move, finish_move = move_plan(True, rows_low, rows_out, move_send, move_recv, move_own)
    near = (
        poly_low, other_low, total_low, iterate_low.at[0:half], iterate_low.at[half : 2 * half],
        value_rows, rows_in, poly.at[0:half],
    )
    loads = [
        pltpu.make_async_copy(source, target, load_sem.at[index])
        for index, (source, target) in enumerate(zip(far, near))
    ]
    for load in loads:
        load.start()

    def place(part, slot, block):
        height = heights[part]
        return whole.at[pl.ds(pl.multiple_of(slot * height, 16), height), lanes(block)]

    def spread(part, source, slot):
        view = place(part, slot, me)
        send_to(source, view, send_x.at[slot], recv_x.at[slot], (across, plane))
        send_to(source, view, send_y.at[slot], recv_y.at[slot], (down, plane))
        send_to(source, view, send_c.at[slot, 0], recv_c.at[slot, 0], (partner, plane))

    def on_plane(body):
        for part in range(count):
            @pl.when(plane == part)
            def _():
                body(part)

    def off_plane(body):
        for part in range(count):
            @pl.when(plane != part)
            def _():
                body(part)

    greet(plane, (partner, across, down), planes)
    for part in (2, 0, 3, 1):
        for rows, place_of, is_turned in tiles_of(moments[part]):
            moment = moments[part][place_of]
            moment = moment if is_turned else moment.T
            blocks[part][rows] = low(MOMENTUM * moment + sums[part][rows])

        @pl.when(plane != part)
        def _():
            offset = lax.rem(plane + 3 - part, 4)
            send_to(blocks[part], place(part, plane, me), send_z.at[part], recv_z.at[offset], (me, part))

        @pl.when(plane == part)
        def _():
            pltpu.make_async_copy(blocks[part], place(part, part, me), own_sem).start()
            spread(part, blocks[part], part)

    def pass_z(part):
        for distance in (1, 3, 2):
            slot = (part + distance) % 4
            view = place(part, slot, me)
            wait_for(view, recv_z.at[(slot + 3 - part) % 4])
            spread(part, view, slot)

    on_plane(pass_z)

    for load in loads:
        load.wait()
    gain_out[1:2] = gain_two[...]
    gain_out[0:1] = jnp.zeros((1, size), f32)

    @pl.loop(0, half // 64)
    def _(index):
        first = pl.multiple_of(index * 64, 64)
        window = pl.ds(first, 64)
        other_window = pl.ds(pl.multiple_of(first + half, 64), 64)
        grad = product_of(iterate_low[window], poly_low[...], ((1,), (0,)))
        grad = grad + product_of(iterate_low[other_window], other_low[...], ((1,), (0,)))
        grad = grad + product_of(value_rows[window], total_low[...], ((1,), (0,)))
        rows = rows_in[window].astype(f32)
        centre = rows - jnp.mean(rows, axis=1, keepdims=True)
        inverse = lax.rsqrt(jnp.mean(centre * centre, axis=1, keepdims=True) + NORM_EPS)
        normed = centre * inverse
        scaled = grad * gains[0:1]
        mean_grad = jnp.mean(scaled, axis=1, keepdims=True)
        mean_cross = jnp.mean(scaled * normed, axis=1, keepdims=True)
        back = inverse * (scaled - mean_grad - normed * mean_cross)
        rows_low[window] = low(poly[window] + back)
        gain_out[0:1] += jnp.sum(grad * normed, axis=0, keepdims=True)

    start_move()
    for index, other in enumerate(planes):
        send_to(gain_out, gain_parts.at[index], send_g.at[index], recv_g.at[index], (me, other))

    def pass_xy(part):
        for slot in range(4):
            view = place(part, slot, across)
            wait_for(view, recv_x.at[slot])
            if slot < 2:
                send_to(view, view, send_d.at[slot], recv_d.at[slot], (down, plane))
            send_to(view, view, send_c.at[slot, 1], recv_c.at[slot, 1], (partner, plane))
            view = place(part, slot, down)
            wait_for(view, recv_y.at[slot])
            if slot >= 2:
                send_to(view, view, send_d.at[slot], recv_d.at[slot], (across, plane))
            send_to(view, view, send_c.at[slot, 2], recv_c.at[slot, 2], (partner, plane))

    on_plane(pass_xy)

    def pass_diagonal(part):
        for slot in range(4):
            view = place(part, slot, diagonal)
            wait_for(view, recv_d.at[slot])
            send_to(view, view, send_c.at[slot, 3], recv_c.at[slot, 3], (partner, plane))
        for slot in range(4):
            for index, block in enumerate((me, across, down, diagonal)):
                wait_for(place(part, slot, flip(block)), recv_c.at[slot, index])
        wait_for(blocks[part], own_sem)

    on_plane(pass_diagonal)

    windows = [pl.ds(first, tile) for first in range(0, size, tile)]
    zero = jnp.zeros((1, 1), f32)
    blank = jnp.zeros((1, size), f32)
    corner = lax.broadcasted_iota(jnp.int32, (tile, tile), 0) == lax.broadcasted_iota(jnp.int32, (tile, tile), 1)

    def gram(part):
        rows = slice(0, 4 * heights[part])
        for group in range(2):
            edge = group * size // 2

            @pl.loop(0, 2)
            def _(index):
                window = pl.ds(pl.multiple_of(edge + index * tile, tile), tile)
                iterate[window, edge:] = product_of(whole[rows, window], whole[rows, edge:], ((0,), (0,)))

    on_plane(gram)

    def upper(window):
        return slice(window.start, size)

    def store(window, result, shift, full, low_copy):
        corner_block = result[:, :tile] - jnp.where(corner, shift, 0.0)
        result = jnp.concatenate([corner_block, result[:, tile:]], axis=1) if result.shape[1] > tile else corner_block
        full[window, upper(window)] = result
        result_low = low(result)
        low_copy[window, upper(window)] = result_low
        for first in range(tile, result.shape[1], tile):
            low_copy[pl.ds(window.start + first, tile), window] = result_low[:, first : first + tile].T
        return result

    def fold(left, right, window):
        sums_of = jnp.sum(left * right, axis=0, keepdims=True)
        weighted = jnp.concatenate([sums_of[:, :tile], 2.0 * sums_of[:, tile:]], axis=1) if sums_of.shape[1] > tile else sums_of
        return jnp.concatenate([blank[:, : window.start], weighted], axis=1) if window.start else weighted

    def finish(row):
        return jnp.sum(row, axis=1, keepdims=True) / size

    def multiply(left, right, window):
        return product_of(left[window], right[:, upper(window)], ((1,), (0,)))

    trace = zero
    for window in windows:
        block = jnp.where(corner, iterate[window, window], 0.0)
        trace = trace + jnp.sum(jnp.sum(block, axis=0, keepdims=True), axis=1, keepdims=True)
    factor = 1.0 / (jnp.sqrt(trace) + NORM_FLOOR)
    squared = factor * factor
    mean = trace * squared / size
    row = blank
    for window in windows:
        rest = store(window, iterate[window, upper(window)] * squared, mean, iterate, iterate_low)
        row = row + fold(rest, rest, window)
    square = finish(row)

    def polynomial(mean, square, with_total):
        linear = QUINTIC_THREE + 2.0 * QUINTIC_FIVE * mean
        shift = QUINTIC_FIVE * square
        poly_mean = QUINTIC_ONE + QUINTIC_THREE * mean + QUINTIC_FIVE * (mean * mean) + shift
        row, total_row = blank, blank
        for window in windows:
            mine = iterate[window, upper(window)]
            rest = linear * mine + QUINTIC_FIVE * multiply(iterate_low, iterate_low, window)
            rest = store(window, rest, shift, poly, poly_low)
            row = row + fold(rest, mine, window)
            if with_total:
                total_row = total_row + fold(rest, total[window, upper(window)], window)
        return (poly_mean, finish(row), finish(total_row))

    def grow_total(poly_mean, total_mean, cross):
        for window in windows:
            result = poly_mean * total[window, upper(window)] + total_mean * poly[window, upper(window)]
            result = result + multiply(poly_low, total_low, window)
            store(window, result, cross, total, other_low)
        total_low[...] = other_low[...]
        return poly_mean * total_mean + cross

    def advance(poly_mean, mean, cross):
        row = blank
        for window in windows:
            rest = poly[window, upper(window)]
            result = poly_mean * iterate[window, upper(window)] + mean * rest
            result = result + multiply(poly_low, iterate_low, window)
            result = store(window, result, cross, product, other_low)
            row = row + fold(result, rest, window)
        product_mean = poly_mean * mean + cross
        cross = finish(row)
        row = blank
        for window in windows:
            result = poly_mean * product[window, upper(window)] + product_mean * poly[window, upper(window)]
            result = result + multiply(poly_low, other_low, window)
            result = store(window, result, cross, iterate, iterate_low)
            row = row + fold(result, result, window)
        return (poly_mean * product_mean + cross, finish(row))

    total_mean, cross, _ = polynomial(mean, square, False)
    for window in windows:
        total[window, upper(window)] = poly[window, upper(window)]
    total_low[...] = poly_low[...]
    mean, square = advance(total_mean, mean, cross)

    def sweep(_, carry):
        mean, square, total_mean = carry
        poly_mean, cross, cross_total = polynomial(mean, square, True)
        total_mean = grow_total(poly_mean, total_mean, cross_total)
        return advance(poly_mean, mean, cross) + (total_mean,)

    mean, square, total_mean = lax.fori_loop(0, NS_ITERS - 2, sweep, (mean, square, total_mean))
    poly_mean, _, cross_total = polynomial(mean, square, True)
    total_mean = grow_total(poly_mean, total_mean, cross_total)

    mine = lanes(me)
    columns = total_low[:, mine]

    def step_home(part):
        height = heights[part]

        @pl.loop(0, 4)
        def _(turn_of):
            slot = lax.rem(part + 1 + turn_of, 4)
            window = pl.ds(pl.multiple_of(slot * height, 16), height)
            result = product_of(whole[window, :], columns, ((1,), (0,)))
            result = result + total_mean * whole[window, mine].astype(f32)
            steps[window, :] = low(factor * result)

            @pl.when(turn_of == 3)
            def _():
                pltpu.make_async_copy(steps.at[window, :], backs[part], back_sem).start()

            @pl.when(turn_of < 3)
            def _():
                send_to(steps.at[window, :], backs[part], send_b.at[turn_of], recv_b.at[part], (me, slot))

    on_plane(step_home)

    for index in range(3):
        wait_for(gain_out, send_g.at[index])
        wait_for(gain_parts.at[index], recv_g.at[index])
    gain_out[...] = gain_out[...] + gain_parts[0] + gain_parts[1] + gain_parts[2]
    for index, other in ((3, across), (4, down), (5, partner)):
        send_to(gain_out, gain_parts.at[index], send_g.at[index], recv_g.at[index], (other, plane))
        wait_for(gain_out, send_g.at[index])
        wait_for(gain_parts.at[index], recv_g.at[index])
        gain_out[...] = gain_out[...] + gain_parts[index]

    on_plane(lambda part: wait_for(backs[part], back_sem))
    off_plane(lambda part: wait_for(backs[part], recv_b.at[part]))
    def last_waits(part):
        for slot in range(4):
            for sem in (send_x.at[slot], send_y.at[slot], send_d.at[slot]):
                wait_for(blocks[part], sem)
            for index in range(4):
                wait_for(blocks[part], send_c.at[slot, index])
        for index in range(3):
            wait_for(blocks[part], send_b.at[index])

    on_plane(last_waits)
    off_plane(lambda part: wait_for(blocks[part], send_z.at[part]))
    finish_move()


def optimize(sums, moments, gain_two, gains, far, collective_id):
    heights = [part.shape[0] for part in sums]
    count, size = len(heights), gains.shape[1]
    f32, bf16 = jnp.float32, jnp.bfloat16
    sem = pltpu.SemaphoreType.DMA
    anywhere = pl.BlockSpec(memory_space=pl.ANY)
    local = pl.BlockSpec(memory_space=pltpu.VMEM)
    half = far[5].shape[0]
    outs = pl.pallas_call(
        functools.partial(optimize_kernel, heights),
        out_shape=[jax.ShapeDtypeStruct((height, 128), bf16) for height in heights]
        + [jax.ShapeDtypeStruct(gains.shape, f32), jax.ShapeDtypeStruct((2, half // 2, size), bf16)],
        in_specs=[local] * (2 * count + 2) + [anywhere] * 7,
        out_specs=[local] * (count + 1) + [anywhere],
        scratch_shapes=[pltpu.VMEM((height, 128), bf16) for height in heights]
        + [pltpu.VMEM((4 * max(heights), size), bf16), pltpu.VMEM((4 * max(heights), 128), bf16)]
        + [pltpu.VMEM((6,) + gains.shape, f32)]
        + [pltpu.VMEM((size, size), f32)] * 4
        + [pltpu.VMEM((size, size), bf16)] * 4
        + [pltpu.VMEM((half, size), bf16)] * 3
        + [sem((8,)), sem, sem((count,)), sem((3,))]
        + [sem((4,))] * 6
        + [sem((4, 4))] * 2
        + [sem((6,))] * 2
        + [sem, sem((3,)), sem((count,)), sem((2,)), sem((2,)), sem],
        compiler_params=pltpu.CompilerParams(
            collective_id=collective_id, has_side_effects=True, vmem_limit_bytes=60 * 1024 * 1024
        ),
        name="optimize",
    )(*sums, *moments, gain_two, gains, *far)
    return (outs[:count], outs[count], outs[count + 1])


def settle_kernel(*refs):
    refs = list(refs)
    sums, steps, moments, weights = (take(refs, 4) for _ in range(4))
    new_moments, new_weights = take(refs, 4), take(refs, 4)
    for part in range(4):
        rate = MUON_RATE * 0.2 * math.sqrt(4 * sums[part].shape[0])
        for rows, place, is_turned in tiles_of(moments[part]):
            gradient, step = sums[part][rows], steps[part][rows].astype(jnp.float32)
            if not is_turned:
                gradient, step = gradient.T, step.T
            kept = weights[part][place].astype(jnp.float32) * (1.0 - MUON_RATE * DECAY_RATE)
            new_moments[part][place] = MOMENTUM * moments[part][place] + gradient
            new_weights[part][place] = kept - rate * step


def settle(sums, steps, moments, weights):
    local = pl.BlockSpec(memory_space=pltpu.VMEM)
    shapes = [jax.ShapeDtypeStruct(moment.shape, jnp.float32) for moment in moments]
    outs = pl.pallas_call(
        settle_kernel,
        out_shape=shapes * 2,
        in_specs=[local] * 16,
        out_specs=[local] * 8,
        compiler_params=pltpu.CompilerParams(vmem_limit_bytes=48 * 1024 * 1024),
        name="settle",
    )(*sums, *steps, *moments, *weights)
    return (outs[:4], outs[4:])


def weight_shards(weights):
    shards = [turn(weight) for weight in weights]
    third = shards[0].shape[0] // 3
    return [shards[0][third * part : third * part + third] for part in range(3)] + shards[1:]


def gather_weights(shards):
    tensor_count, dp_count = lax.axis_size("tensor"), lax.axis_size("dp")
    wholes = [lax.all_gather(shard, ("tensor", "dp")) for shard in shards]
    wholes = [
        whole.reshape(tensor_count, dp_count, *whole.shape[1:]).transpose(0, 2, 1, 3)
        for whole in wholes
    ]
    return [whole.reshape(*whole.shape[:2], -1) for whole in wholes]


def reduce_grads(grads):
    tensor_count, dp_count = lax.axis_size("tensor"), lax.axis_size("dp")
    sums = []
    for grad in grads:
        blocks = grad.reshape(*grad.shape[:2], dp_count, -1).transpose(0, 2, 1, 3)
        blocks = blocks.reshape(-1, *blocks.shape[2:])
        part = lax.psum_scatter(blocks, ("tensor", "dp"), scatter_dimension=0, tiled=True)
        sums.append(part[0].astype(jnp.float32))
    return sums


def lane_of(shape):
    return lax.broadcasted_iota(jnp.int32, shape, 1)

def turned(vectors, cosine, sine):
    lane = lax.rem(lane_of(vectors.shape), 64)
    swapped = jnp.where(lane < 32, pltpu.roll(vectors, 96, 1), pltpu.roll(vectors, 32, 1))
    return vectors * cosine + swapped * sine

def project_kernel(rows, query_weight, key_weight, value_weight, cosine, sine, queries, pair):
    rows = rows[...]
    for weight, target in ((query_weight, 0), (key_weight, 1)):
        result = product_of(rows, weight[0], ((1,), (1,)))
        for first in range(0, result.shape[1], 128):
            part = turned(result[:, first : first + 128], cosine[...], sine[...])
            if target == 0:
                queries[:, first : first + 128] = low(part * SCORE_SCALE)
            else:
                pair[0, :, first : first + 128] = low(part)
    pair[1] = low(product_of(rows, value_weight[0], ((1,), (1,))))

def project(rows, query_weight, key_weight, value_weight, cosine, sine):
    count, width = rows.shape
    groups, height, _ = query_weight.shape
    whole = lambda *shape: pl.BlockSpec(shape, lambda i: (0,) * len(shape))
    weight = pl.BlockSpec((1, height, width), lambda i: (i, 0, 0))
    return pl.pallas_call(
        project_kernel,
        grid=(groups,),
        out_shape=[jax.ShapeDtypeStruct((count, width), jnp.bfloat16), jax.ShapeDtypeStruct((2, count, width), jnp.bfloat16)],
        in_specs=[whole(count, width), weight, weight, weight, whole(count, 128), whole(count, 128)],
        out_specs=[pl.BlockSpec((count, height), lambda i: (0, i)), pl.BlockSpec((2, count, height), lambda i: (0, 0, i))],
        compiler_params=pltpu.CompilerParams(vmem_limit_bytes=40 * 1024 * 1024),
        name="project",
    )(rows, query_weight, key_weight, value_weight, cosine, sine)

def head_rows(transposed, head):
    rows = lax.broadcasted_iota(jnp.int32, transposed.shape, 0)
    return jnp.where(lax.div(rows, 64) == head, transposed, jnp.zeros_like(transposed))

def head_lanes(values, head):
    return jnp.where(lax.div(lane_of(values.shape), 64) == head, values, jnp.zeros_like(values))

def scores_of(keys, queries_turned, bias):
    scores = product_of(keys, queries_turned, ((1,), (0,)))
    return scores + jnp.concatenate([bias] * (scores.shape[1] // 128), axis=1)

def attend_kernel(queries, own, other, bias, context, log_total):
    query_turned = queries[...].T
    keys = jnp.concatenate([own[0], other[0]], axis=0)
    value_turned = jnp.concatenate([own[1].T, other[1].T], axis=1)
    parts, logs = [], []
    for head in range(2):
        scores = scores_of(keys, head_rows(query_turned, head), bias[...])
        highest = jnp.max(scores, axis=0, keepdims=True)
        weights = jnp.exp(scores - highest)
        total = jnp.sum(weights, axis=0, keepdims=True)
        part = product_of(value_turned[64 * head : 64 * head + 64], low(weights), ((1,), (0,)))
        parts.append(part / total)
        logs.append(highest + jnp.log(total))
    context[...] = low(jnp.concatenate(parts, axis=0)).T
    log_total[0] = jnp.concatenate(logs + logs * 3, axis=0)

def attend(queries, own, other, bias):
    count, width = queries.shape
    pairs = width // 128
    column = pl.BlockSpec((count, 128), lambda i: (0, i))
    double = pl.BlockSpec((2, count, 128), lambda i: (0, 0, i))
    return pl.pallas_call(
        attend_kernel,
        grid=(pairs,),
        out_shape=[jax.ShapeDtypeStruct((count, width), jnp.bfloat16), jax.ShapeDtypeStruct((pairs, 8, count), jnp.float32)],
        in_specs=[column, double, double, pl.BlockSpec((2 * count, 128), lambda i: (0, 0))],
        out_specs=[column, pl.BlockSpec((1, 8, count), lambda i: (i, 0, 0))],
        compiler_params=pltpu.CompilerParams(vmem_limit_bytes=40 * 1024 * 1024),
        name="attend",
    )(queries, own, other, bias)

def attend_back_kernel(queries, own, other, bias, grad, context, log_total, cosine, sine, grad_query, grad_own, grad_other):
    count = queries.shape[0]
    query_turned, grad_turned = queries[...].T, grad[...].T
    inner = (grad[...].astype(jnp.float32) * context[...].astype(jnp.float32)).T
    query_parts = [None, None]
    for half, (pair, result) in enumerate(((own, grad_own), (other, grad_other))):
        keys, values = pair[0], pair[1]
        key_turned = keys.T
        grad_keys, grad_values = None, None
        window = pl.ds(half * count, count)
        for head in range(2):
            lanes_of_head = slice(64 * head, 64 * head + 64)
            scores = scores_of(keys, head_rows(query_turned, head), bias[window])
            weights = jnp.exp(scores - log_total[0, head : head + 1])
            grad_weights = product_of(values, head_rows(grad_turned, head), ((1,), (0,)))
            inner_row = jnp.sum(inner[lanes_of_head], axis=0, keepdims=True)
            grad_scores = low(weights * (grad_weights - inner_row))
            value_part = product_of(low(weights), head_lanes(grad[...], head), ((1,), (0,)))
            key_part = product_of(grad_scores, head_lanes(queries[...], head), ((1,), (0,)))
            query_part = product_of(key_turned[lanes_of_head], grad_scores, ((1,), (0,)))
            grad_values = value_part if head == 0 else grad_values + value_part
            grad_keys = key_part if head == 0 else grad_keys + key_part
            query_parts[head] = query_part if half == 0 else query_parts[head] + query_part
        result[0] = turned(grad_keys, cosine[window], -sine[window]).astype(result.dtype)
        result[1] = grad_values.astype(result.dtype)
    grad_rows = jnp.concatenate(query_parts, axis=0).T * SCORE_SCALE
    own_rows = pl.ds(0, count)
    grad_query[...] = low(turned(grad_rows, cosine[own_rows], -sine[own_rows]))

def attend_back(queries, own, other, bias, grad, context, log_total, cosine, sine):
    count, width = queries.shape
    pairs = width // 128
    column = pl.BlockSpec((count, 128), lambda i: (0, i))
    double = pl.BlockSpec((2, count, 128), lambda i: (0, 0, i))
    table = pl.BlockSpec((2 * count, 128), lambda i: (0, 0))
    return pl.pallas_call(
        attend_back_kernel,
        grid=(pairs,),
        out_shape=[
            jax.ShapeDtypeStruct((count, width), jnp.bfloat16),
            jax.ShapeDtypeStruct((2, count, width), jnp.float32),
            jax.ShapeDtypeStruct((2, count, width), jnp.bfloat16),
        ],
        in_specs=[column, double, double, table, column, column, pl.BlockSpec((1, 8, count), lambda i: (i, 0, 0)), table, table],
        out_specs=[column, double, double],
        compiler_params=pltpu.CompilerParams(vmem_limit_bytes=48 * 1024 * 1024),
        name="attend_back",
    )(queries, own, other, bias, grad, context, log_total, cosine, sine)

def feed_kernel(rows, cotangent, in_weight, out_weight, result, grad_rows, grad_in, grad_out):
    height = out_weight.shape[1]
    @pl.when(pl.program_id(0) == 0)
    def _():
        result[...] = jnp.zeros_like(result)
        grad_rows[...] = jnp.zeros_like(grad_rows)
    gate = product_of(in_weight[0, 0:height], rows[...], ((1,), (1,)))
    up = product_of(in_weight[0, height:], rows[...], ((1,), (1,)))
    grad_hidden = product_of(out_weight[0], cotangent[...], ((1,), (1,)))
    below = 0.5 + 0.5 * lax.erf(gate * math.sqrt(0.5))
    active = gate * below
    hidden = low(active * up)
    slope = below + gate * jnp.exp(-0.5 * gate * gate) * (1.0 / math.sqrt(2.0 * math.pi))
    grad_gate = low(grad_hidden * up * slope)
    grad_up = low(grad_hidden * active)
    grad_out[0] = low(product_of(hidden, cotangent[...], ((1,), (0,))))
    grad_in[0, 0:height] = low(product_of(grad_gate, rows[...], ((1,), (0,))))
    grad_in[0, height:] = low(product_of(grad_up, rows[...], ((1,), (0,))))
    result[...] += product_of(hidden, out_weight[0], ((0,), (0,)))
    grad_rows[...] += product_of(grad_gate, in_weight[0, 0:height], ((0,), (0,)))
    grad_rows[...] += product_of(grad_up, in_weight[0, height:], ((0,), (0,)))

def feed(rows, cotangent, in_weight, out_weight):
    count, width = rows.shape
    groups, height, _ = out_weight.shape
    whole = pl.BlockSpec((count, width), lambda i: (0, 0))
    block = lambda size: pl.BlockSpec((1, size, width), lambda i: (i, 0, 0))
    return pl.pallas_call(
        feed_kernel,
        grid=(groups,),
        out_shape=[
            jax.ShapeDtypeStruct((count, width), jnp.float32),
            jax.ShapeDtypeStruct((count, width), jnp.float32),
            jax.ShapeDtypeStruct(in_weight.shape, jnp.bfloat16),
            jax.ShapeDtypeStruct(out_weight.shape, jnp.bfloat16),
        ],
        in_specs=[whole, whole, block(2 * height), block(height)],
        out_specs=[whole, whole, block(2 * height), block(height)],
        compiler_params=pltpu.CompilerParams(vmem_limit_bytes=60 * 1024 * 1024),
        name="feed",
    )(rows, cotangent, in_weight, out_weight)


def turn(block):
    return block.transpose(*range(1, block.ndim), 0).reshape(-1, block.shape[0])


def turn_back(rows, like):
    rows = rows.reshape(*like.shape[1:], like.shape[0])
    return rows.transpose(rows.ndim - 1, *range(rows.ndim - 1))


def orthogonal_steps(blocks, gain_part):
    tensor_count = lax.axis_size("tensor")
    heights = [block.shape[0] for block in blocks]
    row_count = blocks[0].shape[1]
    first_row = lax.axis_index("dp") * row_count
    gain_grad = lax.psum(gain_part, BOTH)
    widest = max(heights)
    stacked = jnp.stack(
        [jnp.pad(block.T, ((0, 0), (0, widest - block.shape[0]))) for block in blocks]
    )
    owned = lax.all_to_all(stacked, "tensor", split_axis=0, concat_axis=0, tiled=True)
    whole = lax.all_gather(owned, "dp", axis=1, tiled=True)
    mean, rest = newton_schulz(einsum("tik,tjk->ij", whole, whole))
    own_rows = lax.dynamic_slice_in_dim(rest, first_row, row_count, 0)
    own_whole = lax.dynamic_slice_in_dim(whole, first_row, row_count, 1)
    step_rows = low(einsum("ij,tjk->tik", low(own_rows), whole) + mean * own_whole)
    returned = lax.all_to_all(step_rows, "tensor", split_axis=0, concat_axis=0, tiled=True)
    return ([returned[index, :, :height].T for index, height in enumerate(heights)], gain_grad)


def view_of(block):
    if block.shape[-1] % 128:
        return turn(block)
    return block.transpose(1, 0, 2) if block.ndim == 3 else block


def unview(view, like):
    if like.shape[-1] % 128:
        return turn_back(view, like)
    return view.transpose(1, 0, 2) if like.ndim == 3 else view


def on_device(
    inputs,
    cotangent,
    lengths,
    qkv_weight,
    attn_out_weight,
    ffn_in_weight,
    ffn_out_weight,
    norm_gains,
    qkv_moment,
    attn_out_moment,
    ffn_in_moment,
    ffn_out_moment,
    gain_first,
    gain_second,
):
    tensor_count = lax.axis_size("tensor")
    dp_count = lax.axis_size("dp")
    dp_index = lax.axis_index("dp")
    tensor_index = lax.axis_index("tensor")
    core = dp_index % 2
    odd = tensor_index % 2 == 1
    upper = tensor_index >= tensor_count // 2
    lists = exchange_lists(dp_count // 2, tensor_count)
    weights = (qkv_weight, attn_out_weight, ffn_in_weight, ffn_out_weight)
    row_count = qkv_weight.shape[0]

    width = inputs.shape[3]
    local_rows = 2 * inputs.shape[2]
    fits = (tensor_count, dp_count, row_count, width) == (4, 8, 128, 1024)
    positions = jnp.concatenate(
        [core * local_rows + jnp.arange(local_rows), (1 - core) * local_rows + jnp.arange(local_rows)]
    )
    shards = weight_shards(weights)
    if fits:
        sizes = lengths.astype(jnp.float32)
        sizes = jnp.broadcast_to(jnp.pad(sizes, ((0, 6), (0, 0))), (8, 128))
        exponents = np.arange(HEAD_DIM // 2, dtype=np.float32) / np.float32(HEAD_DIM // 2)
        frequency = np.power(np.float32(ROPE_BASE), -exponents).astype(np.float32)
        frequency = jnp.asarray(np.tile(frequency, (8, 4)))
        outs = forward(shards, inputs[:, 0], cotangent[:, 0], sizes, norm_gains, frequency, 1)
        wholes, (rows_low, cotangent_low) = outs[:6], outs[6:8]
        low_one, queries, own, other, context, log_total, bias, middle, low_two = outs[8:17]
        cosine, sine = outs[17:]
    else:
        cosine, sine = rotary(positions)
        wholes = gather_weights(shards)
        rows_low = to_sequences(inputs[:, 0], lists, odd, upper)
        cotangent_low = to_sequences(cotangent[:, 0], lists, odd, upper)
    query_all, key_all, value_all, attn_all, ffn_in_all, ffn_out_all = wholes
    attn_rows = attn_all.reshape(-1, width)
    rows_in = rows_low.astype(jnp.float32)
    grad_rows = cotangent_low.astype(jnp.float32)
    normed_one, inverse_one, scaled_one = layer_norm_parts(rows_in, norm_gains[0])
    if not fits:
        own_lengths = swap_partner(lengths)
        both_lengths = jnp.where(
            core == 0,
            jnp.concatenate([lengths, own_lengths], 1),
            jnp.concatenate([own_lengths, lengths], 1),
        )
        length = lax.dynamic_index_in_dim(both_lengths.reshape(-1), tensor_index, 0, keepdims=False)
        bias = jnp.where(positions < length, 0.0, MASK_VALUE).astype(jnp.float32)
        bias = jnp.broadcast_to(bias[:, None], (positions.shape[0], 128))
        low_one = low(scaled_one)
        queries, own = project(
            low_one, query_all, key_all, value_all, cosine[:local_rows], sine[:local_rows]
        )
        other = swap_partner(own)
        context, log_total = attend(queries, own, other, bias)
        middle = rows_in + einsum("sk,kn->sn", context, attn_rows)
    normed_two, inverse_two, scaled_two = layer_norm_parts(middle, norm_gains[1])
    if not fits:
        low_two = low(scaled_two)
    if fits:
        outs = backward(
            (attn_all, ffn_in_all, ffn_out_all),
            low_two,
            cotangent_low,
            middle,
            queries,
            own,
            other,
            context,
            low_one,
            bias,
            log_total,
            cosine,
            sine,
            norm_gains,
            2,
        )
        sums, (grad_query, grad_pair, outputs, grad_middle, gain_two) = outs[:4], outs[4:]
    else:
        ffn_branch, grad_scaled_two, grad_ffn_in, grad_ffn_out = feed(
            low_two, cotangent_low, ffn_in_all, ffn_out_all
        )
        result = low(middle + ffn_branch)
        grad_from_two, gain_two = layer_norm_back(
            grad_scaled_two, normed_two, inverse_two, norm_gains[1]
        )
        grad_middle = grad_rows + grad_from_two
        grad_branch = low(grad_middle)
        grad_context = low(einsum("sn,kn->sk", grad_branch, attn_rows))
        grad_attn_out = low(einsum("sk,sn->kn", context, grad_branch)).reshape(attn_all.shape)
        grad_query, grad_own, grad_other = attend_back(
            queries, own, other, bias, grad_context, context, log_total, cosine, sine
        )
        grad_pair = low(grad_own + swap_partner(grad_other).astype(jnp.float32))
    moments = (qkv_moment, attn_out_moment, ffn_in_moment, ffn_out_moment)
    grad_parts = (grad_query, grad_pair[0], grad_pair[1])
    weight_parts = [part.reshape(-1, width) for part in (query_all, key_all, value_all)]
    if fits:
        far = (*weight_parts, grad_query, grad_pair, rows_low, grad_middle)
        viewed = [view_of(moment) for moment in moments]
        steps, gain_grad, input_grad = optimize(sums, viewed, gain_two, norm_gains, far, 3)
        outs = settle(sums, steps, viewed, [view_of(weight) for weight in weights])
        new_moments, new_weights = (
            [unview(part, like) for part, like in zip(parts, moments)] for parts in outs
        )
    else:
        grad_scaled_one = sum(
            einsum("sk,kn->sn", part, weight) for part, weight in zip(grad_parts, weight_parts)
        )
        grad_from_one, gain_one = layer_norm_back(
            grad_scaled_one, normed_one, inverse_one, norm_gains[0]
        )
        grads = [low(einsum("sk,sn->kn", part, low_one)) for part in grad_parts]
        grads = [grad.reshape(query_all.shape) for grad in grads]
        sums = reduce_grads(grads + [grad_attn_out, grad_ffn_in, grad_ffn_out])
        sums = [jnp.concatenate(sums[:3])] + list(sums[3:])
        outputs = from_sequences(result, lists, odd, upper)
        input_grad = from_sequences(low(grad_middle + grad_from_one), lists, odd, upper)
        turned_sums = [turn_back(part, moment) for part, moment in zip(sums, moments)]
        new_moments = [MOMENTUM * moment + part for moment, part in zip(moments, turned_sums)]
        steps, gain_grad = orthogonal_steps(
            [low(turn(moment)) for moment in new_moments], jnp.stack([gain_one, gain_two])
        )
        new_weights = [
            weight.astype(jnp.float32) * (1.0 - MUON_RATE * DECAY_RATE)
            - MUON_RATE
            * 0.2
            * math.sqrt(step.shape[0] * tensor_count)
            * turn_back(step, weight).astype(jnp.float32)
            for weight, step in zip(weights, steps)
        ]
    outputs, input_grad = outputs[:, None], input_grad[:, None].astype(jnp.float32)
    gain_first_new = BETA_ONE * gain_first + (1.0 - BETA_ONE) * gain_grad
    gain_second_new = BETA_TWO * gain_second + (1.0 - BETA_TWO) * gain_grad * gain_grad
    first_hat = gain_first_new / (1.0 - BETA_ONE**STEP)
    second_hat = gain_second_new / (1.0 - BETA_TWO**STEP)
    norm_gains_new = norm_gains - ADAM_RATE * (
        first_hat / (jnp.sqrt(second_hat) + ADAM_EPS) + DECAY_RATE * norm_gains
    )
    return (
        outputs,
        input_grad,
        new_moments[0],
        new_weights[0],
        new_moments[1],
        new_weights[1],
        new_moments[2],
        new_weights[2],
        new_moments[3],
        new_weights[3],
        gain_first_new,
        gain_second_new,
        norm_gains_new,
    )


def solution(mesh):
    in_specs = (
        P(None, "dp", "tensor", None),
        P(None, "dp", "tensor", None),
        P(None, "dp"),
        P("dp", None, "tensor"),
        P("dp", "tensor"),
        P("dp", None, "tensor"),
        P("dp", "tensor"),
        P(),
        P("dp", None, "tensor"),
        P("dp", "tensor"),
        P("dp", None, "tensor"),
        P("dp", "tensor"),
        P(),
        P(),
    )
    out_specs = (
        P(None, "dp", "tensor", None),
        P(None, "dp", "tensor", None),
        P("dp", None, "tensor"),
        P("dp", None, "tensor"),
        P("dp", "tensor"),
        P("dp", "tensor"),
        P("dp", None, "tensor"),
        P("dp", None, "tensor"),
        P("dp", "tensor"),
        P("dp", "tensor"),
        P(),
        P(),
        P(),
    )
    return jax.shard_map(
        on_device, mesh=mesh, in_specs=in_specs, out_specs=out_specs, check_vma=False
    )
```

```python
import functools
import math

import jax
import jax.numpy as jnp
import numpy as np
from jax import lax
from jax.experimental import pallas as pl
from jax.experimental.pallas import tpu as pltpu
from jax.sharding import PartitionSpec as P

HEAD_DIM = 64
NS_ITERS = 5
STEP = 10
SCORE_SCALE = 1.0 / math.sqrt(HEAD_DIM)


ROPE_BASE = 160000.0
NORM_EPS = 1e-05
MASK_VALUE = -1e30
MOMENTUM = 0.95
MUON_RATE = 0.1
DECAY_RATE = 0.01
QUINTIC_ONE = 3.4445
QUINTIC_THREE = -4.775
QUINTIC_FIVE = 2.0315
NORM_FLOOR = 1e-07
BETA_ONE = 0.9
BETA_TWO = 0.95
ADAM_RATE = 0.2
ADAM_EPS = 1e-08
BOTH = ("dp", "tensor")
MESH = pl.DeviceIdType.MESH


def rotary(positions):
    half_size = HEAD_DIM // 2
    exponents = jnp.arange(half_size).astype(jnp.float32) / half_size
    frequency = jnp.power(ROPE_BASE, -exponents)
    angles = positions.astype(jnp.float32)[:, None] * frequency[None, :]
    cosine, sine = jnp.cos(angles), jnp.sin(angles)
    return (
        jnp.concatenate([cosine] * 4, axis=1),
        jnp.concatenate([-sine, sine, -sine, sine], axis=1),
    )


def layer_norm_parts(vectors, gain):
    centre = vectors - jnp.mean(vectors, axis=-1, keepdims=True)
    inverse = lax.rsqrt(jnp.mean(centre * centre, axis=-1, keepdims=True) + NORM_EPS)
    normed = centre * inverse
    return (normed, inverse, normed * gain)


def layer_norm_back(grad_out, normed, inverse, gain):
    grad_normed = grad_out * gain
    mean_grad = jnp.mean(grad_normed, axis=-1, keepdims=True)
    mean_cross = jnp.mean(grad_normed * normed, axis=-1, keepdims=True)
    return (
        inverse * (grad_normed - mean_grad - normed * mean_cross),
        jnp.sum(grad_out * normed, axis=0),
    )


def einsum(spec, *operands):
    return jnp.einsum(spec, *operands, preferred_element_type=jnp.float32)


def low(values):
    return values.astype(jnp.bfloat16)


def exchange_lists(chip_count, tensor_count):
    first_list, second_list = [], []
    for chip in range(chip_count):
        for core in range(2):
            for slot in range(tensor_count):
                for micro in range(2):
                    source = (2 * chip + core) * tensor_count + slot
                    target = (2 * chip + slot // 2) * tensor_count + 2 * micro + core
                    pair = (source, target)
                    (first_list if slot % 2 == micro else second_list).append(pair)
    return (first_list, second_list)


def to_sequences(blocks, lists, odd, upper):
    first = lax.ppermute(jnp.where(odd, blocks[1], blocks[0]), BOTH, lists[0])
    second = lax.ppermute(jnp.where(odd, blocks[0], blocks[1]), BOTH, lists[1])
    return jnp.where(
        upper, jnp.concatenate([second, first]), jnp.concatenate([first, second])
    )


def from_sequences(rows, lists, odd, upper):
    half = rows.shape[0] // 2
    top, bottom = rows[:half], rows[half:]
    back = [[(target, source) for source, target in pairs] for pairs in lists]
    first = lax.ppermute(jnp.where(upper, bottom, top), BOTH, back[0])
    second = lax.ppermute(jnp.where(upper, top, bottom), BOTH, back[1])
    return jnp.where(odd, jnp.stack([second, first]), jnp.stack([first, second]))


def swap_partner(values):
    count = lax.axis_size("dp")
    return lax.ppermute(values, "dp", [(index, index ^ 1) for index in range(count)])


def mean_split(matrix):
    mean = jnp.trace(matrix) / matrix.shape[0]
    return (mean, matrix - mean * jnp.eye(matrix.shape[0], dtype=jnp.float32))


def split_product(left, right):
    left_mean, left_rest = left
    right_mean, right_rest = right
    product = einsum("ij,jk->ik", low(left_rest), low(right_rest))
    product = product + left_mean * right_rest + right_mean * left_rest
    mean, rest = mean_split(product)
    return (mean + left_mean * right_mean, rest)


def newton_schulz(gram):
    factor = 1.0 / (jnp.sqrt(jnp.trace(gram)) + NORM_FLOOR)
    iterate = mean_split(gram * (factor * factor))
    whole = None
    for sweep_index in range(NS_ITERS):
        square = split_product(iterate, iterate)
        poly = (
            QUINTIC_ONE + QUINTIC_THREE * iterate[0] + QUINTIC_FIVE * square[0],
            QUINTIC_THREE * iterate[1] + QUINTIC_FIVE * square[1],
        )
        whole = poly if whole is None else split_product(poly, whole)
        if sweep_index < NS_ITERS - 1:
            iterate = split_product(poly, split_product(poly, iterate))
    return (whole[0] * factor, whole[1] * factor)


def step_of(rows):
    return next(step for step in (128, 64, 48, 32, 16) if rows % step == 0)


def lanes(block):
    return pl.ds(pl.multiple_of(block * 128, 128), 128)

def neighbours():
    me = lax.axis_index("dp")
    core, across, down = lax.rem(me, 2), lax.rem(lax.div(me, 2), 2), lax.div(me, 4)
    return (me, me + 1 - 2 * core, me + 2 - 4 * across, me + 4 - 8 * down)

def greet(plane, others, planes):
    barrier = pltpu.get_barrier_semaphore()
    me = lax.axis_index("dp")
    crossed = list(others[:1])
    for other in others:
        pl.semaphore_signal(barrier, inc=1, device_id=(other, plane), device_id_type=MESH)
    for other in planes:
        for same_place in [me] + crossed:
            pl.semaphore_signal(barrier, inc=1, device_id=(same_place, other), device_id_type=MESH)
    return len(others) + len(planes) * (1 + len(crossed))


def greeted(total):
    pl.semaphore_wait(pltpu.get_barrier_semaphore(), total)

def add_into(target, source, rows, step):
    @pl.loop(0, rows // step)
    def _(index):
        window = pl.ds(pl.multiple_of(index * step, step), step)
        total = target[:, window].astype(jnp.float32) + source[:, window].astype(jnp.float32)
        target[:, window] = total.astype(jnp.bfloat16)


def send_to(source, target, send, recv, device):
    pltpu.make_async_remote_copy(
        source, target, send, recv, device_id=device, device_id_type=MESH
    ).start()


def wait_for(view, sem):
    pltpu.make_async_copy(view, view, sem).wait()


def move_plan(outward, source, target, send, recv, own):
    me, partner, _, _ = neighbours()
    plane = lax.axis_index("tensor")
    core = lax.rem(me, 2)
    column = me - core
    high, parity = lax.div(plane, 2), lax.rem(plane, 2)
    height = target.shape[1] if outward else source.shape[1]

    def owner_of(slot):
        return (column + parity, 2 * core + slot)

    def keeper_of(micro):
        return (column + high, 2 * micro + core)

    def same(device):
        return jnp.logical_and(device[0] == me, device[1] == plane)

    def half(rows, index):
        return rows.at[pl.ds(pl.multiple_of(index * height, height), height), :]

    def start():
        for index in range(2):
            if outward:
                device = owner_of(index)
                piece, goal, arrival = half(source, index), target.at[high], high
            else:
                device = keeper_of(index)
                piece, goal, arrival = source.at[index], half(target, parity), parity

            @pl.when(same(device))
            def _():
                pltpu.make_async_copy(piece, goal, own).start()

            @pl.when(jnp.logical_not(same(device)))
            def _():
                send_to(piece, goal, send.at[index], recv.at[arrival], device)

    def finish():
        for index in range(2):
            if outward:
                sent_to, came_from = owner_of(index), keeper_of(index)
                piece, goal = half(source, index), target.at[index]
            else:
                sent_to, came_from = keeper_of(index), owner_of(index)
                piece, goal = source.at[index], half(target, index)

            @pl.when(same(sent_to))
            def _():
                wait_for(piece, own)

            @pl.when(jnp.logical_not(same(sent_to)))
            def _():
                wait_for(piece, send.at[index])

            @pl.when(jnp.logical_not(same(came_from)))
            def _():
                wait_for(goal, recv.at[index])

    return (start, finish)


def scatter_plan(grads, sums, buffers, sems):
    held, from_x, from_y, from_yx, from_xy, from_z = buffers[:6]
    staging = buffers[6][0]
    (load_sem, send_c, recv_c, send_x, recv_x, send_y, recv_y, send_yx, recv_yx, send_xy, recv_xy, send_z, recv_z) = sems
    me, partner, across, down = neighbours()
    plane = lax.axis_index("tensor")
    planes = [lax.rem(plane + offset, 4) for offset in (1, 2, 3)]
    flip = lambda block: block + 1 - 2 * lax.rem(block, 2)
    blocks = (me, across, down, across + down - me)
    order = (3, 1, 2, 0)

    def view(part, block):
        ref, first, rows = grads[part]
        return ref.at[:, pl.ds(first, rows), lanes(block)]

    def slot(part, index):
        return staging.at[index, :, pl.ds(0, grads[part][2])]

    def stage_core(part):
        for index in order:
            send_to(view(part, flip(blocks[index])), held[part].at[index], send_c.at[part, index], recv_c.at[part, index], (partner, plane))

    def load(part):
        for index in order:
            pltpu.make_async_copy(view(part, blocks[index]), slot(part, index), load_sem.at[part, index]).start()

    def stage_first(part):
        rows = grads[part][2]
        load(part)
        for index in order:
            wait_for(slot(part, index), load_sem.at[part, index])
            wait_for(held[part].at[index], recv_c.at[part, index])
            add_into(held[part].at[index], slot(part, index), rows, step_of(rows))
            if index % 2 == 1:
                send_to(held[part].at[index, 0:2], from_x[part].at[index // 2], send_x.at[part, index // 2], recv_x.at[part, index // 2], (across, plane))
            if index // 2 == 1:
                send_to(held[part].at[index, 2:4], from_y[part].at[index % 2], send_y.at[part, index % 2], recv_y.at[part, index % 2], (down, plane))

    def stage_second(part):
        rows = grads[part][2]
        for side in (1, 0):
            wait_for(from_x[part].at[side], recv_x.at[part, side])
            add_into(held[part].at[2 * side, 0:2], from_x[part].at[side], rows, step_of(rows))
            if side == 1:
                send_to(held[part].at[2, 0:2], from_yx[part], send_yx.at[part], recv_yx.at[part], (down, plane))
            wait_for(from_y[part].at[side], recv_y.at[part, side])
            add_into(held[part].at[side, 2:4], from_y[part].at[side], rows, step_of(rows))
            if side == 1:
                send_to(held[part].at[1, 2:4], from_xy[part], send_xy.at[part], recv_xy.at[part], (across, plane))

    def stage_third(part):
        rows = grads[part][2]
        wait_for(from_yx[part], recv_yx.at[part])
        add_into(held[part].at[0, 0:2], from_yx[part], rows, step_of(rows))
        wait_for(from_xy[part], recv_xy.at[part])
        add_into(held[part].at[0, 2:4], from_xy[part], rows, step_of(rows))
        for index, other in enumerate(planes):
            send_to(held[part].at[0, other], from_z[part].at[index], send_z.at[part, index], recv_z.at[part, index], (me, other))

    def stage_last(part):
        rows = grads[part][2]
        step = step_of(rows)
        target, first = sums[part]
        for index in range(3):
            wait_for(from_z[part].at[index], recv_z.at[part, index])

        @pl.loop(0, rows // step)
        def _(index):
            offset = pl.multiple_of(index * step, step)
            window = pl.ds(offset, step)
            total = held[part][0, plane, window].astype(jnp.float32)
            for other in range(3):
                total = total + from_z[part][other, window].astype(jnp.float32)
            target[pl.ds(pl.multiple_of(first + offset, 16), step)] = total

    def finish(part):
        for index in range(4):
            wait_for(held[part].at[index], send_c.at[part, index])
        for side in range(2):
            wait_for(from_x[part].at[side], send_x.at[part, side])
            wait_for(from_y[part].at[side], send_y.at[part, side])
        wait_for(from_yx[part], send_yx.at[part])
        wait_for(from_xy[part], send_xy.at[part])
        for index in range(3):
            wait_for(from_z[part].at[index], send_z.at[part, index])

    return ((stage_core, stage_first, stage_second, stage_third, stage_last), finish)


def scatter_scratch(heights):
    sem = pltpu.SemaphoreType.DMA
    count = len(heights)
    leads = ((4, 4), (2, 2), (2, 2), (2,), (2,), (3,))
    buffers = [pltpu.VMEM(lead + (rows, 128), jnp.bfloat16) for lead in leads for rows in heights]
    buffers.append(pltpu.VMEM((4, 4, max(heights), 128), jnp.bfloat16))
    sems = [sem((count, 4))] * 3 + [sem((count, 2))] * 4 + [sem((count,))] * 4 + [sem((count, 3))] * 2
    return (buffers, sems)


def take(refs, count):
    taken, refs[:] = refs[:count], refs[count:]
    return taken


def gather_plan(shards, wholes, sems):
    own_sem, send_up, send_down, recv_z, send_x, recv_x, send_y, recv_y, send_d, recv_d, send_c, recv_c = sems
    me, partner, across, down = neighbours()
    plane = lax.axis_index("tensor")
    diagonal = across + down - me
    flip = lambda block: block + 1 - 2 * lax.rem(block, 2)

    def place(part, slot, block):
        return wholes[part].at[slot, :, lanes(block)]

    def spread(part, source, slot):
        view = place(part, slot, me)
        send_to(source, view, send_x.at[part, slot], recv_x.at[part, slot], (across, plane))
        send_to(source, view, send_y.at[part, slot], recv_y.at[part, slot], (down, plane))
        send_to(source, view, send_c.at[part, slot, 0], recv_c.at[part, slot, 0], (partner, plane))

    def pass_on(part, source, slot, upward):
        view = place(part, slot, me)
        sem = (send_up if upward else send_down).at[part, slot]
        send_to(source, view, sem, recv_z.at[part, slot], (me, plane + 1 if upward else plane - 1))

    def stage_own(part):
        pltpu.make_async_copy(shards[part], place(part, plane, me), own_sem.at[part]).start()

        @pl.when(plane < 3)
        def _():
            pass_on(part, shards[part], plane, True)

        @pl.when(plane > 0)
        def _():
            pass_on(part, shards[part], plane, False)

        spread(part, shards[part], plane)

    def stage_z(part):
        for distance in (1, 2, 3):
            for upward in (True, False):
                slot = plane - distance if upward else plane + distance

                @pl.when(slot >= 0 if upward else slot <= 3)
                def _():
                    view = place(part, slot, me)
                    wait_for(view, recv_z.at[part, slot])

                    @pl.when(plane < 3 if upward else plane > 0)
                    def _():
                        pass_on(part, view, slot, upward)

                    spread(part, view, slot)

    def stage_xy(part):
        for slot in range(4):
            view = place(part, slot, across)
            wait_for(view, recv_x.at[part, slot])
            if slot < 2:
                send_to(view, view, send_d.at[part, slot], recv_d.at[part, slot], (down, plane))
            send_to(view, view, send_c.at[part, slot, 1], recv_c.at[part, slot, 1], (partner, plane))
            view = place(part, slot, down)
            wait_for(view, recv_y.at[part, slot])
            if slot >= 2:
                send_to(view, view, send_d.at[part, slot], recv_d.at[part, slot], (across, plane))
            send_to(view, view, send_c.at[part, slot, 2], recv_c.at[part, slot, 2], (partner, plane))

    def stage_diagonal(part):
        for slot in range(4):
            view = place(part, slot, diagonal)
            wait_for(view, recv_d.at[part, slot])
            send_to(view, view, send_c.at[part, slot, 3], recv_c.at[part, slot, 3], (partner, plane))

    def arrive(part):
        wait_for(shards[part], own_sem.at[part])
        for slot in range(4):
            for index, block in enumerate((me, across, down, diagonal)):
                wait_for(place(part, slot, flip(block)), recv_c.at[part, slot, index])

    def finish(part):
        for slot in range(4):
            @pl.when(jnp.logical_and(slot <= plane, plane < 3))
            def _():
                wait_for(shards[part], send_up.at[part, slot])

            @pl.when(jnp.logical_and(slot >= plane, plane > 0))
            def _():
                wait_for(shards[part], send_down.at[part, slot])

            for sem in (send_x, send_y, send_d):
                wait_for(shards[part], sem.at[part, slot])
            for index in range(4):
                wait_for(shards[part], send_c.at[part, slot, index])

    return (stage_own, stage_z, stage_xy, stage_diagonal, arrive, finish)


def normed_rows(rows, gain):
    centre = rows - jnp.mean(rows, axis=1, keepdims=True)
    inverse = lax.rsqrt(jnp.mean(centre * centre, axis=1, keepdims=True) + NORM_EPS)
    return centre * inverse * gain


def forward_kernel(*refs):
    refs = list(refs)
    shards, (inputs, cotangent, lengths, gains, frequency) = take(refs, 6), take(refs, 5)
    wholes, (far_rows, grad_rows) = take(refs, 6), take(refs, 2)
    far = [far_rows] + take(refs, 4)
    context, log_total, bias, middle, low_two, cosine, sine = take(refs, 7)
    near = take(refs, 5)
    rows_low, low_one, queries, own, other = near
    other_lengths, weight, attn_weight = take(refs, 3)
    sems = take(refs, 12)
    pair_send, pair_recv, length_send, length_recv, weight_sem, attn_sem, out_sem = take(refs, 7)
    move_send, move_recv, move_own = refs
    outward = [
        pltpu.make_async_copy(source, target, out_sem.at[index])
        for index, (source, target) in enumerate(zip(near, far))
    ]
    me, partner, across, down = neighbours()
    plane = lax.axis_index("tensor")
    core = lax.rem(me, 2)
    stage_own, stage_z, stage_xy, stage_diagonal, arrive, finish = gather_plan(shards, wholes, sems)
    moves = [
        move_plan(False, source, target, move_send.at[index], move_recv.at[index], move_own.at[index])
        for index, (source, target) in enumerate(((inputs, rows_low), (cotangent, grad_rows)))
    ]
    greeted(greet(plane, (partner, across, down), [lax.rem(plane + offset, 4) for offset in (1, 2, 3)]))
    count, width = rows_low.shape
    third = shards[0].shape[0]
    step = 64

    stage_own(0)
    stage_own(1)
    send_to(lengths, other_lengths, length_send, length_recv, (partner, plane))
    stage_z(0)
    stage_own(2)
    stage_z(1)
    stage_xy(0)
    stage_own(3)
    stage_z(2)
    stage_xy(1)
    stage_diagonal(0)
    stage_own(4)
    stage_z(3)
    stage_xy(2)
    stage_diagonal(1)
    stage_own(5)
    stage_z(4)
    moves[0][0]()
    stage_xy(3)
    stage_diagonal(2)
    stage_z(5)
    moves[1][0]()
    stage_diagonal(3)
    stage_xy(4)
    wait_for(other_lengths, length_recv)
    mine = core == lax.rem(plane, 2)
    both = jnp.where(mine, lengths[...], other_lengths[...])
    length = jnp.where(plane < 2, both[0:1], both[1:2])
    position = lax.broadcasted_iota(jnp.int32, bias.shape, 0)
    position = lax.rem(position + core * count, 2 * count).astype(jnp.float32)
    bias[...] = jnp.where(position < length, 0.0, MASK_VALUE)

    @pl.loop(0, bias.shape[0] // 128)
    def _(index):
        first = pl.multiple_of(index * 128, 128)
        place = lax.broadcasted_iota(jnp.int32, (128, 128), 0) + first + core * count
        angles = lax.rem(place, 2 * count).astype(jnp.float32) * frequency[0:1]
        half_lane = lax.rem(lane_of((128, 128)), HEAD_DIM) < HEAD_DIM // 2
        cosine[pl.ds(first, 128)] = jnp.cos(angles)
        turned_sine = jnp.sin(angles)
        sine[pl.ds(first, 128)] = jnp.where(half_lane, -turned_sine, turned_sine)

    moves[0][1]()

    @pl.loop(0, count // step)
    def _(index):
        window = pl.ds(pl.multiple_of(index * step, step), step)
        low_one[window] = low(normed_rows(rows_low[window].astype(jnp.float32), gains[0:1]))

    outward[0].start()
    outward[1].start()
    for part in range(3):
        arrive(part)

    def load(group):
        for part in range(3):
            slot = lax.rem(group, 2)
            pltpu.make_async_copy(wholes[part].at[group], weight.at[slot, part], weight_sem.at[slot, part]).start()

    load(0)

    @pl.loop(0, 4)
    def _(group):
        @pl.when(group < 3)
        def _():
            load(group + 1)

        slot = lax.rem(group, 2)
        for part in range(3):
            wait_for(weight.at[slot, part], weight_sem.at[slot, part])
            result = product_of(low_one[...], weight[slot, part], ((1,), (1,)))
            for first in range(0, third, 128):
                columns = pl.ds(pl.multiple_of(group * third + first, 128), 128)
                piece = result[:, first : first + 128]
                if part < 2:
                    piece = turned(piece, cosine[0:count], sine[0:count])
                if part == 0:
                    queries[:, columns] = low(piece * SCORE_SCALE)
                else:
                    own[part - 1, :, columns] = low(piece)

    send_to(own, other, pair_send, pair_recv, (partner, plane))
    outward[2].start()
    outward[3].start()
    wait_for(other, pair_recv)
    outward[4].start()
    arrive(3)
    attn_copy = pltpu.make_async_copy(wholes[3], attn_weight, attn_sem)
    attn_copy.start()
    schedule = {3: (stage_xy, 5), 6: (stage_diagonal, 4)}

    @pl.loop(0, width // 128)
    def _(index):
        for place, (stage, part) in schedule.items():
            @pl.when(index == place)
            def _():
                stage(part)

        attend_pair(lanes(index), queries, own, other, bias, context, log_total.at[index])

    attn_copy.wait()

    @pl.loop(0, count // 128)
    def _(index):
        window = pl.ds(pl.multiple_of(index * 128, 128), 128)
        rows = rows_low[window].astype(jnp.float32)
        for group in range(4):
            piece = context[window, third * group : third * group + third]
            rows = rows + product_of(piece, attn_weight[group], ((1,), (0,)))
        middle[window] = rows
        low_two[window] = low(normed_rows(rows, gains[1:2]))

    stage_diagonal(5)
    for part in (4, 5):
        arrive(part)
    for part in range(6):
        finish(part)
    for copy in outward:
        copy.wait()
    wait_for(own, pair_send)
    wait_for(lengths, length_send)
    moves[1][1]()


def forward(shards, inputs, cotangent, lengths, gains, frequency, collective_id):
    sem = pltpu.SemaphoreType.DMA
    anywhere = pl.BlockSpec(memory_space=pl.ANY)
    local = pl.BlockSpec(memory_space=pltpu.VMEM)
    bf16, f32 = jnp.bfloat16, jnp.float32
    count, width = 2 * inputs.shape[1], inputs.shape[2]
    third = shards[0].shape[0]
    shape = jax.ShapeDtypeStruct
    return pl.pallas_call(
        forward_kernel,
        out_shape=[shape((4, shard.shape[0], width), bf16) for shard in shards]
        + [
            shape((count, width), bf16),
            shape((count, width), bf16),
            shape((count, width), bf16),
            shape((count, width), bf16),
            shape((2, count, width), bf16),
            shape((2, count, width), bf16),
            shape((count, width), bf16),
            shape((width // 128, 8, count), f32),
            shape((2 * count, 128), f32),
            shape((count, width), f32),
            shape((count, width), bf16),
            shape((2 * count, 128), f32),
            shape((2 * count, 128), f32),
        ],
        in_specs=[anywhere] * 8 + [local] * 3,
        out_specs=[anywhere] * 12 + [local] * 7,
        scratch_shapes=[
            pltpu.VMEM((count, width), bf16),
            pltpu.VMEM((count, width), bf16),
            pltpu.VMEM((count, width), bf16),
            pltpu.VMEM((2, count, width), bf16),
            pltpu.VMEM((2, count, width), bf16),
            pltpu.VMEM(lengths.shape, f32),
            pltpu.VMEM((2, 3, third, width), bf16),
            pltpu.VMEM((4, third, width), bf16),
            sem((6,)),
        ]
        + [sem((6, 4))] * 9
        + [sem((6, 4, 4))] * 2
        + [sem, sem, sem, sem, sem((2, 3)), sem, sem((5,))]
        + [sem((2, 2)), sem((2, 2)), sem((2,))],
        compiler_params=pltpu.CompilerParams(
            collective_id=collective_id, has_side_effects=True, vmem_limit_bytes=58 * 1024 * 1024
        ),
        name="forward",
    )(*shards, inputs, cotangent, lengths, gains, frequency)


def attend_pair(columns, queries, own, other, bias, context, log_total):
    query_turned = queries[:, columns].T
    keys = jnp.concatenate([own[0, :, columns], other[0, :, columns]], axis=0)
    value_turned = jnp.concatenate([own[1, :, columns].T, other[1, :, columns].T], axis=1)
    parts, logs = [], []
    for head in range(2):
        scores = scores_of(keys, head_rows(query_turned, head), bias[...])
        highest = jnp.max(scores, axis=0, keepdims=True)
        weights = jnp.exp(scores - highest)
        total = jnp.sum(weights, axis=0, keepdims=True)
        part = product_of(value_turned[64 * head : 64 * head + 64], low(weights), ((1,), (0,)))
        parts.append(part / total)
        logs.append(highest + jnp.log(total))
    context[:, columns] = low(jnp.concatenate(parts, axis=0)).T
    log_total[...] = jnp.concatenate(logs + logs * 3, axis=0)


def add_rows(target, source, extent):
    step = step_of(extent)

    @pl.loop(0, extent // step)
    def _(index):
        window = pl.ds(pl.multiple_of(index * step, step), step)
        target[window] = low(target[window].astype(jnp.float32) + source[window].astype(jnp.float32))


def slot_of(part):
    return (4 - part) % 4


def slot_plan(grads, sums, buffers, sems):
    held, from_x, from_y, from_yx, from_xy = buffers[:5]
    from_z, staging = buffers[5][0], buffers[6][0]
    (load_sem, send_c, recv_c, send_x, recv_x, send_y, recv_y, send_yx, recv_yx, send_xy, recv_xy, send_z, recv_z) = sems
    me, partner, across, down = neighbours()
    plane = lax.axis_index("tensor")
    flip = lambda block: block + 1 - 2 * lax.rem(block, 2)
    blocks = (me, across, down, across + down - me)
    order = (3, 1, 2, 0)
    rows, early = grads.shape[1], from_x[0].shape[1]
    late = rows - early
    one, two = pl.ds(0, early), pl.ds(early, late)

    def stage_core(part):
        for index in order:
            send_to(grads.at[slot_of(part), :, lanes(flip(blocks[index]))], held[part].at[index], send_c.at[part, index], recv_c.at[part, index], (partner, plane))

    def stage_first(part):
        for index in order:
            pltpu.make_async_copy(grads.at[slot_of(part), :, lanes(blocks[index])], staging.at[index], load_sem.at[part, index]).start()
        for index in order:
            wait_for(staging.at[index], load_sem.at[part, index])
            wait_for(held[part].at[index], recv_c.at[part, index])
            add_rows(held[part].at[index], staging.at[index], rows)
            if index % 2 == 1:
                send_to(held[part].at[index, one], from_x[part].at[index // 2], send_x.at[part, index // 2], recv_x.at[part, index // 2], (across, plane))
            if index // 2 == 1:
                send_to(held[part].at[index, two], from_y[part].at[index % 2], send_y.at[part, index % 2], recv_y.at[part, index % 2], (down, plane))

    def stage_second(part):
        for side in (1, 0):
            wait_for(from_x[part].at[side], recv_x.at[part, side])
            add_rows(held[part].at[2 * side, one], from_x[part].at[side], early)
            if side == 1:
                send_to(held[part].at[2, one], from_yx[part], send_yx.at[part], recv_yx.at[part], (down, plane))
            wait_for(from_y[part].at[side], recv_y.at[part, side])
            add_rows(held[part].at[side, two], from_y[part].at[side], late)
            if side == 1:
                send_to(held[part].at[1, two], from_xy[part], send_xy.at[part], recv_xy.at[part], (across, plane))

    def stage_third(part):
        wait_for(from_yx[part], recv_yx.at[part])
        add_rows(held[part].at[0, one], from_yx[part], early)
        wait_for(from_xy[part], recv_xy.at[part])
        add_rows(held[part].at[0, two], from_xy[part], late)

        @pl.when(plane != slot_of(part))
        def _():
            offset = lax.rem(plane + 3 - slot_of(part), 4)
            send_to(held[part].at[0], from_z.at[offset], send_z.at[part], recv_z.at[offset], (me, slot_of(part)))

    def stage_last(part):
        @pl.when(plane == slot_of(part))
        def _():
            for offset in range(3):
                wait_for(from_z.at[offset], recv_z.at[offset])
            for target, first, extent in sums:
                step = step_of(extent)

                @pl.loop(0, extent // step)
                def _(index):
                    offset = pl.multiple_of(index * step, step)
                    window = pl.ds(pl.multiple_of(first + offset, 16), step)
                    total = held[part][0, window].astype(jnp.float32)
                    for other in range(3):
                        total = total + from_z[other, window].astype(jnp.float32)
                    target[pl.ds(offset, step)] = total

    def finish(part):
        for index in range(4):
            wait_for(held[part].at[index], send_c.at[part, index])
        for side in range(2):
            wait_for(from_x[part].at[side], send_x.at[part, side])
            wait_for(from_y[part].at[side], send_y.at[part, side])
        wait_for(from_yx[part], send_yx.at[part])
        wait_for(from_xy[part], send_xy.at[part])

        @pl.when(plane != slot_of(part))
        def _():
            wait_for(from_z.at[0], send_z.at[part])

    return ((stage_core, stage_first, stage_second, stage_third, stage_last), finish)


def slot_scratch(rows, early):
    sem = pltpu.SemaphoreType.DMA
    late = rows - early
    shapes = [(4, rows)] * 4 + [(2, early)] * 4 + [(2, late)] * 4 + [(early,)] * 4 + [(late,)] * 4
    shapes += [(3, rows), (4, rows)]
    buffers = [pltpu.VMEM(shape + (128,), jnp.bfloat16) for shape in shapes]
    sems = [sem((4, 4))] * 3 + [sem((4, 2))] * 4 + [sem((4,))] * 4 + [sem((4,)), sem((3,))]
    return (buffers, sems)


def backward_kernel(*refs):
    refs = list(refs)
    f32, bf16 = jnp.float32, jnp.bfloat16
    in_weight, out_weight, attn_weight, far_two, far_cot, far_middle = take(refs, 6)
    far_query, far_own, far_other, far_context, far_one = take(refs, 5)
    bias, log_total, cosine, sine, gains = take(refs, 5)
    sums, (far_grad_query, far_pair, rows_out, far_grad_middle, gain_two) = take(refs, 4), take(refs, 5)
    grad_feed, weight_grads = take(refs, 1)[0], take(refs, 4)
    branch, cotangent, low_rows, queries, own, other, grad, context = take(refs, 8)
    grad_query, grad_pair, grad_other, arrived, staged = take(refs, 5)
    result, grad_rows, middle = take(refs, 3)
    slot_buffers = [take(refs, 4) for _ in range(5)] + [take(refs, 1), take(refs, 1)]
    slot_sems = take(refs, 13)
    buffers = [take(refs, 4) for _ in range(6)] + [take(refs, 1)]
    sems = take(refs, 13)
    pair_send, pair_recv, stage_sem, load_sem, out_sem, weight_sem, feed_sem, middle_sem = take(refs, 8)
    move_send, move_recv, move_own = refs
    me, partner, across, down = neighbours()
    plane = lax.axis_index("tensor")
    height, third = out_weight.shape[1], attn_weight.shape[1]
    count, width = cotangent.shape
    sum_qkv, sum_attn, sum_in, sum_out = sums
    feed_sums = [(sum_in, 0, 2 * height), (sum_out, 2 * height, height)]
    feed_stages, feed_finish = slot_plan(grad_feed, feed_sums, slot_buffers, slot_sems)
    parts = [(ref, 0, third) for ref in weight_grads]
    targets = [(sum_attn, 0)] + [(sum_qkv, third * index) for index in range(3)]
    stages, finish = scatter_plan(parts, targets, buffers, sems)
    start_move, finish_move = move_plan(True, cotangent, rows_out, move_send, move_recv, move_own)

    def call(stage, part):
        if part < 4:
            feed_stages[stage](part)
        else:
            stages[stage](part - 4)

    pieces = ((0, 336), (336, height - 336))
    weight_slots = (
        (own.at[0], own.at[1], grad_pair.at[0]),
        (other.at[0], other.at[1], grad_pair.at[1]),
    )
    grad_slots = ((grad_other.at[0], grad_other.at[1], grad_query), (queries, context, grad))

    def weight_copies(group, piece):
        first, extent = pieces[piece]
        sources = ((in_weight, first), (in_weight, height + first), (out_weight, first))
        return [
            pltpu.make_async_copy(source.at[lax.rem(4 - group, 4), pl.ds(offset, extent)], target.at[pl.ds(0, extent)], weight_sem.at[piece, index])
            for index, ((source, offset), target) in enumerate(zip(sources, weight_slots[piece]))
        ]

    def grad_copies(group, piece):
        first, extent = pieces[piece]
        return [
            pltpu.make_async_copy(source.at[pl.ds(0, extent)], grad_feed.at[lax.rem(4 - group, 4), pl.ds(index * height + first, extent)], feed_sem.at[piece, index])
            for index, source in enumerate(grad_slots[piece])
        ]

    def start_all(copies):
        for copy in copies:
            copy.start()

    def wait_all(copies):
        for copy in copies:
            copy.wait()

    first_loads = [
        pltpu.make_async_copy(far_two, branch, load_sem.at[0]),
        pltpu.make_async_copy(far_cot, cotangent, load_sem.at[1]),
    ]
    expected = greet(plane, (partner, across, down), [lax.rem(plane + offset, 4) for offset in (1, 2, 3)])
    start_all(first_loads)
    start_all(weight_copies(0, 0))
    start_all(weight_copies(0, 1))
    result[...] = jnp.zeros_like(result)
    grad_rows[...] = jnp.zeros_like(grad_rows)
    wait_all(first_loads)
    greeted(expected)
    feed_calls = {(1, 1): ((1, 0),), (2, 1): ((1, 1),), (3, 0): ((2, 0),), (3, 1): ((1, 2),)}

    @pl.loop(0, 4)
    def _(group):
        @pl.when(group > 0)
        def _():
            for piece in range(2):
                wait_all(grad_copies(group - 1, piece))
            for part in range(3):
                @pl.when(group == part + 1)
                def _():
                    call(0, part)

        for piece, (_, extent) in enumerate(pieces):
            for (when, place), calls in feed_calls.items():
                if place == piece:
                    @pl.when(group == when)
                    def _():
                        for stage, part in calls:
                            call(stage, part)

            window = pl.ds(0, extent)
            wait_all(weight_copies(group, piece))
            gate_weight, up_weight, down_weight = (ref[window] for ref in weight_slots[piece])
            gate = product_of(gate_weight, branch[...], ((1,), (1,)))
            up = product_of(up_weight, branch[...], ((1,), (1,)))
            grad_hidden = product_of(down_weight, cotangent[...], ((1,), (1,)))
            below = 0.5 + 0.5 * lax.erf(gate * math.sqrt(0.5))
            active = gate * below
            hidden = low(active * up)
            slope = below + gate * jnp.exp(-0.5 * gate * gate) * (1.0 / math.sqrt(2.0 * math.pi))
            grad_gate = low(grad_hidden * up * slope)
            grad_up = low(grad_hidden * active)
            grad_slots[piece][2][window] = low(product_of(hidden, cotangent[...], ((1,), (0,))))
            grad_slots[piece][0][window] = low(product_of(grad_gate, branch[...], ((1,), (0,))))
            grad_slots[piece][1][window] = low(product_of(grad_up, branch[...], ((1,), (0,))))
            start_all(grad_copies(group, piece))
            result[...] += product_of(hidden, down_weight, ((0,), (0,)))
            grad_rows[...] += product_of(grad_gate, gate_weight, ((0,), (0,)))
            grad_rows[...] += product_of(grad_up, up_weight, ((0,), (0,)))

            @pl.when(group < 3)
            def _():
                start_all(weight_copies(group + 1, piece))

    step = 64

    def middle_copy(index):
        window = pl.ds(pl.multiple_of(index * step, step), step)
        slot = lax.rem(index, 2)
        return pltpu.make_async_copy(far_middle.at[window], middle.at[slot], middle_sem.at[slot])

    middle_copy(0).start()
    for piece in range(2):
        wait_all(grad_copies(3, piece))
    call(0, 3)
    near = (queries, own, other, context, low_rows)
    loads = [
        pltpu.make_async_copy(source, target, load_sem.at[index])
        for index, (source, target) in enumerate(zip((far_query, far_own, far_other, far_context, far_one), near))
    ]
    start_all(loads)
    attn_loads = [
        pltpu.make_async_copy(
            attn_weight.at[group], grad_other.at[group // 2, pl.ds(group % 2 * third, third)], weight_sem.at[group // 2, group % 2]
        )
        for group in range(4)
    ]
    start_all(attn_loads)
    gain_two[...] = jnp.zeros_like(gain_two)

    @pl.loop(0, count // step)
    def _(index):
        @pl.when(index < count // step - 1)
        def _():
            middle_copy(index + 1).start()

        middle_copy(index).wait()
        window = pl.ds(pl.multiple_of(index * step, step), step)
        rows = middle[lax.rem(index, 2)]
        centre = rows - jnp.mean(rows, axis=1, keepdims=True)
        inverse = lax.rsqrt(jnp.mean(centre * centre, axis=1, keepdims=True) + NORM_EPS)
        normed = centre * inverse
        scaled = grad_rows[window] * gains[1:2]
        mean_grad = jnp.mean(scaled, axis=1, keepdims=True)
        mean_cross = jnp.mean(scaled * normed, axis=1, keepdims=True)
        gain_two[...] += jnp.sum(grad_rows[window] * normed, axis=0, keepdims=True)
        total = cotangent[window].astype(f32) + inverse * (scaled - mean_grad - normed * mean_cross)
        grad_rows[window] = total
        branch[window] = low(total)
        cotangent[window] = low(rows + result[window])

    call(3, 0)
    call(2, 1)
    start_move()
    middle_out = pltpu.make_async_copy(grad_rows, far_grad_middle, out_sem.at[2])
    middle_out.start()
    wait_all(attn_loads)

    @pl.loop(0, count // 128)
    def _(index):
        window = pl.ds(pl.multiple_of(index * 128, 128), 128)
        for part in range(2):
            columns = slice(part * count, part * count + count)
            grad[window, columns] = low(product_of(branch[window], grad_other[part], ((1,), (1,))))

    wait_all(loads)

    def weight_grad(which, values, rows):
        target = weight_grads[which]
        for group in range(4):
            slot = staged.at[group % 2]
            if group >= 2:
                wait_for(slot, stage_sem.at[group % 2])
            block = values[:, third * group : third * group + third]
            slot[...] = low(product_of(block, rows[...], ((0,), (0,))))
            pltpu.make_async_copy(slot, target.at[group], stage_sem.at[group % 2]).start()
        for group in range(2):
            wait_for(staged.at[group], stage_sem.at[group])

    weight_grad(0, context, branch)
    call(0, 4)

    def exchanged(index):
        return (arrived.at[:, :, lanes(index)], pair_recv.at[index])

    def add_pair(index):
        wait_for(*exchanged(index))
        columns = lanes(index)
        for which in range(2):
            total = grad_pair[which, :, columns].astype(f32)
            total = total + arrived[which, :, columns].astype(f32)
            grad_pair[which, :, columns] = low(total)

    last_pair = width // 128 - 1
    schedule = {0: ((1, 3),), 2: ((3, 1), (2, 2)), 5: ((3, 2), (1, 4)), 7: ((2, 3),)}

    @pl.loop(0, last_pair + 1)
    def _(index):
        for position, calls in schedule.items():
            @pl.when(index == position)
            def _():
                for stage, part in calls:
                    call(stage, part)

        attend_back_pair(lanes(index), queries, own, other, bias, grad, context, log_total.at[index], cosine, sine, grad_query, grad_pair, grad_other)
        target, sem = exchanged(index)
        send_to(grad_other.at[:, :, lanes(index)], target, pair_send.at[index], sem, (partner, plane))

        @pl.when(index > 0)
        def _():
            add_pair(index - 1)

    query_copy = pltpu.make_async_copy(grad_query, far_grad_query, out_sem.at[0])
    query_copy.start()
    weight_grad(1, grad_query, low_rows)
    call(0, 5)
    call(3, 3)
    add_pair(last_pair)
    pair_copy = pltpu.make_async_copy(grad_pair, far_pair, out_sem.at[1])
    pair_copy.start()
    weight_grad(2, grad_pair.at[0], low_rows)
    call(0, 6)
    weight_grad(3, grad_pair.at[1], low_rows)
    call(0, 7)
    done = {(3, 3), (1, 4), (3, 2), (2, 3), (1, 0), (2, 0), (1, 1), (3, 0), (2, 1), (1, 2), (3, 1), (2, 2), (1, 3)}
    for turn_of in range(10):
        for stage in (3, 2, 1):
            part = turn_of - (stage - 1)
            if 0 <= part < 8 and (stage, part) not in done:
                call(stage, part)
    for part in range(8):
        call(4, part)
    for part in range(4):
        feed_finish(part)
        finish(part)
    for index in range(last_pair + 1):
        wait_for(arrived.at[:, :, lanes(index)], pair_send.at[index])
    query_copy.wait()
    pair_copy.wait()
    middle_out.wait()
    finish_move()


def backward(wholes, low_two, cotangent, middle, queries, own, other, context, low_one, bias, log_total, cosine, sine, gains, collective_id):
    attn_all, in_all, out_all = wholes
    height, third = out_all.shape[1], attn_all.shape[1]
    count, width = queries.shape
    early = 3 * height // 32 * 16 + 16
    slot_buffers, slot_sems = slot_scratch(3 * height, early)
    buffers, sems = scatter_scratch([third] * 4)
    sem = pltpu.SemaphoreType.DMA
    anywhere = pl.BlockSpec(memory_space=pl.ANY)
    local = pl.BlockSpec(memory_space=pltpu.VMEM)
    bf16, f32 = jnp.bfloat16, jnp.float32
    shape, vmem = jax.ShapeDtypeStruct, pltpu.VMEM
    outs = pl.pallas_call(
        backward_kernel,
        out_shape=[shape((rows, 128), f32) for rows in (3 * third, third, 2 * height, height)]
        + [
            shape((count, width), bf16),
            shape((2, count, width), bf16),
            shape((2, count // 2, width), bf16),
            shape((count, width), f32),
            shape((1, width), f32),
            shape((4, 3 * height, width), bf16),
        ]
        + [shape(attn_all.shape, bf16)] * 4,
        in_specs=[anywhere] * 11 + [local] * 5,
        out_specs=[local] * 4 + [anywhere] * 4 + [local] + [anywhere] * 5,
        scratch_shapes=[vmem((count, width), bf16)] * 4
        + [vmem((2, count, width), bf16)] * 2
        + [vmem((count, width), bf16)] * 3
        + [vmem((2, count, width), bf16)] * 3
        + [vmem((2, third, width), bf16)]
        + [vmem((count, width), f32)] * 2
        + [vmem((2, 64, width), f32)]
        + slot_buffers
        + slot_sems
        + buffers
        + sems
        + [sem((8,)), sem((8,)), sem((2,)), sem((5,)), sem((3,)), sem((2, 3)), sem((2, 3)), sem((2,))]
        + [sem((2,)), sem((2,)), sem],
        compiler_params=pltpu.CompilerParams(
            collective_id=collective_id, has_side_effects=True, vmem_limit_bytes=62 * 1024 * 1024
        ),
        name="backward",
    )(in_all, out_all, attn_all, low_two, cotangent, middle, queries, own, other, context, low_one, bias, log_total, cosine, sine, gains)
    return outs[:9]


def attend_back_pair(columns, queries, own, other, bias, grad, context, log_total, cosine, sine, grad_query, grad_own, grad_other):
    count = queries.shape[0]
    query_rows, grad_rows = queries[:, columns], grad[:, columns]
    query_turned, grad_turned = query_rows.T, grad_rows.T
    inner = (grad_rows.astype(jnp.float32) * context[:, columns].astype(jnp.float32)).T
    query_parts = [None, None]
    for half, (pair, result) in enumerate(((own, grad_own), (other, grad_other))):
        keys, values = pair[0, :, columns], pair[1, :, columns]
        key_turned = keys.T
        grad_keys, grad_values = None, None
        window = pl.ds(half * count, count)
        for head in range(2):
            lanes_of_head = slice(64 * head, 64 * head + 64)
            scores = scores_of(keys, head_rows(query_turned, head), bias[window])
            weights = jnp.exp(scores - log_total[head : head + 1])
            grad_weights = product_of(values, head_rows(grad_turned, head), ((1,), (0,)))
            inner_row = jnp.sum(inner[lanes_of_head], axis=0, keepdims=True)
            grad_scores = low(weights * (grad_weights - inner_row))
            value_part = product_of(low(weights), head_lanes(grad_rows, head), ((1,), (0,)))
            key_part = product_of(grad_scores, head_lanes(query_rows, head), ((1,), (0,)))
            query_part = product_of(key_turned[lanes_of_head], grad_scores, ((1,), (0,)))
            grad_values = value_part if head == 0 else grad_values + value_part
            grad_keys = key_part if head == 0 else grad_keys + key_part
            query_parts[head] = query_part if half == 0 else query_parts[head] + query_part
        result[0, :, columns] = turned(grad_keys, cosine[window], -sine[window]).astype(result.dtype)
        result[1, :, columns] = grad_values.astype(result.dtype)
    query_rows = jnp.concatenate(query_parts, axis=0).T * SCORE_SCALE
    own_rows = pl.ds(0, count)
    grad_query[:, columns] = low(turned(query_rows, cosine[own_rows], -sine[own_rows]))


def product_of(left, right, dims):
    return lax.dot_general(left, right, (dims, ((), ())), preferred_element_type=jnp.float32)

def tiles_of(like):
    if len(like.shape) == 2 and like.shape[1] == 128:
        return [(pl.ds(0, like.shape[0]), (slice(None), slice(None)), True)]
    width = like.shape[-1]
    tiles = []
    for part in range(like.shape[0] if len(like.shape) == 3 else 1):
        for first in range(0, width, 128):
            columns = slice(first, first + 128)
            place = (part, slice(None), columns) if len(like.shape) == 3 else (slice(None), columns)
            tiles.append((pl.ds(part * width + first, 128), place, False))
    return tiles


def optimize_kernel(heights, *refs):
    refs = list(refs)
    count, size, tile = len(heights), 1024, 256
    f32, bf16 = jnp.float32, jnp.bfloat16
    sums, moments = take(refs, count), take(refs, count)
    (gain_two, gains), far = take(refs, 2), take(refs, 7)
    far = far[:4] + [far[4].at[0], far[4].at[1]] + far[5:]
    backs, (gain_out, rows_out), blocks = take(refs, count), take(refs, 2), take(refs, count)
    whole, steps, gain_parts = take(refs, 3)
    iterate, poly, product, total = take(refs, 4)
    iterate_low, poly_low, other_low, total_low = take(refs, 4)
    value_rows, rows_in, rows_low = take(refs, 3)
    load_sem, own_sem, send_z, recv_z, send_x, recv_x, send_y, recv_y, send_d, recv_d, send_c, recv_c = take(refs, 12)
    send_g, recv_g, back_sem, send_b, recv_b, move_send, move_recv, move_own = refs
    me, partner, across, down = neighbours()
    plane = lax.axis_index("tensor")
    diagonal = across + down - me
    planes = [lax.rem(plane + offset, 4) for offset in (1, 2, 3)]
    flip = lambda block: block + 1 - 2 * lax.rem(block, 2)
    half = rows_low.shape[0]
    start_move, finish_move = move_plan(True, rows_low, rows_out, move_send, move_recv, move_own)
    near = (
        poly_low, other_low, total_low, iterate_low.at[0:half], iterate_low.at[half : 2 * half],
        value_rows, rows_in, poly.at[0:half],
    )
    loads = [
        pltpu.make_async_copy(source, target, load_sem.at[index])
        for index, (source, target) in enumerate(zip(far, near))
    ]
    expected = greet(plane, (partner, across, down), planes)
    for load in loads:
        load.start()

    def place(part, slot, block):
        height = heights[part]
        return whole.at[pl.ds(pl.multiple_of(slot * height, 16), height), lanes(block)]

    def spread(part, source, slot):
        view = place(part, slot, me)
        send_to(source, view, send_x.at[slot], recv_x.at[slot], (across, plane))
        send_to(source, view, send_y.at[slot], recv_y.at[slot], (down, plane))
        send_to(source, view, send_c.at[slot, 0], recv_c.at[slot, 0], (partner, plane))

    def on_plane(body):
        for part in range(count):
            @pl.when(plane == part)
            def _():
                body(part)

    def off_plane(body):
        for part in range(count):
            @pl.when(plane != part)
            def _():
                body(part)

    for part in (2, 0, 3, 1):
        for rows, place_of, is_turned in tiles_of(moments[part]):
            moment = moments[part][place_of]
            moment = moment if is_turned else moment.T
            blocks[part][rows] = low(MOMENTUM * moment + sums[part][rows])
        if part == 2:
            greeted(expected)

        @pl.when(plane != part)
        def _():
            offset = lax.rem(plane + 3 - part, 4)
            send_to(blocks[part], place(part, plane, me), send_z.at[part], recv_z.at[offset], (me, part))

        @pl.when(plane == part)
        def _():
            pltpu.make_async_copy(blocks[part], place(part, part, me), own_sem).start()
            spread(part, blocks[part], part)

    def pass_z(part):
        for distance in (1, 3, 2):
            slot = (part + distance) % 4
            view = place(part, slot, me)
            wait_for(view, recv_z.at[(slot + 3 - part) % 4])
            spread(part, view, slot)

    on_plane(pass_z)

    for load in loads:
        load.wait()
    gain_out[1:2] = gain_two[...]
    gain_out[0:1] = jnp.zeros((1, size), f32)

    @pl.loop(0, half // 64)
    def _(index):
        first = pl.multiple_of(index * 64, 64)
        window = pl.ds(first, 64)
        other_window = pl.ds(pl.multiple_of(first + half, 64), 64)
        grad = product_of(iterate_low[window], poly_low[...], ((1,), (0,)))
        grad = grad + product_of(iterate_low[other_window], other_low[...], ((1,), (0,)))
        grad = grad + product_of(value_rows[window], total_low[...], ((1,), (0,)))
        rows = rows_in[window].astype(f32)
        centre = rows - jnp.mean(rows, axis=1, keepdims=True)
        inverse = lax.rsqrt(jnp.mean(centre * centre, axis=1, keepdims=True) + NORM_EPS)
        normed = centre * inverse
        scaled = grad * gains[0:1]
        mean_grad = jnp.mean(scaled, axis=1, keepdims=True)
        mean_cross = jnp.mean(scaled * normed, axis=1, keepdims=True)
        back = inverse * (scaled - mean_grad - normed * mean_cross)
        rows_low[window] = low(poly[window] + back)
        gain_out[0:1] += jnp.sum(grad * normed, axis=0, keepdims=True)

    start_move()
    for index, other in enumerate(planes):
        send_to(gain_out, gain_parts.at[index], send_g.at[index], recv_g.at[index], (me, other))

    def pass_xy(part):
        for slot in range(4):
            view = place(part, slot, across)
            wait_for(view, recv_x.at[slot])
            if slot < 2:
                send_to(view, view, send_d.at[slot], recv_d.at[slot], (down, plane))
            send_to(view, view, send_c.at[slot, 1], recv_c.at[slot, 1], (partner, plane))
            view = place(part, slot, down)
            wait_for(view, recv_y.at[slot])
            if slot >= 2:
                send_to(view, view, send_d.at[slot], recv_d.at[slot], (across, plane))
            send_to(view, view, send_c.at[slot, 2], recv_c.at[slot, 2], (partner, plane))

    on_plane(pass_xy)

    def pass_diagonal(part):
        for slot in range(4):
            view = place(part, slot, diagonal)
            wait_for(view, recv_d.at[slot])
            send_to(view, view, send_c.at[slot, 3], recv_c.at[slot, 3], (partner, plane))
        for slot in range(4):
            for index, block in enumerate((me, across, down, diagonal)):
                wait_for(place(part, slot, flip(block)), recv_c.at[slot, index])
        wait_for(blocks[part], own_sem)

    on_plane(pass_diagonal)

    windows = [pl.ds(first, tile) for first in range(0, size, tile)]
    zero = jnp.zeros((1, 1), f32)
    blank = jnp.zeros((1, size), f32)
    corner = lax.broadcasted_iota(jnp.int32, (tile, tile), 0) == lax.broadcasted_iota(jnp.int32, (tile, tile), 1)

    def gram(part):
        rows = slice(0, 4 * heights[part])
        for group in range(2):
            edge = group * size // 2

            @pl.loop(0, 2)
            def _(index):
                window = pl.ds(pl.multiple_of(edge + index * tile, tile), tile)
                iterate[window, edge:] = product_of(whole[rows, window], whole[rows, edge:], ((0,), (0,)))

    on_plane(gram)

    def upper(window):
        return slice(window.start, size)

    def store(window, result, shift, full, low_copy):
        corner_block = result[:, :tile] - jnp.where(corner, shift, 0.0)
        result = jnp.concatenate([corner_block, result[:, tile:]], axis=1) if result.shape[1] > tile else corner_block
        full[window, upper(window)] = result
        result_low = low(result)
        low_copy[window, upper(window)] = result_low
        for first in range(tile, result.shape[1], tile):
            low_copy[pl.ds(window.start + first, tile), window] = result_low[:, first : first + tile].T
        return result

    def fold(left, right, window):
        sums_of = jnp.sum(left * right, axis=0, keepdims=True)
        weighted = jnp.concatenate([sums_of[:, :tile], 2.0 * sums_of[:, tile:]], axis=1) if sums_of.shape[1] > tile else sums_of
        return jnp.concatenate([blank[:, : window.start], weighted], axis=1) if window.start else weighted

    def finish(row):
        return jnp.sum(row, axis=1, keepdims=True) / size

    def multiply(left, right, window):
        return product_of(left[window], right[:, upper(window)], ((1,), (0,)))

    trace = zero
    for window in windows:
        block = jnp.where(corner, iterate[window, window], 0.0)
        trace = trace + jnp.sum(jnp.sum(block, axis=0, keepdims=True), axis=1, keepdims=True)
    factor = 1.0 / (jnp.sqrt(trace) + NORM_FLOOR)
    squared = factor * factor
    mean = trace * squared / size
    row = blank
    for window in windows:
        rest = store(window, iterate[window, upper(window)] * squared, mean, iterate, iterate_low)
        row = row + fold(rest, rest, window)
    square = finish(row)

    def polynomial(mean, square, with_total):
        linear = QUINTIC_THREE + 2.0 * QUINTIC_FIVE * mean
        shift = QUINTIC_FIVE * square
        poly_mean = QUINTIC_ONE + QUINTIC_THREE * mean + QUINTIC_FIVE * (mean * mean) + shift
        row, total_row = blank, blank
        for window in windows:
            mine = iterate[window, upper(window)]
            rest = linear * mine + QUINTIC_FIVE * multiply(iterate_low, iterate_low, window)
            rest = store(window, rest, shift, poly, poly_low)
            row = row + fold(rest, mine, window)
            if with_total:
                total_row = total_row + fold(rest, total[window, upper(window)], window)
        return (poly_mean, finish(row), finish(total_row))

    def grow_total(poly_mean, total_mean, cross):
        for window in windows:
            result = poly_mean * total[window, upper(window)] + total_mean * poly[window, upper(window)]
            result = result + multiply(poly_low, total_low, window)
            store(window, result, cross, total, other_low)
        total_low[...] = other_low[...]
        return poly_mean * total_mean + cross

    def advance(poly_mean, mean, cross):
        row = blank
        for window in windows:
            rest = poly[window, upper(window)]
            result = poly_mean * iterate[window, upper(window)] + mean * rest
            result = result + multiply(poly_low, iterate_low, window)
            result = store(window, result, cross, product, other_low)
            row = row + fold(result, rest, window)
        product_mean = poly_mean * mean + cross
        cross = finish(row)
        row = blank
        for window in windows:
            result = poly_mean * product[window, upper(window)] + product_mean * poly[window, upper(window)]
            result = result + multiply(poly_low, other_low, window)
            result = store(window, result, cross, iterate, iterate_low)
            row = row + fold(result, result, window)
        return (poly_mean * product_mean + cross, finish(row))

    total_mean, cross, _ = polynomial(mean, square, False)
    for window in windows:
        total[window, upper(window)] = poly[window, upper(window)]
    total_low[...] = poly_low[...]
    mean, square = advance(total_mean, mean, cross)

    def sweep(_, carry):
        mean, square, total_mean = carry
        poly_mean, cross, cross_total = polynomial(mean, square, True)
        total_mean = grow_total(poly_mean, total_mean, cross_total)
        return advance(poly_mean, mean, cross) + (total_mean,)

    mean, square, total_mean = lax.fori_loop(0, NS_ITERS - 2, sweep, (mean, square, total_mean))
    poly_mean, _, cross_total = polynomial(mean, square, True)
    total_mean = grow_total(poly_mean, total_mean, cross_total)

    mine = lanes(me)
    columns = total_low[:, mine]

    def step_home(part):
        height = heights[part]

        @pl.loop(0, 4)
        def _(turn_of):
            slot = lax.rem(part + 1 + turn_of, 4)
            window = pl.ds(pl.multiple_of(slot * height, 16), height)
            result = product_of(whole[window, :], columns, ((1,), (0,)))
            result = result + total_mean * whole[window, mine].astype(f32)
            steps[window, :] = low(factor * result)

            @pl.when(turn_of == 3)
            def _():
                pltpu.make_async_copy(steps.at[window, :], backs[part], back_sem).start()

            @pl.when(turn_of < 3)
            def _():
                send_to(steps.at[window, :], backs[part], send_b.at[turn_of], recv_b.at[part], (me, slot))

    on_plane(step_home)

    for index in range(3):
        wait_for(gain_out, send_g.at[index])
        wait_for(gain_parts.at[index], recv_g.at[index])
    gain_out[...] = gain_out[...] + gain_parts[0] + gain_parts[1] + gain_parts[2]
    for index, other in ((3, across), (4, down), (5, partner)):
        send_to(gain_out, gain_parts.at[index], send_g.at[index], recv_g.at[index], (other, plane))
        wait_for(gain_out, send_g.at[index])
        wait_for(gain_parts.at[index], recv_g.at[index])
        gain_out[...] = gain_out[...] + gain_parts[index]

    on_plane(lambda part: wait_for(backs[part], back_sem))
    off_plane(lambda part: wait_for(backs[part], recv_b.at[part]))
    def last_waits(part):
        for slot in range(4):
            for sem in (send_x.at[slot], send_y.at[slot], send_d.at[slot]):
                wait_for(blocks[part], sem)
            for index in range(4):
                wait_for(blocks[part], send_c.at[slot, index])
        for index in range(3):
            wait_for(blocks[part], send_b.at[index])

    on_plane(last_waits)
    off_plane(lambda part: wait_for(blocks[part], send_z.at[part]))
    finish_move()


def optimize(sums, moments, gain_two, gains, far, collective_id):
    heights = [part.shape[0] for part in sums]
    count, size = len(heights), gains.shape[1]
    f32, bf16 = jnp.float32, jnp.bfloat16
    sem = pltpu.SemaphoreType.DMA
    anywhere = pl.BlockSpec(memory_space=pl.ANY)
    local = pl.BlockSpec(memory_space=pltpu.VMEM)
    half = far[5].shape[0]
    outs = pl.pallas_call(
        functools.partial(optimize_kernel, heights),
        out_shape=[jax.ShapeDtypeStruct((height, 128), bf16) for height in heights]
        + [jax.ShapeDtypeStruct(gains.shape, f32), jax.ShapeDtypeStruct((2, half // 2, size), bf16)],
        in_specs=[local] * (2 * count + 2) + [anywhere] * 7,
        out_specs=[local] * (count + 1) + [anywhere],
        scratch_shapes=[pltpu.VMEM((height, 128), bf16) for height in heights]
        + [pltpu.VMEM((4 * max(heights), size), bf16), pltpu.VMEM((4 * max(heights), 128), bf16)]
        + [pltpu.VMEM((6,) + gains.shape, f32)]
        + [pltpu.VMEM((size, size), f32)] * 4
        + [pltpu.VMEM((size, size), bf16)] * 4
        + [pltpu.VMEM((half, size), bf16)] * 3
        + [sem((8,)), sem, sem((count,)), sem((3,))]
        + [sem((4,))] * 6
        + [sem((4, 4))] * 2
        + [sem((6,))] * 2
        + [sem, sem((3,)), sem((count,)), sem((2,)), sem((2,)), sem],
        compiler_params=pltpu.CompilerParams(
            collective_id=collective_id, has_side_effects=True, vmem_limit_bytes=60 * 1024 * 1024
        ),
        name="optimize",
    )(*sums, *moments, gain_two, gains, *far)
    return (outs[:count], outs[count], outs[count + 1])


def settle_kernel(*refs):
    refs = list(refs)
    sums, steps, moments, weights = (take(refs, 4) for _ in range(4))
    new_moments, new_weights = take(refs, 4), take(refs, 4)
    for part in range(4):
        rate = MUON_RATE * 0.2 * math.sqrt(4 * sums[part].shape[0])
        for rows, place, is_turned in tiles_of(moments[part]):
            gradient, step = sums[part][rows], steps[part][rows].astype(jnp.float32)
            if not is_turned:
                gradient, step = gradient.T, step.T
            kept = weights[part][place].astype(jnp.float32) * (1.0 - MUON_RATE * DECAY_RATE)
            new_moments[part][place] = MOMENTUM * moments[part][place] + gradient
            new_weights[part][place] = kept - rate * step


def settle(sums, steps, moments, weights):
    local = pl.BlockSpec(memory_space=pltpu.VMEM)
    shapes = [jax.ShapeDtypeStruct(moment.shape, jnp.float32) for moment in moments]
    outs = pl.pallas_call(
        settle_kernel,
        out_shape=shapes * 2,
        in_specs=[local] * 16,
        out_specs=[local] * 8,
        compiler_params=pltpu.CompilerParams(vmem_limit_bytes=48 * 1024 * 1024),
        name="settle",
    )(*sums, *steps, *moments, *weights)
    return (outs[:4], outs[4:])


def weight_shards(weights):
    shards = [turn(weight) for weight in weights]
    third = shards[0].shape[0] // 3
    return [shards[0][third * part : third * part + third] for part in range(3)] + shards[1:]


def gather_weights(shards):
    tensor_count, dp_count = lax.axis_size("tensor"), lax.axis_size("dp")
    wholes = [lax.all_gather(shard, ("tensor", "dp")) for shard in shards]
    wholes = [
        whole.reshape(tensor_count, dp_count, *whole.shape[1:]).transpose(0, 2, 1, 3)
        for whole in wholes
    ]
    return [whole.reshape(*whole.shape[:2], -1) for whole in wholes]


def reduce_grads(grads):
    tensor_count, dp_count = lax.axis_size("tensor"), lax.axis_size("dp")
    sums = []
    for grad in grads:
        blocks = grad.reshape(*grad.shape[:2], dp_count, -1).transpose(0, 2, 1, 3)
        blocks = blocks.reshape(-1, *blocks.shape[2:])
        part = lax.psum_scatter(blocks, ("tensor", "dp"), scatter_dimension=0, tiled=True)
        sums.append(part[0].astype(jnp.float32))
    return sums


def lane_of(shape):
    return lax.broadcasted_iota(jnp.int32, shape, 1)

def turned(vectors, cosine, sine):
    lane = lax.rem(lane_of(vectors.shape), 64)
    swapped = jnp.where(lane < 32, pltpu.roll(vectors, 96, 1), pltpu.roll(vectors, 32, 1))
    return vectors * cosine + swapped * sine

def project_kernel(rows, query_weight, key_weight, value_weight, cosine, sine, queries, pair):
    rows = rows[...]
    for weight, target in ((query_weight, 0), (key_weight, 1)):
        result = product_of(rows, weight[0], ((1,), (1,)))
        for first in range(0, result.shape[1], 128):
            part = turned(result[:, first : first + 128], cosine[...], sine[...])
            if target == 0:
                queries[:, first : first + 128] = low(part * SCORE_SCALE)
            else:
                pair[0, :, first : first + 128] = low(part)
    pair[1] = low(product_of(rows, value_weight[0], ((1,), (1,))))

def project(rows, query_weight, key_weight, value_weight, cosine, sine):
    count, width = rows.shape
    groups, height, _ = query_weight.shape
    whole = lambda *shape: pl.BlockSpec(shape, lambda i: (0,) * len(shape))
    weight = pl.BlockSpec((1, height, width), lambda i: (i, 0, 0))
    return pl.pallas_call(
        project_kernel,
        grid=(groups,),
        out_shape=[jax.ShapeDtypeStruct((count, width), jnp.bfloat16), jax.ShapeDtypeStruct((2, count, width), jnp.bfloat16)],
        in_specs=[whole(count, width), weight, weight, weight, whole(count, 128), whole(count, 128)],
        out_specs=[pl.BlockSpec((count, height), lambda i: (0, i)), pl.BlockSpec((2, count, height), lambda i: (0, 0, i))],
        compiler_params=pltpu.CompilerParams(vmem_limit_bytes=40 * 1024 * 1024),
        name="project",
    )(rows, query_weight, key_weight, value_weight, cosine, sine)

def head_rows(transposed, head):
    rows = lax.broadcasted_iota(jnp.int32, transposed.shape, 0)
    return jnp.where(lax.div(rows, 64) == head, transposed, jnp.zeros_like(transposed))

def head_lanes(values, head):
    return jnp.where(lax.div(lane_of(values.shape), 64) == head, values, jnp.zeros_like(values))

def scores_of(keys, queries_turned, bias):
    scores = product_of(keys, queries_turned, ((1,), (0,)))
    return scores + jnp.concatenate([bias] * (scores.shape[1] // 128), axis=1)

def attend_kernel(queries, own, other, bias, context, log_total):
    query_turned = queries[...].T
    keys = jnp.concatenate([own[0], other[0]], axis=0)
    value_turned = jnp.concatenate([own[1].T, other[1].T], axis=1)
    parts, logs = [], []
    for head in range(2):
        scores = scores_of(keys, head_rows(query_turned, head), bias[...])
        highest = jnp.max(scores, axis=0, keepdims=True)
        weights = jnp.exp(scores - highest)
        total = jnp.sum(weights, axis=0, keepdims=True)
        part = product_of(value_turned[64 * head : 64 * head + 64], low(weights), ((1,), (0,)))
        parts.append(part / total)
        logs.append(highest + jnp.log(total))
    context[...] = low(jnp.concatenate(parts, axis=0)).T
    log_total[0] = jnp.concatenate(logs + logs * 3, axis=0)

def attend(queries, own, other, bias):
    count, width = queries.shape
    pairs = width // 128
    column = pl.BlockSpec((count, 128), lambda i: (0, i))
    double = pl.BlockSpec((2, count, 128), lambda i: (0, 0, i))
    return pl.pallas_call(
        attend_kernel,
        grid=(pairs,),
        out_shape=[jax.ShapeDtypeStruct((count, width), jnp.bfloat16), jax.ShapeDtypeStruct((pairs, 8, count), jnp.float32)],
        in_specs=[column, double, double, pl.BlockSpec((2 * count, 128), lambda i: (0, 0))],
        out_specs=[column, pl.BlockSpec((1, 8, count), lambda i: (i, 0, 0))],
        compiler_params=pltpu.CompilerParams(vmem_limit_bytes=40 * 1024 * 1024),
        name="attend",
    )(queries, own, other, bias)

def attend_back_kernel(queries, own, other, bias, grad, context, log_total, cosine, sine, grad_query, grad_own, grad_other):
    count = queries.shape[0]
    query_turned, grad_turned = queries[...].T, grad[...].T
    inner = (grad[...].astype(jnp.float32) * context[...].astype(jnp.float32)).T
    query_parts = [None, None]
    for half, (pair, result) in enumerate(((own, grad_own), (other, grad_other))):
        keys, values = pair[0], pair[1]
        key_turned = keys.T
        grad_keys, grad_values = None, None
        window = pl.ds(half * count, count)
        for head in range(2):
            lanes_of_head = slice(64 * head, 64 * head + 64)
            scores = scores_of(keys, head_rows(query_turned, head), bias[window])
            weights = jnp.exp(scores - log_total[0, head : head + 1])
            grad_weights = product_of(values, head_rows(grad_turned, head), ((1,), (0,)))
            inner_row = jnp.sum(inner[lanes_of_head], axis=0, keepdims=True)
            grad_scores = low(weights * (grad_weights - inner_row))
            value_part = product_of(low(weights), head_lanes(grad[...], head), ((1,), (0,)))
            key_part = product_of(grad_scores, head_lanes(queries[...], head), ((1,), (0,)))
            query_part = product_of(key_turned[lanes_of_head], grad_scores, ((1,), (0,)))
            grad_values = value_part if head == 0 else grad_values + value_part
            grad_keys = key_part if head == 0 else grad_keys + key_part
            query_parts[head] = query_part if half == 0 else query_parts[head] + query_part
        result[0] = turned(grad_keys, cosine[window], -sine[window]).astype(result.dtype)
        result[1] = grad_values.astype(result.dtype)
    grad_rows = jnp.concatenate(query_parts, axis=0).T * SCORE_SCALE
    own_rows = pl.ds(0, count)
    grad_query[...] = low(turned(grad_rows, cosine[own_rows], -sine[own_rows]))

def attend_back(queries, own, other, bias, grad, context, log_total, cosine, sine):
    count, width = queries.shape
    pairs = width // 128
    column = pl.BlockSpec((count, 128), lambda i: (0, i))
    double = pl.BlockSpec((2, count, 128), lambda i: (0, 0, i))
    table = pl.BlockSpec((2 * count, 128), lambda i: (0, 0))
    return pl.pallas_call(
        attend_back_kernel,
        grid=(pairs,),
        out_shape=[
            jax.ShapeDtypeStruct((count, width), jnp.bfloat16),
            jax.ShapeDtypeStruct((2, count, width), jnp.float32),
            jax.ShapeDtypeStruct((2, count, width), jnp.bfloat16),
        ],
        in_specs=[column, double, double, table, column, column, pl.BlockSpec((1, 8, count), lambda i: (i, 0, 0)), table, table],
        out_specs=[column, double, double],
        compiler_params=pltpu.CompilerParams(vmem_limit_bytes=48 * 1024 * 1024),
        name="attend_back",
    )(queries, own, other, bias, grad, context, log_total, cosine, sine)

def feed_kernel(rows, cotangent, in_weight, out_weight, result, grad_rows, grad_in, grad_out):
    height = out_weight.shape[1]
    @pl.when(pl.program_id(0) == 0)
    def _():
        result[...] = jnp.zeros_like(result)
        grad_rows[...] = jnp.zeros_like(grad_rows)
    gate = product_of(in_weight[0, 0:height], rows[...], ((1,), (1,)))
    up = product_of(in_weight[0, height:], rows[...], ((1,), (1,)))
    grad_hidden = product_of(out_weight[0], cotangent[...], ((1,), (1,)))
    below = 0.5 + 0.5 * lax.erf(gate * math.sqrt(0.5))
    active = gate * below
    hidden = low(active * up)
    slope = below + gate * jnp.exp(-0.5 * gate * gate) * (1.0 / math.sqrt(2.0 * math.pi))
    grad_gate = low(grad_hidden * up * slope)
    grad_up = low(grad_hidden * active)
    grad_out[0] = low(product_of(hidden, cotangent[...], ((1,), (0,))))
    grad_in[0, 0:height] = low(product_of(grad_gate, rows[...], ((1,), (0,))))
    grad_in[0, height:] = low(product_of(grad_up, rows[...], ((1,), (0,))))
    result[...] += product_of(hidden, out_weight[0], ((0,), (0,)))
    grad_rows[...] += product_of(grad_gate, in_weight[0, 0:height], ((0,), (0,)))
    grad_rows[...] += product_of(grad_up, in_weight[0, height:], ((0,), (0,)))

def feed(rows, cotangent, in_weight, out_weight):
    count, width = rows.shape
    groups, height, _ = out_weight.shape
    whole = pl.BlockSpec((count, width), lambda i: (0, 0))
    block = lambda size: pl.BlockSpec((1, size, width), lambda i: (i, 0, 0))
    return pl.pallas_call(
        feed_kernel,
        grid=(groups,),
        out_shape=[
            jax.ShapeDtypeStruct((count, width), jnp.float32),
            jax.ShapeDtypeStruct((count, width), jnp.float32),
            jax.ShapeDtypeStruct(in_weight.shape, jnp.bfloat16),
            jax.ShapeDtypeStruct(out_weight.shape, jnp.bfloat16),
        ],
        in_specs=[whole, whole, block(2 * height), block(height)],
        out_specs=[whole, whole, block(2 * height), block(height)],
        compiler_params=pltpu.CompilerParams(vmem_limit_bytes=60 * 1024 * 1024),
        name="feed",
    )(rows, cotangent, in_weight, out_weight)


def turn(block):
    return block.transpose(*range(1, block.ndim), 0).reshape(-1, block.shape[0])


def turn_back(rows, like):
    rows = rows.reshape(*like.shape[1:], like.shape[0])
    return rows.transpose(rows.ndim - 1, *range(rows.ndim - 1))


def orthogonal_steps(blocks, gain_part):
    tensor_count = lax.axis_size("tensor")
    heights = [block.shape[0] for block in blocks]
    row_count = blocks[0].shape[1]
    first_row = lax.axis_index("dp") * row_count
    gain_grad = lax.psum(gain_part, BOTH)
    widest = max(heights)
    stacked = jnp.stack(
        [jnp.pad(block.T, ((0, 0), (0, widest - block.shape[0]))) for block in blocks]
    )
    owned = lax.all_to_all(stacked, "tensor", split_axis=0, concat_axis=0, tiled=True)
    whole = lax.all_gather(owned, "dp", axis=1, tiled=True)
    mean, rest = newton_schulz(einsum("tik,tjk->ij", whole, whole))
    own_rows = lax.dynamic_slice_in_dim(rest, first_row, row_count, 0)
    own_whole = lax.dynamic_slice_in_dim(whole, first_row, row_count, 1)
    step_rows = low(einsum("ij,tjk->tik", low(own_rows), whole) + mean * own_whole)
    returned = lax.all_to_all(step_rows, "tensor", split_axis=0, concat_axis=0, tiled=True)
    return ([returned[index, :, :height].T for index, height in enumerate(heights)], gain_grad)


def view_of(block):
    if block.shape[-1] % 128:
        return turn(block)
    return block.transpose(1, 0, 2) if block.ndim == 3 else block


def unview(view, like):
    if like.shape[-1] % 128:
        return turn_back(view, like)
    return view.transpose(1, 0, 2) if like.ndim == 3 else view


def on_device(
    inputs,
    cotangent,
    lengths,
    qkv_weight,
    attn_out_weight,
    ffn_in_weight,
    ffn_out_weight,
    norm_gains,
    qkv_moment,
    attn_out_moment,
    ffn_in_moment,
    ffn_out_moment,
    gain_first,
    gain_second,
):
    tensor_count = lax.axis_size("tensor")
    dp_count = lax.axis_size("dp")
    dp_index = lax.axis_index("dp")
    tensor_index = lax.axis_index("tensor")
    core = dp_index % 2
    odd = tensor_index % 2 == 1
    upper = tensor_index >= tensor_count // 2
    lists = exchange_lists(dp_count // 2, tensor_count)
    weights = (qkv_weight, attn_out_weight, ffn_in_weight, ffn_out_weight)
    row_count = qkv_weight.shape[0]

    width = inputs.shape[3]
    local_rows = 2 * inputs.shape[2]
    fits = (tensor_count, dp_count, row_count, width) == (4, 8, 128, 1024)
    positions = jnp.concatenate(
        [core * local_rows + jnp.arange(local_rows), (1 - core) * local_rows + jnp.arange(local_rows)]
    )
    shards = weight_shards(weights)
    if fits:
        sizes = lengths.astype(jnp.float32)
        sizes = jnp.broadcast_to(jnp.pad(sizes, ((0, 6), (0, 0))), (8, 128))
        exponents = np.arange(HEAD_DIM // 2, dtype=np.float32) / np.float32(HEAD_DIM // 2)
        frequency = np.power(np.float32(ROPE_BASE), -exponents).astype(np.float32)
        frequency = jnp.asarray(np.tile(frequency, (8, 4)))
        outs = forward(shards, inputs[:, 0], cotangent[:, 0], sizes, norm_gains, frequency, 1)
        wholes, (rows_low, cotangent_low) = outs[:6], outs[6:8]
        low_one, queries, own, other, context, log_total, bias, middle, low_two = outs[8:17]
        cosine, sine = outs[17:]
    else:
        cosine, sine = rotary(positions)
        wholes = gather_weights(shards)
        rows_low = to_sequences(inputs[:, 0], lists, odd, upper)
        cotangent_low = to_sequences(cotangent[:, 0], lists, odd, upper)
    query_all, key_all, value_all, attn_all, ffn_in_all, ffn_out_all = wholes
    attn_rows = attn_all.reshape(-1, width)
    rows_in = rows_low.astype(jnp.float32)
    grad_rows = cotangent_low.astype(jnp.float32)
    normed_one, inverse_one, scaled_one = layer_norm_parts(rows_in, norm_gains[0])
    if not fits:
        own_lengths = swap_partner(lengths)
        both_lengths = jnp.where(
            core == 0,
            jnp.concatenate([lengths, own_lengths], 1),
            jnp.concatenate([own_lengths, lengths], 1),
        )
        length = lax.dynamic_index_in_dim(both_lengths.reshape(-1), tensor_index, 0, keepdims=False)
        bias = jnp.where(positions < length, 0.0, MASK_VALUE).astype(jnp.float32)
        bias = jnp.broadcast_to(bias[:, None], (positions.shape[0], 128))
        low_one = low(scaled_one)
        queries, own = project(
            low_one, query_all, key_all, value_all, cosine[:local_rows], sine[:local_rows]
        )
        other = swap_partner(own)
        context, log_total = attend(queries, own, other, bias)
        middle = rows_in + einsum("sk,kn->sn", context, attn_rows)
    normed_two, inverse_two, scaled_two = layer_norm_parts(middle, norm_gains[1])
    if not fits:
        low_two = low(scaled_two)
    if fits:
        outs = backward(
            (attn_all, ffn_in_all, ffn_out_all),
            low_two,
            cotangent_low,
            middle,
            queries,
            own,
            other,
            context,
            low_one,
            bias,
            log_total,
            cosine,
            sine,
            norm_gains,
            2,
        )
        sums, (grad_query, grad_pair, outputs, grad_middle, gain_two) = outs[:4], outs[4:]
    else:
        ffn_branch, grad_scaled_two, grad_ffn_in, grad_ffn_out = feed(
            low_two, cotangent_low, ffn_in_all, ffn_out_all
        )
        result = low(middle + ffn_branch)
        grad_from_two, gain_two = layer_norm_back(
            grad_scaled_two, normed_two, inverse_two, norm_gains[1]
        )
        grad_middle = grad_rows + grad_from_two
        grad_branch = low(grad_middle)
        grad_context = low(einsum("sn,kn->sk", grad_branch, attn_rows))
        grad_attn_out = low(einsum("sk,sn->kn", context, grad_branch)).reshape(attn_all.shape)
        grad_query, grad_own, grad_other = attend_back(
            queries, own, other, bias, grad_context, context, log_total, cosine, sine
        )
        grad_pair = low(grad_own + swap_partner(grad_other).astype(jnp.float32))
    moments = (qkv_moment, attn_out_moment, ffn_in_moment, ffn_out_moment)
    grad_parts = (grad_query, grad_pair[0], grad_pair[1])
    weight_parts = [part.reshape(-1, width) for part in (query_all, key_all, value_all)]
    if fits:
        far = (*weight_parts, grad_query, grad_pair, rows_low, grad_middle)
        viewed = [view_of(moment) for moment in moments]
        steps, gain_grad, input_grad = optimize(sums, viewed, gain_two, norm_gains, far, 3)
        outs = settle(sums, steps, viewed, [view_of(weight) for weight in weights])
        new_moments, new_weights = (
            [unview(part, like) for part, like in zip(parts, moments)] for parts in outs
        )
    else:
        grad_scaled_one = sum(
            einsum("sk,kn->sn", part, weight) for part, weight in zip(grad_parts, weight_parts)
        )
        grad_from_one, gain_one = layer_norm_back(
            grad_scaled_one, normed_one, inverse_one, norm_gains[0]
        )
        grads = [low(einsum("sk,sn->kn", part, low_one)) for part in grad_parts]
        grads = [grad.reshape(query_all.shape) for grad in grads]
        sums = reduce_grads(grads + [grad_attn_out, grad_ffn_in, grad_ffn_out])
        sums = [jnp.concatenate(sums[:3])] + list(sums[3:])
        outputs = from_sequences(result, lists, odd, upper)
        input_grad = from_sequences(low(grad_middle + grad_from_one), lists, odd, upper)
        turned_sums = [turn_back(part, moment) for part, moment in zip(sums, moments)]
        new_moments = [MOMENTUM * moment + part for moment, part in zip(moments, turned_sums)]
        steps, gain_grad = orthogonal_steps(
            [low(turn(moment)) for moment in new_moments], jnp.stack([gain_one, gain_two])
        )
        new_weights = [
            weight.astype(jnp.float32) * (1.0 - MUON_RATE * DECAY_RATE)
            - MUON_RATE
            * 0.2
            * math.sqrt(step.shape[0] * tensor_count)
            * turn_back(step, weight).astype(jnp.float32)
            for weight, step in zip(weights, steps)
        ]
    outputs, input_grad = outputs[:, None], input_grad[:, None].astype(jnp.float32)
    gain_first_new = BETA_ONE * gain_first + (1.0 - BETA_ONE) * gain_grad
    gain_second_new = BETA_TWO * gain_second + (1.0 - BETA_TWO) * gain_grad * gain_grad
    first_hat = gain_first_new / (1.0 - BETA_ONE**STEP)
    second_hat = gain_second_new / (1.0 - BETA_TWO**STEP)
    norm_gains_new = norm_gains - ADAM_RATE * (
        first_hat / (jnp.sqrt(second_hat) + ADAM_EPS) + DECAY_RATE * norm_gains
    )
    return (
        outputs,
        input_grad,
        new_moments[0],
        new_weights[0],
        new_moments[1],
        new_weights[1],
        new_moments[2],
        new_weights[2],
        new_moments[3],
        new_weights[3],
        gain_first_new,
        gain_second_new,
        norm_gains_new,
    )


def solution(mesh):
    in_specs = (
        P(None, "dp", "tensor", None),
        P(None, "dp", "tensor", None),
        P(None, "dp"),
        P("dp", None, "tensor"),
        P("dp", "tensor"),
        P("dp", None, "tensor"),
        P("dp", "tensor"),
        P(),
        P("dp", None, "tensor"),
        P("dp", "tensor"),
        P("dp", None, "tensor"),
        P("dp", "tensor"),
        P(),
        P(),
    )
    out_specs = (
        P(None, "dp", "tensor", None),
        P(None, "dp", "tensor", None),
        P("dp", None, "tensor"),
        P("dp", None, "tensor"),
        P("dp", "tensor"),
        P("dp", "tensor"),
        P("dp", None, "tensor"),
        P("dp", None, "tensor"),
        P("dp", "tensor"),
        P("dp", "tensor"),
        P(),
        P(),
        P(),
    )
    return jax.shard_map(
        on_device, mesh=mesh, in_specs=in_specs, out_specs=out_specs, check_vma=False
    )
```
